32 devices in a mesh: wide: 8 (over z, x), narrow: 4 (over y, core).
Axes of the slice: x: 2, y: 2, z: 4, core: 2. Of those that a mesh axis runs over, the one named last changes fastest.
Arguments:
- latents: float32 [128, 4096], P(('wide', 'narrow')), may hold values from -6 to 6
- noise: float32 [128, 4096], P(('wide', 'narrow')), may hold values from -6 to 6
- timesteps: int32 [128], P(('wide', 'narrow')), may hold values from 0 to 999
- labels: int32 [128], P(('wide', 'narrow')), may hold values from 0 to 999
- routes: int32 [32768, 2], P(('wide', 'narrow')), may hold values from 0 to 15, all different within a row; in each aligned block of 1024 rows (0 to 1023, 1024 to 2047, ...) at most 1024 rows name the same one
- mats: float32 [384, 6296], P(('wide', 'narrow')), may hold values from -4 to 4
- up_weights: float32 [18, 384, 1536], P(None, ('wide', 'narrow')), may hold values from -0.3125 to 0.3125
- down_weights: float32 [18, 1536, 384], P(None, ('wide', 'narrow')), may hold values from -0.15625 to 0.15625
- biases: float32 [5760], P(('wide', 'narrow')), may hold values from -1.8 to 1.8
- mats_row: float32 [10, 384], P(None, ('wide', 'narrow')), may hold values from 1.5258789e-06 to 1.2207031e-05
- mats_col: float32 [6296], replicated, may hold values from 1.5258789e-06 to 0.09
- up_row: float32 [18, 384], P(None, ('wide', 'narrow')), may hold values from 1.5258789e-06 to 1.2207031e-05
- up_col: float32 [18, 1536], replicated, may hold values from 1.5258789e-06 to 1.2207031e-05
- down_row: float32 [18, 1536], P(None, ('wide', 'narrow')), may hold values from 1.5258789e-06 to 1.2207031e-05
- down_col: float32 [18, 384], replicated, may hold values from 1.5258789e-06 to 1.2207031e-05
- bias_state: float32 [5760], P(('wide', 'narrow')), may hold values from 1.5258789e-06 to 1.2207031e-05
Outputs:
- loss: float32 [], replicated
- mats_grad: float32 [384, 6296], P(('wide', 'narrow'))
- mats_new: float32 [384, 6296], P(('wide', 'narrow'))
- mats_copy: bfloat16 [384, 6296], P(('wide', 'narrow'))
- mats_row_new: float32 [10, 384], P(None, ('wide', 'narrow'))
- mats_col_new: float32 [6296], replicated
- up_grad: float32 [18, 384, 1536], P(None, ('wide', 'narrow'))
- up_new: float32 [18, 384, 1536], P(None, ('wide', 'narrow'))
- up_copy: bfloat16 [18, 384, 1536], P(None, ('wide', 'narrow'))
- up_row_new: float32 [18, 384], P(None, ('wide', 'narrow'))
- up_col_new: float32 [18, 1536], replicated
- down_grad: float32 [18, 1536, 384], P(None, ('wide', 'narrow'))
- down_new: float32 [18, 1536, 384], P(None, ('wide', 'narrow'))
- down_copy: bfloat16 [18, 1536, 384], P(None, ('wide', 'narrow'))
- down_row_new: float32 [18, 1536], P(None, ('wide', 'narrow'))
- down_col_new: float32 [18, 384], replicated
- bias_grad: float32 [5760], P(('wide', 'narrow'))
- bias_new: float32 [5760], P(('wide', 'narrow'))
- bias_copy: bfloat16 [5760], P(('wide', 'narrow'))
- bias_state_new: float32 [5760], P(('wide', 'narrow'))
The draws below stay inside these ranges and needn't reach their ends.
Inputs may be any that keep to these rules, and one draw needn't show every extreme that they name: `routes`: each patch names two different experts.
All inputs are finite; a program needn't handle non-finite values.
Results may differ from the reference program's by a relative error of at most 0.0055.
The reference program's roundings to bfloat16 on the way count: a program that leaves them out, or rounds other values in their place, can miss the bound.
Values may be sent and summed in bfloat16 or wider, within the bound.
A program may use at most 448 MiB of HBM per device.

```python
import math
import jax
import jax.numpy as jnp
import numpy as np
from jax import lax

D = 384
HEADS = 6
HD = 64
FF = 1536
EXPERTS = 16
SHARED = 2
PD = 16
GRID = 16
FREQ = 256
CLASSES = 1000
LAT_DEV = 4
BLK = 128
NMAT = 10
PATCHES = 256
ITEMS = 128
TOK_DEV = 1024
TOKENS = 32768
NSTACK = 18
KIN = 6296
NB = 5760


def draw_mats(key, part):
    widths = [3 * D, D, 6 * D, D, 2 * D, EXPERTS, PD, PD, FREQ, CLASSES]
    spreads = [1.0 / math.sqrt(D), 4.0 / math.sqrt(D), 1.0 / math.sqrt(D), 1.0 / math.sqrt(D), 1.0 / math.sqrt(D), 0.7 / math.sqrt(D), 1.0 / math.sqrt(D), 1.0 / math.sqrt(PD), 1.0 / math.sqrt(FREQ), 1.0]
    column_scale = jnp.concatenate([jnp.full((width,), spread, jnp.float32) for width, spread in zip(widths, spreads)])
    values = jnp.clip(jax.random.normal(key, (D, KIN), jnp.float32), -4.0, 4.0)
    return values * column_scale[None, :]


def draw_mats_col(key, part):
    widths = [3 * D, D, 6 * D, D, 2 * D, EXPERTS, PD, PD, FREQ]
    centres = [0.0003, 0.0003, 0.0003, 0.0003, 0.0003, 1e-05, 0.02, 0.0003, 0.0003]
    centre = jnp.concatenate([jnp.full((width,), level, jnp.float32) for width, level in zip(widths, centres)])
    key_general = jax.random.fold_in(key, 11)
    key_table = jax.random.fold_in(key, 12)
    low_factor = 0.5
    high_factor = 2.0
    fractions = jax.random.uniform(key_general, (centre.shape[0],), jnp.float32)
    general = centre * jnp.exp(math.log(low_factor) + fractions * (math.log(high_factor) - math.log(low_factor)))
    table_low = 0.05 / TOKENS
    table_high = 0.4 / TOKENS
    table_fractions = jax.random.uniform(key_table, (CLASSES,), jnp.float32)
    table_part = table_low * jnp.exp(table_fractions * math.log(table_high / table_low))
    table_part = jnp.clip(table_part, table_low, table_high)
    general = jnp.clip(general, 2.5e-06, 0.08)
    return jnp.concatenate([general, table_part], 0).astype(jnp.float32)


def with_ends(array, own_key, low, largest):
    longest = array.shape.index(max(array.shape))
    spots = []
    for shift in (0, 1):
        where = [jax.random.randint(jax.random.fold_in(own_key, axis), (), 0, length) for axis, length in enumerate(array.shape)]
        where[longest] = (where[longest] + shift) % array.shape[longest]
        spots.append(tuple(where))
    return array.at[spots[0]].set(low).at[spots[1]].set(largest)


def block_scale(key, shape, cuts, least, high):
    loudness, own = 1.0, jax.random.fold_in(key, 6)
    for axis_at, shards_of in cuts:
        draws = jnp.exp(jax.random.uniform(jax.random.fold_in(own, axis_at), (shards_of,), jnp.float32, least / len(cuts), high / len(cuts)))
        loudness = loudness * jnp.repeat(draws, shape[axis_at] // shards_of).reshape([-1 if axis == axis_at else 1 for axis in range(len(shape))])
    return loudness


def assign_block(key, own, number, rows, amount, top, limit, skew):
    order = jax.random.permutation(key, amount)
    heavy_load, usual = shares(amount, rows * top, limit, skew, True), shares(amount, rows * top, limit, skew, False)
    places = jnp.arange(amount)

    def named(tallies, rotation):
        used = int((tallies > 0).sum())
        fixed = max(1, used // 4)
        moved = fixed + (places - fixed + rotation * (used - fixed)) % max(1, amount - fixed)
        return jnp.zeros((amount,), jnp.int32).at[order[jnp.where(places < fixed, places, moved)]].set(jnp.asarray(tallies, jnp.int32))

    tallies = jnp.where(number % 4 == 0, named(heavy_load, number // 4), named(usual, number - number // 4 - 1))
    mixed = jax.random.permutation(jax.random.fold_in(own, 3), amount)
    source_of, taker = mixed[0:amount // 2 * 2:2], mixed[1:amount // 2 * 2:2]
    slack = jnp.minimum(tallies[source_of] - 1, limit - tallies[taker]) // 2
    slack = jnp.where((source_of == order[0]) | (taker == order[0]) | (tallies[taker] == 0), 0, jnp.maximum(slack, 0))
    moved = jax.random.randint(jax.random.fold_in(own, 4), (amount // 2,), 0, 1 << 20) % (slack + 1)
    tallies = tallies.at[source_of].add(-moved).at[taker].add(moved)
    members = jnp.searchsorted(jnp.cumsum(tallies), jnp.arange(rows * top), side="right").astype(jnp.int32)
    grid = members.reshape(top, rows).T
    grid = grid[jax.random.permutation(jax.random.fold_in(own, 1), rows)]
    rotation = jax.random.randint(jax.random.fold_in(own, 2), (rows, 1), 0, top)
    return jnp.take_along_axis(grid, (jnp.arange(top)[None, :] + rotation) % top, axis=1)


def shares(number_of, total, limit, skew, full):
    portions = [(1 << 20) // math.isqrt(standing ** skew) + 1 for standing in range(1, number_of + 1)]
    largest = limit if full else min(limit, max(-(-total // number_of), total * portions[0] // sum(portions)))
    least = 1 if total - largest >= number_of - 1 else 0
    given, surplus = [largest] + [least] * (number_of - 1), total - largest - least * (number_of - 1)
    while surplus > 0:
        movable = [i for i in range(1, number_of) if given[i] < largest] or [i for i in range(1, number_of) if given[i] < limit]
        whole, left = sum([portions[i] for i in movable]), surplus
        for i in movable:
            addition = min(limit - given[i], max(1, left * portions[i] // whole), surplus)
            given[i] = given[i] + addition
            surplus = surplus - addition
    return np.array(given)


def bell_draw(rng, extent, deviation, reach, cuts=(), kind=jnp.bfloat16):
    gain = block_scale(rng, extent, cuts, -0.22, 0.18) if cuts else 1.0
    array = jax.random.normal(rng, extent, jnp.float32) * deviation * gain
    return jnp.minimum(jnp.maximum(array, -reach), reach).astype(kind)


def setup_inputs(seed: int = 0) -> dict:
    keys = jax.random.split(jax.random.key(seed), 17)
    latents = bell_draw(keys[0], (ITEMS, PATCHES * PD), 1.0, 6.0, ((0, 32),), jnp.float32)
    noise = bell_draw(keys[1], (ITEMS, PATCHES * PD), 1.0, 6.0, ((0, 32),), jnp.float32)
    timesteps = with_ends(jax.random.randint(keys[2], (ITEMS,), 0, 1000), jax.random.fold_in(keys[2], 1), 0, 999).astype(jnp.int32)
    labels = with_ends(jax.random.randint(keys[3], (ITEMS,), 0, CLASSES), jax.random.fold_in(keys[3], 1), 0, CLASSES - 1).astype(jnp.int32)
    routes_keys = jax.random.split(jax.random.fold_in(keys[4], 1), TOKENS // TOK_DEV)
    routes_turns = jax.random.permutation(jax.random.fold_in(keys[4], 3), TOKENS // TOK_DEV)
    routes = jax.vmap(lambda own, number: assign_block(jax.random.fold_in(keys[4], 2), own, number, TOK_DEV, EXPERTS, 2, min(TOK_DEV, 16 * TOK_DEV // EXPERTS), 2))(routes_keys, routes_turns).reshape((TOKENS, 2))
    mats = draw_mats(jax.random.fold_in(keys[16], 71), 0)
    up_weights = bell_draw(keys[6], (NSTACK, D, FF), D ** -0.5, 0.3125, ((1, 32),), jnp.float32)
    down_weights = bell_draw(keys[7], (NSTACK, FF, D), FF ** -0.5, 0.15625, ((1, 32),), jnp.float32)
    biases = bell_draw(keys[8], (NB,), 0.3, 1.8, ((0, 32),), jnp.float32)
    mats_row = jnp.clip(jnp.exp(math.log(1.220703143189894e-05) - 2.0794415 * jax.random.uniform(keys[9], (NMAT, D), jnp.float32) ** block_scale(keys[9], (NMAT, D), ((1, 32),), -0.2, 0.2)), 1.5258789289873675e-06, 1.220703143189894e-05)
    mats_col = draw_mats_col(jax.random.fold_in(keys[16], 71), 0)
    up_row = jnp.clip(jnp.exp(math.log(1.220703143189894e-05) - 2.0794415 * jax.random.uniform(keys[11], (NSTACK, D), jnp.float32) ** block_scale(keys[11], (NSTACK, D), ((1, 32),), -0.2, 0.2)), 1.5258789289873675e-06, 1.220703143189894e-05)
    up_col = jnp.clip(jnp.exp(jax.random.uniform(keys[12], (NSTACK, FF), jnp.float32, math.log(1.5258789289873675e-06), math.log(1.220703143189894e-05))), 1.5258789289873675e-06, 1.220703143189894e-05)
    down_row = jnp.clip(jnp.exp(math.log(1.220703143189894e-05) - 2.0794415 * jax.random.uniform(keys[13], (NSTACK, FF), jnp.float32) ** block_scale(keys[13], (NSTACK, FF), ((1, 32),), -0.2, 0.2)), 1.5258789289873675e-06, 1.220703143189894e-05)
    down_col = jnp.clip(jnp.exp(jax.random.uniform(keys[14], (NSTACK, D), jnp.float32, math.log(1.5258789289873675e-06), math.log(1.220703143189894e-05))), 1.5258789289873675e-06, 1.220703143189894e-05)
    bias_state = jnp.clip(jnp.exp(math.log(1.220703143189894e-05) - 2.0794415 * jax.random.uniform(keys[15], (NB,), jnp.float32) ** block_scale(keys[15], (NB,), ((0, 32),), -0.2, 0.2)), 1.5258789289873675e-06, 1.220703143189894e-05)
    return {"latents": latents, "noise": noise, "timesteps": timesteps, "labels": labels, "routes": routes, "mats": mats, "up_weights": up_weights, "down_weights": down_weights, "biases": biases, "mats_row": mats_row, "mats_col": mats_col, "up_row": up_row, "up_col": up_col, "down_row": down_row, "down_col": down_col, "bias_state": bias_state}


@jax.custom_vjp
def low(v):
    return lax.optimization_barrier(v.astype(jnp.bfloat16)).astype(jnp.float32)

@jax.custom_vjp
def low_back(v):
    return v

def low_keep(v):
    return (low(v), None)

def low_pass(kept, grad):
    return (grad,)

def back_keep(v):
    return (v, None)

def back_low(kept, grad):
    return (low(grad),)
low.defvjp(low_keep, low_pass)
low_back.defvjp(back_keep, back_low)
eps_norm = 1e-06
eps_fact = 1e-30
decay = 0.5
clip_level = 0.1
learn_rate = 0.5

def column_widths():
    return [3 * D, D, 6 * D, D, 2 * D, EXPERTS, PD, PD, FREQ, CLASSES]

def bias_widths():
    return [3 * D, D, 6 * D, D, D, D, 2 * D]

def cut_pieces(source, widths, along):
    pieces = []
    start = 0
    for width in widths:
        pieces.append(lax.slice_in_dim(source, start, start + width, axis=along))
        start = start + width
    return pieces

def matmul(left, right):
    return jnp.dot(left, right, precision=lax.Precision.HIGHEST, preferred_element_type=jnp.float32)

def sincos(coords, width):
    omegas = 1.0 / 10000.0 ** (jnp.arange(width // 2, dtype=jnp.float32) / (width / 2.0))
    angles = coords[:, None] * omegas[None, :]
    return jnp.concatenate([jnp.sin(angles), jnp.cos(angles)], 1)

def positions():
    places = jnp.arange(PATCHES, dtype=jnp.int32)
    grid_row = (places // GRID).astype(jnp.float32)
    grid_col = (places % GRID).astype(jnp.float32)
    return jnp.concatenate([sincos(grid_row, D // 2), sincos(grid_col, D // 2)], 1)

def time_features(steps_f):
    half_width = FREQ // 2
    freq_rates = jnp.exp(-math.log(10000.0) * jnp.arange(half_width, dtype=jnp.float32) / half_width)
    angles = steps_f[:, None] * freq_rates[None, :]
    return jnp.concatenate([jnp.cos(angles), jnp.sin(angles)], 1)

def noise_level(steps_f):
    alpha_bar = jnp.cos((steps_f / 1000.0 + 0.008) / 1.008 * (math.pi / 2)) ** 2
    return (jnp.sqrt(alpha_bar), jnp.sqrt(1.0 - alpha_bar))

def layer_norm(source):
    centred = source - lax.optimization_barrier(jnp.mean(source, -1, keepdims=True))
    return centred * lax.rsqrt(lax.optimization_barrier(jnp.mean(centred * centred, -1, keepdims=True)) + eps_norm)

def gelu_tanh(values):
    return jax.nn.gelu(values, approximate=True)

def pack_slots(routes):
    assigned = routes.shape[0] * 2
    flat_ids = routes.reshape(-1)
    route_hot = (flat_ids[:, None] == jnp.arange(EXPERTS, dtype=jnp.int32)[None, :]).astype(jnp.int32)
    counts = lax.optimization_barrier(jnp.sum(route_hot, 0, dtype=jnp.int32))
    rank_in = lax.optimization_barrier(jnp.sum((jnp.cumsum(route_hot, 0, dtype=jnp.int32) - route_hot) * route_hot, 1, dtype=jnp.int32))
    padded = (counts + BLK - 1) // BLK * BLK
    slot_ends = jnp.cumsum(padded, dtype=jnp.int32)
    starts = slot_ends - padded
    slot_of = lax.optimization_barrier(jnp.sum(route_hot * starts[None, :], 1, dtype=jnp.int32)) + rank_in
    num_slots = assigned + EXPERTS * BLK
    slot_token = jnp.zeros((num_slots,), jnp.int32).at[slot_of].set(jnp.arange(assigned, dtype=jnp.int32) // 2)
    block_first = jnp.arange(num_slots // BLK, dtype=jnp.int32) * BLK
    block_owner = jnp.minimum(lax.optimization_barrier(jnp.sum((slot_ends[None, :] <= block_first[:, None]).astype(jnp.int32), 1, dtype=jnp.int32)), EXPERTS - 1)
    return (slot_of, slot_token, block_owner)

def group_loss(weights, group_data):
    mats, up_w, down_w, bias_all = weights
    latents, noise, timesteps, labels, routes = group_data
    w_qkv, w_proj, w_mod, w_time2, w_final, w_router, w_head, w_patch, w_time1, w_table = cut_pieces(mats, column_widths(), 1)
    b_qkv, b_proj, b_mod, b_patch, b_time1, b_time2, b_final = cut_pieces(bias_all, bias_widths(), 0)
    num_latents = latents.shape[0]
    rows_here = num_latents * PATCHES
    steps_f = timesteps.astype(jnp.float32)
    signal, spread = noise_level(steps_f)
    noisy = signal[:, None] * latents + spread[:, None] * noise
    patches = low(noisy.reshape(rows_here, PD))
    embedded = low_back(matmul(patches, w_patch.T)).reshape(num_latents, PATCHES, D) + b_patch + positions()[None]
    freq_low = low(time_features(steps_f))
    pre_time = low_back(matmul(freq_low, w_time1.T)) + b_time1
    hid_time = low(jax.nn.silu(pre_time))
    label_hot = (labels[:, None] == jnp.arange(CLASSES, dtype=jnp.int32)[None, :]).astype(jnp.float32)
    cond = low_back(matmul(hid_time, w_time2)) + b_time2 + matmul(label_hot, w_table.T)
    cond_act = low(jax.nn.silu(cond))
    modulation = low_back(matmul(cond_act, w_mod)) + b_mod
    final_mod = low_back(matmul(cond_act, w_final)) + b_final
    shift_attn, scale_attn, gate_attn, shift_moe, scale_moe, gate_moe = [member[:, None, :] for member in jnp.split(modulation, 6, 1)]
    shift_fin, scale_fin = [member[:, None, :] for member in jnp.split(final_mod, 2, 1)]
    attn_in = low((layer_norm(embedded) * (1.0 + scale_attn) + shift_attn).reshape(rows_here, D))
    qkv_out = low(low_back(matmul(attn_in, w_qkv)) + b_qkv).reshape(num_latents, PATCHES, 3, HEADS, HD)
    scores = low_back(jnp.einsum('lqhd,lkhd->lhqk', qkv_out[:, :, 0], qkv_out[:, :, 1], precision=lax.Precision.HIGHEST)) * HD ** (-0.5)
    probs = jax.nn.softmax(scores, -1)
    attended = low(low_back(jnp.einsum('lhqk,lkhd->lqhd', low(probs), qkv_out[:, :, 2], precision=lax.Precision.HIGHEST))).reshape(rows_here, D)
    attn_out = (low_back(matmul(attended, w_proj)) + b_proj).reshape(num_latents, PATCHES, D)
    middle = embedded + gate_attn * attn_out
    moe_in = low((layer_norm(middle) * (1.0 + scale_moe) + shift_moe).reshape(rows_here, D))
    logits = low_back(matmul(moe_in, w_router))
    route_hot = (routes[:, :, None] == jnp.arange(EXPERTS, dtype=jnp.int32)[None, None, :]).astype(jnp.float32)
    gate_vals = jax.nn.softmax(lax.optimization_barrier(jnp.sum(route_hot * logits[:, None, :], 2)), -1)
    slot_of, slot_token, block_owner = pack_slots(routes)
    slot_rows = moe_in[slot_token].reshape(-1, BLK, D)

    def expert_block(inputs):
        row_block, owner_id = inputs
        pre_act = low_back(matmul(row_block, up_w[owner_id]))
        return low_back(matmul(low(gelu_tanh(pre_act)), down_w[owner_id]))
    expert_out = lax.map(jax.checkpoint(expert_block), (slot_rows, block_owner)).reshape(-1, D)
    routed = expert_out[slot_of].reshape(rows_here, 2, D)
    moe_out = lax.optimization_barrier(jnp.sum(gate_vals[:, :, None] * routed, 1))
    for shared_id in range(SHARED):
        pre_act = low_back(matmul(moe_in, up_w[EXPERTS + shared_id]))
        moe_out = moe_out + low_back(matmul(low(gelu_tanh(pre_act)), down_w[EXPERTS + shared_id]))
    final_state = middle + gate_moe * moe_out.reshape(num_latents, PATCHES, D)
    head_in = low((layer_norm(final_state) * (1.0 + scale_fin) + shift_fin).reshape(rows_here, D))
    predicted = low_back(matmul(head_in, w_head))
    errors = predicted - noise.reshape(rows_here, PD)
    return jnp.sum(errors * errors)

def adafactor_stack(master, grad, row_old, col_old):
    squares = grad * grad + eps_fact
    row_new = decay * row_old + (1.0 - decay) * lax.optimization_barrier(jnp.mean(squares, 2))
    col_new = decay * col_old + (1.0 - decay) * lax.optimization_barrier(jnp.mean(squares, 1))
    row_mean = lax.optimization_barrier(jnp.mean(row_new, 1))
    update = grad * lax.rsqrt(row_new[:, :, None] * col_new[:, None, :] / row_mean[:, None, None])
    update_rms = jnp.sqrt(lax.optimization_barrier(jnp.mean(update * update, (1, 2))))
    master_new = master - learn_rate * (update / jnp.maximum(1.0, update_rms / clip_level)[:, None, None])
    return (master_new, row_new, col_new)

def reference(latents, noise, timesteps, labels, routes, mats, up_weights, down_weights, biases, mats_row, mats_col, up_row, up_col, down_row, down_col, bias_state):
    groups = ITEMS // LAT_DEV
    grouped = (latents.reshape(groups, LAT_DEV, PATCHES * PD), noise.reshape(groups, LAT_DEV, PATCHES * PD), timesteps.reshape(groups, LAT_DEV), labels.reshape(groups, LAT_DEV), routes.reshape(groups, TOK_DEV, 2))

    def total_loss(masters):
        copies = tuple((low(master) for master in masters))

        def add_group(loss_sum, group_data):
            return (loss_sum + jax.checkpoint(group_loss)(copies, group_data), None)
        loss_sum, unused = lax.scan(add_group, jnp.zeros((), jnp.float32), grouped)
        return loss_sum / TOKENS
    loss_value, pull_back = jax.vjp(total_loss, (mats, up_weights, down_weights, biases))
    grad_mats, grad_up, grad_down, grad_bias = pull_back(jnp.ones((), jnp.float32))[0]
    widths = column_widths()
    master_pieces = cut_pieces(mats, widths, 1)
    grad_pieces = cut_pieces(grad_mats, widths, 1)
    col_pieces = cut_pieces(mats_col, widths, 0)
    new_pieces, row_list, col_list = ([], [], [])
    for piece_id in range(len(widths)):
        master_new, row_new, col_new = adafactor_stack(master_pieces[piece_id][None], grad_pieces[piece_id][None], mats_row[piece_id][None], col_pieces[piece_id][None])
        new_pieces.append(master_new[0])
        row_list.append(row_new[0])
        col_list.append(col_new[0])
    mats_new = jnp.concatenate(new_pieces, 1)
    up_new, up_row_new, up_col_new = adafactor_stack(up_weights, grad_up, up_row, up_col)
    down_new, down_row_new, down_col_new = adafactor_stack(down_weights, grad_down, down_row, down_col)
    bias_state_new = decay * bias_state + (1.0 - decay) * (grad_bias * grad_bias + eps_fact)
    bias_update = grad_bias * lax.rsqrt(bias_state_new)
    bias_rms = jnp.sqrt(jnp.mean(bias_update * bias_update))
    bias_new = biases - learn_rate * (bias_update / jnp.maximum(1.0, bias_rms / clip_level))
    return (loss_value, grad_mats, mats_new, mats_new.astype(jnp.bfloat16), jnp.stack(row_list, 0), jnp.concatenate(col_list, 0), grad_up, up_new, up_new.astype(jnp.bfloat16), up_row_new, up_col_new, grad_down, down_new, down_new.astype(jnp.bfloat16), down_row_new, down_col_new, grad_bias, bias_new, bias_new.astype(jnp.bfloat16), bias_state_new)
```

```python
import math
from types import SimpleNamespace

import jax
import jax.numpy as jnp
from jax import lax
from jax.experimental import pallas as pl
from jax.experimental.pallas import tpu as pltpu
from jax.sharding import PartitionSpec as P

WIDE = "wide"
NARROW = "narrow"
AXES = (WIDE, NARROW)
MESH_ID = pl.DeviceIdType.MESH

D = 384
HEADS = 6
HD = 64
FF = 1536
EXPERTS = 16
SHARED = 2
PD = 16
GRID = 16
FREQ = 256
CLASSES = 1000
BLK = 256
WIDE_PIECES = 8
NARROW_PIECES = 4
PIECE = 48
ROWS = 12
LAT_ROWS = 16
LAT_COLS = 1536
PATCHES = 256


eps_norm = 1e-06
eps_fact = 1e-30
decay = 0.5
clip_level = 0.1
learn_rate = 0.5

SQRT_2_PI = math.sqrt(2.0 / math.pi)
VMEM_ROOM = 56 * 1024 * 1024
REDUCE_ROOM = 60 * 1024 * 1024


def column_widths():
    return [3 * D, D, 6 * D, D, 2 * D, EXPERTS, PD, PD, FREQ, CLASSES]


def bias_widths():
    return [3 * D, D, 6 * D, D, D, D, 2 * D]


def cut_pieces(source, widths, along):
    pieces = []
    start = 0
    for width in widths:
        pieces.append(lax.slice_in_dim(source, start, start + width, axis=along))
        start = start + width
    return pieces


def product(left, right):
    return jnp.dot(left, right, preferred_element_type=jnp.float32)


def contract(left, right, left_dim, right_dim):
    return lax.dot_general(
        left, right, (((left_dim,), (right_dim,)), ((), ())), preferred_element_type=jnp.float32
    )


def gelu_tanh(values):
    return jax.nn.gelu(values, approximate=True)


def slope_back(function, source, grad_out):
    return jax.vjp(function, source)[1](grad_out)[0]


def layer_norm(source):
    centred = source - jnp.mean(source, -1, keepdims=True)
    inv_std = lax.rsqrt(jnp.mean(centred * centred, -1, keepdims=True) + eps_norm)
    return (centred * inv_std, inv_std)


def norm_back(grad_norm, normed, inv_std):
    return inv_std * (
        grad_norm
        - jnp.mean(grad_norm, -1, keepdims=True)
        - normed * jnp.mean(grad_norm * normed, -1, keepdims=True)
    )


def linear_back(grad_out, inputs, weight):
    grad_low = grad_out.astype(jnp.bfloat16)
    return (
        contract(inputs, grad_low, 0, 0),
        contract(grad_low, weight, 1, 1),
        jnp.sum(grad_out, 0),
    )


def sincos(coords, width):
    omegas = 1.0 / 10000.0 ** (jnp.arange(width // 2, dtype=jnp.float32) / (width / 2.0))
    angles = coords[:, None] * omegas[None, :]
    return jnp.concatenate([jnp.sin(angles), jnp.cos(angles)], 1)


def positions():
    places = jnp.arange(PATCHES, dtype=jnp.int32)
    grid_row = (places // GRID).astype(jnp.float32)
    grid_col = (places % GRID).astype(jnp.float32)
    return jnp.concatenate([sincos(grid_row, D // 2), sincos(grid_col, D // 2)], 1)


def time_features(steps_f):
    half_width = FREQ // 2
    freq_rates = jnp.exp(
        -math.log(10000.0) * jnp.arange(half_width, dtype=jnp.float32) / half_width
    )
    angles = steps_f[:, None] * freq_rates[None, :]
    return jnp.concatenate([jnp.cos(angles), jnp.sin(angles)], 1)


def noise_level(steps_f):
    alpha_bar = jnp.cos((steps_f / 1000.0 + 0.008) / 1.008 * (math.pi / 2)) ** 2
    return (jnp.sqrt(alpha_bar), jnp.sqrt(1.0 - alpha_bar))


def pack_slots(routes):
    ids = jnp.arange(EXPERTS, dtype=jnp.int32)[:, None]
    named = [(routes[:, k][None, :] == ids) for k in range(2)]
    either = (named[0] | named[1]).astype(jnp.bfloat16)
    rows_here = routes.shape[0]
    place = jnp.arange(rows_here, dtype=jnp.int32)
    before = (place[:, None] < place[None, :]).astype(jnp.bfloat16)
    rank_in = product(either, before)
    counts = jnp.sum(either.astype(jnp.float32), 1).astype(jnp.int32)
    padded = (counts + 7) // 8 * 8
    starts = jnp.sum(jnp.where(ids > ids.T, padded[None, :], 0), 1)
    slots = rank_in.astype(jnp.int32) + starts[:, None]
    slot_of = jnp.stack([jnp.sum(jnp.where(member, slots, 0), 0) for member in named], 0)
    return (slot_of, jnp.stack([starts, counts], 0))


def gelu_slope(values):
    inner = SQRT_2_PI * (values + 0.044715 * values * values * values)
    bend = jnp.tanh(inner)
    return (
        0.5 * values * (1.0 + bend),
        0.5 * (1.0 + bend)
        + 0.5
        * values
        * (1.0 - bend * bend)
        * SQRT_2_PI
        * (1.0 + 3.0 * 0.044715 * values * values),
    )


def gelu_only(values):
    inner = SQRT_2_PI * (values + 0.044715 * values * values * values)
    return 0.5 * values * (1.0 + jnp.tanh(inner))


def slot_pick(slots_ref, base, rows):
    place = base + lax.broadcasted_iota(jnp.int32, (rows, slots_ref.shape[1]), 0)
    return ((slots_ref[0:1, :] == place) | (slots_ref[1:2, :] == place)).astype(jnp.bfloat16)


def forward_kernel(meta, slot_at, slots_ref, x_ref, up_ref, down_ref, routed_ref, shared_ref, y_ref):
    stack_id = pl.program_id(0)
    tokens = x_ref.shape[0]

    def expert(rows):
        total = None
        for cut in range(0, FF, D):
            pre_act = product(rows, up_ref[0, :, cut : cut + D])
            part = product(gelu_only(pre_act).astype(jnp.bfloat16), down_ref[0, cut : cut + D, :])
            total = part if total is None else total + part
        return total

    @pl.when(stack_id < EXPERTS)
    def _():
        owner = jnp.minimum(stack_id, EXPERTS - 1)
        start = meta[0, owner]

        def block(number, unused):
            base = pl.multiple_of(start + number * BLK, 8)
            rows = product(slot_pick(slots_ref, base, BLK), x_ref[...]).astype(jnp.bfloat16)
            y_ref[pl.ds(base, BLK), :] = expert(rows)
            return unused

        lax.fori_loop(0, (meta[1, owner] + BLK - 1) // BLK, block, 0)

    @pl.when(stack_id >= EXPERTS)
    def _():
        @pl.when(stack_id == EXPERTS)
        def _():
            shared_ref[...] = jnp.zeros_like(shared_ref)

        def block(number, unused):
            base = pl.multiple_of(number * BLK, BLK)
            shared_ref[pl.ds(base, BLK), :] += expert(x_ref[pl.ds(base, BLK), :])
            return unused

        lax.fori_loop(0, tokens // BLK, block, 0)

    @pl.when(stack_id == EXPERTS + SHARED - 1)
    def _():
        def group(number, unused):
            for step in range(8):
                token = number * 8 + step
                for k in range(2):
                    routed_ref[k, pl.ds(token, 1), :] = y_ref[pl.ds(slot_at[k, token], 1), :]
            return unused

        lax.fori_loop(0, tokens // 8, group, 0)


def slot_room(tokens):
    return tokens * 2 + EXPERTS * 8 + BLK


def whole_block(shape):
    return pl.BlockSpec(shape, lambda e, *unused: (0,) * len(shape))


def experts_forward(slot_of, meta, moe_in, up_full, down_full):
    tokens = moe_in.shape[0]
    return pl.pallas_call(
        forward_kernel,
        grid_spec=pltpu.PrefetchScalarGridSpec(
            num_scalar_prefetch=2,
            grid=(EXPERTS + SHARED,),
            in_specs=[
                whole_block((2, tokens)),
                whole_block((tokens, D)),
                pl.BlockSpec((1, D, FF), lambda e, *unused: (e, 0, 0)),
                pl.BlockSpec((1, FF, D), lambda e, *unused: (e, 0, 0)),
            ],
            out_specs=[whole_block((2, tokens, D)), whole_block((tokens, D))],
            scratch_shapes=[pltpu.VMEM((slot_room(tokens), D), jnp.float32)],
        ),
        out_shape=[
            jax.ShapeDtypeStruct((2, tokens, D), jnp.float32),
            jax.ShapeDtypeStruct((tokens, D), jnp.float32),
        ],
        compiler_params=pltpu.CompilerParams(vmem_limit_bytes=VMEM_ROOM),
        cost_estimate=pl.CostEstimate(
            flops=20_000_000_000, bytes_accessed=50_000_000, transcendentals=0
        ),
        name="experts_forward",
    )(meta, slot_of, slot_of, moe_in, up_full, down_full)


def backward_kernel(
    meta,
    slot_at,
    slots_ref,
    x_ref,
    pair_ref,
    both_ref,
    up_ref,
    down_ref,
    up_out,
    down_out,
    dx_ref,
    up_sum,
    down_sum,
    dx_slots,
):
    stack_id = pl.program_id(0)
    tokens = x_ref.shape[0]
    up_sum[...] = jnp.zeros_like(up_sum)
    down_sum[...] = jnp.zeros_like(down_sum)

    def expert(rows, grads):
        total = None
        for cut in range(0, FF, D):
            up_part = up_ref[0, :, cut : cut + D]
            activated, slope = gelu_slope(product(rows, up_part))
            grad_act = contract(grads, down_ref[0, cut : cut + D, :], 1, 1)
            grad_pre = (grad_act * slope).astype(jnp.bfloat16)
            down_sum[cut : cut + D, :] += contract(activated.astype(jnp.bfloat16), grads, 0, 0)
            up_sum[:, cut : cut + D] += contract(rows, grad_pre, 0, 0)
            part = contract(grad_pre, up_part, 1, 1)
            total = part if total is None else total + part
        return total

    @pl.when(stack_id < EXPERTS)
    def _():
        owner = jnp.minimum(stack_id, EXPERTS - 1)
        start = meta[0, owner]
        stop = start + meta[1, owner]

        def block(number, unused):
            base = pl.multiple_of(start + number * BLK, 8)
            rows = product(slot_pick(slots_ref, base, BLK), x_ref[...]).astype(jnp.bfloat16)
            place = base + lax.broadcasted_iota(jnp.int32, (BLK, tokens), 0)
            place = jnp.where(place < stop, place, -1)
            grads = None
            for k in range(2):
                part = product(
                    (slots_ref[k : k + 1, :] == place).astype(jnp.bfloat16), pair_ref[k]
                )
                grads = part if grads is None else grads + part
            dx_slots[pl.ds(base, BLK), :] = expert(rows, grads.astype(jnp.bfloat16))
            return unused

        lax.fori_loop(0, (meta[1, owner] + BLK - 1) // BLK, block, 0)

    @pl.when(stack_id >= EXPERTS)
    def _():
        @pl.when(stack_id == EXPERTS)
        def _():
            dx_ref[...] = jnp.zeros_like(dx_ref)

        def block(number, unused):
            base = pl.multiple_of(number * BLK, BLK)
            dx_ref[pl.ds(base, BLK), :] += expert(
                x_ref[pl.ds(base, BLK), :], both_ref[pl.ds(base, BLK), :]
            )
            return unused

        lax.fori_loop(0, tokens // BLK, block, 0)

    for n in range(NARROW_PIECES):
        up_out[0, :, n] = (
            up_sum[:, n * D : (n + 1) * D]
            .astype(jnp.bfloat16)
            .reshape(WIDE_PIECES, PIECE, D)
        )
    down_out[0] = down_sum[...].astype(jnp.bfloat16).reshape(WIDE_PIECES, NARROW_PIECES, PIECE, D)

    @pl.when(stack_id == EXPERTS + SHARED - 1)
    def _():
        def group(number, unused):
            for step in range(8):
                token = number * 8 + step
                dx_ref[pl.ds(token, 1), :] += (
                    dx_slots[pl.ds(slot_at[0, token], 1), :]
                    + dx_slots[pl.ds(slot_at[1, token], 1), :]
                )
            return unused

        lax.fori_loop(0, tokens // 8, group, 0)


def experts_backward(slot_of, meta, moe_in, grad_pair, grad_both, up_full, down_full):
    tokens = moe_in.shape[0]
    slabs = (EXPERTS + SHARED, WIDE_PIECES, NARROW_PIECES, PIECE, D)
    slab_spec = pl.BlockSpec((1,) + slabs[1:], lambda e, *unused: (e, 0, 0, 0, 0))
    return pl.pallas_call(
        backward_kernel,
        grid_spec=pltpu.PrefetchScalarGridSpec(
            num_scalar_prefetch=2,
            grid=(EXPERTS + SHARED,),
            in_specs=[
                whole_block((2, tokens)),
                whole_block((tokens, D)),
                whole_block((2, tokens, D)),
                whole_block((tokens, D)),
                pl.BlockSpec((1, D, FF), lambda e, *unused: (e, 0, 0)),
                pl.BlockSpec((1, FF, D), lambda e, *unused: (e, 0, 0)),
            ],
            out_specs=[slab_spec, slab_spec, whole_block((tokens, D))],
            scratch_shapes=[
                pltpu.VMEM((D, FF), jnp.float32),
                pltpu.VMEM((FF, D), jnp.float32),
                pltpu.VMEM((slot_room(tokens), D), jnp.float32),
            ],
        ),
        out_shape=[
            jax.ShapeDtypeStruct(slabs, jnp.bfloat16),
            jax.ShapeDtypeStruct(slabs, jnp.bfloat16),
            jax.ShapeDtypeStruct((tokens, D), jnp.float32),
        ],
        compiler_params=pltpu.CompilerParams(vmem_limit_bytes=VMEM_ROOM),
        cost_estimate=pl.CostEstimate(
            flops=45_000_000_000, bytes_accessed=90_000_000, transcendentals=0
        ),
        name="experts_backward",
    )(meta, slot_of, slot_of, moe_in, grad_pair, grad_both, up_full, down_full)


def reduce_kernel(
    down_ref,
    thin_ref,
    up_ref,
    mats_ref,
    lat_in,
    out_ref,
    rows_ref,
    lat_ref,
    own,
    got_core,
    out_one,
    keep_one,
    got_one,
    out_two,
    keep_two,
    got_two,
    keep_z,
    out_rise,
    out_fall,
    got_rise,
    got_fall,
    row_parts,
    own_sem,
    core_send,
    core_recv,
    one_send,
    one_recv,
    two_send,
    two_recv,
    rise_send,
    rise_recv,
    fall_send,
    fall_recv,
    row_send,
    row_recv,
    lat_own,
    lat_send,
    lat_recv,
):
    counts = [member.shape[0] for member in (down_ref, thin_ref, up_ref, mats_ref)]
    slabs = sum(counts)
    direct = counts[0] + counts[1]
    ahead = 2
    wide, narrow = lax.axis_index(WIDE), lax.axis_index(NARROW)
    z, x = wide // 2, wide % 2
    y, c = narrow // 2, narrow % 2
    x_one, y_one = x + (1 - c) * (1 - 2 * x), y + c * (1 - 2 * y)
    x_two, y_two = x + c * (1 - 2 * x), y + (1 - c) * (1 - 2 * y)
    to_core = (wide, y * 2 + 1 - c)
    to_one = (z * 2 + x_one, y_one * 2 + c)
    to_two = (z * 2 + x_two, y_two * 2 + c)
    to_rise = (jnp.minimum(z + 1, 3) * 2 + x, narrow)
    to_fall = (jnp.maximum(z - 1, 0) * 2 + x, narrow)
    first_mine = x * (1 - c) + y * c
    second_mine = y * (1 - c) + x * c
    first_step, second_step = 2 - c, 1 + c

    mates = [
        (wide, (y + (k // 2) * (1 - 2 * y)) * 2 + c + (k % 2) * (1 - 2 * c)) for k in range(1, 4)
    ]
    levels = [(((z + k) % 4) * 2 + x, narrow) for k in range(1, 4)]
    to_x = (z * 2 + 1 - x, narrow)
    barrier = pltpu.get_barrier_semaphore()
    for target in mates + levels + [to_x]:
        pl.semaphore_signal(barrier, inc=1, device_id=target, device_id_type=MESH_ID)
    pl.semaphore_wait(barrier, 7)

    def remote(source, target, send, recv, device):
        return pltpu.make_async_remote_copy(
            src_ref=source,
            dst_ref=target,
            send_sem=send,
            recv_sem=recv,
            device_id=device,
            device_id_type=MESH_ID,
        )

    def core_copy(source, s):
        return remote(
            source.at[:, 1 - c], got_core.at[s], core_send.at[s % 4], core_recv.at[s], to_core
        )

    def own_copy(source, s):
        return pltpu.make_async_copy(source.at[:, c], own.at[s % 3], own_sem.at[s % 3])

    def one_copy(s):
        return remote(
            out_one.at[s % 2], got_one.at[s], one_send.at[s % 2], one_recv.at[s], to_one
        )

    def two_copy(s):
        return remote(
            out_two.at[s % 2], got_two.at[s], two_send.at[s % 2], two_recv.at[s], to_two
        )

    def rise_copy(s):
        return remote(
            out_rise.at[s % 2], got_rise.at[s], rise_send.at[s % 2], rise_recv.at[s], to_rise
        )

    def fall_copy(s):
        return remote(
            out_fall.at[s % 2], got_fall.at[s], fall_send.at[s % 2], fall_recv.at[s], to_fall
        )

    def row_copy(s, k):
        mate = mates[k - 1]
        return remote(
            row_parts.at[s % 2, mate[1]],
            rows_ref.at[s - direct, narrow],
            row_send.at[s % 2, k - 1],
            row_recv.at[s - direct, k - 1],
            mate,
        )

    def lat_level(k):
        spot = lat_ref.at[z, x, y, c]
        return remote(spot, spot, lat_send.at[k - 1], lat_recv.at[k - 1], levels[k - 1])

    def lat_x():
        spot = lat_ref.at[:, x, y, c]
        return remote(spot, spot, lat_send.at[3], lat_recv.at[3], to_x)

    def lat_y():
        spot = lat_ref.at[:, :, y, c]
        return remote(spot, spot, lat_send.at[4], lat_recv.at[4], mates[1])

    def lat_core():
        spot = lat_ref.at[:, :, :, c]
        return remote(spot, spot, lat_send.at[5], lat_recv.at[5], mates[0])

    own_lat = pltpu.make_async_copy(lat_in, lat_ref.at[z, x, y, c], lat_own.at[0])
    own_lat.start()
    own_lat.wait()
    for k in range(1, 4):
        lat_level(k).start()

    def begin(source, s):
        @pl.when(s >= 4)
        def _():
            core_copy(source, s).wait_send()

        core_copy(source, s).start()
        own_copy(source, s).start()

    def stage_core(s):
        own_copy(down_ref.at[0], s).wait()
        core_copy(down_ref.at[0], s).wait_recv()

        @pl.when(s >= 2)
        def _():
            one_copy(s).wait_send()

        for level in range(4):
            for other in range(2):
                place = level * 2 + other
                base = level * 4 + other * second_step
                send_at = base + (1 - first_mine) * first_step
                keep_at = base + first_mine * first_step
                out_one[s % 2, place] = (
                    own[s % 3, send_at].astype(jnp.float32)
                    + got_core[s, send_at].astype(jnp.float32)
                ).astype(jnp.bfloat16)
                keep_one[s % 2, place] = own[s % 3, keep_at].astype(jnp.float32) + got_core[
                    s, keep_at
                ].astype(jnp.float32)
        one_copy(s).start()

    def stage_one(s):
        one_copy(s).wait_recv()

        @pl.when(s >= 2)
        def _():
            two_copy(s).wait_send()

        for level in range(4):
            send_at = level * 2 + 1 - second_mine
            keep_at = level * 2 + second_mine
            out_two[s % 2, level] = (
                keep_one[s % 2, send_at] + got_one[s, send_at].astype(jnp.float32)
            ).astype(jnp.bfloat16)
            keep_two[s % 2, level] = keep_one[s % 2, keep_at] + got_one[s, keep_at].astype(
                jnp.float32
            )
        two_copy(s).start()

    def stage_two(s):
        two_copy(s).wait_recv()
        for level in range(4):
            keep_z[s % 4, level] = keep_two[s % 2, level] + got_two[s, level].astype(jnp.float32)
        stage_z(s, 0)

    def stage_z(s, hop):
        def pass_on(copy, out, got, shift):
            @pl.when(s >= 2)
            def _():
                copy(s).wait_send()

            if hop > 0:
                copy(s).wait_recv()
            for level in range(3):
                value = keep_z[s % 4, level + shift]
                if hop > 0:
                    value = value + got[s, level].astype(jnp.float32)
                out[s % 2, level] = value.astype(jnp.bfloat16)
            copy(s).start()

        @pl.when(z == hop)
        def _():
            pass_on(rise_copy, out_rise, got_rise, 1)

        @pl.when(z == 3 - hop)
        def _():
            pass_on(fall_copy, out_fall, got_fall, 0)

    def finish(s):
        @pl.when(z == 3)
        def _():
            rise_copy(s).wait_recv()

        @pl.when(z == 0)
        def _():
            fall_copy(s).wait_recv()

        total = keep_z[s % 4, z]
        rise = got_rise[s, jnp.maximum(z - 1, 0)].astype(jnp.float32)
        fall = got_fall[s, jnp.minimum(z, 2)].astype(jnp.float32)
        total = total + jnp.where(z > 0, rise, 0.0) + jnp.where(z < 3, fall, 0.0)

        @pl.when(s < direct)
        def _():
            out_ref[jnp.minimum(s, direct - 1)] = total

        @pl.when(s >= direct)
        def _():
            @pl.when(s >= direct + 2)
            def _():
                for k in range(1, 4):
                    row_copy(s, k).wait_send()

            for n in range(NARROW_PIECES):
                row_parts[s % 2, n] = total[n * ROWS : (n + 1) * ROWS]
            rows_ref[s - direct, narrow] = row_parts[s % 2, narrow]
            for k in range(1, 4):
                row_copy(s, k).start()

    def rows_in(s):
        @pl.when(s >= direct)
        def _():
            for k in range(1, 4):
                row_copy(s, k).wait_recv()

    def inside(s):
        return (s >= 0) & (s < slabs)

    def tick(t, unused):
        first = 0
        for source, count in zip((down_ref, thin_ref, up_ref, mats_ref), counts):

            @pl.when((t >= first) & (t < first + count))
            def _():
                begin(source.at[jnp.clip(t - first, 0, count - 1)], t)

            first += count

        @pl.when(t == 4)
        def _():
            for k in range(1, 4):
                lat_level(k).wait_recv()
            lat_x().start()

        @pl.when(t == 6)
        def _():
            lat_x().wait_recv()
            lat_y().start()

        @pl.when(t == 8)
        def _():
            lat_y().wait_recv()
            lat_core().start()

        for lag, stage in enumerate(
            (
                stage_core,
                stage_one,
                stage_two,
                lambda s: stage_z(s, 1),
                lambda s: stage_z(s, 2),
                finish,
                rows_in,
            )
        ):
            s = t - ahead - lag

            @pl.when(inside(s))
            def _():
                stage(s)

        return unused

    lax.fori_loop(0, slabs + ahead + 6, tick, 0)

    for back in range(4):
        core_copy(down_ref.at[0], slabs - 1 - back).wait_send()
    for back in range(2):
        one_copy(slabs - 1 - back).wait_send()
        two_copy(slabs - 1 - back).wait_send()
        for k in range(1, 4):
            row_copy(slabs - 1 - back, k).wait_send()

        @pl.when(z < 3)
        def _():
            rise_copy(slabs - 1 - back).wait_send()

        @pl.when(z > 0)
        def _():
            fall_copy(slabs - 1 - back).wait_send()

    for k in range(1, 4):
        lat_level(k).wait_send()
    lat_x().wait_send()
    lat_y().wait_send()
    lat_core().wait()


def reduce_slabs(down_slabs, up_slabs, mats_slabs, thin, lat):
    members = (down_slabs, thin, up_slabs, mats_slabs)
    slabs = sum(member.shape[0] for member in members)
    direct = down_slabs.shape[0] + thin.shape[0]
    turned = slabs - direct
    low, full = jnp.bfloat16, jnp.float32
    sources = [
        member.reshape(member.shape[0], WIDE_PIECES * NARROW_PIECES // 2, 2, PIECE, D)
        for member in members
    ]
    dma = pltpu.SemaphoreType.DMA
    vmem = pl.BlockSpec(memory_space=pltpu.VMEM)
    sums, rows, lats = pl.pallas_call(
        reduce_kernel,
        out_shape=[
            jax.ShapeDtypeStruct((direct, PIECE, D), full),
            jax.ShapeDtypeStruct((turned, NARROW_PIECES, ROWS, D), full),
            jax.ShapeDtypeStruct((4, 2, 2, 2, LAT_ROWS, LAT_COLS), low),
        ],
        in_specs=[pl.BlockSpec(memory_space=pl.ANY)] * 5,
        out_specs=[vmem, vmem, pl.BlockSpec(memory_space=pl.ANY)],
        scratch_shapes=[
            pltpu.VMEM((3, 16, PIECE, D), low),
            pltpu.VMEM((slabs, 16, PIECE, D), low),
            pltpu.VMEM((2, 8, PIECE, D), low),
            pltpu.VMEM((2, 8, PIECE, D), full),
            pltpu.VMEM((slabs, 8, PIECE, D), low),
            pltpu.VMEM((2, 4, PIECE, D), low),
            pltpu.VMEM((2, 4, PIECE, D), full),
            pltpu.VMEM((slabs, 4, PIECE, D), low),
            pltpu.VMEM((4, 4, PIECE, D), full),
            pltpu.VMEM((2, 3, PIECE, D), low),
            pltpu.VMEM((2, 3, PIECE, D), low),
            pltpu.VMEM((slabs, 3, PIECE, D), low),
            pltpu.VMEM((slabs, 3, PIECE, D), low),
            pltpu.VMEM((2, NARROW_PIECES, ROWS, D), full),
            dma((3,)),
            dma((4,)),
            dma((slabs,)),
            dma((2,)),
            dma((slabs,)),
            dma((2,)),
            dma((slabs,)),
            dma((2,)),
            dma((slabs,)),
            dma((2,)),
            dma((slabs,)),
            dma((2, 3)),
            dma((turned, 3)),
            dma((1,)),
            dma((6,)),
            dma((6,)),
        ],
        compiler_params=pltpu.CompilerParams(
            collective_id=0, has_side_effects=True, vmem_limit_bytes=REDUCE_ROOM
        ),
        name="reduce_slabs",
    )(*sources, lat)
    return sums, rows, lats.reshape(-1, LAT_COLS)


def thin_slab(thin, grad_bias):
    owners = WIDE_PIECES * NARROW_PIECES
    top = thin.reshape(owners, ROWS, -1)
    top = jnp.pad(top, ((0, 0), (0, 0), (0, D - top.shape[2])))
    line = grad_bias.reshape(owners, 1, -1)
    line = jnp.pad(line, ((0, 0), (0, PIECE - ROWS - 1), (0, D - line.shape[2])))
    both = jnp.concatenate([top, line], 1).astype(jnp.bfloat16)
    return both.reshape(1, WIDE_PIECES, NARROW_PIECES, PIECE, D)


def lat_block(lows, grad_cond, labels):
    high = lax.reduce_precision(grad_cond, 8, 7)
    middle = lax.reduce_precision(grad_cond - high, 8, 7)
    label_parts = jnp.stack([labels // 32, labels % 32], 1).astype(jnp.bfloat16)
    whole = jnp.concatenate(
        [
            lows,
            middle.astype(jnp.bfloat16),
            (grad_cond - high - middle).astype(jnp.bfloat16),
            label_parts,
        ],
        1,
    )
    room = LAT_ROWS * LAT_COLS // labels.shape[0] - whole.shape[1]
    return jnp.pad(whole, ((0, 0), (0, room))).reshape(LAT_ROWS, LAT_COLS)


def plain_grads(
    down_slabs, up_slabs, mats_slabs, thin, grad_bias, lows, grad_cond, labels, row_count
):
    def scattered(member, up_form):
        order = (0, 1, 3, 2, 4) if up_form else (0, 1, 2, 3, 4)
        member = member.astype(jnp.float32).transpose(order)
        member = member.reshape(member.shape[0], -1, FF if up_form else D)
        return lax.psum_scatter(member, AXES, scatter_dimension=1, tiled=True)

    proj_grad = scattered(mats_slabs, True)
    row_start = lax.axis_index(AXES) * row_count
    thin_grad = lax.psum_scatter(thin, AXES, scatter_dimension=0, tiled=True)
    bias_grad = lax.psum_scatter(grad_bias, AXES, scatter_dimension=0, tiled=True)
    grad_mod, grad_time2, grad_fin, grad_time1, grad_table = latent_grads(
        lows, grad_cond, labels, row_start, row_count
    )
    mats_grad = jnp.concatenate(
        [proj_grad[0], grad_mod, grad_time2, grad_fin, thin_grad, grad_time1, grad_table], 1
    )
    return (mats_grad, scattered(up_slabs, True), scattered(down_slabs, False), bias_grad)


def update_kernel(
    sums_ref,
    rows_ref,
    lat_ref,
    loss_ref,
    mats_ref,
    up_ref,
    down_ref,
    bias_ref,
    mats_row,
    mats_col,
    up_row,
    up_col,
    down_row,
    down_col,
    bias_state,
    loss_out,
    mats_grad,
    mats_new,
    mats_copy,
    mats_row_new,
    mats_col_new,
    up_grad,
    up_new,
    up_copy,
    up_row_new,
    up_col_new,
    down_grad,
    down_new,
    down_copy,
    down_row_new,
    down_col_new,
    bias_grad,
    bias_new,
    bias_copy,
    bias_state_new,
    part,
    got_plane,
    mine,
    got_level,
    column,
    result,
    squares_plane,
    squares_level,
    sems,
):
    full, low = jnp.float32, jnp.bfloat16
    wide, narrow = lax.axis_index(WIDE), lax.axis_index(NARROW)
    z, spot = wide // 2, (wide % 2) * 4 + narrow

    def plane_device(k):
        there = (spot + k) % 8
        return (z * 2 + there // 4, there % 4)

    def level_device(k):
        return (((z + k) % 4) * 2 + wide % 2, narrow)

    barrier = pltpu.get_barrier_semaphore()
    for k in range(1, 8):
        pl.semaphore_signal(barrier, inc=1, device_id=plane_device(k), device_id_type=MESH_ID)
    for k in range(1, 4):
        pl.semaphore_signal(barrier, inc=1, device_id=level_device(k), device_id_type=MESH_ID)
    pl.semaphore_wait(barrier, 10)

    def remote(source, target, phase, k, device):
        return pltpu.make_async_remote_copy(
            src_ref=source,
            dst_ref=target,
            send_sem=sems.at[0, phase, k],
            recv_sem=sems.at[1, phase, k],
            device_id=device,
            device_id_type=MESH_ID,
        )

    def exchange(copies):
        for copy in copies:
            copy.start()
        for copy in copies:
            copy.wait()

    lane = lax.broadcasted_iota(jnp.int32, (1, 128), 1)

    def spread(value, place):
        return jnp.where(lane == place, value, 0.0)

    def pick(row, place):
        return jnp.sum(jnp.where(lane == place, row, 0.0), 1, keepdims=True)

    def total(values):
        return jnp.sum(jnp.sum(values, 1, keepdims=True), 0, keepdims=True)

    count = lat_ref.shape[0] // 4
    order = lax.broadcasted_iota(jnp.int32, (count, count * 4), 0) * 4
    place = lax.broadcasted_iota(jnp.int32, (count, count * 4), 1)
    quarters = [
        product((place == order + k).astype(low), lat_ref[...]).astype(low) for k in range(4)
    ]
    owner_row = (wide * NARROW_PIECES + narrow) * ROWS
    chosen = (
        lax.broadcasted_iota(jnp.int32, (16, D), 1)
        == lax.broadcasted_iota(jnp.int32, (16, D), 0) + owner_row
    ).astype(low)

    def rows_of(member):
        return contract(chosen, member, 1, 1).astype(low)

    act_rows = rows_of(quarters[0][:, :D])
    hid_rows = rows_of(quarters[0][:, D : 2 * D])
    high = quarters[2][:, 2 * D : 3 * D]
    for j in range(NARROW_PIECES):
        mats_grad[:, j * D : (j + 1) * D] = rows_ref[EXPERTS + SHARED, j]
    mats_grad[:, 4 * D : 6 * D] = product(act_rows, quarters[0][:, 2 * D :])[:ROWS]
    mats_grad[:, 6 * D : 10 * D] = product(act_rows, quarters[1])[:ROWS]
    mats_grad[:, 10 * D : 11 * D] = product(hid_rows, high)[:ROWS]
    mats_grad[:, 11 * D : 13 * D] = product(act_rows, quarters[2][:, : 2 * D])[:ROWS]
    time_rows = rows_of(quarters[2][:, 3 * D :])
    time_one = product(time_rows, quarters[3][:, :FREQ])
    label_at = FREQ + 2 * D
    labels = quarters[3][:, label_at : label_at + 128].astype(full)
    label = labels[:, 0:1] * 32.0 + labels[:, 1:2]
    label_hot = (
        lax.broadcasted_iota(jnp.int32, (count, 1024), 1).astype(full) == label
    ).astype(low)
    table = (
        product(rows_of(high), label_hot)
        + product(rows_of(quarters[3][:, FREQ : FREQ + D]), label_hot)
        + product(rows_of(quarters[3][:, FREQ + D : FREQ + 2 * D]), label_hot)
    )
    start_last = 13 * D
    width_last = mats_grad.shape[1] - start_last
    room = 11 * 128
    thin = sums_ref[EXPERTS + SHARED][:16, :128]
    thin = jnp.where(
        (lax.broadcasted_iota(jnp.int32, (16, 128), 1) < EXPERTS + 2 * PD)
        & (lax.broadcasted_iota(jnp.int32, (16, 128), 0) < ROWS),
        thin,
        0.0,
    )

    def padded(member):
        return jnp.concatenate(
            [member, jnp.zeros((16, room - member.shape[1]), full)], 1
        )

    last = (
        padded(thin)
        + pltpu.roll(padded(time_one), EXPERTS + 2 * PD, 1)
        + pltpu.roll(padded(table), EXPERTS + 2 * PD + FREQ, 1)
    )
    mats_grad[:, start_last:] = last[:ROWS, :width_last]
    bias_grad[...] = sums_ref[EXPERTS + SHARED][ROWS : ROWS + 1, : bias_grad.shape[1]]

    part[...] = jnp.zeros_like(part)
    widths = column_widths()
    mats_at, line_at = 360, 416
    total_cols = mats_grad.shape[1]
    cuts = [(at, min(at + 128, total_cols)) for at in range(0, total_cols, 128)]
    for number, (begin, end) in enumerate(cuts):
        values = mats_grad[:, begin:end]
        part[mats_at + number : mats_at + number + 1, : end - begin] = jnp.sum(
            values * values + eps_fact, 0, keepdims=True
        )
    bounds = [sum(widths[:k]) for k in range(len(widths) + 1)]
    last_lane = lax.broadcasted_iota(jnp.int32, (ROWS, width_last), 1) + start_last
    last_sq = mats_grad[:, start_last:] * mats_grad[:, start_last:] + eps_fact
    line = spread(loss_ref[...], 46)
    for k in range(len(widths)):
        if k < 5:
            values = mats_grad[:, bounds[k] : bounds[k + 1]]
            sq = values * values + eps_fact
        else:
            sq = jnp.where((last_lane >= bounds[k]) & (last_lane < bounds[k + 1]), last_sq, 0.0)
        new = decay * mats_row[:, k : k + 1] + (1.0 - decay) * (
            jnp.sum(sq, 1, keepdims=True) / widths[k]
        )
        mats_row_new[:, k : k + 1] = new
        line = line + spread(jnp.sum(new, 0, keepdims=True), k)

    def begin_up(e, line):
        for j in range(NARROW_PIECES):
            up_grad[e, :, j * D : (j + 1) * D] = rows_ref[e, j]
        values = up_grad[e]
        sq = values * values + eps_fact
        new = decay * up_row[e] + (1.0 - decay) * (jnp.sum(sq, 1, keepdims=True) / FF)
        up_row_new[e] = new
        cols = jnp.sum(sq, 0, keepdims=True)
        for k in range(FF // 128):
            part[pl.ds(24 * k + e, 1), :] = cols[:, 128 * k : 128 * (k + 1)]
        return line + spread(jnp.sum(new, 0, keepdims=True), 10 + e)

    def begin_down(e, line):
        values = sums_ref[e]
        down_grad[e] = values
        sq = values * values + eps_fact
        new = decay * down_row[e] + (1.0 - decay) * (jnp.sum(sq, 1, keepdims=True) / D)
        down_row_new[e] = new
        cols = jnp.sum(sq, 0, keepdims=True)
        for k in range(D // 128):
            part[pl.ds(24 * (12 + k) + e, 1), :] = cols[:, 128 * k : 128 * (k + 1)]
        return line + spread(jnp.sum(new, 0, keepdims=True), 28 + e)

    line = lax.fori_loop(0, EXPERTS + SHARED, begin_up, line)
    line = lax.fori_loop(0, EXPERTS + SHARED, begin_down, line)
    part[line_at : line_at + 1, :] = line

    exchange(
        [
            remote(
                part.at[pl.ds(((spot + k) % 8) * 64, 64)], got_plane.at[k], 0, k, plane_device(k)
            )
            for k in range(1, 8)
        ]
    )
    here = part[pl.ds(pl.multiple_of(spot * 64, 64), 64), :]
    for k in range(1, 8):
        here = here + got_plane[k]
    mine[...] = here.reshape(4, 16, 128)
    exchange(
        [
            remote(mine.at[(z + k) % 4], got_level.at[k], 1, k, level_device(k))
            for k in range(1, 4)
        ]
    )
    column[z] = mine[z] + got_level[1] + got_level[2] + got_level[3]
    exchange(
        [remote(column.at[z], column.at[z], 2, k, level_device(k)) for k in range(1, 4)]
    )
    result[spot] = column[...]
    exchange(
        [remote(result.at[spot], result.at[spot], 3, k, plane_device(k)) for k in range(1, 8)]
    )

    def sums_row(row, width=128):
        if isinstance(row, int):
            return result[row // 64, (row // 16) % 4, row % 16 : row % 16 + 1, :width]
        return result[row // 64, (row // 16) % 4, pl.ds(row % 16, 1), :width]

    line = sums_row(line_at)
    loss_out[...] = pick(line, 46)
    for number, (begin, end) in enumerate(cuts):
        mats_col_new[:, begin:end] = decay * mats_col[:, begin:end] + (1.0 - decay) * (
            sums_row(mats_at + number, end - begin) / D
        )

    squares = jnp.zeros((1, 128), full)
    for k in range(5):
        begin, end = bounds[k], bounds[k + 1]
        step = mats_grad[:, begin:end] * lax.rsqrt(
            mats_row_new[:, k : k + 1] * mats_col_new[:, begin:end] / (pick(line, k) / D)
        )
        mats_new[:, begin:end] = step
        squares = squares + spread(total(step * step), k)

    def by_piece(values):
        chosen_value = values[0]
        for k in range(6, len(widths)):
            chosen_value = jnp.where(last_lane >= bounds[k], values[k - 5], chosen_value)
        return chosen_value

    row_last = by_piece([mats_row_new[:, k : k + 1] for k in range(5, len(widths))])
    mean_last = by_piece([pick(line, k) / D for k in range(5, len(widths))])
    step_last = mats_grad[:, start_last:] * lax.rsqrt(
        row_last * mats_col_new[:, start_last:] / mean_last
    )
    mats_new[:, start_last:] = step_last
    for k in range(5, len(widths)):
        inside = (last_lane >= bounds[k]) & (last_lane < bounds[k + 1])
        squares = squares + spread(total(jnp.where(inside, step_last * step_last, 0.0)), k)

    def step_up(e, squares):
        cols = jnp.concatenate([sums_row(24 * k + e) for k in range(FF // 128)], 1)
        new = decay * up_col[pl.ds(e, 1), :] + (1.0 - decay) * (cols / D)
        up_col_new[pl.ds(e, 1), :] = new
        step = up_grad[e] * lax.rsqrt(up_row_new[e] * new / (pick(line, 10 + e) / D))
        up_new[e] = step
        return squares + spread(total(step * step), 10 + e)

    def step_down(e, squares):
        cols = jnp.concatenate([sums_row(24 * (12 + k) + e) for k in range(D // 128)], 1)
        new = decay * down_col[pl.ds(e, 1), :] + (1.0 - decay) * (cols / FF)
        down_col_new[pl.ds(e, 1), :] = new
        step = down_grad[e] * lax.rsqrt(down_row_new[e] * new / (pick(line, 28 + e) / FF))
        down_new[e] = step
        return squares + spread(total(step * step), 28 + e)

    squares = lax.fori_loop(0, EXPERTS + SHARED, step_up, squares)
    squares = lax.fori_loop(0, EXPERTS + SHARED, step_down, squares)
    state = decay * bias_state[...] + (1.0 - decay) * (
        bias_grad[...] * bias_grad[...] + eps_fact
    )
    bias_state_new[...] = state
    bias_step = bias_grad[...] * lax.rsqrt(state)
    squares = squares + spread(total(bias_step * bias_step), 46)
    squares_plane[spot] = jnp.broadcast_to(squares, (8, 128))
    exchange(
        [
            remote(squares_plane.at[spot], squares_plane.at[spot], 4, k, plane_device(k))
            for k in range(1, 8)
        ]
    )
    squares_level[z] = jnp.sum(squares_plane[...], 0)
    exchange(
        [
            remote(squares_level.at[z], squares_level.at[z], 5, k, level_device(k))
            for k in range(1, 4)
        ]
    )
    squares = jnp.sum(squares_level[...], 0)[0:1]

    def clipped(place, entries):
        rms = jnp.sqrt(pick(squares, place) / entries)
        return jnp.maximum(1.0, rms / clip_level)

    def settle(new_ref, copy_ref, index, master, step, limit):
        value = master - learn_rate * (step / limit)
        new_ref[index] = value
        copy_ref[index] = value.astype(low)

    for k in range(5):
        index = (slice(None), slice(bounds[k], bounds[k + 1]))
        settle(
            mats_new, mats_copy, index, mats_ref[index], mats_new[index], clipped(k, D * widths[k])
        )
    limit = by_piece([clipped(k, D * widths[k]) for k in range(5, len(widths))])
    index = (slice(None), slice(start_last, None))
    settle(mats_new, mats_copy, index, mats_ref[index], mats_new[index], limit)

    def settle_pair(e, unused):
        settle(up_new, up_copy, e, up_ref[e], up_new[e], clipped(10 + e, D * FF))
        settle(down_new, down_copy, e, down_ref[e], down_new[e], clipped(28 + e, D * FF))
        return unused

    lax.fori_loop(0, EXPERTS + SHARED, settle_pair, 0)
    index = (slice(None), slice(None))
    settle(bias_new, bias_copy, index, bias_ref[...], bias_step, clipped(46, 15 * D))


def update_kernel_call(sums, rows, lat, masters, factors, loss_part):
    mats, up_weights, down_weights, biases = masters
    mats_row, mats_col, up_row, up_col, down_row, down_col, bias_state = factors
    full, low = jnp.float32, jnp.bfloat16
    args = (
        sums,
        rows,
        lat,
        loss_part.reshape(1, 1),
        mats,
        up_weights,
        down_weights,
        biases.reshape(1, -1),
        mats_row.T,
        mats_col.reshape(1, -1),
        up_row[:, :, None],
        up_col,
        down_row[:, :, None],
        down_col,
        bias_state.reshape(1, -1),
    )

    def like(member, kind):
        return jax.ShapeDtypeStruct(member.shape, kind)

    stacks = []
    for at in (4, 5, 6):
        stacks.append([like(args[at], full), like(args[at], full), like(args[at], low)])
        stacks[-1] += [like(args[2 * at], full), like(args[2 * at + 1], full)]
    lines = [like(args[7], full), like(args[7], full), like(args[7], low), like(args[7], full)]
    vmem = pl.BlockSpec(memory_space=pltpu.VMEM)
    dma = pltpu.SemaphoreType.DMA
    outs = pl.pallas_call(
        update_kernel,
        out_shape=[jax.ShapeDtypeStruct((1, 1), full)] + stacks[0] + stacks[1] + stacks[2] + lines,
        in_specs=[vmem] * len(args),
        out_specs=[vmem] * 20,
        scratch_shapes=[
            pltpu.VMEM((512, 128), full),
            pltpu.VMEM((8, 64, 128), full),
            pltpu.VMEM((4, 16, 128), full),
            pltpu.VMEM((4, 16, 128), full),
            pltpu.VMEM((4, 16, 128), full),
            pltpu.VMEM((8, 4, 16, 128), full),
            pltpu.VMEM((8, 8, 128), full),
            pltpu.VMEM((4, 8, 128), full),
            dma((2, 6, 8)),
        ],
        compiler_params=pltpu.CompilerParams(
            collective_id=1, has_side_effects=True, vmem_limit_bytes=VMEM_ROOM
        ),
        name="update",
    )(*args)
    return (
        outs[0][0, 0],
        outs[1],
        outs[2],
        outs[3],
        outs[4].T,
        outs[5].reshape(-1),
        outs[6],
        outs[7],
        outs[8],
        outs[9][:, :, 0],
        outs[10],
        outs[11],
        outs[12],
        outs[13],
        outs[14][:, :, 0],
        outs[15],
        outs[16].reshape(-1),
        outs[17].reshape(-1),
        outs[18].reshape(-1),
        outs[19].reshape(-1),
    )


def split_weights(weights):
    mats_full, up_full, down_full, bias_full = weights
    matrices = cut_pieces(mats_full, column_widths(), 1)
    vectors = [member.astype(jnp.float32) for member in cut_pieces(bias_full, bias_widths(), 0)]
    return (matrices, vectors, up_full, down_full)


def forward(weights, latents, noise, timesteps, labels, routes):
    matrices, vectors, up_full, down_full = split_weights(weights)
    w_qkv, w_proj, w_mod, w_time2, w_final, w_router, w_head, w_patch, w_time1, w_table = matrices
    b_qkv, b_proj, b_mod, b_patch, b_time1, b_time2, b_final = vectors
    num_latents = latents.shape[0]
    rows_here = num_latents * PATCHES
    steps_f = timesteps.astype(jnp.float32)
    signal, spread = noise_level(steps_f)
    noisy = signal[:, None] * latents + spread[:, None] * noise
    patches = noisy.reshape(rows_here, PD).astype(jnp.bfloat16)
    embedded = (
        contract(patches, w_patch, 1, 1).reshape(num_latents, PATCHES, D)
        + b_patch
        + positions()[None]
    )
    freq_low = time_features(steps_f).astype(jnp.bfloat16)
    pre_time = contract(freq_low, w_time1, 1, 1) + b_time1
    hid_time = jax.nn.silu(pre_time).astype(jnp.bfloat16)
    label_hot = (labels[:, None] == jnp.arange(CLASSES, dtype=jnp.int32)[None, :]).astype(
        jnp.float32
    )
    label_emb = lax.dot_general(
        label_hot,
        w_table.astype(jnp.float32),
        (((1,), (1,)), ((), ())),
        precision=lax.Precision.HIGHEST,
        preferred_element_type=jnp.float32,
    )
    cond = product(hid_time, w_time2) + b_time2 + label_emb
    cond_act = jax.nn.silu(cond).astype(jnp.bfloat16)
    modulation = product(cond_act, w_mod) + b_mod
    final_mod = product(cond_act, w_final) + b_final
    shift_attn, scale_attn, gate_attn, shift_moe, scale_moe, gate_moe = [
        member[:, None, :] for member in jnp.split(modulation, 6, 1)
    ]
    shift_fin, scale_fin = [member[:, None, :] for member in jnp.split(final_mod, 2, 1)]
    normed_one, inv_one = layer_norm(embedded)
    attn_in = (
        (normed_one * (1.0 + scale_attn) + shift_attn).astype(jnp.bfloat16).reshape(rows_here, D)
    )
    qkv_out = (
        (product(attn_in, w_qkv) + b_qkv)
        .astype(jnp.bfloat16)
        .reshape(num_latents, PATCHES, 3, HEADS, HD)
    )
    scores = jnp.einsum(
        "lqhd,lkhd->lhqk", qkv_out[:, :, 0], qkv_out[:, :, 1], preferred_element_type=jnp.float32
    ) * HD ** (-0.5)
    log_totals = jax.nn.logsumexp(scores, -1)
    probs_low = jax.nn.softmax(scores, -1).astype(jnp.bfloat16)
    attended = (
        jnp.einsum(
            "lhqk,lkhd->lqhd", probs_low, qkv_out[:, :, 2], preferred_element_type=jnp.float32
        )
        .astype(jnp.bfloat16)
        .reshape(rows_here, D)
    )
    attn_out = (product(attended, w_proj) + b_proj).reshape(num_latents, PATCHES, D)
    middle = embedded + gate_attn * attn_out
    normed_two, inv_two = layer_norm(middle)
    moe_in = (normed_two * (1.0 + scale_moe) + shift_moe).astype(jnp.bfloat16).reshape(rows_here, D)
    logits = product(moe_in, w_router)
    route_hot = (routes[:, :, None] == jnp.arange(EXPERTS, dtype=jnp.int32)[None, None, :]).astype(
        jnp.float32
    )
    gate_vals = jax.nn.softmax(jnp.sum(route_hot * logits[:, None, :], 2), -1)
    slot_of, slot_meta = pack_slots(routes)
    routed, shared_out = experts_forward(slot_of, slot_meta, moe_in, up_full, down_full)
    moe_out = gate_vals[:, 0:1] * routed[0] + gate_vals[:, 1:2] * routed[1] + shared_out
    moe_out = moe_out.reshape(num_latents, PATCHES, D)
    final_state = middle + gate_moe * moe_out
    normed_fin, inv_fin = layer_norm(final_state)
    head_in = (
        (normed_fin * (1.0 + scale_fin) + shift_fin).astype(jnp.bfloat16).reshape(rows_here, D)
    )
    errors = product(head_in, w_head) - noise.reshape(rows_here, PD)
    return SimpleNamespace(
        patches=patches,
        freq_low=freq_low,
        pre_time=pre_time,
        hid_time=hid_time,
        label_hot=label_hot,
        cond=cond,
        cond_act=cond_act,
        scale_attn=scale_attn,
        gate_attn=gate_attn,
        scale_moe=scale_moe,
        gate_moe=gate_moe,
        scale_fin=scale_fin,
        normed_one=normed_one,
        inv_one=inv_one,
        attn_in=attn_in,
        qkv_out=qkv_out,
        log_totals=log_totals,
        attended=attended,
        attn_out=attn_out,
        normed_two=normed_two,
        inv_two=inv_two,
        moe_in=moe_in,
        route_hot=route_hot,
        gate_vals=gate_vals,
        slot_of=slot_of,
        slot_meta=slot_meta,
        routed=routed,
        moe_out=moe_out,
        normed_fin=normed_fin,
        inv_fin=inv_fin,
        head_in=head_in,
        errors=errors,
    )


def backward(weights, kept, total_tokens):
    matrices, vectors, up_full, down_full = split_weights(weights)
    w_qkv, w_proj, w_mod, w_time2, w_final, w_router, w_head, w_patch, w_time1, w_table = matrices
    num_latents = kept.normed_one.shape[0]
    rows_here = num_latents * PATCHES
    grad_head, grad_head_in, unused = linear_back(
        kept.errors * (2.0 / total_tokens), kept.head_in, w_head
    )
    grad_head_in = grad_head_in.reshape(num_latents, PATCHES, D)
    grad_final_mod = jnp.concatenate(
        [jnp.sum(grad_head_in, 1), jnp.sum(grad_head_in * kept.normed_fin, 1)], 1
    )
    grad_state = norm_back(
        grad_head_in * (1.0 + kept.scale_fin), kept.normed_fin, kept.inv_fin
    )
    grad_gate_moe = jnp.sum(kept.moe_out * grad_state, 1)
    grad_moe = (kept.gate_moe * grad_state).reshape(rows_here, D)
    grad_moe_low = grad_moe.astype(jnp.bfloat16)
    moe_in = kept.moe_in
    gate_vals = kept.gate_vals
    routed = kept.routed
    grad_gates = jnp.stack([jnp.sum(routed[k] * grad_moe, 1) for k in range(2)], 1)
    grad_pair = jnp.stack(
        [(gate_vals[:, k : k + 1] * grad_moe).astype(jnp.bfloat16) for k in range(2)], 0
    )
    up_slabs, down_slabs, grad_moe_in = experts_backward(
        kept.slot_of, kept.slot_meta, moe_in, grad_pair, grad_moe_low, up_full, down_full
    )
    grad_picked = gate_vals * (grad_gates - jnp.sum(gate_vals * grad_gates, 1, keepdims=True))
    grad_logits = jnp.sum(kept.route_hot * grad_picked[:, :, None], 1)
    grad_router, grad_from_router, unused = linear_back(grad_logits, moe_in, w_router)
    grad_moe_in = (grad_moe_in + grad_from_router).reshape(num_latents, PATCHES, D)
    grad_middle = grad_state + norm_back(
        grad_moe_in * (1.0 + kept.scale_moe), kept.normed_two, kept.inv_two
    )
    grad_gate_attn = jnp.sum(kept.attn_out * grad_middle, 1)
    grad_proj, grad_attended, grad_b_proj = linear_back(
        (kept.gate_attn * grad_middle).reshape(rows_here, D), kept.attended, w_proj
    )
    grad_att_low = grad_attended.astype(jnp.bfloat16).reshape(num_latents, PATCHES, HEADS, HD)
    qkv_out = kept.qkv_out
    queries = qkv_out[:, :, 0]
    key_rows = qkv_out[:, :, 1]
    values = qkv_out[:, :, 2]
    scores = jnp.einsum(
        "lqhd,lkhd->lhqk", queries, key_rows, preferred_element_type=jnp.float32
    ) * HD ** (-0.5)
    probs = jnp.exp(scores - kept.log_totals[..., None])
    probs_low = probs.astype(jnp.bfloat16)
    grad_values = jnp.einsum(
        "lhqk,lqhd->lkhd", probs_low, grad_att_low, preferred_element_type=jnp.float32
    )
    grad_probs = jnp.einsum(
        "lqhd,lkhd->lhqk", grad_att_low, values, preferred_element_type=jnp.float32
    )
    grad_scores = (
        probs * (grad_probs - jnp.sum(probs * grad_probs, -1, keepdims=True)) * HD ** (-0.5)
    ).astype(jnp.bfloat16)
    grad_queries = jnp.einsum(
        "lhqk,lkhd->lqhd", grad_scores, key_rows, preferred_element_type=jnp.float32
    )
    grad_keys = jnp.einsum(
        "lhqk,lqhd->lkhd", grad_scores, queries, preferred_element_type=jnp.float32
    )
    grad_qkv = jnp.stack([grad_queries, grad_keys, grad_values], 2).reshape(rows_here, 3 * D)
    grad_w_qkv, grad_attn_in, grad_b_qkv = linear_back(grad_qkv, kept.attn_in, w_qkv)
    grad_attn_in = grad_attn_in.reshape(num_latents, PATCHES, D)
    grad_embedded = grad_middle + norm_back(
        grad_attn_in * (1.0 + kept.scale_attn), kept.normed_one, kept.inv_one
    )
    grad_emb_flat = grad_embedded.reshape(rows_here, D)
    grad_patch = contract(grad_emb_flat.astype(jnp.bfloat16), kept.patches, 0, 0)
    grad_b_patch = jnp.sum(grad_emb_flat, 0)
    grad_modulation = jnp.concatenate(
        [
            jnp.sum(grad_attn_in, 1),
            jnp.sum(grad_attn_in * kept.normed_one, 1),
            grad_gate_attn,
            jnp.sum(grad_moe_in, 1),
            jnp.sum(grad_moe_in * kept.normed_two, 1),
            grad_gate_moe,
        ],
        1,
    )
    grad_mod_low = grad_modulation.astype(jnp.bfloat16)
    grad_fin_low = grad_final_mod.astype(jnp.bfloat16)
    grad_act = contract(grad_mod_low, w_mod, 1, 1) + contract(grad_fin_low, w_final, 1, 1)
    grad_cond = slope_back(jax.nn.silu, kept.cond, grad_act)
    grad_cond_low = grad_cond.astype(jnp.bfloat16)
    grad_hid_time = contract(grad_cond_low, w_time2, 1, 1)
    grad_pre_time = slope_back(jax.nn.silu, kept.pre_time, grad_hid_time)
    grad_time_low = grad_pre_time.astype(jnp.bfloat16)
    mats_slabs = (
        jnp.concatenate([grad_w_qkv, grad_proj], 1)
        .astype(jnp.bfloat16)
        .reshape(1, WIDE_PIECES, PIECE, NARROW_PIECES, D)
        .transpose(0, 1, 3, 2, 4)
    )
    thin = jnp.concatenate([grad_router, grad_head, grad_patch], 1)
    grad_bias = jnp.concatenate(
        [
            grad_b_qkv,
            grad_b_proj,
            jnp.sum(grad_modulation, 0),
            grad_b_patch,
            jnp.sum(grad_pre_time, 0),
            jnp.sum(grad_cond, 0),
            jnp.sum(grad_final_mod, 0),
        ]
    )
    lows = jnp.concatenate(
        [
            kept.cond_act,
            kept.hid_time,
            grad_mod_low,
            grad_fin_low,
            grad_cond_low,
            grad_time_low,
            kept.freq_low,
        ],
        1,
    )
    return (up_slabs, down_slabs, mats_slabs, thin, grad_bias, lows, grad_cond)


def latent_grads(lows, grad_cond, labels, row_start, row_count):
    lows = lax.all_gather(lows, AXES, axis=0, tiled=True)
    grad_cond = lax.all_gather(grad_cond, AXES, axis=0, tiled=True)
    labels = lax.all_gather(labels, AXES, axis=0, tiled=True)
    cond_act, hid_time, grad_mod, grad_fin, grad_low, grad_time, freq_low = cut_pieces(
        lows, [D, D, 6 * D, 2 * D, D, D, FREQ], 1
    )

    def rows_of(member):
        return lax.dynamic_slice_in_dim(member, row_start, row_count, 1)

    label_hot = (labels[:, None] == jnp.arange(CLASSES, dtype=jnp.int32)[None, :]).astype(
        jnp.float32
    )
    grad_table = lax.dot_general(
        rows_of(grad_cond),
        label_hot,
        (((0,), (0,)), ((), ())),
        precision=lax.Precision.HIGHEST,
        preferred_element_type=jnp.float32,
    )
    return (
        contract(rows_of(cond_act), grad_mod, 0, 0),
        contract(rows_of(hid_time), grad_low, 0, 0),
        contract(rows_of(cond_act), grad_fin, 0, 0),
        contract(rows_of(grad_time), freq_low, 0, 0),
        grad_table,
    )


def factor_start(grad, row_old):
    squares = grad * grad + eps_fact
    row_new = decay * row_old + (1.0 - decay) * jnp.mean(squares, 2)
    return (row_new, jnp.sum(squares, 1), jnp.sum(row_new, 1))


def factor_update(grad, row_new, col_total, row_total, col_old, row_count):
    col_new = decay * col_old + (1.0 - decay) * (col_total / row_count)
    row_mean = row_total / row_count
    update = grad * lax.rsqrt(row_new[:, :, None] * col_new[:, None, :] / row_mean[:, None, None])
    return (col_new, update, jnp.sum(update * update, (1, 2)))


def clip_apply(master, update, square_total, entry_count):
    update_rms = jnp.sqrt(square_total / entry_count)
    return master - learn_rate * (update / jnp.maximum(1.0, update_rms / clip_level)[:, None, None])


def update_plain(grads, masters, factors, loss_part):
    mats_grad, up_grad, down_grad, bias_grad = grads
    mats, up_weights, down_weights, biases = masters
    mats_row, mats_col, up_row, up_col, down_row, down_col, bias_state = factors
    widths = column_widths()
    grad_pieces = cut_pieces(mats_grad, widths, 1)
    starts = [
        factor_start(grad_pieces[k][None], mats_row[k][None]) for k in range(len(widths))
    ]
    up_row_new, up_col_part, up_row_part = factor_start(up_grad, up_row)
    down_row_new, down_col_part, down_row_part = factor_start(down_grad, down_row)
    col_totals, row_totals, up_cols, up_rows, down_cols, down_rows, loss_total = lax.psum(
        (
            jnp.concatenate([member[1] for member in starts], 1)[0],
            jnp.concatenate([member[2] for member in starts], 0),
            up_col_part,
            up_row_part,
            down_col_part,
            down_row_part,
            loss_part,
        ),
        AXES,
    )
    col_total_pieces = cut_pieces(col_totals, widths, 0)
    col_old_pieces = cut_pieces(mats_col, widths, 0)
    steps = [
        factor_update(
            grad_pieces[k][None],
            starts[k][0],
            col_total_pieces[k][None],
            row_totals[k][None],
            col_old_pieces[k][None],
            D,
        )
        for k in range(len(widths))
    ]
    up_col_new, up_update, up_square = factor_update(
        up_grad, up_row_new, up_cols, up_rows, up_col, D
    )
    down_col_new, down_update, down_square = factor_update(
        down_grad, down_row_new, down_cols, down_rows, down_col, FF
    )
    bias_state_new = decay * bias_state + (1.0 - decay) * (bias_grad * bias_grad + eps_fact)
    bias_update = bias_grad * lax.rsqrt(bias_state_new)
    square_mats, square_up, square_down, square_bias = lax.psum(
        (
            jnp.concatenate([member[2] for member in steps], 0),
            up_square,
            down_square,
            jnp.sum(bias_update * bias_update),
        ),
        AXES,
    )
    master_pieces = cut_pieces(mats, widths, 1)
    mats_new = jnp.concatenate(
        [
            clip_apply(
                master_pieces[k][None], steps[k][1], square_mats[k][None], D * widths[k]
            )[0]
            for k in range(len(widths))
        ],
        1,
    )
    up_new = clip_apply(up_weights, up_update, square_up, D * FF)
    down_new = clip_apply(down_weights, down_update, square_down, D * FF)
    bias_rms = jnp.sqrt(square_bias / (15 * D))
    bias_new = biases - learn_rate * (bias_update / jnp.maximum(1.0, bias_rms / clip_level))
    return (
        loss_total,
        mats_grad,
        mats_new,
        mats_new.astype(jnp.bfloat16),
        jnp.concatenate([member[0] for member in starts], 0),
        jnp.concatenate([member[0][0] for member in steps], 0),
        up_grad,
        up_new,
        up_new.astype(jnp.bfloat16),
        up_row_new,
        up_col_new,
        down_grad,
        down_new,
        down_new.astype(jnp.bfloat16),
        down_row_new,
        down_col_new,
        bias_grad,
        bias_new,
        bias_new.astype(jnp.bfloat16),
        bias_state_new,
    )


def body(
    latents,
    noise,
    timesteps,
    labels,
    routes,
    mats,
    up_weights,
    down_weights,
    biases,
    *factors,
):
    rows_here = mats.shape[0]
    flat = jnp.concatenate([mats.reshape(-1), biases], 0).astype(jnp.bfloat16)
    flat = lax.all_gather(flat, AXES, axis=0, tiled=False)
    gathered = (
        flat[:, : rows_here * mats.shape[1]].reshape(-1, mats.shape[1]),
        lax.all_gather(up_weights.astype(jnp.bfloat16), AXES, axis=1, tiled=True),
        lax.all_gather(down_weights.astype(jnp.bfloat16), AXES, axis=1, tiled=True),
        flat[:, rows_here * mats.shape[1] :].reshape(-1),
    )
    kept = forward(gathered, latents, noise, timesteps, labels, routes)
    total_tokens = latents.shape[0] * PATCHES * lax.axis_size(AXES)
    up_slabs, down_slabs, mats_slabs, thin, grad_bias, lows, grad_cond = backward(
        gathered, kept, total_tokens
    )
    loss_part = jnp.sum(kept.errors * kept.errors)
    masters = (mats, up_weights, down_weights, biases)
    kernel_fits = lax.axis_size(WIDE) == WIDE_PIECES and lax.axis_size(NARROW) == NARROW_PIECES
    if kernel_fits:
        sums, rows, lat = reduce_slabs(
            down_slabs,
            up_slabs,
            mats_slabs,
            thin_slab(thin, grad_bias),
            lat_block(lows, grad_cond, labels),
        )
        outs = update_kernel_call(sums, rows, lat, masters, factors, loss_part)
    else:
        grads = plain_grads(
            down_slabs, up_slabs, mats_slabs, thin, grad_bias, lows, grad_cond, labels, rows_here
        )
        outs = update_plain(grads, masters, factors, loss_part)
    return (outs[0] / total_tokens,) + tuple(outs[1:])


def solution(mesh):
    rows = P(AXES, None)
    middle_rows = P(None, AXES, None)
    row_factor = P(None, AXES)
    line = P(AXES)
    in_specs = (
        (rows, rows, line, line, rows)
        + (rows, middle_rows, middle_rows, line)
        + (row_factor, P(), row_factor, P(), row_factor, P(), line)
    )
    out_specs = (
        (P(), rows, rows, rows, row_factor, P())
        + (middle_rows, middle_rows, middle_rows, row_factor, P()) * 2
        + (line, line, line, line)
    )
    return jax.shard_map(body, mesh=mesh, in_specs=in_specs, out_specs=out_specs, check_vma=False)
```

```python
import math
from types import SimpleNamespace

import jax
import jax.numpy as jnp
from jax import lax
from jax.experimental import pallas as pl
from jax.experimental.pallas import tpu as pltpu
from jax.sharding import PartitionSpec as P

WIDE = "wide"
NARROW = "narrow"
AXES = (WIDE, NARROW)
MESH_ID = pl.DeviceIdType.MESH

D = 384
HEADS = 6
HD = 64
FF = 1536
EXPERTS = 16
SHARED = 2
PD = 16
GRID = 16
FREQ = 256
CLASSES = 1000
BLK = 256
WIDE_PIECES = 8
NARROW_PIECES = 4
PIECE = 48
ROWS = 12
LAT_ROWS = 16
LQK = "lqhd,lkhd->lhqk"
CUT = 768
LAT_COLS = 1536
PATCHES = 256


eps_norm = 1e-06
eps_fact = 1e-30
decay = 0.5
clip_level = 0.1
learn_rate = 0.5

SQRT_2_PI = math.sqrt(2.0 / math.pi)
VMEM_ROOM = 56 * 1024 * 1024
REDUCE_ROOM = 60 * 1024 * 1024


def column_widths():
    return [3 * D, D, 6 * D, D, 2 * D, EXPERTS, PD, PD, FREQ, CLASSES]


def bias_widths():
    return [3 * D, D, 6 * D, D, D, D, 2 * D]


def cut_pieces(source, widths, along):
    pieces = []
    start = 0
    for width in widths:
        pieces.append(lax.slice_in_dim(source, start, start + width, axis=along))
        start = start + width
    return pieces


def product(left, right):
    return jnp.dot(left, right, preferred_element_type=jnp.float32)


def contract(left, right, left_dim, right_dim):
    return lax.dot_general(
        left, right, (((left_dim,), (right_dim,)), ((), ())), preferred_element_type=jnp.float32
    )


def gelu_tanh(values):
    return jax.nn.gelu(values, approximate=True)


def slope_back(function, source, grad_out):
    return jax.vjp(function, source)[1](grad_out)[0]


def layer_norm(source):
    centred = source - jnp.mean(source, -1, keepdims=True)
    inv_std = lax.rsqrt(jnp.mean(centred * centred, -1, keepdims=True) + eps_norm)
    return (centred * inv_std, inv_std)


def norm_back(grad_norm, normed, inv_std):
    return inv_std * (
        grad_norm
        - jnp.mean(grad_norm, -1, keepdims=True)
        - normed * jnp.mean(grad_norm * normed, -1, keepdims=True)
    )


def linear_back(grad_out, inputs, weight):
    grad_low = grad_out.astype(jnp.bfloat16)
    return (
        contract(inputs, grad_low, 0, 0),
        contract(grad_low, weight, 1, 1),
        jnp.sum(grad_out, 0),
    )


def sincos(coords, width):
    omegas = 1.0 / 10000.0 ** (jnp.arange(width // 2, dtype=jnp.float32) / (width / 2.0))
    angles = coords[:, None] * omegas[None, :]
    return jnp.concatenate([jnp.sin(angles), jnp.cos(angles)], 1)


def positions():
    places = jnp.arange(PATCHES, dtype=jnp.int32)
    grid_row = (places // GRID).astype(jnp.float32)
    grid_col = (places % GRID).astype(jnp.float32)
    return jnp.concatenate([sincos(grid_row, D // 2), sincos(grid_col, D // 2)], 1)


def time_features(steps_f):
    half_width = FREQ // 2
    freq_rates = jnp.exp(
        -math.log(10000.0) * jnp.arange(half_width, dtype=jnp.float32) / half_width
    )
    angles = steps_f[:, None] * freq_rates[None, :]
    return jnp.concatenate([jnp.cos(angles), jnp.sin(angles)], 1)


def noise_level(steps_f):
    alpha_bar = jnp.cos((steps_f / 1000.0 + 0.008) / 1.008 * (math.pi / 2)) ** 2
    return (jnp.sqrt(alpha_bar), jnp.sqrt(1.0 - alpha_bar))


def pack_slots(routes):
    ids = jnp.arange(EXPERTS, dtype=jnp.int32)[:, None]
    named = [(routes[:, k][None, :] == ids) for k in range(2)]
    either = (named[0] | named[1]).astype(jnp.bfloat16)
    rows_here = routes.shape[0]
    place = jnp.arange(rows_here, dtype=jnp.int32)
    before = (place[:, None] < place[None, :]).astype(jnp.bfloat16)
    rank_in = product(either, before)
    counts = jnp.sum(either.astype(jnp.float32), 1).astype(jnp.int32)
    padded = (counts + 7) // 8 * 8
    starts = jnp.sum(jnp.where(ids > ids.T, padded[None, :], 0), 1)
    slots = rank_in.astype(jnp.int32) + starts[:, None]
    slot_of = jnp.stack([jnp.sum(jnp.where(member, slots, 0), 0) for member in named], 0)
    return (slot_of, jnp.stack([starts, counts], 0))


def gelu_slope(values):
    inner = SQRT_2_PI * (values + 0.044715 * values * values * values)
    bend = jnp.tanh(inner)
    return (
        0.5 * values * (1.0 + bend),
        0.5 * (1.0 + bend)
        + 0.5
        * values
        * (1.0 - bend * bend)
        * SQRT_2_PI
        * (1.0 + 3.0 * 0.044715 * values * values),
    )


def gelu_only(values):
    inner = SQRT_2_PI * (values + 0.044715 * values * values * values)
    return 0.5 * values * (1.0 + jnp.tanh(inner))


def up_columns(chunks, cut):
    return jnp.concatenate([chunks[cut // D + k] for k in range(CUT // D)], 1)


def slot_pick(slots_ref, base, rows):
    place = base + lax.broadcasted_iota(jnp.int32, (rows, slots_ref.shape[1]), 0)
    return ((slots_ref[0:1, :] == place) | (slots_ref[1:2, :] == place)).astype(jnp.bfloat16)


def forward_kernel(meta, slot_at, slots_ref, x_ref, up_ref, down_ref, routed_ref, y_ref):
    stack_id = pl.program_id(0)
    tokens = x_ref.shape[0]

    def expert(rows):
        total = None
        for cut in range(0, FF, CUT):
            pre_act = product(rows, up_columns(up_ref[0], cut))
            part = product(gelu_only(pre_act).astype(jnp.bfloat16), down_ref[0, cut : cut + CUT])
            total = part if total is None else total + part
        return total

    start = meta[0, stack_id]

    def block(number, unused):
        base = pl.multiple_of(start + number * BLK, 8)
        rows = product(slot_pick(slots_ref, base, BLK), x_ref[...]).astype(jnp.bfloat16)
        y_ref[pl.ds(base, BLK), :] = expert(rows)
        return unused

    lax.fori_loop(0, (meta[1, stack_id] + BLK - 1) // BLK, block, 0)

    @pl.when(stack_id == EXPERTS - 1)
    def _():
        def group(number, unused):
            for step in range(8):
                token = number * 8 + step
                for k in range(2):
                    routed_ref[k, pl.ds(token, 1), :] = y_ref[pl.ds(slot_at[k, token], 1), :]
            return unused

        lax.fori_loop(0, tokens // 8, group, 0)


def slot_room(tokens):
    return tokens * 2 + EXPERTS * 8 + BLK


def whole_block(shape):
    return pl.BlockSpec(shape, lambda e, *unused: (0,) * len(shape))


def experts_forward(slot_of, meta, moe_in, up_full, down_full):
    tokens = moe_in.shape[0]
    return pl.pallas_call(
        forward_kernel,
        grid_spec=pltpu.PrefetchScalarGridSpec(
            num_scalar_prefetch=2,
            grid=(EXPERTS,),
            in_specs=[
                whole_block((2, tokens)),
                whole_block((tokens, D)),
                pl.BlockSpec((1, NARROW_PIECES, D, D), lambda e, *unused: (e, 0, 0, 0)),
                pl.BlockSpec((1, FF, D), lambda e, *unused: (e, 0, 0)),
            ],
            out_specs=whole_block((2, tokens, D)),
            scratch_shapes=[pltpu.VMEM((slot_room(tokens), D), jnp.float32)],
        ),
        out_shape=jax.ShapeDtypeStruct((2, tokens, D), jnp.float32),
        compiler_params=pltpu.CompilerParams(vmem_limit_bytes=VMEM_ROOM),
        cost_estimate=pl.CostEstimate(
            flops=20_000_000_000, bytes_accessed=50_000_000, transcendentals=0
        ),
        name="experts_forward",
    )(meta, slot_of, slot_of, moe_in, up_full, down_full)


def backward_kernel(
    meta,
    slot_at,
    slots_ref,
    x_ref,
    pair_ref,
    both_ref,
    up_ref,
    down_ref,
    up_out,
    down_out,
    dx_ref,
    up_sum,
    down_sum,
    dx_slots,
):
    stack_id = pl.program_id(0)
    tokens = x_ref.shape[0]
    up_sum[...] = jnp.zeros_like(up_sum)
    down_sum[...] = jnp.zeros_like(down_sum)

    def expert(rows, grads):
        total = None
        for cut in range(0, FF, CUT):
            up_part = up_columns(up_ref[0], cut)
            activated, slope = gelu_slope(product(rows, up_part))
            grad_act = contract(grads, down_ref[0, cut : cut + CUT], 1, 1)
            grad_pre = (grad_act * slope).astype(jnp.bfloat16)
            down_sum[cut : cut + CUT, :] += contract(activated.astype(jnp.bfloat16), grads, 0, 0)
            up_sum[:, cut : cut + CUT] += contract(rows, grad_pre, 0, 0)
            part = contract(grad_pre, up_part, 1, 1)
            total = part if total is None else total + part
        return total

    @pl.when(stack_id < EXPERTS)
    def _():
        owner = jnp.minimum(stack_id, EXPERTS - 1)
        start = meta[0, owner]
        stop = start + meta[1, owner]

        def block(number, unused):
            base = pl.multiple_of(start + number * BLK, 8)
            rows = product(slot_pick(slots_ref, base, BLK), x_ref[...]).astype(jnp.bfloat16)
            place = base + lax.broadcasted_iota(jnp.int32, (BLK, tokens), 0)
            place = jnp.where(place < stop, place, -1)
            grads = None
            for k in range(2):
                part = product(
                    (slots_ref[k : k + 1, :] == place).astype(jnp.bfloat16), pair_ref[k]
                )
                grads = part if grads is None else grads + part
            dx_slots[pl.ds(base, BLK), :] = expert(rows, grads.astype(jnp.bfloat16))
            return unused

        lax.fori_loop(0, (meta[1, owner] + BLK - 1) // BLK, block, 0)

    @pl.when(stack_id >= EXPERTS)
    def _():
        @pl.when(stack_id == EXPERTS)
        def _():
            dx_ref[...] = jnp.zeros_like(dx_ref)

        def block(number, unused):
            base = pl.multiple_of(number * BLK, BLK)
            dx_ref[pl.ds(base, BLK), :] += expert(
                x_ref[pl.ds(base, BLK), :], both_ref[pl.ds(base, BLK), :]
            )
            return unused

        lax.fori_loop(0, tokens // BLK, block, 0)

    for n in range(NARROW_PIECES):
        up_out[0, :, n] = (
            up_sum[:, n * D : (n + 1) * D]
            .astype(jnp.bfloat16)
            .reshape(WIDE_PIECES, PIECE, D)
        )
    down_out[0] = down_sum[...].astype(jnp.bfloat16).reshape(WIDE_PIECES, NARROW_PIECES, PIECE, D)

    @pl.when(stack_id == EXPERTS + SHARED - 1)
    def _():
        def group(number, unused):
            for step in range(8):
                token = number * 8 + step
                dx_ref[pl.ds(token, 1), :] += (
                    dx_slots[pl.ds(slot_at[0, token], 1), :]
                    + dx_slots[pl.ds(slot_at[1, token], 1), :]
                )
            return unused

        lax.fori_loop(0, tokens // 8, group, 0)


def experts_backward(slot_of, meta, moe_in, grad_pair, grad_both, up_full, down_full):
    tokens = moe_in.shape[0]
    slabs = (EXPERTS + SHARED, WIDE_PIECES, NARROW_PIECES, PIECE, D)
    slab_spec = pl.BlockSpec((1,) + slabs[1:], lambda e, *unused: (e, 0, 0, 0, 0))
    return pl.pallas_call(
        backward_kernel,
        grid_spec=pltpu.PrefetchScalarGridSpec(
            num_scalar_prefetch=2,
            grid=(EXPERTS + SHARED,),
            in_specs=[
                whole_block((2, tokens)),
                whole_block((tokens, D)),
                whole_block((2, tokens, D)),
                whole_block((tokens, D)),
                pl.BlockSpec((1, NARROW_PIECES, D, D), lambda e, *unused: (e, 0, 0, 0)),
                pl.BlockSpec((1, FF, D), lambda e, *unused: (e, 0, 0)),
            ],
            out_specs=[slab_spec, slab_spec, whole_block((tokens, D))],
            scratch_shapes=[
                pltpu.VMEM((D, FF), jnp.float32),
                pltpu.VMEM((FF, D), jnp.float32),
                pltpu.VMEM((slot_room(tokens), D), jnp.float32),
            ],
        ),
        out_shape=[
            jax.ShapeDtypeStruct(slabs, jnp.bfloat16),
            jax.ShapeDtypeStruct(slabs, jnp.bfloat16),
            jax.ShapeDtypeStruct((tokens, D), jnp.float32),
        ],
        compiler_params=pltpu.CompilerParams(vmem_limit_bytes=VMEM_ROOM),
        cost_estimate=pl.CostEstimate(
            flops=45_000_000_000, bytes_accessed=90_000_000, transcendentals=0
        ),
        name="experts_backward",
    )(meta, slot_of, slot_of, moe_in, grad_pair, grad_both, up_full, down_full)


def reduce_kernel(
    down_ref,
    thin_ref,
    up_ref,
    mats_ref,
    lat_in,
    out_ref,
    rows_ref,
    lat_ref,
    own,
    got_core,
    out_one,
    keep_one,
    got_one,
    out_two,
    keep_two,
    got_two,
    keep_z,
    out_rise,
    out_fall,
    got_rise,
    got_fall,
    row_parts,
    own_sem,
    core_send,
    core_recv,
    one_send,
    one_recv,
    two_send,
    two_recv,
    rise_send,
    rise_recv,
    fall_send,
    fall_recv,
    row_send,
    row_recv,
    lat_own,
    lat_send,
    lat_recv,
):
    counts = [member.shape[0] for member in (down_ref, thin_ref, up_ref, mats_ref)]
    slabs = sum(counts)
    direct = counts[0] + counts[1]
    ahead = 2
    wide, narrow = lax.axis_index(WIDE), lax.axis_index(NARROW)
    z, x = wide // 2, wide % 2
    y, c = narrow // 2, narrow % 2
    x_one, y_one = x + (1 - c) * (1 - 2 * x), y + c * (1 - 2 * y)
    x_two, y_two = x + c * (1 - 2 * x), y + (1 - c) * (1 - 2 * y)
    to_core = (wide, y * 2 + 1 - c)
    to_one = (z * 2 + x_one, y_one * 2 + c)
    to_two = (z * 2 + x_two, y_two * 2 + c)
    to_rise = (jnp.minimum(z + 1, 3) * 2 + x, narrow)
    to_fall = (jnp.maximum(z - 1, 0) * 2 + x, narrow)
    first_mine = x * (1 - c) + y * c
    second_mine = y * (1 - c) + x * c
    first_step, second_step = 2 - c, 1 + c

    mates = [
        (wide, (y + (k // 2) * (1 - 2 * y)) * 2 + c + (k % 2) * (1 - 2 * c)) for k in range(1, 4)
    ]
    levels = [(((z + k) % 4) * 2 + x, narrow) for k in range(1, 4)]
    to_x = (z * 2 + 1 - x, narrow)
    barrier = pltpu.get_barrier_semaphore()
    for target in mates + levels + [to_x]:
        pl.semaphore_signal(barrier, inc=1, device_id=target, device_id_type=MESH_ID)
    pl.semaphore_wait(barrier, 7)

    def remote(source, target, send, recv, device):
        return pltpu.make_async_remote_copy(
            src_ref=source,
            dst_ref=target,
            send_sem=send,
            recv_sem=recv,
            device_id=device,
            device_id_type=MESH_ID,
        )

    def core_copy(source, s):
        return remote(
            source.at[:, 1 - c], got_core.at[s], core_send.at[s % 4], core_recv.at[s], to_core
        )

    def own_copy(source, s):
        return pltpu.make_async_copy(source.at[:, c], own.at[s % 3], own_sem.at[s % 3])

    def one_copy(s):
        return remote(
            out_one.at[s % 2], got_one.at[s], one_send.at[s % 2], one_recv.at[s], to_one
        )

    def two_copy(s):
        return remote(
            out_two.at[s % 2], got_two.at[s], two_send.at[s % 2], two_recv.at[s], to_two
        )

    def rise_copy(s):
        return remote(
            out_rise.at[s % 2], got_rise.at[s], rise_send.at[s % 2], rise_recv.at[s], to_rise
        )

    def fall_copy(s):
        return remote(
            out_fall.at[s % 2], got_fall.at[s], fall_send.at[s % 2], fall_recv.at[s], to_fall
        )

    def row_copy(s, k):
        mate = mates[k - 1]
        return remote(
            row_parts.at[s % 2, mate[1]],
            rows_ref.at[s - direct, narrow],
            row_send.at[s % 2, k - 1],
            row_recv.at[s - direct, k - 1],
            mate,
        )

    def lat_level(k):
        spot = lat_ref.at[z, x, y, c]
        return remote(spot, spot, lat_send.at[k - 1], lat_recv.at[k - 1], levels[k - 1])

    def lat_x():
        spot = lat_ref.at[:, x, y, c]
        return remote(spot, spot, lat_send.at[3], lat_recv.at[3], to_x)

    def lat_y():
        spot = lat_ref.at[:, :, y, c]
        return remote(spot, spot, lat_send.at[4], lat_recv.at[4], mates[1])

    def lat_core():
        spot = lat_ref.at[:, :, :, c]
        return remote(spot, spot, lat_send.at[5], lat_recv.at[5], mates[0])

    own_lat = pltpu.make_async_copy(lat_in, lat_ref.at[z, x, y, c], lat_own.at[0])
    own_lat.start()
    own_lat.wait()
    for k in range(1, 4):
        lat_level(k).start()

    def begin(source, s):
        @pl.when(s >= 4)
        def _():
            core_copy(source, s).wait_send()

        core_copy(source, s).start()
        own_copy(source, s).start()

    def stage_core(s):
        own_copy(down_ref.at[0], s).wait()
        core_copy(down_ref.at[0], s).wait_recv()

        @pl.when(s >= 2)
        def _():
            one_copy(s).wait_send()

        for level in range(4):
            for other in range(2):
                place = level * 2 + other
                base = level * 4 + other * second_step
                send_at = base + (1 - first_mine) * first_step
                keep_at = base + first_mine * first_step
                out_one[s % 2, place] = (
                    own[s % 3, send_at].astype(jnp.float32)
                    + got_core[s, send_at].astype(jnp.float32)
                ).astype(jnp.bfloat16)
                keep_one[s % 2, place] = own[s % 3, keep_at].astype(jnp.float32) + got_core[
                    s, keep_at
                ].astype(jnp.float32)
        one_copy(s).start()

    def stage_one(s):
        one_copy(s).wait_recv()

        @pl.when(s >= 2)
        def _():
            two_copy(s).wait_send()

        for level in range(4):
            send_at = level * 2 + 1 - second_mine
            keep_at = level * 2 + second_mine
            out_two[s % 2, level] = (
                keep_one[s % 2, send_at] + got_one[s, send_at].astype(jnp.float32)
            ).astype(jnp.bfloat16)
            keep_two[s % 2, level] = keep_one[s % 2, keep_at] + got_one[s, keep_at].astype(
                jnp.float32
            )
        two_copy(s).start()

    def stage_two(s):
        two_copy(s).wait_recv()
        for level in range(4):
            keep_z[s % 4, level] = keep_two[s % 2, level] + got_two[s, level].astype(jnp.float32)
        stage_z(s, 0)

    def stage_z(s, hop):
        def pass_on(copy, out, got, shift):
            @pl.when(s >= 2)
            def _():
                copy(s).wait_send()

            if hop > 0:
                copy(s).wait_recv()
            for level in range(3):
                value = keep_z[s % 4, level + shift]
                if hop > 0:
                    value = value + got[s, level].astype(jnp.float32)
                out[s % 2, level] = value.astype(jnp.bfloat16)
            copy(s).start()

        @pl.when(z == hop)
        def _():
            pass_on(rise_copy, out_rise, got_rise, 1)

        @pl.when(z == 3 - hop)
        def _():
            pass_on(fall_copy, out_fall, got_fall, 0)

    def finish(s):
        @pl.when(z == 3)
        def _():
            rise_copy(s).wait_recv()

        @pl.when(z == 0)
        def _():
            fall_copy(s).wait_recv()

        total = keep_z[s % 4, z]
        rise = got_rise[s, jnp.maximum(z - 1, 0)].astype(jnp.float32)
        fall = got_fall[s, jnp.minimum(z, 2)].astype(jnp.float32)
        total = total + jnp.where(z > 0, rise, 0.0) + jnp.where(z < 3, fall, 0.0)

        @pl.when(s < direct)
        def _():
            out_ref[jnp.minimum(s, direct - 1)] = total

        @pl.when(s >= direct)
        def _():
            @pl.when(s >= direct + 2)
            def _():
                for k in range(1, 4):
                    row_copy(s, k).wait_send()

            for n in range(NARROW_PIECES):
                row_parts[s % 2, n] = total[n * ROWS : (n + 1) * ROWS]
            rows_ref[s - direct, narrow] = row_parts[s % 2, narrow]
            for k in range(1, 4):
                row_copy(s, k).start()

    def rows_in(s):
        @pl.when(s >= direct)
        def _():
            for k in range(1, 4):
                row_copy(s, k).wait_recv()

    def inside(s):
        return (s >= 0) & (s < slabs)

    def tick(t, unused):
        first = 0
        for source, count in zip((down_ref, thin_ref, up_ref, mats_ref), counts):

            @pl.when((t >= first) & (t < first + count))
            def _():
                begin(source.at[jnp.clip(t - first, 0, count - 1)], t)

            first += count

        @pl.when(t == 4)
        def _():
            for k in range(1, 4):
                lat_level(k).wait_recv()
            lat_x().start()

        @pl.when(t == 6)
        def _():
            lat_x().wait_recv()
            lat_y().start()

        @pl.when(t == 8)
        def _():
            lat_y().wait_recv()
            lat_core().start()

        for lag, stage in enumerate(
            (
                stage_core,
                stage_one,
                stage_two,
                lambda s: stage_z(s, 1),
                lambda s: stage_z(s, 2),
                finish,
                rows_in,
            )
        ):
            s = t - ahead - lag

            @pl.when(inside(s))
            def _():
                stage(s)

        return unused

    lax.fori_loop(0, slabs + ahead + 6, tick, 0)

    for back in range(4):
        core_copy(down_ref.at[0], slabs - 1 - back).wait_send()
    for back in range(2):
        one_copy(slabs - 1 - back).wait_send()
        two_copy(slabs - 1 - back).wait_send()
        for k in range(1, 4):
            row_copy(slabs - 1 - back, k).wait_send()

        @pl.when(z < 3)
        def _():
            rise_copy(slabs - 1 - back).wait_send()

        @pl.when(z > 0)
        def _():
            fall_copy(slabs - 1 - back).wait_send()

    for k in range(1, 4):
        lat_level(k).wait_send()
    lat_x().wait_send()
    lat_y().wait_send()
    lat_core().wait()


def reduce_slabs(down_slabs, up_slabs, mats_slabs, thin, lat):
    members = (down_slabs, thin, up_slabs, mats_slabs)
    slabs = sum(member.shape[0] for member in members)
    direct = down_slabs.shape[0] + thin.shape[0]
    turned = slabs - direct
    low, full = jnp.bfloat16, jnp.float32
    sources = [
        member.reshape(member.shape[0], WIDE_PIECES * NARROW_PIECES // 2, 2, PIECE, D)
        for member in members
    ]
    dma = pltpu.SemaphoreType.DMA
    vmem = pl.BlockSpec(memory_space=pltpu.VMEM)
    sums, rows, lats = pl.pallas_call(
        reduce_kernel,
        out_shape=[
            jax.ShapeDtypeStruct((direct, PIECE, D), full),
            jax.ShapeDtypeStruct((turned, NARROW_PIECES, ROWS, D), full),
            jax.ShapeDtypeStruct((4, 2, 2, 2, LAT_ROWS, LAT_COLS), low),
        ],
        in_specs=[pl.BlockSpec(memory_space=pl.ANY)] * 5,
        out_specs=[vmem, vmem, pl.BlockSpec(memory_space=pl.ANY)],
        scratch_shapes=[
            pltpu.VMEM((3, 16, PIECE, D), low),
            pltpu.VMEM((slabs, 16, PIECE, D), low),
            pltpu.VMEM((2, 8, PIECE, D), low),
            pltpu.VMEM((2, 8, PIECE, D), full),
            pltpu.VMEM((slabs, 8, PIECE, D), low),
            pltpu.VMEM((2, 4, PIECE, D), low),
            pltpu.VMEM((2, 4, PIECE, D), full),
            pltpu.VMEM((slabs, 4, PIECE, D), low),
            pltpu.VMEM((4, 4, PIECE, D), full),
            pltpu.VMEM((2, 3, PIECE, D), low),
            pltpu.VMEM((2, 3, PIECE, D), low),
            pltpu.VMEM((slabs, 3, PIECE, D), low),
            pltpu.VMEM((slabs, 3, PIECE, D), low),
            pltpu.VMEM((2, NARROW_PIECES, ROWS, D), full),
            dma((3,)),
            dma((4,)),
            dma((slabs,)),
            dma((2,)),
            dma((slabs,)),
            dma((2,)),
            dma((slabs,)),
            dma((2,)),
            dma((slabs,)),
            dma((2,)),
            dma((slabs,)),
            dma((2, 3)),
            dma((turned, 3)),
            dma((1,)),
            dma((6,)),
            dma((6,)),
        ],
        compiler_params=pltpu.CompilerParams(
            collective_id=0, has_side_effects=True, vmem_limit_bytes=REDUCE_ROOM
        ),
        name="reduce_slabs",
    )(*sources, lat)
    return sums, rows, lats.reshape(-1, LAT_COLS)


def thin_slab(thin, grad_bias):
    owners = WIDE_PIECES * NARROW_PIECES
    top = thin.reshape(owners, ROWS, -1)
    top = jnp.pad(top, ((0, 0), (0, 0), (0, D - top.shape[2])))
    line = grad_bias.reshape(owners, 1, -1)
    line = jnp.pad(line, ((0, 0), (0, PIECE - ROWS - 1), (0, D - line.shape[2])))
    both = jnp.concatenate([top, line], 1).astype(jnp.bfloat16)
    return both.reshape(1, WIDE_PIECES, NARROW_PIECES, PIECE, D)


def lat_block(lows, grad_cond, labels):
    high = lax.reduce_precision(grad_cond, 8, 7)
    middle = lax.reduce_precision(grad_cond - high, 8, 7)
    label_parts = jnp.stack([labels // 32, labels % 32], 1).astype(jnp.bfloat16)
    whole = jnp.concatenate(
        [
            lows,
            middle.astype(jnp.bfloat16),
            (grad_cond - high - middle).astype(jnp.bfloat16),
            label_parts,
        ],
        1,
    )
    room = LAT_ROWS * LAT_COLS // labels.shape[0] - whole.shape[1]
    return jnp.pad(whole, ((0, 0), (0, room))).reshape(LAT_ROWS, LAT_COLS)


def plain_grads(
    down_slabs, up_slabs, mats_slabs, thin, grad_bias, lows, grad_cond, labels, row_count
):
    def scattered(member, up_form):
        order = (0, 1, 3, 2, 4) if up_form else (0, 1, 2, 3, 4)
        member = member.astype(jnp.float32).transpose(order)
        member = member.reshape(member.shape[0], -1, FF if up_form else D)
        return lax.psum_scatter(member, AXES, scatter_dimension=1, tiled=True)

    proj_grad = scattered(mats_slabs, True)
    row_start = lax.axis_index(AXES) * row_count
    thin_grad = lax.psum_scatter(thin, AXES, scatter_dimension=0, tiled=True)
    bias_grad = lax.psum_scatter(grad_bias, AXES, scatter_dimension=0, tiled=True)
    grad_mod, grad_time2, grad_fin, grad_time1, grad_table = latent_grads(
        lows, grad_cond, labels, row_start, row_count
    )
    mats_grad = jnp.concatenate(
        [proj_grad[0], grad_mod, grad_time2, grad_fin, thin_grad, grad_time1, grad_table], 1
    )
    return (mats_grad, scattered(up_slabs, True), scattered(down_slabs, False), bias_grad)


def update_kernel(
    sums_ref,
    rows_ref,
    lat_ref,
    loss_ref,
    mats_ref,
    up_ref,
    down_ref,
    bias_ref,
    mats_row,
    mats_col,
    up_row,
    up_col,
    down_row,
    down_col,
    bias_state,
    loss_out,
    mats_grad,
    mats_new,
    mats_copy,
    mats_row_new,
    mats_col_new,
    up_grad,
    up_new,
    up_copy,
    up_row_new,
    up_col_new,
    down_grad,
    down_new,
    down_copy,
    down_row_new,
    down_col_new,
    bias_grad,
    bias_new,
    bias_copy,
    bias_state_new,
    part,
    got_plane,
    mine,
    got_level,
    column,
    result,
    squares_plane,
    squares_level,
    sems,
):
    full, low = jnp.float32, jnp.bfloat16
    wide, narrow = lax.axis_index(WIDE), lax.axis_index(NARROW)
    z, spot = wide // 2, (wide % 2) * 4 + narrow

    def plane_device(k):
        there = (spot + k) % 8
        return (z * 2 + there // 4, there % 4)

    def level_device(k):
        return (((z + k) % 4) * 2 + wide % 2, narrow)

    barrier = pltpu.get_barrier_semaphore()
    for k in range(1, 8):
        pl.semaphore_signal(barrier, inc=1, device_id=plane_device(k), device_id_type=MESH_ID)
    for k in range(1, 4):
        pl.semaphore_signal(barrier, inc=1, device_id=level_device(k), device_id_type=MESH_ID)
    pl.semaphore_wait(barrier, 10)

    def remote(source, target, phase, k, device):
        return pltpu.make_async_remote_copy(
            src_ref=source,
            dst_ref=target,
            send_sem=sems.at[0, phase, k],
            recv_sem=sems.at[1, phase, k],
            device_id=device,
            device_id_type=MESH_ID,
        )

    def exchange(copies):
        for copy in copies:
            copy.start()
        for copy in copies:
            copy.wait()

    lane = lax.broadcasted_iota(jnp.int32, (1, 128), 1)

    def spread(value, place):
        return jnp.where(lane == place, value, 0.0)

    def pick(row, place):
        return jnp.sum(jnp.where(lane == place, row, 0.0), 1, keepdims=True)

    def total(values):
        return jnp.sum(jnp.sum(values, 1, keepdims=True), 0, keepdims=True)

    count = lat_ref.shape[0] // 4
    order = lax.broadcasted_iota(jnp.int32, (count, count * 4), 0) * 4
    place = lax.broadcasted_iota(jnp.int32, (count, count * 4), 1)
    quarters = [
        product((place == order + k).astype(low), lat_ref[...]).astype(low) for k in range(4)
    ]
    owner_row = (wide * NARROW_PIECES + narrow) * ROWS
    chosen = (
        lax.broadcasted_iota(jnp.int32, (16, D), 1)
        == lax.broadcasted_iota(jnp.int32, (16, D), 0) + owner_row
    ).astype(low)

    def rows_of(member):
        return contract(chosen, member, 1, 1).astype(low)

    act_rows = rows_of(quarters[0][:, :D])
    hid_rows = rows_of(quarters[0][:, D : 2 * D])
    high = quarters[2][:, 2 * D : 3 * D]
    for j in range(NARROW_PIECES):
        mats_grad[:, j * D : (j + 1) * D] = rows_ref[EXPERTS + SHARED, j]
    mats_grad[:, 4 * D : 6 * D] = product(act_rows, quarters[0][:, 2 * D :])[:ROWS]
    mats_grad[:, 6 * D : 10 * D] = product(act_rows, quarters[1])[:ROWS]
    mats_grad[:, 10 * D : 11 * D] = product(hid_rows, high)[:ROWS]
    mats_grad[:, 11 * D : 13 * D] = product(act_rows, quarters[2][:, : 2 * D])[:ROWS]
    time_rows = rows_of(quarters[2][:, 3 * D :])
    time_one = product(time_rows, quarters[3][:, :FREQ])
    label_at = FREQ + 2 * D
    labels = quarters[3][:, label_at : label_at + 128].astype(full)
    label = labels[:, 0:1] * 32.0 + labels[:, 1:2]
    label_hot = (
        lax.broadcasted_iota(jnp.int32, (count, 1024), 1).astype(full) == label
    ).astype(low)
    table = (
        product(rows_of(high), label_hot)
        + product(rows_of(quarters[3][:, FREQ : FREQ + D]), label_hot)
        + product(rows_of(quarters[3][:, FREQ + D : FREQ + 2 * D]), label_hot)
    )
    start_last = 13 * D
    width_last = mats_grad.shape[1] - start_last
    room = 11 * 128
    thin = sums_ref[EXPERTS + SHARED][:16, :128]
    thin = jnp.where(
        (lax.broadcasted_iota(jnp.int32, (16, 128), 1) < EXPERTS + 2 * PD)
        & (lax.broadcasted_iota(jnp.int32, (16, 128), 0) < ROWS),
        thin,
        0.0,
    )

    def padded(member):
        return jnp.concatenate(
            [member, jnp.zeros((16, room - member.shape[1]), full)], 1
        )

    last = (
        padded(thin)
        + pltpu.roll(padded(time_one), EXPERTS + 2 * PD, 1)
        + pltpu.roll(padded(table), EXPERTS + 2 * PD + FREQ, 1)
    )
    mats_grad[:, start_last:] = last[:ROWS, :width_last]
    bias_grad[...] = sums_ref[EXPERTS + SHARED][ROWS : ROWS + 1, : bias_grad.shape[1]]

    part[...] = jnp.zeros_like(part)
    widths = column_widths()
    mats_at, line_at = 360, 416
    total_cols = mats_grad.shape[1]
    cuts = [(at, min(at + 128, total_cols)) for at in range(0, total_cols, 128)]
    for number, (begin, end) in enumerate(cuts):
        values = mats_grad[:, begin:end]
        part[mats_at + number : mats_at + number + 1, : end - begin] = jnp.sum(
            values * values + eps_fact, 0, keepdims=True
        )
    bounds = [sum(widths[:k]) for k in range(len(widths) + 1)]
    last_lane = lax.broadcasted_iota(jnp.int32, (ROWS, width_last), 1) + start_last
    last_sq = mats_grad[:, start_last:] * mats_grad[:, start_last:] + eps_fact
    line = spread(loss_ref[...], 46)
    for k in range(len(widths)):
        if k < 5:
            values = mats_grad[:, bounds[k] : bounds[k + 1]]
            sq = values * values + eps_fact
        else:
            sq = jnp.where((last_lane >= bounds[k]) & (last_lane < bounds[k + 1]), last_sq, 0.0)
        new = decay * mats_row[:, k : k + 1] + (1.0 - decay) * (
            jnp.sum(sq, 1, keepdims=True) / widths[k]
        )
        mats_row_new[:, k : k + 1] = new
        line = line + spread(jnp.sum(new, 0, keepdims=True), k)

    def begin_up(e, line):
        for j in range(NARROW_PIECES):
            up_grad[e, :, j * D : (j + 1) * D] = rows_ref[e, j]
        values = up_grad[e]
        sq = values * values + eps_fact
        new = decay * up_row[e] + (1.0 - decay) * (jnp.sum(sq, 1, keepdims=True) / FF)
        up_row_new[e] = new
        cols = jnp.sum(sq, 0, keepdims=True)
        for k in range(FF // 128):
            part[pl.ds(24 * k + e, 1), :] = cols[:, 128 * k : 128 * (k + 1)]
        return line + spread(jnp.sum(new, 0, keepdims=True), 10 + e)

    def begin_down(e, line):
        values = sums_ref[e]
        down_grad[e] = values
        sq = values * values + eps_fact
        new = decay * down_row[e] + (1.0 - decay) * (jnp.sum(sq, 1, keepdims=True) / D)
        down_row_new[e] = new
        cols = jnp.sum(sq, 0, keepdims=True)
        for k in range(D // 128):
            part[pl.ds(24 * (12 + k) + e, 1), :] = cols[:, 128 * k : 128 * (k + 1)]
        return line + spread(jnp.sum(new, 0, keepdims=True), 28 + e)

    line = lax.fori_loop(0, EXPERTS + SHARED, begin_up, line)
    line = lax.fori_loop(0, EXPERTS + SHARED, begin_down, line)
    part[line_at : line_at + 1, :] = line

    exchange(
        [
            remote(
                part.at[pl.ds(((spot + k) % 8) * 64, 64)], got_plane.at[k], 0, k, plane_device(k)
            )
            for k in range(1, 8)
        ]
    )
    here = part[pl.ds(pl.multiple_of(spot * 64, 64), 64), :]
    for k in range(1, 8):
        here = here + got_plane[k]
    mine[...] = here.reshape(4, 16, 128)
    exchange(
        [
            remote(mine.at[(z + k) % 4], got_level.at[k], 1, k, level_device(k))
            for k in range(1, 4)
        ]
    )
    column[z] = mine[z] + got_level[1] + got_level[2] + got_level[3]
    exchange(
        [remote(column.at[z], column.at[z], 2, k, level_device(k)) for k in range(1, 4)]
    )
    result[spot] = column[...]
    exchange(
        [remote(result.at[spot], result.at[spot], 3, k, plane_device(k)) for k in range(1, 8)]
    )

    def sums_row(row, width=128):
        if isinstance(row, int):
            return result[row // 64, (row // 16) % 4, row % 16 : row % 16 + 1, :width]
        return result[row // 64, (row // 16) % 4, pl.ds(row % 16, 1), :width]

    line = sums_row(line_at)
    loss_out[...] = pick(line, 46)
    for number, (begin, end) in enumerate(cuts):
        mats_col_new[:, begin:end] = decay * mats_col[:, begin:end] + (1.0 - decay) * (
            sums_row(mats_at + number, end - begin) / D
        )

    squares = jnp.zeros((1, 128), full)
    for k in range(5):
        begin, end = bounds[k], bounds[k + 1]
        step = mats_grad[:, begin:end] * lax.rsqrt(
            mats_row_new[:, k : k + 1] * mats_col_new[:, begin:end] / (pick(line, k) / D)
        )
        mats_new[:, begin:end] = step
        squares = squares + spread(total(step * step), k)

    def by_piece(values):
        chosen_value = values[0]
        for k in range(6, len(widths)):
            chosen_value = jnp.where(last_lane >= bounds[k], values[k - 5], chosen_value)
        return chosen_value

    row_last = by_piece([mats_row_new[:, k : k + 1] for k in range(5, len(widths))])
    mean_last = by_piece([pick(line, k) / D for k in range(5, len(widths))])
    step_last = mats_grad[:, start_last:] * lax.rsqrt(
        row_last * mats_col_new[:, start_last:] / mean_last
    )
    mats_new[:, start_last:] = step_last
    for k in range(5, len(widths)):
        inside = (last_lane >= bounds[k]) & (last_lane < bounds[k + 1])
        squares = squares + spread(total(jnp.where(inside, step_last * step_last, 0.0)), k)

    def step_up(e, squares):
        cols = jnp.concatenate([sums_row(24 * k + e) for k in range(FF // 128)], 1)
        new = decay * up_col[pl.ds(e, 1), :] + (1.0 - decay) * (cols / D)
        up_col_new[pl.ds(e, 1), :] = new
        step = up_grad[e] * lax.rsqrt(up_row_new[e] * new / (pick(line, 10 + e) / D))
        up_new[e] = step
        return squares + spread(total(step * step), 10 + e)

    def step_down(e, squares):
        cols = jnp.concatenate([sums_row(24 * (12 + k) + e) for k in range(D // 128)], 1)
        new = decay * down_col[pl.ds(e, 1), :] + (1.0 - decay) * (cols / FF)
        down_col_new[pl.ds(e, 1), :] = new
        step = down_grad[e] * lax.rsqrt(down_row_new[e] * new / (pick(line, 28 + e) / FF))
        down_new[e] = step
        return squares + spread(total(step * step), 28 + e)

    squares = lax.fori_loop(0, EXPERTS + SHARED, step_up, squares)
    squares = lax.fori_loop(0, EXPERTS + SHARED, step_down, squares)
    state = decay * bias_state[...] + (1.0 - decay) * (
        bias_grad[...] * bias_grad[...] + eps_fact
    )
    bias_state_new[...] = state
    bias_step = bias_grad[...] * lax.rsqrt(state)
    squares = squares + spread(total(bias_step * bias_step), 46)
    squares_plane[spot] = jnp.broadcast_to(squares, (8, 128))
    exchange(
        [
            remote(squares_plane.at[spot], squares_plane.at[spot], 4, k, plane_device(k))
            for k in range(1, 8)
        ]
    )
    squares_level[z] = jnp.sum(squares_plane[...], 0)
    exchange(
        [
            remote(squares_level.at[z], squares_level.at[z], 5, k, level_device(k))
            for k in range(1, 4)
        ]
    )
    squares = jnp.sum(squares_level[...], 0)[0:1]

    def clipped(place, entries):
        rms = jnp.sqrt(pick(squares, place) / entries)
        return jnp.maximum(1.0, rms / clip_level)

    def settle(new_ref, copy_ref, index, master, step, limit):
        value = master - learn_rate * (step / limit)
        new_ref[index] = value
        copy_ref[index] = value.astype(low)

    for k in range(5):
        index = (slice(None), slice(bounds[k], bounds[k + 1]))
        settle(
            mats_new, mats_copy, index, mats_ref[index], mats_new[index], clipped(k, D * widths[k])
        )
    limit = by_piece([clipped(k, D * widths[k]) for k in range(5, len(widths))])
    index = (slice(None), slice(start_last, None))
    settle(mats_new, mats_copy, index, mats_ref[index], mats_new[index], limit)

    def settle_pair(e, unused):
        settle(up_new, up_copy, e, up_ref[e], up_new[e], clipped(10 + e, D * FF))
        settle(down_new, down_copy, e, down_ref[e], down_new[e], clipped(28 + e, D * FF))
        return unused

    lax.fori_loop(0, EXPERTS + SHARED, settle_pair, 0)
    index = (slice(None), slice(None))
    settle(bias_new, bias_copy, index, bias_ref[...], bias_step, clipped(46, 15 * D))


def update_kernel_call(sums, rows, lat, masters, factors, loss_part):
    mats, up_weights, down_weights, biases = masters
    mats_row, mats_col, up_row, up_col, down_row, down_col, bias_state = factors
    full, low = jnp.float32, jnp.bfloat16
    args = (
        sums,
        rows,
        lat,
        loss_part.reshape(1, 1),
        mats,
        up_weights,
        down_weights,
        biases.reshape(1, -1),
        mats_row.T,
        mats_col.reshape(1, -1),
        up_row[:, :, None],
        up_col,
        down_row[:, :, None],
        down_col,
        bias_state.reshape(1, -1),
    )

    def like(member, kind):
        return jax.ShapeDtypeStruct(member.shape, kind)

    stacks = []
    for at in (4, 5, 6):
        stacks.append([like(args[at], full), like(args[at], full), like(args[at], low)])
        stacks[-1] += [like(args[2 * at], full), like(args[2 * at + 1], full)]
    lines = [like(args[7], full), like(args[7], full), like(args[7], low), like(args[7], full)]
    vmem = pl.BlockSpec(memory_space=pltpu.VMEM)
    dma = pltpu.SemaphoreType.DMA
    outs = pl.pallas_call(
        update_kernel,
        out_shape=[jax.ShapeDtypeStruct((1, 1), full)] + stacks[0] + stacks[1] + stacks[2] + lines,
        in_specs=[vmem] * len(args),
        out_specs=[vmem] * 20,
        scratch_shapes=[
            pltpu.VMEM((512, 128), full),
            pltpu.VMEM((8, 64, 128), full),
            pltpu.VMEM((4, 16, 128), full),
            pltpu.VMEM((4, 16, 128), full),
            pltpu.VMEM((4, 16, 128), full),
            pltpu.VMEM((8, 4, 16, 128), full),
            pltpu.VMEM((8, 8, 128), full),
            pltpu.VMEM((4, 8, 128), full),
            dma((2, 6, 8)),
        ],
        compiler_params=pltpu.CompilerParams(
            collective_id=1, has_side_effects=True, vmem_limit_bytes=VMEM_ROOM
        ),
        name="update",
    )(*args)
    return (
        outs[0][0, 0],
        outs[1],
        outs[2],
        outs[3],
        outs[4].T,
        outs[5].reshape(-1),
        outs[6],
        outs[7],
        outs[8],
        outs[9][:, :, 0],
        outs[10],
        outs[11],
        outs[12],
        outs[13],
        outs[14][:, :, 0],
        outs[15],
        outs[16].reshape(-1),
        outs[17].reshape(-1),
        outs[18].reshape(-1),
        outs[19].reshape(-1),
    )


def gather_kernel(
    mats_in,
    bias_in,
    down_in,
    up_in,
    patches,
    places,
    freq_low,
    label_hot,
    mats_out,
    bias_out,
    down_out,
    up_out,
    mods_out,
    fin_out,
    time_out,
    cond_out,
    qkv_out,
    att_out,
    middle_out,
    moe_out,
    logits_out,
    shared_out,
    mats_got,
    mats_own,
    up_got,
    up_wide,
    up_own,
    embedded,
    down_here,
    up_here,
    near_send,
    near_recv,
    own_sem,
    level_send,
    level_recv,
    one_send,
    one_recv,
    two_send,
    two_recv,
    core_send,
    core_recv,
    bias_send,
    bias_recv,
    here_sem,
):
    n_down, n_up = down_in.shape[0], up_own.shape[0]
    slabs = 1 + n_down + n_up
    wide, narrow = lax.axis_index(WIDE), lax.axis_index(NARROW)
    z, x = wide // 2, wide % 2
    y, c = narrow // 2, narrow % 2
    mates = [
        (wide, (y + (k // 2) * (1 - 2 * y)) * 2 + c + (k % 2) * (1 - 2 * c)) for k in range(1, 4)
    ]
    levels = [(((z + k) % 4) * 2 + x, narrow) for k in range(1, 4)]
    to_x = (z * 2 + 1 - x, narrow)
    to_core, to_y = mates[0], mates[1]
    to_one = (z * 2 + x + (1 - c) * (1 - 2 * x), (y + c * (1 - 2 * y)) * 2 + c)
    to_two = (z * 2 + x + c * (1 - 2 * x), (y + (1 - c) * (1 - 2 * y)) * 2 + c)
    barrier = pltpu.get_barrier_semaphore()
    for target in mates + levels + [to_x]:
        pl.semaphore_signal(barrier, inc=1, device_id=target, device_id_type=MESH_ID)
    pl.semaphore_wait(barrier, 7)

    def remote(source, target, send, recv, device):
        return pltpu.make_async_remote_copy(
            src_ref=source,
            dst_ref=target,
            send_sem=send,
            recv_sem=recv,
            device_id=device,
            device_id_type=MESH_ID,
        )

    def near_mats(k):
        return remote(
            mats_in.at[mates[k - 1][1]],
            mats_got.at[narrow],
            near_send.at[0, k],
            near_recv.at[0, k],
            mates[k - 1],
        )

    def near_up(k):
        return remote(
            up_in.at[mates[k - 1][1]],
            up_got.at[narrow],
            near_send.at[1, k],
            near_recv.at[1, k],
            mates[k - 1],
        )

    own_mats = pltpu.make_async_copy(mats_in.at[narrow], mats_got.at[narrow], own_sem.at[0])
    own_up = pltpu.make_async_copy(up_in.at[narrow], up_got.at[narrow], own_sem.at[1])
    own_bias = pltpu.make_async_copy(bias_in, bias_out.at[z, x, y, c], own_sem.at[2])
    own_mats.start()
    own_up.start()
    own_bias.start()
    for k in range(1, 4):
        near_mats(k).start()

    def bias_level(k):
        return remote(
            bias_in, bias_out.at[z, x, y, c], bias_send.at[k - 1], bias_recv.at[k - 1], levels[k - 1]
        )

    def bias_x():
        part = bias_out.at[:, x, y, c]
        return remote(part, part, bias_send.at[3], bias_recv.at[3], to_x)

    def bias_y():
        part = bias_out.at[:, :, y, c]
        return remote(part, part, bias_send.at[4], bias_recv.at[4], to_y)

    def bias_core():
        part = bias_out.at[:, :, :, c]
        return remote(part, part, bias_send.at[5], bias_recv.at[5], to_core)

    for k in range(1, 4):
        bias_level(k).start()
    own_mats.wait()
    for k in range(1, 4):
        near_mats(k).wait_recv()
        near_up(k).start()
    for n in range(NARROW_PIECES):
        mats_own[n * ROWS : (n + 1) * ROWS] = mats_got[n].astype(jnp.float32)[:ROWS]
    mats_got[0, :, :] = mats_own[:16].astype(jnp.bfloat16)
    mats_got[1, :, :] = mats_own[16:32].astype(jnp.bfloat16)
    mats_got[2, :, :] = mats_own[32:].astype(jnp.bfloat16)
    own_bias.wait()

    def turn(number):
        return (number + EXPERTS) % n_up

    def whole(kind, s):
        if kind == 0:
            return mats_out
        if kind == 1:
            return down_out.at[turn(s - 1)]
        return up_out.at[turn(s - 1 - n_down)]

    def source(kind, s):
        if kind == 0:
            return mats_got.at[pl.ds(0, 3)]
        if kind == 1:
            return down_in.at[turn(s - 1)]
        return up_own.at[turn(s - 1 - n_down)]

    def piece(ref, kind, at):
        z_at, x_at, y_at, c_at = at
        if kind == 1:
            return ref.at[z_at, x_at, y_at, c_at]
        return ref.at[y_at, c_at, z_at, x_at]

    every = slice(None)

    def own_copy(kind, s):
        return pltpu.make_async_copy(
            source(kind, s), piece(whole(kind, s), kind, (z, x, y, c)), own_sem.at[3 + s % 2]
        )

    def level_copy(kind, s, k):
        return remote(
            source(kind, s),
            piece(whole(kind, s), kind, (z, x, y, c)),
            level_send.at[s % 4, k - 1],
            level_recv.at[s, k - 1],
            levels[k - 1],
        )

    def one_copy(kind, s):
        part = piece(whole(kind, s), kind, (every, x, y, c))
        return remote(part, part, one_send.at[s % 4], one_recv.at[s], to_one)

    def two_copy(kind, s, first):
        at = (every, every, y, c) if first == 0 else (every, x, every, c)
        part = piece(whole(kind, s), kind, at)
        return remote(part, part, two_send.at[s % 4], two_recv.at[s], to_two)

    def core_copy(kind, s):
        part = piece(whole(kind, s), kind, (every, every, every, c))
        return remote(part, part, core_send.at[s % 4], core_recv.at[s], to_core)

    def stage_level(kind, s):
        own_copy(kind, s).start()
        for k in range(1, 4):
            level_copy(kind, s, k).start()

    def stage_one(kind, s):
        own_copy(kind, s).wait()
        for k in range(1, 4):
            level_copy(kind, s, k).wait_recv()
        one_copy(kind, s).start()

    def stage_two(kind, s):
        one_copy(kind, s).wait_recv()
        for first in range(2):

            @pl.when(c == first)
            def _():
                two_copy(kind, s, first).start()

    def stage_core(kind, s):
        two_copy(kind, s, 0).wait_recv()
        core_copy(kind, s).start()

    def stage_last(kind, s):
        core_copy(kind, s).wait_recv()

    def stage_sent(kind, s):
        for k in range(1, 4):
            level_copy(kind, s, k).wait_send()
        one_copy(kind, s).wait_send()
        two_copy(kind, s, 0).wait_send()
        core_copy(kind, s).wait_send()

    stages = (
        (stage_sent, 4),
        (stage_level, 0),
        (stage_one, 1),
        (stage_two, 2),
        (stage_core, 3),
        (stage_last, 4),
    )

    lats = patches.shape[0] // PATCHES
    shared_at = 1 + n_down + SHARED + 4
    low, full = jnp.bfloat16, jnp.float32

    def matrix(number, begin, end):
        chunk = mats_out[number // 2, number % 2]
        return chunk.reshape(D, chunk.shape[-1])[:, begin:end]

    def bias_rows():
        return jnp.sum(bias_out[...].astype(full).reshape(-1, 16, D), 0)

    def wide_row(rows, begin, end):
        return jnp.concatenate([rows[k : k + 1] for k in range(begin, end)], 1)

    def conditions():
        rows = bias_rows()
        pre_time = contract(freq_low[...], matrix(3, 1408, 1664), 1, 1) + rows[11:12]
        hid_time = jax.nn.silu(pre_time).astype(low)
        cond = (
            product(hid_time, matrix(3, 1024, 1408))
            + rows[12:13]
            + contract(label_hot[...], matrix(3, 0, 1024), 1, 1)
        )
        act = jax.nn.silu(cond).astype(low)
        time_out[...] = pre_time
        cond_out[...] = cond
        mods_out[:, : 4 * D] = product(act, matrix(1, 0, 4 * D)) + wide_row(rows, 4, 8)
        mods_out[:, 4 * D :] = product(act, matrix(2, 0, 2 * D)) + wide_row(rows, 8, 10)
        fin_out[...] = product(act, matrix(2, 2 * D, 4 * D)) + wide_row(rows, 13, 15)

    def mod_row(start, number):
        return mods_out[pl.ds(start // PATCHES, 1), number * D : (number + 1) * D]

    def attention_in(start):
        rows = bias_rows()
        span = pl.ds(start, PATCHES)
        emb = contract(patches[span, :], matrix(2, 4 * D, 4 * D + 128), 1, 1)
        emb = emb + rows[10:11] + places[...]
        embedded[...] = emb
        normed, unused_std = layer_norm(emb)
        attn_in = (normed * (1.0 + mod_row(start, 1)) + mod_row(start, 0)).astype(low)
        qkv_out[span, :] = (
            product(attn_in, matrix(0, 0, 3 * D)) + wide_row(rows, 0, 3)
        ).astype(low)

    def attention_heads(start):
        span = pl.ds(start, PATCHES)
        lane = lax.broadcasted_iota(jnp.int32, (PATCHES, 2 * HD), 1)
        for pair in range(HEADS // 2):
            at = pair * 2 * HD
            queries = qkv_out[span, at : at + 2 * HD]
            keys = qkv_out[span, D + at : D + at + 2 * HD]
            values = qkv_out[span, 2 * D + at : 2 * D + at + 2 * HD]
            halves = []
            for half in range(2):
                mine = (lane < HD) if half == 0 else (lane >= HD)
                scores = contract(jnp.where(mine, queries, 0), keys, 1, 1) * HD ** (-0.5)
                powers = jnp.exp(scores - jnp.max(scores, 1, keepdims=True))
                probs = (powers / jnp.sum(powers, 1, keepdims=True)).astype(low)
                halves.append(product(probs, values))
            att_out[span, at : at + 2 * HD] = jnp.where(lane < HD, halves[0], halves[1]).astype(low)

    def attention_out(start):
        rows = bias_rows()
        span = pl.ds(start, PATCHES)
        attn = product(att_out[span, :], matrix(0, 3 * D, 4 * D)) + rows[3:4]
        middle = embedded[...] + mod_row(start, 2) * attn
        middle_out[span, :] = middle
        normed, unused_std = layer_norm(middle)
        moe_in = (normed * (1.0 + mod_row(start, 4)) + mod_row(start, 3)).astype(low)
        moe_out[span, :] = moe_in
        logits_out[span, :] = product(moe_in, matrix(0, 4 * D, 4 * D + 128))

    def fetch(shared_id):
        e = EXPERTS + shared_id
        first = pltpu.make_async_copy(down_out.at[e], down_here, here_sem.at[0])
        second = pltpu.make_async_copy(up_out.at[e], up_here, here_sem.at[1])
        first.start()
        second.start()
        first.wait()
        second.wait()

    def shared_block(shared_id, start):
        span = pl.ds(start, PATCHES)
        rows = moe_out[span, :]
        chunks = [up_here[n // 2, n % 2].reshape(D, D) for n in range(NARROW_PIECES)]
        down = down_here[...].reshape(FF, D)
        total = None
        for cut in range(0, FF, CUT):
            pre_act = product(rows, up_columns(chunks, cut))
            part = product(gelu_only(pre_act).astype(low), down[cut : cut + CUT])
            total = part if total is None else total + part
        if shared_id == 0:
            shared_out[span, :] = total
        else:
            shared_out[span, :] += total

    def tick(t, unused):
        @pl.when(t == 1)
        def _():
            for k in range(1, 4):
                bias_level(k).wait_recv()
            bias_x().start()

        @pl.when(t == 2)
        def _():
            bias_x().wait_recv()
            bias_y().start()

        @pl.when(t == 3)
        def _():
            bias_y().wait_recv()
            bias_core().start()

        @pl.when(t == 6)
        def _():
            own_up.wait()
            for k in range(1, 4):
                near_up(k).wait_recv()
            for n in range(NARROW_PIECES):
                up_wide[n] = up_got[n].astype(jnp.float32)

            for e in range(n_up):
                up_own[e] = jnp.concatenate(
                    [up_wide[n, e * ROWS : (e + 1) * ROWS] for n in range(NARROW_PIECES)], 0
                ).astype(jnp.bfloat16)

        for stage, lag in stages:
            s = t - lag

            @pl.when(s == 0)
            def _():
                stage(0, 0)

            @pl.when((s >= 1) & (s < 1 + n_down))
            def _():
                stage(1, jnp.clip(s, 1, n_down))

            @pl.when((s >= 1 + n_down) & (s < slabs))
            def _():
                stage(2, jnp.clip(s, 1 + n_down, slabs - 1))

        @pl.when(t == 5)
        def _():
            bias_core().wait_recv()
            conditions()

        for number, unit in enumerate((attention_in, attention_heads, attention_out)):

            @pl.when((t >= 6) & (t < 6 + 3 * lats) & ((t - 6) % 3 == number))
            def _():
                unit(pl.multiple_of(jnp.clip((t - 6) // 3, 0, lats - 1) * PATCHES, PATCHES))

        for shared_id in range(SHARED):
            begin = shared_at + shared_id * lats

            @pl.when(t == begin)
            def _():
                fetch(shared_id)

            @pl.when((t >= begin) & (t < begin + lats))
            def _():
                shared_block(
                    shared_id, pl.multiple_of(jnp.clip(t - begin, 0, lats - 1) * PATCHES, PATCHES)
                )

        return unused

    lax.fori_loop(0, slabs + 4, tick, 0)
    for k in range(1, 4):
        near_mats(k).wait_send()
        near_up(k).wait_send()
        bias_level(k).wait_send()
    bias_x().wait_send()
    bias_y().wait_send()
    bias_core().wait_send()


def gather_weights(
    mats, up_weights, down_weights, biases, patches, places, freq_low, label_hot
):
    low = jnp.bfloat16
    owner = lax.axis_index(AXES)
    m = mats.astype(low)
    rows = m.shape[0]

    thin = 13 * D

    def thin_part(at):
        return jnp.pad(m[:, at : at + 16], ((0, 0), (0, 112)))

    mats_in = jnp.stack(
        [
            jnp.concatenate([m[:, : 4 * D], thin_part(thin)], 1),
            jnp.concatenate([m[:, 4 * D : 8 * D], thin_part(thin + 16)], 1),
            jnp.concatenate(
                [m[:, 8 * D : 10 * D], m[:, 11 * D : 13 * D], thin_part(thin + 32)], 1
            ),
            jnp.concatenate(
                [
                    m[:, thin + 48 + FREQ :],
                    jnp.zeros((rows, 24), low),
                    m[:, 10 * D : 11 * D],
                    m[:, thin + 48 : thin + 48 + FREQ],
                ],
                1,
            ),
        ],
        0,
    )
    mats_in = jnp.pad(mats_in, ((0, 0), (0, 16 - rows), (0, 0)))
    line = lax.dynamic_update_slice(
        jnp.zeros((16 * D,), low), biases.astype(low), (owner * biases.shape[0],)
    )
    n_up = up_weights.shape[0]
    up_in = (
        up_weights.astype(low)
        .reshape(n_up, rows, NARROW_PIECES, D)
        .transpose(2, 0, 1, 3)
        .reshape(NARROW_PIECES, n_up * rows, D)
    )
    room = (n_up * rows + 15) // 16 * 16
    up_in = jnp.pad(up_in, ((0, 0), (0, room - n_up * rows), (0, 0)))
    slabs = 1 + 2 * n_up
    spread = mats_in.shape[2]
    dma = pltpu.SemaphoreType.DMA
    anywhere = pl.BlockSpec(memory_space=pl.ANY)
    tokens = patches.shape[0]
    full, vmem = jnp.float32, pl.BlockSpec(memory_space=pltpu.VMEM)
    outs = pl.pallas_call(
        gather_kernel,
        out_shape=[
            jax.ShapeDtypeStruct((2, 2, 4, 2, 3, 16, spread), low),
            jax.ShapeDtypeStruct((4, 2, 2, 2, 16, D), low),
            jax.ShapeDtypeStruct((n_up, 4, 2, 2, 2, PIECE, D), low),
            jax.ShapeDtypeStruct((n_up, 2, 2, 4, 2, PIECE, D), low),
            jax.ShapeDtypeStruct((8, 6 * D), full),
            jax.ShapeDtypeStruct((8, 2 * D), full),
            jax.ShapeDtypeStruct((8, D), full),
            jax.ShapeDtypeStruct((8, D), full),
            jax.ShapeDtypeStruct((tokens, 3 * D), low),
            jax.ShapeDtypeStruct((tokens, D), low),
            jax.ShapeDtypeStruct((tokens, D), full),
            jax.ShapeDtypeStruct((tokens, D), low),
            jax.ShapeDtypeStruct((tokens, 128), full),
            jax.ShapeDtypeStruct((tokens, D), full),
        ],
        in_specs=[anywhere] * 4 + [vmem] * 4,
        out_specs=[vmem] * 2 + [anywhere] * 2 + [vmem] * 10,
        scratch_shapes=[
            pltpu.VMEM((NARROW_PIECES, 16, spread), low),
            pltpu.VMEM((PIECE, spread), jnp.float32),
            pltpu.VMEM((NARROW_PIECES, room, D), low),
            pltpu.VMEM((NARROW_PIECES, room, D), jnp.float32),
            pltpu.VMEM((n_up, PIECE, D), low),
            pltpu.VMEM((PATCHES, D), full),
            pltpu.VMEM((4, 2, 2, 2, PIECE, D), low),
            pltpu.VMEM((2, 2, 4, 2, PIECE, D), low),
            dma((2, 4)),
            dma((2, 4)),
            dma((5,)),
            dma((4, 3)),
            dma((slabs, 3)),
            dma((4,)),
            dma((slabs,)),
            dma((4,)),
            dma((slabs,)),
            dma((4,)),
            dma((slabs,)),
            dma((6,)),
            dma((6,)),
            dma((2,)),
        ],
        compiler_params=pltpu.CompilerParams(
            collective_id=2, has_side_effects=True, vmem_limit_bytes=VMEM_ROOM
        ),
        name="gather_weights",
    )(
        mats_in,
        line.reshape(16, D),
        down_weights.astype(low),
        up_in,
        patches,
        places,
        freq_low,
        label_hot,
    )
    return outs


def split_weights(weights):
    mats_full, up_full, down_full, bias_full = weights
    matrices = cut_pieces(mats_full, column_widths(), 1)
    vectors = [member.astype(jnp.float32) for member in cut_pieces(bias_full, bias_widths(), 0)]
    up_full = up_full.reshape(-1, D, NARROW_PIECES, D).transpose(0, 2, 1, 3)
    return (matrices, vectors, up_full, down_full)


def forward(weights, latents, noise, timesteps, labels, routes):
    matrices, vectors, up_full, down_full = weights
    w_qkv, w_proj, w_mod, w_time2, w_final, w_router, w_head, w_patch, w_time1, w_table = matrices
    b_qkv, b_proj, b_mod, b_patch, b_time1, b_time2, b_final = vectors
    num_latents = latents.shape[0]
    rows_here = num_latents * PATCHES
    steps_f = timesteps.astype(jnp.float32)
    signal, spread = noise_level(steps_f)
    noisy = signal[:, None] * latents + spread[:, None] * noise
    patches = noisy.reshape(rows_here, PD).astype(jnp.bfloat16)
    embedded = (
        contract(patches, w_patch, 1, 1).reshape(num_latents, PATCHES, D)
        + b_patch
        + positions()[None]
    )
    freq_low = time_features(steps_f).astype(jnp.bfloat16)
    pre_time = contract(freq_low, w_time1, 1, 1) + b_time1
    hid_time = jax.nn.silu(pre_time).astype(jnp.bfloat16)
    label_hot = (labels[:, None] == jnp.arange(CLASSES, dtype=jnp.int32)[None, :]).astype(
        jnp.float32
    )
    label_emb = lax.dot_general(
        label_hot,
        w_table.astype(jnp.float32),
        (((1,), (1,)), ((), ())),
        precision=lax.Precision.HIGHEST,
        preferred_element_type=jnp.float32,
    )
    cond = product(hid_time, w_time2) + b_time2 + label_emb
    cond_act = jax.nn.silu(cond).astype(jnp.bfloat16)
    modulation = product(cond_act, w_mod) + b_mod
    final_mod = product(cond_act, w_final) + b_final
    shift_attn, scale_attn, gate_attn, shift_moe, scale_moe, gate_moe = [
        member[:, None, :] for member in jnp.split(modulation, 6, 1)
    ]
    shift_fin, scale_fin = [member[:, None, :] for member in jnp.split(final_mod, 2, 1)]
    normed_one, inv_one = layer_norm(embedded)
    attn_in = (
        (normed_one * (1.0 + scale_attn) + shift_attn).astype(jnp.bfloat16).reshape(rows_here, D)
    )
    qkv_out = (
        (product(attn_in, w_qkv) + b_qkv)
        .astype(jnp.bfloat16)
        .reshape(num_latents, PATCHES, 3, HEADS, HD)
    )
    scores = jnp.einsum(
        LQK, qkv_out[:, :, 0], qkv_out[:, :, 1], preferred_element_type=jnp.float32
    ) * HD ** (-0.5)
    log_totals = jax.nn.logsumexp(scores, -1)
    probs_low = jax.nn.softmax(scores, -1).astype(jnp.bfloat16)
    attended = (
        jnp.einsum(
            "lhqk,lkhd->lqhd", probs_low, qkv_out[:, :, 2], preferred_element_type=jnp.float32
        )
        .astype(jnp.bfloat16)
        .reshape(rows_here, D)
    )
    attn_out = (product(attended, w_proj) + b_proj).reshape(num_latents, PATCHES, D)
    middle = embedded + gate_attn * attn_out
    normed_two, inv_two = layer_norm(middle)
    moe_in = (normed_two * (1.0 + scale_moe) + shift_moe).astype(jnp.bfloat16).reshape(rows_here, D)
    logits = product(moe_in, w_router)
    route_hot = (routes[:, :, None] == jnp.arange(EXPERTS, dtype=jnp.int32)[None, None, :]).astype(
        jnp.float32
    )
    gate_vals = jax.nn.softmax(jnp.sum(route_hot * logits[:, None, :], 2), -1)
    slot_of, slot_meta = pack_slots(routes)
    routed = experts_forward(slot_of, slot_meta, moe_in, up_full, down_full)
    moe_out = gate_vals[:, 0:1] * routed[0] + gate_vals[:, 1:2] * routed[1]
    for shared_id in range(EXPERTS, EXPERTS + SHARED):
        for cut in range(0, FF, CUT):
            pre_act = product(moe_in, up_columns(up_full[shared_id], cut))
            activated = gelu_only(pre_act).astype(jnp.bfloat16)
            moe_out = moe_out + product(activated, down_full[shared_id, cut : cut + CUT])
    moe_out = moe_out.reshape(num_latents, PATCHES, D)
    final_state = middle + gate_moe * moe_out
    normed_fin, inv_fin = layer_norm(final_state)
    head_in = (
        (normed_fin * (1.0 + scale_fin) + shift_fin).astype(jnp.bfloat16).reshape(rows_here, D)
    )
    errors = product(head_in, w_head) - noise.reshape(rows_here, PD)
    return SimpleNamespace(
        patches=patches,
        freq_low=freq_low,
        pre_time=pre_time,
        hid_time=hid_time,
        label_hot=label_hot,
        cond=cond,
        cond_act=cond_act,
        scale_attn=scale_attn,
        gate_attn=gate_attn,
        scale_moe=scale_moe,
        gate_moe=gate_moe,
        scale_fin=scale_fin,
        normed_one=normed_one,
        inv_one=inv_one,
        attn_in=attn_in,
        qkv_out=qkv_out,
        log_totals=log_totals,
        attended=attended,
        attn_out=attn_out,
        normed_two=normed_two,
        inv_two=inv_two,
        moe_in=moe_in,
        route_hot=route_hot,
        gate_vals=gate_vals,
        slot_of=slot_of,
        slot_meta=slot_meta,
        routed=routed,
        moe_out=moe_out,
        normed_fin=normed_fin,
        inv_fin=inv_fin,
        head_in=head_in,
        errors=errors,
    )


def forward_fused(mats, up_weights, down_weights, biases, latents, noise, timesteps, labels, routes):
    num_latents = latents.shape[0]
    rows_here = num_latents * PATCHES
    steps_f = timesteps.astype(jnp.float32)
    signal, spread = noise_level(steps_f)
    noisy = signal[:, None] * latents + spread[:, None] * noise
    patches = noisy.reshape(rows_here, PD).astype(jnp.bfloat16)
    freq_low = time_features(steps_f).astype(jnp.bfloat16)
    label_low = (labels[:, None] == jnp.arange(1024, dtype=jnp.int32)[None, :]).astype(jnp.bfloat16)
    less = ((0, 8 - num_latents), (0, 0))
    outs = gather_weights(
        mats,
        up_weights,
        down_weights,
        biases,
        jnp.pad(patches, ((0, 0), (0, 128 - PD))),
        positions(),
        jnp.pad(freq_low, less),
        jnp.pad(label_low, less),
    )
    mats_full, bias_full, down_full, up_full = outs[:4]
    modulation, final_mod, pre_time, cond = [member[:num_latents] for member in outs[4:8]]
    qkv_out, attended, middle, moe_in, logits, shared_out = outs[8:]
    logits = logits[:, :EXPERTS]
    n_up = up_full.shape[0]
    full = mats_full.reshape(NARROW_PIECES, D, -1)
    matrices = [
        full[0][:, : 3 * D],
        full[0][:, 3 * D : 4 * D],
        jnp.concatenate([full[1][:, : 4 * D], full[2][:, : 2 * D]], 1),
        full[3][:, 1024 : 1024 + D],
        full[2][:, 2 * D : 4 * D],
        full[0][:, 4 * D : 4 * D + 16],
        full[1][:, 4 * D : 4 * D + 16],
        full[2][:, 4 * D : 4 * D + 16],
        full[3][:, 1024 + D :],
        full[3][:, :CLASSES],
    ]
    line = jnp.sum(bias_full.reshape(-1, 16, D).astype(jnp.float32), 0).reshape(-1)[: 15 * D]
    vectors = cut_pieces(line, bias_widths(), 0)
    up_full = up_full.reshape(n_up, NARROW_PIECES, D, D)
    down_full = down_full.reshape(n_up, FF, D)
    weights = (matrices, vectors, up_full, down_full)
    w_qkv, w_proj, w_mod, w_time2, w_final, w_router, w_head, w_patch, w_time1, w_table = matrices
    b_qkv, b_proj, b_mod, b_patch, b_time1, b_time2, b_final = vectors
    shift_attn, scale_attn, gate_attn, shift_moe, scale_moe, gate_moe = [
        member[:, None, :] for member in jnp.split(modulation, 6, 1)
    ]
    shift_fin, scale_fin = [member[:, None, :] for member in jnp.split(final_mod, 2, 1)]
    embedded = (
        contract(patches, w_patch, 1, 1).reshape(num_latents, PATCHES, D)
        + b_patch
        + positions()[None]
    )
    normed_one, inv_one = layer_norm(embedded)
    attn_in = (
        (normed_one * (1.0 + scale_attn) + shift_attn).astype(jnp.bfloat16).reshape(rows_here, D)
    )
    qkv_out = qkv_out.reshape(num_latents, PATCHES, 3, HEADS, HD)
    scores = jnp.einsum(
        LQK, qkv_out[:, :, 0], qkv_out[:, :, 1], preferred_element_type=jnp.float32
    ) * HD ** (-0.5)
    attn_out = (product(attended, w_proj) + b_proj).reshape(num_latents, PATCHES, D)
    middle = middle.reshape(num_latents, PATCHES, D)
    normed_two, inv_two = layer_norm(middle)
    route_hot = (routes[:, :, None] == jnp.arange(EXPERTS, dtype=jnp.int32)[None, None, :]).astype(
        jnp.float32
    )
    gate_vals = jax.nn.softmax(jnp.sum(route_hot * logits[:, None, :], 2), -1)
    slot_of, slot_meta = pack_slots(routes)
    routed = experts_forward(slot_of, slot_meta, moe_in, up_full, down_full)
    moe_out = gate_vals[:, 0:1] * routed[0] + gate_vals[:, 1:2] * routed[1] + shared_out
    moe_out = moe_out.reshape(num_latents, PATCHES, D)
    final_state = middle + gate_moe * moe_out
    normed_fin, inv_fin = layer_norm(final_state)
    head_in = (
        (normed_fin * (1.0 + scale_fin) + shift_fin).astype(jnp.bfloat16).reshape(rows_here, D)
    )
    errors = product(head_in, w_head) - noise.reshape(rows_here, PD)
    kept = SimpleNamespace(
        patches=patches,
        freq_low=freq_low,
        pre_time=pre_time,
        hid_time=jax.nn.silu(pre_time).astype(jnp.bfloat16),
        cond=cond,
        cond_act=jax.nn.silu(cond).astype(jnp.bfloat16),
        scale_attn=scale_attn,
        gate_attn=gate_attn,
        scale_moe=scale_moe,
        gate_moe=gate_moe,
        scale_fin=scale_fin,
        normed_one=normed_one,
        inv_one=inv_one,
        attn_in=attn_in,
        qkv_out=qkv_out,
        log_totals=jax.nn.logsumexp(scores, -1),
        attended=attended,
        attn_out=attn_out,
        normed_two=normed_two,
        inv_two=inv_two,
        moe_in=moe_in,
        route_hot=route_hot,
        gate_vals=gate_vals,
        slot_of=slot_of,
        slot_meta=slot_meta,
        routed=routed,
        moe_out=moe_out,
        normed_fin=normed_fin,
        inv_fin=inv_fin,
        head_in=head_in,
        errors=errors,
    )
    return weights, kept


def backward(weights, kept, total_tokens):
    matrices, vectors, up_full, down_full = weights
    w_qkv, w_proj, w_mod, w_time2, w_final, w_router, w_head, w_patch, w_time1, w_table = matrices
    num_latents = kept.normed_one.shape[0]
    rows_here = num_latents * PATCHES
    grad_head, grad_head_in, unused = linear_back(
        kept.errors * (2.0 / total_tokens), kept.head_in, w_head
    )
    grad_head_in = grad_head_in.reshape(num_latents, PATCHES, D)
    grad_final_mod = jnp.concatenate(
        [jnp.sum(grad_head_in, 1), jnp.sum(grad_head_in * kept.normed_fin, 1)], 1
    )
    grad_state = norm_back(
        grad_head_in * (1.0 + kept.scale_fin), kept.normed_fin, kept.inv_fin
    )
    grad_gate_moe = jnp.sum(kept.moe_out * grad_state, 1)
    grad_moe = (kept.gate_moe * grad_state).reshape(rows_here, D)
    grad_moe_low = grad_moe.astype(jnp.bfloat16)
    moe_in = kept.moe_in
    gate_vals = kept.gate_vals
    routed = kept.routed
    grad_gates = jnp.stack([jnp.sum(routed[k] * grad_moe, 1) for k in range(2)], 1)
    grad_pair = jnp.stack(
        [(gate_vals[:, k : k + 1] * grad_moe).astype(jnp.bfloat16) for k in range(2)], 0
    )
    up_slabs, down_slabs, grad_moe_in = experts_backward(
        kept.slot_of, kept.slot_meta, moe_in, grad_pair, grad_moe_low, up_full, down_full
    )
    grad_picked = gate_vals * (grad_gates - jnp.sum(gate_vals * grad_gates, 1, keepdims=True))
    grad_logits = jnp.sum(kept.route_hot * grad_picked[:, :, None], 1)
    grad_router, grad_from_router, unused = linear_back(grad_logits, moe_in, w_router)
    grad_moe_in = (grad_moe_in + grad_from_router).reshape(num_latents, PATCHES, D)
    grad_middle = grad_state + norm_back(
        grad_moe_in * (1.0 + kept.scale_moe), kept.normed_two, kept.inv_two
    )
    grad_gate_attn = jnp.sum(kept.attn_out * grad_middle, 1)
    grad_proj, grad_attended, grad_b_proj = linear_back(
        (kept.gate_attn * grad_middle).reshape(rows_here, D), kept.attended, w_proj
    )
    grad_att_low = grad_attended.astype(jnp.bfloat16).reshape(num_latents, PATCHES, HEADS, HD)
    qkv_out = kept.qkv_out
    queries = qkv_out[:, :, 0]
    key_rows = qkv_out[:, :, 1]
    values = qkv_out[:, :, 2]
    scores = jnp.einsum(
        LQK, queries, key_rows, preferred_element_type=jnp.float32
    ) * HD ** (-0.5)
    probs = jnp.exp(scores - kept.log_totals[..., None])
    probs_low = probs.astype(jnp.bfloat16)
    grad_values = jnp.einsum(
        "lhqk,lqhd->lkhd", probs_low, grad_att_low, preferred_element_type=jnp.float32
    )
    grad_probs = jnp.einsum(
        LQK, grad_att_low, values, preferred_element_type=jnp.float32
    )
    grad_scores = (
        probs * (grad_probs - jnp.sum(probs * grad_probs, -1, keepdims=True)) * HD ** (-0.5)
    ).astype(jnp.bfloat16)
    grad_queries = jnp.einsum(
        "lhqk,lkhd->lqhd", grad_scores, key_rows, preferred_element_type=jnp.float32
    )
    grad_keys = jnp.einsum(
        "lhqk,lqhd->lkhd", grad_scores, queries, preferred_element_type=jnp.float32
    )
    grad_qkv = jnp.stack([grad_queries, grad_keys, grad_values], 2).reshape(rows_here, 3 * D)
    grad_w_qkv, grad_attn_in, grad_b_qkv = linear_back(grad_qkv, kept.attn_in, w_qkv)
    grad_attn_in = grad_attn_in.reshape(num_latents, PATCHES, D)
    grad_embedded = grad_middle + norm_back(
        grad_attn_in * (1.0 + kept.scale_attn), kept.normed_one, kept.inv_one
    )
    grad_emb_flat = grad_embedded.reshape(rows_here, D)
    grad_patch = contract(grad_emb_flat.astype(jnp.bfloat16), kept.patches, 0, 0)
    grad_b_patch = jnp.sum(grad_emb_flat, 0)
    grad_modulation = jnp.concatenate(
        [
            jnp.sum(grad_attn_in, 1),
            jnp.sum(grad_attn_in * kept.normed_one, 1),
            grad_gate_attn,
            jnp.sum(grad_moe_in, 1),
            jnp.sum(grad_moe_in * kept.normed_two, 1),
            grad_gate_moe,
        ],
        1,
    )
    grad_mod_low = grad_modulation.astype(jnp.bfloat16)
    grad_fin_low = grad_final_mod.astype(jnp.bfloat16)
    grad_act = contract(grad_mod_low, w_mod, 1, 1) + contract(grad_fin_low, w_final, 1, 1)
    grad_cond = slope_back(jax.nn.silu, kept.cond, grad_act)
    grad_cond_low = grad_cond.astype(jnp.bfloat16)
    grad_hid_time = contract(grad_cond_low, w_time2, 1, 1)
    grad_pre_time = slope_back(jax.nn.silu, kept.pre_time, grad_hid_time)
    grad_time_low = grad_pre_time.astype(jnp.bfloat16)
    mats_slabs = (
        jnp.concatenate([grad_w_qkv, grad_proj], 1)
        .astype(jnp.bfloat16)
        .reshape(1, WIDE_PIECES, PIECE, NARROW_PIECES, D)
        .transpose(0, 1, 3, 2, 4)
    )
    thin = jnp.concatenate([grad_router, grad_head, grad_patch], 1)
    grad_bias = jnp.concatenate(
        [
            grad_b_qkv,
            grad_b_proj,
            jnp.sum(grad_modulation, 0),
            grad_b_patch,
            jnp.sum(grad_pre_time, 0),
            jnp.sum(grad_cond, 0),
            jnp.sum(grad_final_mod, 0),
        ]
    )
    lows = jnp.concatenate(
        [
            kept.cond_act,
            kept.hid_time,
            grad_mod_low,
            grad_fin_low,
            grad_cond_low,
            grad_time_low,
            kept.freq_low,
        ],
        1,
    )
    return (up_slabs, down_slabs, mats_slabs, thin, grad_bias, lows, grad_cond)


def latent_grads(lows, grad_cond, labels, row_start, row_count):
    lows = lax.all_gather(lows, AXES, axis=0, tiled=True)
    grad_cond = lax.all_gather(grad_cond, AXES, axis=0, tiled=True)
    labels = lax.all_gather(labels, AXES, axis=0, tiled=True)
    cond_act, hid_time, grad_mod, grad_fin, grad_low, grad_time, freq_low = cut_pieces(
        lows, [D, D, 6 * D, 2 * D, D, D, FREQ], 1
    )

    def rows_of(member):
        return lax.dynamic_slice_in_dim(member, row_start, row_count, 1)

    label_hot = (labels[:, None] == jnp.arange(CLASSES, dtype=jnp.int32)[None, :]).astype(
        jnp.float32
    )
    grad_table = lax.dot_general(
        rows_of(grad_cond),
        label_hot,
        (((0,), (0,)), ((), ())),
        precision=lax.Precision.HIGHEST,
        preferred_element_type=jnp.float32,
    )
    return (
        contract(rows_of(cond_act), grad_mod, 0, 0),
        contract(rows_of(hid_time), grad_low, 0, 0),
        contract(rows_of(cond_act), grad_fin, 0, 0),
        contract(rows_of(grad_time), freq_low, 0, 0),
        grad_table,
    )


def factor_start(grad, row_old):
    squares = grad * grad + eps_fact
    row_new = decay * row_old + (1.0 - decay) * jnp.mean(squares, 2)
    return (row_new, jnp.sum(squares, 1), jnp.sum(row_new, 1))


def factor_update(grad, row_new, col_total, row_total, col_old, row_count):
    col_new = decay * col_old + (1.0 - decay) * (col_total / row_count)
    row_mean = row_total / row_count
    update = grad * lax.rsqrt(row_new[:, :, None] * col_new[:, None, :] / row_mean[:, None, None])
    return (col_new, update, jnp.sum(update * update, (1, 2)))


def clip_apply(master, update, square_total, entry_count):
    update_rms = jnp.sqrt(square_total / entry_count)
    return master - learn_rate * (update / jnp.maximum(1.0, update_rms / clip_level)[:, None, None])


def update_plain(grads, masters, factors, loss_part):
    mats_grad, up_grad, down_grad, bias_grad = grads
    mats, up_weights, down_weights, biases = masters
    mats_row, mats_col, up_row, up_col, down_row, down_col, bias_state = factors
    widths = column_widths()
    grad_pieces = cut_pieces(mats_grad, widths, 1)
    starts = [
        factor_start(grad_pieces[k][None], mats_row[k][None]) for k in range(len(widths))
    ]
    up_row_new, up_col_part, up_row_part = factor_start(up_grad, up_row)
    down_row_new, down_col_part, down_row_part = factor_start(down_grad, down_row)
    col_totals, row_totals, up_cols, up_rows, down_cols, down_rows, loss_total = lax.psum(
        (
            jnp.concatenate([member[1] for member in starts], 1)[0],
            jnp.concatenate([member[2] for member in starts], 0),
            up_col_part,
            up_row_part,
            down_col_part,
            down_row_part,
            loss_part,
        ),
        AXES,
    )
    col_total_pieces = cut_pieces(col_totals, widths, 0)
    col_old_pieces = cut_pieces(mats_col, widths, 0)
    steps = [
        factor_update(
            grad_pieces[k][None],
            starts[k][0],
            col_total_pieces[k][None],
            row_totals[k][None],
            col_old_pieces[k][None],
            D,
        )
        for k in range(len(widths))
    ]
    up_col_new, up_update, up_square = factor_update(
        up_grad, up_row_new, up_cols, up_rows, up_col, D
    )
    down_col_new, down_update, down_square = factor_update(
        down_grad, down_row_new, down_cols, down_rows, down_col, FF
    )
    bias_state_new = decay * bias_state + (1.0 - decay) * (bias_grad * bias_grad + eps_fact)
    bias_update = bias_grad * lax.rsqrt(bias_state_new)
    square_mats, square_up, square_down, square_bias = lax.psum(
        (
            jnp.concatenate([member[2] for member in steps], 0),
            up_square,
            down_square,
            jnp.sum(bias_update * bias_update),
        ),
        AXES,
    )
    master_pieces = cut_pieces(mats, widths, 1)
    mats_new = jnp.concatenate(
        [
            clip_apply(
                master_pieces[k][None], steps[k][1], square_mats[k][None], D * widths[k]
            )[0]
            for k in range(len(widths))
        ],
        1,
    )
    up_new = clip_apply(up_weights, up_update, square_up, D * FF)
    down_new = clip_apply(down_weights, down_update, square_down, D * FF)
    bias_rms = jnp.sqrt(square_bias / (15 * D))
    bias_new = biases - learn_rate * (bias_update / jnp.maximum(1.0, bias_rms / clip_level))
    return (
        loss_total,
        mats_grad,
        mats_new,
        mats_new.astype(jnp.bfloat16),
        jnp.concatenate([member[0] for member in starts], 0),
        jnp.concatenate([member[0][0] for member in steps], 0),
        up_grad,
        up_new,
        up_new.astype(jnp.bfloat16),
        up_row_new,
        up_col_new,
        down_grad,
        down_new,
        down_new.astype(jnp.bfloat16),
        down_row_new,
        down_col_new,
        bias_grad,
        bias_new,
        bias_new.astype(jnp.bfloat16),
        bias_state_new,
    )


def body(
    latents,
    noise,
    timesteps,
    labels,
    routes,
    mats,
    up_weights,
    down_weights,
    biases,
    *factors,
):
    rows_here = mats.shape[0]
    kernel_fits = lax.axis_size(WIDE) == WIDE_PIECES and lax.axis_size(NARROW) == NARROW_PIECES
    if kernel_fits:
        gathered, kept = forward_fused(
            mats, up_weights, down_weights, biases, latents, noise, timesteps, labels, routes
        )
    else:
        flat = jnp.concatenate([mats.reshape(-1), biases], 0).astype(jnp.bfloat16)
        flat = lax.all_gather(flat, AXES, axis=0, tiled=False)
        gathered = split_weights(
            (
                flat[:, : rows_here * mats.shape[1]].reshape(-1, mats.shape[1]),
                lax.all_gather(up_weights.astype(jnp.bfloat16), AXES, axis=1, tiled=True),
                lax.all_gather(down_weights.astype(jnp.bfloat16), AXES, axis=1, tiled=True),
                flat[:, rows_here * mats.shape[1] :].reshape(-1),
            )
        )
        kept = forward(gathered, latents, noise, timesteps, labels, routes)
    total_tokens = latents.shape[0] * PATCHES * lax.axis_size(AXES)
    up_slabs, down_slabs, mats_slabs, thin, grad_bias, lows, grad_cond = backward(
        gathered, kept, total_tokens
    )
    loss_part = jnp.sum(kept.errors * kept.errors)
    masters = (mats, up_weights, down_weights, biases)
    if kernel_fits:
        sums, rows, lat = reduce_slabs(
            down_slabs,
            up_slabs,
            mats_slabs,
            thin_slab(thin, grad_bias),
            lat_block(lows, grad_cond, labels),
        )
        outs = update_kernel_call(sums, rows, lat, masters, factors, loss_part)
    else:
        grads = plain_grads(
            down_slabs, up_slabs, mats_slabs, thin, grad_bias, lows, grad_cond, labels, rows_here
        )
        outs = update_plain(grads, masters, factors, loss_part)
    return (outs[0] / total_tokens,) + tuple(outs[1:])


def solution(mesh):
    rows = P(AXES, None)
    middle_rows = P(None, AXES, None)
    row_factor = P(None, AXES)
    line = P(AXES)
    in_specs = (
        (rows, rows, line, line, rows)
        + (rows, middle_rows, middle_rows, line)
        + (row_factor, P(), row_factor, P(), row_factor, P(), line)
    )
    out_specs = (
        (P(), rows, rows, rows, row_factor, P())
        + (middle_rows, middle_rows, middle_rows, row_factor, P()) * 2
        + (line, line, line, line)
    )
    return jax.shard_map(body, mesh=mesh, in_specs=in_specs, out_specs=out_specs, check_vma=False)
```

```python
import math
from types import SimpleNamespace

import jax
import jax.numpy as jnp
from jax import lax
from jax.experimental import pallas as pl
from jax.experimental.pallas import tpu as pltpu
from jax.sharding import PartitionSpec as P

WIDE = "wide"
NARROW = "narrow"
AXES = (WIDE, NARROW)
MESH_ID = pl.DeviceIdType.MESH

D = 384
HEADS = 6
HD = 64
FF = 1536
EXPERTS = 16
SHARED = 2
PD = 16
GRID = 16
FREQ = 256
CLASSES = 1000
BLK = 256
WIDE_PIECES = 8
NARROW_PIECES = 4
PIECE = 48
ROWS = 12
LAT_ROWS = 16
LQK = "lqhd,lkhd->lhqk"
CUT = 768
LAT_COLS = 1536
PATCHES = 256


eps_norm = 1e-06
eps_fact = 1e-30
decay = 0.5
clip_level = 0.1
learn_rate = 0.5

SQRT_2_PI = math.sqrt(2.0 / math.pi)
VMEM_ROOM = 56 * 1024 * 1024
REDUCE_ROOM = 60 * 1024 * 1024


def column_widths():
    return [3 * D, D, 6 * D, D, 2 * D, EXPERTS, PD, PD, FREQ, CLASSES]


def bias_widths():
    return [3 * D, D, 6 * D, D, D, D, 2 * D]


def cut_pieces(source, widths, along):
    pieces = []
    start = 0
    for width in widths:
        pieces.append(lax.slice_in_dim(source, start, start + width, axis=along))
        start = start + width
    return pieces


def product(left, right):
    return jnp.dot(left, right, preferred_element_type=jnp.float32)


def contract(left, right, left_dim, right_dim):
    return lax.dot_general(
        left, right, (((left_dim,), (right_dim,)), ((), ())), preferred_element_type=jnp.float32
    )


def gelu_tanh(values):
    return jax.nn.gelu(values, approximate=True)


def slope_back(function, source, grad_out):
    return jax.vjp(function, source)[1](grad_out)[0]


def layer_norm(source):
    centred = source - jnp.mean(source, -1, keepdims=True)
    inv_std = lax.rsqrt(jnp.mean(centred * centred, -1, keepdims=True) + eps_norm)
    return (centred * inv_std, inv_std)


def norm_back(grad_norm, normed, inv_std):
    return inv_std * (
        grad_norm
        - jnp.mean(grad_norm, -1, keepdims=True)
        - normed * jnp.mean(grad_norm * normed, -1, keepdims=True)
    )


def linear_back(grad_out, inputs, weight):
    grad_low = grad_out.astype(jnp.bfloat16)
    return (
        contract(inputs, grad_low, 0, 0),
        contract(grad_low, weight, 1, 1),
        jnp.sum(grad_out, 0),
    )


def sincos(coords, width):
    omegas = 1.0 / 10000.0 ** (jnp.arange(width // 2, dtype=jnp.float32) / (width / 2.0))
    angles = coords[:, None] * omegas[None, :]
    return jnp.concatenate([jnp.sin(angles), jnp.cos(angles)], 1)


def positions():
    places = jnp.arange(PATCHES, dtype=jnp.int32)
    grid_row = (places // GRID).astype(jnp.float32)
    grid_col = (places % GRID).astype(jnp.float32)
    return jnp.concatenate([sincos(grid_row, D // 2), sincos(grid_col, D // 2)], 1)


def time_features(steps_f):
    half_width = FREQ // 2
    freq_rates = jnp.exp(
        -math.log(10000.0) * jnp.arange(half_width, dtype=jnp.float32) / half_width
    )
    angles = steps_f[:, None] * freq_rates[None, :]
    return jnp.concatenate([jnp.cos(angles), jnp.sin(angles)], 1)


def noise_level(steps_f):
    alpha_bar = jnp.cos((steps_f / 1000.0 + 0.008) / 1.008 * (math.pi / 2)) ** 2
    return (jnp.sqrt(alpha_bar), jnp.sqrt(1.0 - alpha_bar))


def pack_slots(routes):
    ids = jnp.arange(EXPERTS, dtype=jnp.int32)[:, None]
    named = [(routes[:, k][None, :] == ids) for k in range(2)]
    either = (named[0] | named[1]).astype(jnp.bfloat16)
    rows_here = routes.shape[0]
    place = jnp.arange(rows_here, dtype=jnp.int32)
    before = (place[:, None] < place[None, :]).astype(jnp.bfloat16)
    rank_in = product(either, before)
    counts = jnp.sum(either.astype(jnp.float32), 1).astype(jnp.int32)
    padded = (counts + 7) // 8 * 8
    starts = jnp.sum(jnp.where(ids > ids.T, padded[None, :], 0), 1)
    slots = rank_in.astype(jnp.int32) + starts[:, None]
    slot_of = jnp.stack([jnp.sum(jnp.where(member, slots, 0), 0) for member in named], 0)
    return (slot_of, jnp.stack([starts, counts], 0))


def gelu_slope(values):
    inner = SQRT_2_PI * (values + 0.044715 * values * values * values)
    bend = jnp.tanh(inner)
    return (
        0.5 * values * (1.0 + bend),
        0.5 * (1.0 + bend)
        + 0.5
        * values
        * (1.0 - bend * bend)
        * SQRT_2_PI
        * (1.0 + 3.0 * 0.044715 * values * values),
    )


def gelu_only(values):
    inner = SQRT_2_PI * (values + 0.044715 * values * values * values)
    return 0.5 * values * (1.0 + jnp.tanh(inner))


def up_columns(chunks, cut):
    return jnp.concatenate([chunks[cut // D + k] for k in range(CUT // D)], 1)


def slot_pick(slots_ref, base, rows):
    place = base + lax.broadcasted_iota(jnp.int32, (rows, slots_ref.shape[1]), 0)
    return ((slots_ref[0:1, :] == place) | (slots_ref[1:2, :] == place)).astype(jnp.bfloat16)


def forward_kernel(meta, slot_at, slots_ref, x_ref, up_ref, down_ref, routed_ref, y_ref):
    stack_id = pl.program_id(0)
    tokens = x_ref.shape[0]

    def expert(rows):
        total = None
        for cut in range(0, FF, CUT):
            pre_act = product(rows, up_columns(up_ref[0], cut))
            part = product(gelu_only(pre_act).astype(jnp.bfloat16), down_ref[0, cut : cut + CUT])
            total = part if total is None else total + part
        return total

    start = meta[0, stack_id]

    def block(number, unused):
        base = pl.multiple_of(start + number * BLK, 8)
        rows = product(slot_pick(slots_ref, base, BLK), x_ref[...]).astype(jnp.bfloat16)
        y_ref[pl.ds(base, BLK), :] = expert(rows)
        return unused

    lax.fori_loop(0, (meta[1, stack_id] + BLK - 1) // BLK, block, 0)

    @pl.when(stack_id == EXPERTS - 1)
    def _():
        def group(number, unused):
            for step in range(8):
                token = number * 8 + step
                for k in range(2):
                    routed_ref[k, pl.ds(token, 1), :] = y_ref[pl.ds(slot_at[k, token], 1), :]
            return unused

        lax.fori_loop(0, tokens // 8, group, 0)


def slot_room(tokens):
    return tokens * 2 + EXPERTS * 8 + BLK


def whole_block(shape):
    return pl.BlockSpec(shape, lambda e, *unused: (0,) * len(shape))


def experts_forward(slot_of, meta, moe_in, up_full, down_full):
    tokens = moe_in.shape[0]
    return pl.pallas_call(
        forward_kernel,
        grid_spec=pltpu.PrefetchScalarGridSpec(
            num_scalar_prefetch=2,
            grid=(EXPERTS,),
            in_specs=[
                whole_block((2, tokens)),
                whole_block((tokens, D)),
                pl.BlockSpec((1, NARROW_PIECES, D, D), lambda e, *unused: (e, 0, 0, 0)),
                pl.BlockSpec((1, FF, D), lambda e, *unused: (e, 0, 0)),
            ],
            out_specs=whole_block((2, tokens, D)),
            scratch_shapes=[pltpu.VMEM((slot_room(tokens), D), jnp.float32)],
        ),
        out_shape=jax.ShapeDtypeStruct((2, tokens, D), jnp.float32),
        compiler_params=pltpu.CompilerParams(vmem_limit_bytes=VMEM_ROOM),
        cost_estimate=pl.CostEstimate(
            flops=20_000_000_000, bytes_accessed=50_000_000, transcendentals=0
        ),
        name="experts_forward",
    )(meta, slot_of, slot_of, moe_in, up_full, down_full)


def backward_kernel(
    meta,
    slot_at,
    slots_ref,
    x_ref,
    pair_ref,
    up_ref,
    down_ref,
    up_out,
    down_out,
    dx_ref,
    up_sum,
    down_sum,
    dx_slots,
):
    stack_id = pl.program_id(0)
    tokens = x_ref.shape[0]
    up_sum[...] = jnp.zeros_like(up_sum)
    down_sum[...] = jnp.zeros_like(down_sum)

    def expert(rows, grads):
        total = None
        for cut in range(0, FF, CUT):
            up_part = up_columns(up_ref[0], cut)
            activated, slope = gelu_slope(product(rows, up_part))
            grad_act = contract(grads, down_ref[0, cut : cut + CUT], 1, 1)
            grad_pre = (grad_act * slope).astype(jnp.bfloat16)
            down_sum[cut : cut + CUT, :] += contract(activated.astype(jnp.bfloat16), grads, 0, 0)
            up_sum[:, cut : cut + CUT] += contract(rows, grad_pre, 0, 0)
            part = contract(grad_pre, up_part, 1, 1)
            total = part if total is None else total + part
        return total

    start = meta[0, stack_id]
    stop = start + meta[1, stack_id]

    def block(number, unused):
        base = pl.multiple_of(start + number * BLK, 8)
        rows = product(slot_pick(slots_ref, base, BLK), x_ref[...]).astype(jnp.bfloat16)
        place = base + lax.broadcasted_iota(jnp.int32, (BLK, tokens), 0)
        place = jnp.where(place < stop, place, -1)
        grads = None
        for k in range(2):
            part = product((slots_ref[k : k + 1, :] == place).astype(jnp.bfloat16), pair_ref[k])
            grads = part if grads is None else grads + part
        dx_slots[pl.ds(base, BLK), :] = expert(rows, grads.astype(jnp.bfloat16))
        return unused

    lax.fori_loop(0, (meta[1, stack_id] + BLK - 1) // BLK, block, 0)
    for n in range(NARROW_PIECES):
        up_out[0, :, n] = (
            up_sum[:, n * D : (n + 1) * D]
            .astype(jnp.bfloat16)
            .reshape(WIDE_PIECES, PIECE, D)
        )
    down_out[0] = down_sum[...].astype(jnp.bfloat16).reshape(WIDE_PIECES, NARROW_PIECES, PIECE, D)

    @pl.when(stack_id == EXPERTS - 1)
    def _():
        def group(number, unused):
            for step in range(8):
                token = number * 8 + step
                dx_ref[pl.ds(token, 1), :] = (
                    dx_slots[pl.ds(slot_at[0, token], 1), :]
                    + dx_slots[pl.ds(slot_at[1, token], 1), :]
                )
            return unused

        lax.fori_loop(0, tokens // 8, group, 0)


def experts_backward(slot_of, meta, moe_in, grad_pair, up_full, down_full):
    tokens = moe_in.shape[0]
    slabs = (EXPERTS, WIDE_PIECES, NARROW_PIECES, PIECE, D)
    slab_spec = pl.BlockSpec((1,) + slabs[1:], lambda e, *unused: (e, 0, 0, 0, 0))
    return pl.pallas_call(
        backward_kernel,
        grid_spec=pltpu.PrefetchScalarGridSpec(
            num_scalar_prefetch=2,
            grid=(EXPERTS,),
            in_specs=[
                whole_block((2, tokens)),
                whole_block((tokens, D)),
                whole_block((2, tokens, D)),
                pl.BlockSpec((1, NARROW_PIECES, D, D), lambda e, *unused: (e, 0, 0, 0)),
                pl.BlockSpec((1, FF, D), lambda e, *unused: (e, 0, 0)),
            ],
            out_specs=[slab_spec, slab_spec, whole_block((tokens, D))],
            scratch_shapes=[
                pltpu.VMEM((D, FF), jnp.float32),
                pltpu.VMEM((FF, D), jnp.float32),
                pltpu.VMEM((slot_room(tokens), D), jnp.float32),
            ],
        ),
        out_shape=[
            jax.ShapeDtypeStruct(slabs, jnp.bfloat16),
            jax.ShapeDtypeStruct(slabs, jnp.bfloat16),
            jax.ShapeDtypeStruct((tokens, D), jnp.float32),
        ],
        compiler_params=pltpu.CompilerParams(vmem_limit_bytes=VMEM_ROOM),
        cost_estimate=pl.CostEstimate(
            flops=45_000_000_000, bytes_accessed=90_000_000, transcendentals=0
        ),
        name="experts_backward",
    )(meta, slot_of, slot_of, moe_in, grad_pair, up_full, down_full)


def reduce_kernel(
    down_ref,
    up_ref,
    up_all,
    down_all,
    moe_in,
    grad_both,
    dx_routed,
    grad_logits,
    middle,
    qkv,
    attended,
    grad_state,
    patches,
    places,
    mods,
    mats_all,
    bias_rows,
    pre_time,
    cond,
    freq_low,
    grad_gate,
    grad_fin,
    thin_in,
    label_parts,
    out_ref,
    rows_ref,
    lat_ref,
    bias_ref,
    own,
    got_core,
    out_one,
    keep_one,
    got_one,
    out_two,
    keep_two,
    got_two,
    keep_z,
    out_z,
    got_z,
    row_parts,
    late,
    up_here,
    down_here,
    up_sum,
    down_sum,
    dx_sum,
    grad_mid,
    grad_att,
    grad_qkv,
    qkv_sum,
    proj_sum,
    patch_sum,
    grad_mods,
    lat_full,
    lat_low,
    own_sem,
    core_send,
    core_recv,
    one_send,
    one_recv,
    two_send,
    two_recv,
    z_send,
    z_recv,
    row_send,
    row_recv,
    lat_own,
    lat_send,
    lat_recv,
    here_sem,
    core_free,
    one_free,
):
    full, low = jnp.float32, jnp.bfloat16
    n_down, n_up, n_late = down_ref.shape[0], up_ref.shape[0], late.shape[0]
    slabs = n_down + n_up + n_late
    ahead, ring = 2, got_core.shape[0]
    wide, narrow = lax.axis_index(WIDE), lax.axis_index(NARROW)
    z, x = wide // 2, wide % 2
    y, c = narrow // 2, narrow % 2
    x_one, y_one = x + (1 - c) * (1 - 2 * x), y + c * (1 - 2 * y)
    x_two, y_two = x + c * (1 - 2 * x), y + (1 - c) * (1 - 2 * y)
    to_one = (z * 2 + x_one, y_one * 2 + c)
    to_two = (z * 2 + x_two, y_two * 2 + c)
    first_mine = x * (1 - c) + y * c
    second_mine = y * (1 - c) + x * c
    first_step, second_step = 2 - c, 1 + c
    mates = [
        (wide, (y + (k // 2) * (1 - 2 * y)) * 2 + c + (k % 2) * (1 - 2 * c)) for k in range(1, 4)
    ]
    levels = [(((z + k) % 4) * 2 + x, narrow) for k in range(1, 4)]
    to_x, to_core = (z * 2 + 1 - x, narrow), mates[0]
    barrier = pltpu.get_barrier_semaphore()
    for target in mates + levels + [to_x]:
        pl.semaphore_signal(barrier, inc=1, device_id=target, device_id_type=MESH_ID)
    pl.semaphore_wait(barrier, 7)

    def remote(source, target, send, recv, device):
        return pltpu.make_async_remote_copy(
            src_ref=source,
            dst_ref=target,
            send_sem=send,
            recv_sem=recv,
            device_id=device,
            device_id_type=MESH_ID,
        )

    def core_copy(source, s):
        return remote(
            source.at[:, 1 - c],
            got_core.at[s % ring],
            core_send.at[s % 4],
            core_recv.at[s % ring],
            to_core,
        )

    def own_copy(source, s):
        return pltpu.make_async_copy(source.at[:, c], own.at[s % 3], own_sem.at[s % 3])

    def one_copy(s):
        return remote(
            out_one.at[s % 2], got_one.at[s % ring], one_send.at[s % 2], one_recv.at[s % ring], to_one
        )

    def two_copy(s):
        return remote(out_two.at[s % 2], got_two.at[s], two_send.at[s % 2], two_recv.at[s], to_two)

    def z_copy(s, k):
        return remote(
            out_z.at[s % 2, (z + k) % 4],
            got_z.at[s, k - 1],
            z_send.at[s % 2, k - 1],
            z_recv.at[s, k - 1],
            levels[k - 1],
        )

    def row_copy(r, k):
        mate = mates[k - 1]
        return remote(
            row_parts.at[r % 2, mate[1]],
            rows_ref.at[r, narrow],
            row_send.at[r % 2, k - 1],
            row_recv.at[r, k - 1],
            mate,
        )

    def lat_level(k):
        return remote(
            lat_low, lat_ref.at[z, x, y, c], lat_send.at[k - 1], lat_recv.at[k - 1], levels[k - 1]
        )

    def lat_x():
        spot = lat_ref.at[:, x, y, c]
        return remote(spot, spot, lat_send.at[3], lat_recv.at[3], to_x)

    def lat_y():
        spot = lat_ref.at[:, :, y, c]
        return remote(spot, spot, lat_send.at[4], lat_recv.at[4], mates[1])

    def lat_core():
        spot = lat_ref.at[:, :, :, c]
        return remote(spot, spot, lat_send.at[5], lat_recv.at[5], to_core)

    def lat_own_copy():
        return pltpu.make_async_copy(lat_low, lat_ref.at[z, x, y, c], lat_own.at[0])

    def begin(source, s):
        @pl.when(s >= 4)
        def _():
            core_copy(source, s).wait_send()

        @pl.when(s >= ring)
        def _():
            pl.semaphore_wait(core_free, 1)

        core_copy(source, s).start()
        own_copy(source, s).start()

    def stage_core(s):
        own_copy(down_ref.at[0], s).wait()
        core_copy(down_ref.at[0], s).wait_recv()

        @pl.when(s >= 2)
        def _():
            one_copy(s).wait_send()

        @pl.when(s >= ring)
        def _():
            pl.semaphore_wait(one_free, 1)

        for level in range(4):
            for other in range(2):
                place = level * 2 + other
                base = level * 4 + other * second_step
                send_at = base + (1 - first_mine) * first_step
                out_one[s % 2, place] = (
                    own[s % 3, send_at].astype(full) + got_core[s % ring, send_at].astype(full)
                ).astype(low)
        one_copy(s).start()
        for level in range(4):
            for other in range(2):
                place = level * 2 + other
                base = level * 4 + other * second_step
                keep_at = base + first_mine * first_step
                keep_one[s % 2, place] = own[s % 3, keep_at].astype(full) + got_core[
                    s % ring, keep_at
                ].astype(full)

        @pl.when(s < slabs - ring)
        def _():
            pl.semaphore_signal(core_free, inc=1, device_id=to_core, device_id_type=MESH_ID)

    def stage_one(s):
        one_copy(s).wait_recv()

        @pl.when(s >= 2)
        def _():
            two_copy(s).wait_send()

        for level in range(4):
            send_at = level * 2 + 1 - second_mine
            out_two[s % 2, level] = (
                keep_one[s % 2, send_at] + got_one[s % ring, send_at].astype(full)
            ).astype(low)
        two_copy(s).start()
        for level in range(4):
            keep_at = level * 2 + second_mine
            keep_two[s % 2, level] = keep_one[s % 2, keep_at] + got_one[s % ring, keep_at].astype(
                full
            )

        @pl.when(s < slabs - ring)
        def _():
            pl.semaphore_signal(one_free, inc=1, device_id=to_one, device_id_type=MESH_ID)

    def stage_two(s):
        two_copy(s).wait_recv()

        @pl.when(s >= 2)
        def _():
            for k in range(1, 4):
                z_copy(s, k).wait_send()

        for level in range(4):
            out_z[s % 2, level] = (
                keep_two[s % 2, level] + got_two[s, level].astype(full)
            ).astype(low)
        for k in range(1, 4):
            z_copy(s, k).start()
        keep_z[s % 2] = keep_two[s % 2, z] + got_two[s, z].astype(full)

    def direct_place(s):
        late_at = s - n_down - n_up
        return (s < n_down) | ((late_at >= 0) & (late_at < SHARED))

    def row_place(s):
        return jnp.where(s < n_down + n_up, s - n_down, s - n_down - SHARED)

    def finish(s):
        total = keep_z[s % 2]
        for k in range(1, 4):
            z_copy(s, k).wait_recv()
        for k in range(3):
            total = total + got_z[s, k].astype(full)

        @pl.when(direct_place(s))
        def _():
            out_ref[jnp.clip(jnp.where(s < n_down, s, s - n_up), 0, n_down + SHARED - 1)] = total

        @pl.when(jnp.logical_not(direct_place(s)))
        def _():
            r = row_place(s)

            @pl.when(r >= 2)
            def _():
                for k in range(1, 4):
                    row_copy(r, k).wait_send()

            for n in range(NARROW_PIECES):
                row_parts[r % 2, n] = total[n * ROWS : (n + 1) * ROWS]
            rows_ref[r, narrow] = row_parts[r % 2, narrow]
            for k in range(1, 4):
                row_copy(r, k).start()

    def rows_in(s):
        @pl.when(jnp.logical_not(direct_place(s)))
        def _():
            for k in range(1, 4):
                row_copy(row_place(s), k).wait_recv()

    tokens = moe_in.shape[0]
    lats = tokens // PATCHES

    def matrix(number, start, stop):
        chunk = mats_all[number // 2, number % 2]
        return chunk.reshape(D, chunk.shape[-1])[:, start:stop]

    def mod_row(start, number):
        return mods[pl.ds(start // PATCHES, 1), number * D : (number + 1) * D]

    def keep_mod(start, number, values):
        grad_mods[pl.ds(start // PATCHES, 1), number * D : (number + 1) * D] = jnp.sum(
            values, 0, keepdims=True
        )

    def add_bias(number, values):
        for k in range(values.shape[1] // D):
            bias_ref[number + k : number + k + 1, :] += jnp.sum(
                values[:, k * D : (k + 1) * D], 0, keepdims=True
            )

    def prepare():
        bias_ref[...] = jnp.zeros_like(bias_ref)
        qkv_sum[...] = jnp.zeros_like(qkv_sum)
        proj_sum[...] = jnp.zeros_like(proj_sum)
        patch_sum[...] = jnp.zeros_like(patch_sum)
        grad_mods[...] = jnp.zeros_like(grad_mods)

    def fetch(shared_id):
        e = EXPERTS + shared_id
        first = pltpu.make_async_copy(down_all.at[e], down_here, here_sem.at[0])
        second = pltpu.make_async_copy(up_all.at[e], up_here, here_sem.at[1])
        first.start()
        second.start()
        first.wait()
        second.wait()
        up_sum[...] = jnp.zeros_like(up_sum)
        down_sum[...] = jnp.zeros_like(down_sum)

    def shared_block(shared_id, start):
        span = pl.ds(start, PATCHES)
        rows, grads = moe_in[span, :], grad_both[span, :]
        total = dx_routed[span, :] if shared_id == 0 else dx_sum[span, :]
        for cut in range(0, FF, CUT):
            up_part = up_columns(up_here, cut)
            activated, slope = gelu_slope(product(rows, up_part))
            grad_act = contract(grads, down_here[cut : cut + CUT], 1, 1)
            grad_pre = (grad_act * slope).astype(low)
            down_sum[cut : cut + CUT, :] += contract(activated.astype(low), grads, 0, 0)
            up_sum[:, cut : cut + CUT] += contract(rows, grad_pre, 0, 0)
            total = total + contract(grad_pre, up_part, 1, 1)
        dx_sum[span, :] = total

    def shared_slabs(shared_id):
        for w in range(WIDE_PIECES):
            for n in range(NARROW_PIECES):
                at = (w * NARROW_PIECES + n) * PIECE
                late[shared_id, w * 2 + n // 2, n % 2] = down_sum[at : at + PIECE, :].astype(low)
                late[SHARED + shared_id, w * 2 + n // 2, n % 2] = up_sum[
                    w * PIECE : (w + 1) * PIECE, n * D : (n + 1) * D
                ].astype(low)

    def back_out(start):
        span = pl.ds(start, PATCHES)
        grads = dx_sum[span, :] + contract(
            grad_logits[span, :].astype(low), matrix(0, 4 * D, 4 * D + 128), 1, 1
        )
        normed, inv_std = layer_norm(middle[span, :])
        keep_mod(start, 3, grads)
        keep_mod(start, 4, grads * normed)
        grads = grad_state[span, :] + norm_back(
            grads * (1.0 + mod_row(start, 4)), normed, inv_std
        )
        grad_mid[...] = grads
        proj = matrix(0, 3 * D, 4 * D)
        rows = attended[span, :]
        keep_mod(start, 2, (product(rows, proj) + bias_rows[3:4, :]) * grads)
        grads = grads * mod_row(start, 2)
        add_bias(3, grads)
        grads = grads.astype(low)
        proj_sum[...] += contract(rows, grads, 0, 0)
        grad_att[...] = contract(grads, proj, 1, 1).astype(low)

    def back_pair(pair, start):
        span = pl.ds(start, PATCHES)
        lane = lax.broadcasted_iota(jnp.int32, (PATCHES, 2 * HD), 1)
        at = pair * 2 * HD
        queries = qkv[span, at : at + 2 * HD]
        keys = qkv[span, D + at : D + at + 2 * HD]
        values = qkv[span, 2 * D + at : 2 * D + at + 2 * HD]
        grads = grad_att[:, at : at + 2 * HD]
        sums = None
        for half in range(2):
            mine = (lane < HD) if half == 0 else (lane >= HD)
            scores = contract(jnp.where(mine, queries, 0), keys, 1, 1) * HD ** (-0.5)
            powers = jnp.exp(scores - jnp.max(scores, 1, keepdims=True))
            probs = powers / jnp.sum(powers, 1, keepdims=True)
            grad_mine = jnp.where(mine, grads, 0)
            grad_probs = contract(grad_mine, values, 1, 1)
            grad_scores = (
                probs
                * (grad_probs - jnp.sum(probs * grad_probs, 1, keepdims=True))
                * HD ** (-0.5)
            ).astype(low)
            parts = (
                product(grad_scores, jnp.where(mine, keys, 0)),
                contract(grad_scores, jnp.where(mine, queries, 0), 0, 0),
                contract(probs.astype(low), grad_mine, 0, 0),
            )
            sums = parts if sums is None else [a + b for a, b in zip(sums, parts)]
        for k in range(3):
            where = k * D + at
            grad_qkv[:, where : where + 2 * HD] = sums[k].astype(low)
            bias_ref[k : k + 1, at : at + 2 * HD] += jnp.sum(sums[k], 0, keepdims=True)

    def back_in(start):
        span = pl.ds(start, PATCHES)
        emb = contract(patches[span, :], matrix(2, 4 * D, 4 * D + 128), 1, 1)
        emb = emb + bias_rows[10:11, :] + places[...]
        normed, inv_std = layer_norm(emb)
        rows = (normed * (1.0 + mod_row(start, 1)) + mod_row(start, 0)).astype(low)
        qkv_sum[...] += contract(rows, grad_qkv[...], 0, 0)
        grads = contract(grad_qkv[...], matrix(0, 0, 3 * D), 1, 1)
        keep_mod(start, 0, grads)
        keep_mod(start, 1, grads * normed)
        grads = grad_mid[...] + norm_back(grads * (1.0 + mod_row(start, 1)), normed, inv_std)
        add_bias(10, grads)
        patch_sum[...] += contract(grads.astype(low), patches[span, :], 0, 0)

    def silu_slope(values):
        gate = jax.nn.sigmoid(values)
        return gate + values * gate * (1.0 - gate)

    def back_conditions():
        grad_mods[:, 5 * D :] = grad_gate[...]
        grads = grad_mods[...]
        mod_low, fin_low = grads.astype(low), grad_fin[...].astype(low)
        grad_act = (
            contract(mod_low[:, : 4 * D], matrix(1, 0, 4 * D), 1, 1)
            + contract(mod_low[:, 4 * D :], matrix(2, 0, 2 * D), 1, 1)
            + contract(fin_low, matrix(2, 2 * D, 4 * D), 1, 1)
        )
        grad_cond = silu_slope(cond[...]) * grad_act
        high = grad_cond.astype(low)
        grad_time = silu_slope(pre_time[...]) * contract(high, matrix(3, 1024, 1408), 1, 1)
        add_bias(4, grads)
        add_bias(11, grad_time)
        add_bias(12, grad_cond)
        add_bias(13, grad_fin[...])
        high = high.astype(full)
        rest = grad_cond - high
        middle_part = rest.astype(low).astype(full)
        act = jax.nn.silu(cond[...]).astype(low).astype(full)
        hid = jax.nn.silu(pre_time[...]).astype(low).astype(full)
        mod_low, fin_low = mod_low.astype(full), fin_low.astype(full)
        quarters = (
            jnp.concatenate([act, hid, mod_low[:, : 2 * D]], 1),
            mod_low[:, 2 * D :],
            jnp.concatenate([fin_low, high, grad_time.astype(low).astype(full)], 1),
            jnp.concatenate(
                [
                    freq_low[...].astype(full),
                    middle_part,
                    rest - middle_part,
                    label_parts[...].astype(full),
                    jnp.zeros((8, D), full),
                ],
                1,
            ),
        )
        for lat in range(lats):
            for k in range(4):
                lat_full[lat * 4 + k : lat * 4 + k + 1, :] = quarters[k][lat : lat + 1, :]
        lat_low[...] = lat_full[...].astype(low)

    def last_slabs():
        for w in range(WIDE_PIECES):
            span = slice(w * PIECE, (w + 1) * PIECE)
            for n in range(3):
                late[2 * SHARED, w * 2 + n // 2, n % 2] = qkv_sum[
                    span, n * D : (n + 1) * D
                ].astype(low)
            late[2 * SHARED, w * 2 + 1, 1] = proj_sum[span, :].astype(low)
            thin = thin_in[span, :] + pltpu.roll(patch_sum[span, :], EXPERTS + PD, 1)
            for n in range(NARROW_PIECES):
                late[2 * SHARED + 1, w * 2 + n // 2, n % 2] = jnp.zeros((PIECE, D), low)
            late[2 * SHARED + 1, w * 2, 0, :, :128] = thin.astype(low)

    first_lat = SHARED * lats
    units = (
        back_out,
        lambda start: back_pair(0, start),
        lambda start: back_pair(1, start),
        lambda start: back_pair(2, start),
        back_in,
    )
    after = first_lat + len(units) * lats

    def tick(t, unused):
        first = 0
        for source, count in ((down_ref, n_down), (up_ref, n_up), (late, n_late)):

            @pl.when((t >= first) & (t < first + count))
            def _():
                begin(source.at[jnp.clip(t - first, 0, count - 1)], t)

            first += count

        for lag, stage in enumerate((stage_core, stage_one, stage_two, finish, rows_in)):
            s = t - ahead - lag

            @pl.when((s >= 0) & (s < slabs))
            def _():
                stage(s)

        @pl.when(t == 0)
        def _():
            prepare()

        for shared_id in range(SHARED):
            start_at = shared_id * lats

            @pl.when(t == start_at)
            def _():
                fetch(shared_id)

            @pl.when((t >= start_at) & (t < start_at + lats))
            def _():
                shared_block(
                    shared_id,
                    pl.multiple_of(jnp.clip(t - start_at, 0, lats - 1) * PATCHES, PATCHES),
                )

            @pl.when(t == start_at + lats - 1)
            def _():
                shared_slabs(shared_id)

        for number, unit in enumerate(units):

            @pl.when((t >= first_lat) & (t < after) & ((t - first_lat) % len(units) == number))
            def _():
                lat = jnp.clip((t - first_lat) // len(units), 0, lats - 1)
                unit(pl.multiple_of(lat * PATCHES, PATCHES))

        @pl.when(t == after)
        def _():
            back_conditions()
            lat_own_copy().start()
            for k in range(1, 4):
                lat_level(k).start()
            lat_own_copy().wait()

        @pl.when(t == after + 1)
        def _():
            last_slabs()

        @pl.when(t == after + 3)
        def _():
            for k in range(1, 4):
                lat_level(k).wait_recv()
            lat_x().start()

        @pl.when(t == after + 5)
        def _():
            lat_x().wait_recv()
            lat_y().start()

        @pl.when(t == after + 7)
        def _():
            lat_y().wait_recv()
            lat_core().start()

        return unused

    lax.fori_loop(0, slabs + ahead + 4, tick, 0)
    for back in range(4):
        core_copy(down_ref.at[0], slabs - 1 - back).wait_send()
    turned = rows_ref.shape[0]
    for back in range(2):
        one_copy(slabs - 1 - back).wait_send()
        two_copy(slabs - 1 - back).wait_send()
        for k in range(1, 4):
            z_copy(slabs - 1 - back, k).wait_send()
            row_copy(turned - 1 - back, k).wait_send()
    for k in range(1, 4):
        lat_level(k).wait_send()
    lat_x().wait_send()
    lat_y().wait_send()
    lat_core().wait()


def reduce_slabs(down_slabs, up_slabs, up_all, down_all, members):
    n_late = 2 * SHARED + 2
    routed = down_slabs.shape[0]
    slabs = 2 * routed + n_late
    direct, turned = routed + SHARED, routed + SHARED + 2
    ring = 6
    low, full = jnp.bfloat16, jnp.float32
    sources = [
        member.reshape(routed, WIDE_PIECES * NARROW_PIECES // 2, 2, PIECE, D)
        for member in (down_slabs, up_slabs)
    ]
    tokens = members[0].shape[0]
    dma, regular = pltpu.SemaphoreType.DMA, pltpu.SemaphoreType.REGULAR
    vmem, anywhere = pl.BlockSpec(memory_space=pltpu.VMEM), pl.BlockSpec(memory_space=pl.ANY)
    sums, rows, lats, bias_sum = pl.pallas_call(
        reduce_kernel,
        out_shape=[
            jax.ShapeDtypeStruct((direct, PIECE, D), full),
            jax.ShapeDtypeStruct((turned, NARROW_PIECES, ROWS, D), full),
            jax.ShapeDtypeStruct((4, 2, 2, 2, LAT_ROWS, LAT_COLS), low),
            jax.ShapeDtypeStruct((16, D), full),
        ],
        in_specs=[anywhere] * 4 + [vmem] * len(members),
        out_specs=[vmem, vmem, anywhere, vmem],
        scratch_shapes=[
            pltpu.VMEM((3, 16, PIECE, D), low),
            pltpu.VMEM((ring, 16, PIECE, D), low),
            pltpu.VMEM((2, 8, PIECE, D), low),
            pltpu.VMEM((2, 8, PIECE, D), full),
            pltpu.VMEM((ring, 8, PIECE, D), low),
            pltpu.VMEM((2, 4, PIECE, D), low),
            pltpu.VMEM((2, 4, PIECE, D), full),
            pltpu.VMEM((slabs, 4, PIECE, D), low),
            pltpu.VMEM((2, PIECE, D), full),
            pltpu.VMEM((2, 4, PIECE, D), low),
            pltpu.VMEM((slabs, 3, PIECE, D), low),
            pltpu.VMEM((2, NARROW_PIECES, ROWS, D), full),
            pltpu.VMEM((n_late, 16, 2, PIECE, D), low),
            pltpu.VMEM((NARROW_PIECES, D, D), low),
            pltpu.VMEM((FF, D), low),
            pltpu.VMEM((D, FF), full),
            pltpu.VMEM((FF, D), full),
            pltpu.VMEM((tokens, D), full),
            pltpu.VMEM((PATCHES, D), full),
            pltpu.VMEM((PATCHES, D), low),
            pltpu.VMEM((PATCHES, 3 * D), low),
            pltpu.VMEM((D, 3 * D), full),
            pltpu.VMEM((D, D), full),
            pltpu.VMEM((D, 128), full),
            pltpu.VMEM((8, 6 * D), full),
            pltpu.VMEM((LAT_ROWS, LAT_COLS), full),
            pltpu.VMEM((LAT_ROWS, LAT_COLS), low),
            dma((3,)),
            dma((4,)),
            dma((ring,)),
            dma((2,)),
            dma((ring,)),
            dma((2,)),
            dma((slabs,)),
            dma((2, 3)),
            dma((slabs, 3)),
            dma((2, 3)),
            dma((turned, 3)),
            dma((1,)),
            dma((6,)),
            dma((6,)),
            dma((2,)),
            regular,
            regular,
        ],
        compiler_params=pltpu.CompilerParams(
            collective_id=0, has_side_effects=True, vmem_limit_bytes=REDUCE_ROOM
        ),
        name="reduce_slabs",
    )(*sources, up_all, down_all, *members)
    return sums, rows, lats.reshape(-1, LAT_COLS), bias_sum


def plain_grads(
    down_slabs, up_slabs, mats_slabs, thin, grad_bias, lows, grad_cond, labels, row_count
):
    def scattered(member):
        return lax.psum_scatter(member, AXES, scatter_dimension=1, tiled=True)

    proj_grad = scattered(mats_slabs)
    row_start = lax.axis_index(AXES) * row_count
    thin_grad = lax.psum_scatter(thin, AXES, scatter_dimension=0, tiled=True)
    bias_grad = lax.psum_scatter(grad_bias, AXES, scatter_dimension=0, tiled=True)
    grad_mod, grad_time2, grad_fin, grad_time1, grad_table = latent_grads(
        lows, grad_cond, labels, row_start, row_count
    )
    mats_grad = jnp.concatenate(
        [proj_grad[0], grad_mod, grad_time2, grad_fin, thin_grad, grad_time1, grad_table], 1
    )
    return (mats_grad, scattered(up_slabs), scattered(down_slabs), bias_grad)


def update_kernel(
    sums_ref,
    rows_ref,
    lat_ref,
    bias_sum,
    loss_ref,
    mats_ref,
    up_ref,
    down_ref,
    bias_ref,
    mats_row,
    mats_col,
    up_row,
    up_col,
    down_row,
    down_col,
    bias_state,
    loss_out,
    mats_grad,
    mats_new,
    mats_copy,
    mats_row_new,
    mats_col_new,
    up_grad,
    up_new,
    up_copy,
    up_row_new,
    up_col_new,
    down_grad,
    down_new,
    down_copy,
    down_row_new,
    down_col_new,
    bias_grad,
    bias_new,
    bias_copy,
    bias_state_new,
    part,
    got_plane,
    mine,
    got_level,
    column,
    result,
    squares_plane,
    squares_level,
    sems,
):
    full, low = jnp.float32, jnp.bfloat16
    wide, narrow = lax.axis_index(WIDE), lax.axis_index(NARROW)
    z, spot = wide // 2, (wide % 2) * 4 + narrow

    def plane_device(k):
        there = (spot + k) % 8
        return (z * 2 + there // 4, there % 4)

    def level_device(k):
        return (((z + k) % 4) * 2 + wide % 2, narrow)

    barrier = pltpu.get_barrier_semaphore()
    for k in range(1, 8):
        pl.semaphore_signal(barrier, inc=1, device_id=plane_device(k), device_id_type=MESH_ID)
    for k in range(1, 4):
        pl.semaphore_signal(barrier, inc=1, device_id=level_device(k), device_id_type=MESH_ID)
    pl.semaphore_wait(barrier, 10)

    def remote(source, target, phase, k, device):
        return pltpu.make_async_remote_copy(
            src_ref=source,
            dst_ref=target,
            send_sem=sems.at[0, phase, k],
            recv_sem=sems.at[1, phase, k],
            device_id=device,
            device_id_type=MESH_ID,
        )

    def exchange(copies):
        for copy in copies:
            copy.start()
        for copy in copies:
            copy.wait()

    lane = lax.broadcasted_iota(jnp.int32, (1, 128), 1)

    def spread(value, place):
        return jnp.where(lane == place, value, 0.0)

    def pick(row, place):
        return jnp.sum(jnp.where(lane == place, row, 0.0), 1, keepdims=True)

    def total(values):
        return jnp.sum(jnp.sum(values, 1, keepdims=True), 0, keepdims=True)

    count = lat_ref.shape[0] // 4
    order = lax.broadcasted_iota(jnp.int32, (count, count * 4), 0) * 4
    place = lax.broadcasted_iota(jnp.int32, (count, count * 4), 1)
    quarters = [
        product((place == order + k).astype(low), lat_ref[...]).astype(low) for k in range(4)
    ]
    owner_row = (wide * NARROW_PIECES + narrow) * ROWS
    chosen = (
        lax.broadcasted_iota(jnp.int32, (16, D), 1)
        == lax.broadcasted_iota(jnp.int32, (16, D), 0) + owner_row
    ).astype(low)

    def rows_of(member):
        return contract(chosen, member, 1, 1).astype(low)

    act_rows = rows_of(quarters[0][:, :D])
    hid_rows = rows_of(quarters[0][:, D : 2 * D])
    high = quarters[2][:, 2 * D : 3 * D]
    for j in range(NARROW_PIECES):
        mats_grad[:, j * D : (j + 1) * D] = rows_ref[EXPERTS + SHARED, j]
    mats_grad[:, 4 * D : 6 * D] = product(act_rows, quarters[0][:, 2 * D :])[:ROWS]
    mats_grad[:, 6 * D : 10 * D] = product(act_rows, quarters[1])[:ROWS]
    mats_grad[:, 10 * D : 11 * D] = product(hid_rows, high)[:ROWS]
    mats_grad[:, 11 * D : 13 * D] = product(act_rows, quarters[2][:, : 2 * D])[:ROWS]
    time_rows = rows_of(quarters[2][:, 3 * D :])
    time_one = product(time_rows, quarters[3][:, :FREQ])
    label_at = FREQ + 2 * D
    labels = quarters[3][:, label_at : label_at + 128].astype(full)
    label = labels[:, 0:1] * 32.0 + labels[:, 1:2]
    label_hot = (
        lax.broadcasted_iota(jnp.int32, (count, 1024), 1).astype(full) == label
    ).astype(low)
    table = (
        product(rows_of(high), label_hot)
        + product(rows_of(quarters[3][:, FREQ : FREQ + D]), label_hot)
        + product(rows_of(quarters[3][:, FREQ + D : FREQ + 2 * D]), label_hot)
    )
    start_last = 13 * D
    width_last = mats_grad.shape[1] - start_last
    room = 11 * 128
    thin = jnp.concatenate(
        [rows_ref[EXPERTS + SHARED + 1, 0][:, :128], jnp.zeros((4, 128), full)], 0
    )
    thin = jnp.where(
        lax.broadcasted_iota(jnp.int32, (16, 128), 1) < EXPERTS + 2 * PD, thin, 0.0
    )

    def padded(member):
        return jnp.concatenate(
            [member, jnp.zeros((16, room - member.shape[1]), full)], 1
        )

    last = (
        padded(thin)
        + pltpu.roll(padded(time_one), EXPERTS + 2 * PD, 1)
        + pltpu.roll(padded(table), EXPERTS + 2 * PD + FREQ, 1)
    )
    mats_grad[:, start_last:] = last[:ROWS, :width_last]

    part[...] = jnp.zeros_like(part)
    widths = column_widths()
    mats_at, line_at, bias_at = 360, 416, 432
    total_cols = mats_grad.shape[1]
    cuts = [(at, min(at + 128, total_cols)) for at in range(0, total_cols, 128)]
    for number, (begin, end) in enumerate(cuts):
        values = mats_grad[:, begin:end]
        part[mats_at + number : mats_at + number + 1, : end - begin] = jnp.sum(
            values * values + eps_fact, 0, keepdims=True
        )
    bounds = [sum(widths[:k]) for k in range(len(widths) + 1)]
    last_lane = lax.broadcasted_iota(jnp.int32, (ROWS, width_last), 1) + start_last
    last_sq = mats_grad[:, start_last:] * mats_grad[:, start_last:] + eps_fact
    line = spread(loss_ref[...], 46)
    for k in range(len(widths)):
        if k < 5:
            values = mats_grad[:, bounds[k] : bounds[k + 1]]
            sq = values * values + eps_fact
        else:
            sq = jnp.where((last_lane >= bounds[k]) & (last_lane < bounds[k + 1]), last_sq, 0.0)
        new = decay * mats_row[:, k : k + 1] + (1.0 - decay) * (
            jnp.sum(sq, 1, keepdims=True) / widths[k]
        )
        mats_row_new[:, k : k + 1] = new
        line = line + spread(jnp.sum(new, 0, keepdims=True), k)

    def begin_up(e, line):
        for j in range(NARROW_PIECES):
            up_grad[e, :, j * D : (j + 1) * D] = rows_ref[e, j]
        values = up_grad[e]
        sq = values * values + eps_fact
        new = decay * up_row[e] + (1.0 - decay) * (jnp.sum(sq, 1, keepdims=True) / FF)
        up_row_new[e] = new
        cols = jnp.sum(sq, 0, keepdims=True)
        for k in range(FF // 128):
            part[pl.ds(24 * k + e, 1), :] = cols[:, 128 * k : 128 * (k + 1)]
        return line + spread(jnp.sum(new, 0, keepdims=True), 10 + e)

    def begin_down(e, line):
        values = sums_ref[e]
        down_grad[e] = values
        sq = values * values + eps_fact
        new = decay * down_row[e] + (1.0 - decay) * (jnp.sum(sq, 1, keepdims=True) / D)
        down_row_new[e] = new
        cols = jnp.sum(sq, 0, keepdims=True)
        for k in range(D // 128):
            part[pl.ds(24 * (12 + k) + e, 1), :] = cols[:, 128 * k : 128 * (k + 1)]
        return line + spread(jnp.sum(new, 0, keepdims=True), 28 + e)

    line = lax.fori_loop(0, EXPERTS + SHARED, begin_up, line)
    line = lax.fori_loop(0, EXPERTS + SHARED, begin_down, line)
    part[line_at : line_at + 1, :] = line
    for k in range(D // 128):
        part[bias_at + 16 * k : bias_at + 16 * (k + 1), :] = bias_sum[:, 128 * k : 128 * (k + 1)]

    exchange(
        [
            remote(
                part.at[pl.ds(((spot + k) % 8) * 64, 64)], got_plane.at[k], 0, k, plane_device(k)
            )
            for k in range(1, 8)
        ]
    )
    here = part[pl.ds(pl.multiple_of(spot * 64, 64), 64), :]
    for k in range(1, 8):
        here = here + got_plane[k]
    mine[...] = here.reshape(4, 16, 128)
    exchange(
        [
            remote(mine.at[(z + k) % 4], got_level.at[k], 1, k, level_device(k))
            for k in range(1, 4)
        ]
    )
    column[z] = mine[z] + got_level[1] + got_level[2] + got_level[3]
    exchange(
        [remote(column.at[z], column.at[z], 2, k, level_device(k)) for k in range(1, 4)]
    )
    result[spot] = column[...]
    exchange(
        [remote(result.at[spot], result.at[spot], 3, k, plane_device(k)) for k in range(1, 8)]
    )

    def sums_row(row, width=128):
        if isinstance(row, int):
            return result[row // 64, (row // 16) % 4, row % 16 : row % 16 + 1, :width]
        return result[row // 64, (row // 16) % 4, pl.ds(row % 16, 1), :width]

    line = sums_row(line_at)
    loss_out[...] = pick(line, 46)
    room = bias_grad.shape[1]
    begin = (wide * NARROW_PIECES + narrow) * room
    parts = []
    for k in range(3):
        block = jnp.minimum(begin // 128 + k, 47)
        parts.append(sums_row(bias_at + (block % 3) * 16 + block // 3))
    parts = jnp.broadcast_to(jnp.concatenate(parts, 1), (8, D))
    bias_grad[...] = pltpu.roll(parts, (D - begin % 128) % D, 1)[0:1, :room]
    for number, (begin, end) in enumerate(cuts):
        mats_col_new[:, begin:end] = decay * mats_col[:, begin:end] + (1.0 - decay) * (
            sums_row(mats_at + number, end - begin) / D
        )

    squares = jnp.zeros((1, 128), full)
    for k in range(5):
        begin, end = bounds[k], bounds[k + 1]
        step = mats_grad[:, begin:end] * lax.rsqrt(
            mats_row_new[:, k : k + 1] * mats_col_new[:, begin:end] / (pick(line, k) / D)
        )
        mats_new[:, begin:end] = step
        squares = squares + spread(total(step * step), k)

    def by_piece(values):
        chosen_value = values[0]
        for k in range(6, len(widths)):
            chosen_value = jnp.where(last_lane >= bounds[k], values[k - 5], chosen_value)
        return chosen_value

    row_last = by_piece([mats_row_new[:, k : k + 1] for k in range(5, len(widths))])
    mean_last = by_piece([pick(line, k) / D for k in range(5, len(widths))])
    step_last = mats_grad[:, start_last:] * lax.rsqrt(
        row_last * mats_col_new[:, start_last:] / mean_last
    )
    mats_new[:, start_last:] = step_last
    for k in range(5, len(widths)):
        inside = (last_lane >= bounds[k]) & (last_lane < bounds[k + 1])
        squares = squares + spread(total(jnp.where(inside, step_last * step_last, 0.0)), k)

    def step_up(e, squares):
        cols = jnp.concatenate([sums_row(24 * k + e) for k in range(FF // 128)], 1)
        new = decay * up_col[pl.ds(e, 1), :] + (1.0 - decay) * (cols / D)
        up_col_new[pl.ds(e, 1), :] = new
        step = up_grad[e] * lax.rsqrt(up_row_new[e] * new / (pick(line, 10 + e) / D))
        up_new[e] = step
        return squares + spread(total(step * step), 10 + e)

    def step_down(e, squares):
        cols = jnp.concatenate([sums_row(24 * (12 + k) + e) for k in range(D // 128)], 1)
        new = decay * down_col[pl.ds(e, 1), :] + (1.0 - decay) * (cols / FF)
        down_col_new[pl.ds(e, 1), :] = new
        step = down_grad[e] * lax.rsqrt(down_row_new[e] * new / (pick(line, 28 + e) / FF))
        down_new[e] = step
        return squares + spread(total(step * step), 28 + e)

    squares = lax.fori_loop(0, EXPERTS + SHARED, step_up, squares)
    squares = lax.fori_loop(0, EXPERTS + SHARED, step_down, squares)
    state = decay * bias_state[...] + (1.0 - decay) * (
        bias_grad[...] * bias_grad[...] + eps_fact
    )
    bias_state_new[...] = state
    bias_step = bias_grad[...] * lax.rsqrt(state)
    squares = squares + spread(total(bias_step * bias_step), 46)
    squares_plane[spot] = jnp.broadcast_to(squares, (8, 128))
    exchange(
        [
            remote(squares_plane.at[spot], squares_plane.at[spot], 4, k, plane_device(k))
            for k in range(1, 8)
        ]
    )
    squares_level[z] = jnp.sum(squares_plane[...], 0)
    exchange(
        [
            remote(squares_level.at[z], squares_level.at[z], 5, k, level_device(k))
            for k in range(1, 4)
        ]
    )
    squares = jnp.sum(squares_level[...], 0)[0:1]

    def clipped(place, entries):
        rms = jnp.sqrt(pick(squares, place) / entries)
        return jnp.maximum(1.0, rms / clip_level)

    def settle(new_ref, copy_ref, index, master, step, limit):
        value = master - learn_rate * (step / limit)
        new_ref[index] = value
        copy_ref[index] = value.astype(low)

    for k in range(5):
        index = (slice(None), slice(bounds[k], bounds[k + 1]))
        settle(
            mats_new, mats_copy, index, mats_ref[index], mats_new[index], clipped(k, D * widths[k])
        )
    limit = by_piece([clipped(k, D * widths[k]) for k in range(5, len(widths))])
    index = (slice(None), slice(start_last, None))
    settle(mats_new, mats_copy, index, mats_ref[index], mats_new[index], limit)

    def settle_pair(e, unused):
        settle(up_new, up_copy, e, up_ref[e], up_new[e], clipped(10 + e, D * FF))
        settle(down_new, down_copy, e, down_ref[e], down_new[e], clipped(28 + e, D * FF))
        return unused

    lax.fori_loop(0, EXPERTS + SHARED, settle_pair, 0)
    index = (slice(None), slice(None))
    settle(bias_new, bias_copy, index, bias_ref[...], bias_step, clipped(46, 15 * D))


def update_kernel_call(sums, rows, lat, bias_sum, masters, factors, loss_part):
    mats, up_weights, down_weights, biases = masters
    mats_row, mats_col, up_row, up_col, down_row, down_col, bias_state = factors
    full, low = jnp.float32, jnp.bfloat16
    args = (
        sums,
        rows,
        lat,
        bias_sum,
        loss_part.reshape(1, 1),
        mats,
        up_weights,
        down_weights,
        biases.reshape(1, -1),
        mats_row.T,
        mats_col.reshape(1, -1),
        up_row[:, :, None],
        up_col,
        down_row[:, :, None],
        down_col,
        bias_state.reshape(1, -1),
    )

    def like(member, kind):
        return jax.ShapeDtypeStruct(member.shape, kind)

    stacks = []
    for at in (5, 6, 7):
        stacks.append([like(args[at], full), like(args[at], full), like(args[at], low)])
        stacks[-1] += [like(args[2 * at - 1], full), like(args[2 * at], full)]
    lines = [like(args[8], kind) for kind in (full, full, low, full)]
    vmem = pl.BlockSpec(memory_space=pltpu.VMEM)
    dma = pltpu.SemaphoreType.DMA
    outs = pl.pallas_call(
        update_kernel,
        out_shape=[jax.ShapeDtypeStruct((1, 1), full)] + stacks[0] + stacks[1] + stacks[2] + lines,
        in_specs=[vmem] * len(args),
        out_specs=[vmem] * 20,
        scratch_shapes=[
            pltpu.VMEM((512, 128), full),
            pltpu.VMEM((8, 64, 128), full),
            pltpu.VMEM((4, 16, 128), full),
            pltpu.VMEM((4, 16, 128), full),
            pltpu.VMEM((4, 16, 128), full),
            pltpu.VMEM((8, 4, 16, 128), full),
            pltpu.VMEM((8, 8, 128), full),
            pltpu.VMEM((4, 8, 128), full),
            dma((2, 6, 8)),
        ],
        compiler_params=pltpu.CompilerParams(
            collective_id=1, has_side_effects=True, vmem_limit_bytes=VMEM_ROOM
        ),
        name="update",
    )(*args)
    return (
        outs[0][0, 0],
        outs[1],
        outs[2],
        outs[3],
        outs[4].T,
        outs[5].reshape(-1),
        outs[6],
        outs[7],
        outs[8],
        outs[9][:, :, 0],
        outs[10],
        outs[11],
        outs[12],
        outs[13],
        outs[14][:, :, 0],
        outs[15],
        outs[16].reshape(-1),
        outs[17].reshape(-1),
        outs[18].reshape(-1),
        outs[19].reshape(-1),
    )


def gather_kernel(
    mats_in,
    bias_in,
    down_in,
    up_in,
    patches,
    places,
    freq_low,
    label_hot,
    mats_out,
    bias_out,
    down_out,
    up_out,
    mods_out,
    fin_out,
    time_out,
    cond_out,
    qkv_out,
    att_out,
    middle_out,
    moe_out,
    logits_out,
    shared_out,
    mats_got,
    mats_own,
    up_got,
    up_wide,
    up_own,
    embedded,
    down_here,
    up_here,
    near_send,
    near_recv,
    own_sem,
    level_send,
    level_recv,
    one_send,
    one_recv,
    two_send,
    two_recv,
    core_send,
    core_recv,
    bias_send,
    bias_recv,
    here_sem,
):
    n_down, n_up = down_in.shape[0], up_own.shape[0]
    slabs = 1 + n_down + n_up
    wide, narrow = lax.axis_index(WIDE), lax.axis_index(NARROW)
    z, x = wide // 2, wide % 2
    y, c = narrow // 2, narrow % 2
    mates = [
        (wide, (y + (k // 2) * (1 - 2 * y)) * 2 + c + (k % 2) * (1 - 2 * c)) for k in range(1, 4)
    ]
    levels = [(((z + k) % 4) * 2 + x, narrow) for k in range(1, 4)]
    to_x = (z * 2 + 1 - x, narrow)
    to_core, to_y = mates[0], mates[1]
    to_one = (z * 2 + x + (1 - c) * (1 - 2 * x), (y + c * (1 - 2 * y)) * 2 + c)
    to_two = (z * 2 + x + c * (1 - 2 * x), (y + (1 - c) * (1 - 2 * y)) * 2 + c)
    barrier = pltpu.get_barrier_semaphore()
    for target in mates + levels + [to_x]:
        pl.semaphore_signal(barrier, inc=1, device_id=target, device_id_type=MESH_ID)
    pl.semaphore_wait(barrier, 7)

    def remote(source, target, send, recv, device):
        return pltpu.make_async_remote_copy(
            src_ref=source,
            dst_ref=target,
            send_sem=send,
            recv_sem=recv,
            device_id=device,
            device_id_type=MESH_ID,
        )

    def near_mats(k):
        return remote(
            mats_in.at[mates[k - 1][1]],
            mats_got.at[narrow],
            near_send.at[0, k],
            near_recv.at[0, k],
            mates[k - 1],
        )

    def near_up(k):
        return remote(
            up_in.at[mates[k - 1][1]],
            up_got.at[narrow],
            near_send.at[1, k],
            near_recv.at[1, k],
            mates[k - 1],
        )

    own_mats = pltpu.make_async_copy(mats_in.at[narrow], mats_got.at[narrow], own_sem.at[0])
    own_up = pltpu.make_async_copy(up_in.at[narrow], up_got.at[narrow], own_sem.at[1])
    own_bias = pltpu.make_async_copy(bias_in, bias_out.at[z, x, y, c], own_sem.at[2])
    own_mats.start()
    own_up.start()
    own_bias.start()
    for k in range(1, 4):
        near_mats(k).start()

    def bias_level(k):
        return remote(
            bias_in, bias_out.at[z, x, y, c], bias_send.at[k - 1], bias_recv.at[k - 1], levels[k - 1]
        )

    def bias_x():
        part = bias_out.at[:, x, y, c]
        return remote(part, part, bias_send.at[3], bias_recv.at[3], to_x)

    def bias_y():
        part = bias_out.at[:, :, y, c]
        return remote(part, part, bias_send.at[4], bias_recv.at[4], to_y)

    def bias_core():
        part = bias_out.at[:, :, :, c]
        return remote(part, part, bias_send.at[5], bias_recv.at[5], to_core)

    for k in range(1, 4):
        bias_level(k).start()
    own_mats.wait()
    for k in range(1, 4):
        near_mats(k).wait_recv()
        near_up(k).start()
    for n in range(NARROW_PIECES):
        mats_own[n * ROWS : (n + 1) * ROWS] = mats_got[n].astype(jnp.float32)[:ROWS]
    mats_got[0, :, :] = mats_own[:16].astype(jnp.bfloat16)
    mats_got[1, :, :] = mats_own[16:32].astype(jnp.bfloat16)
    mats_got[2, :, :] = mats_own[32:].astype(jnp.bfloat16)
    own_bias.wait()

    def turn(number):
        return (number + EXPERTS) % n_up

    def whole(kind, s):
        if kind == 0:
            return mats_out
        if kind == 1:
            return down_out.at[turn(s - 1)]
        return up_out.at[turn(s - 1 - n_down)]

    def source(kind, s):
        if kind == 0:
            return mats_got.at[pl.ds(0, 3)]
        if kind == 1:
            return down_in.at[turn(s - 1)]
        return up_own.at[turn(s - 1 - n_down)]

    def piece(ref, kind, at):
        z_at, x_at, y_at, c_at = at
        if kind == 1:
            return ref.at[z_at, x_at, y_at, c_at]
        return ref.at[y_at, c_at, z_at, x_at]

    every = slice(None)

    def own_copy(kind, s):
        return pltpu.make_async_copy(
            source(kind, s), piece(whole(kind, s), kind, (z, x, y, c)), own_sem.at[3 + s % 2]
        )

    def level_copy(kind, s, k):
        return remote(
            source(kind, s),
            piece(whole(kind, s), kind, (z, x, y, c)),
            level_send.at[s % 4, k - 1],
            level_recv.at[s, k - 1],
            levels[k - 1],
        )

    def one_copy(kind, s):
        part = piece(whole(kind, s), kind, (every, x, y, c))
        return remote(part, part, one_send.at[s % 4], one_recv.at[s], to_one)

    def two_copy(kind, s, first):
        at = (every, every, y, c) if first == 0 else (every, x, every, c)
        part = piece(whole(kind, s), kind, at)
        return remote(part, part, two_send.at[s % 4], two_recv.at[s], to_two)

    def core_copy(kind, s):
        part = piece(whole(kind, s), kind, (every, every, every, c))
        return remote(part, part, core_send.at[s % 4], core_recv.at[s], to_core)

    def stage_level(kind, s):
        own_copy(kind, s).start()
        for k in range(1, 4):
            level_copy(kind, s, k).start()

    def stage_one(kind, s):
        own_copy(kind, s).wait()
        for k in range(1, 4):
            level_copy(kind, s, k).wait_recv()
        one_copy(kind, s).start()

    def stage_two(kind, s):
        one_copy(kind, s).wait_recv()
        for first in range(2):

            @pl.when(c == first)
            def _():
                two_copy(kind, s, first).start()

    def stage_core(kind, s):
        two_copy(kind, s, 0).wait_recv()
        core_copy(kind, s).start()

    def stage_last(kind, s):
        core_copy(kind, s).wait_recv()

    def stage_sent(kind, s):
        for k in range(1, 4):
            level_copy(kind, s, k).wait_send()
        one_copy(kind, s).wait_send()
        two_copy(kind, s, 0).wait_send()
        core_copy(kind, s).wait_send()

    stages = (
        (stage_sent, 4),
        (stage_level, 0),
        (stage_one, 1),
        (stage_two, 2),
        (stage_core, 3),
        (stage_last, 4),
    )

    lats = patches.shape[0] // PATCHES
    shared_at = 1 + n_down + SHARED + 4
    low, full = jnp.bfloat16, jnp.float32

    def matrix(number, begin, end):
        chunk = mats_out[number // 2, number % 2]
        return chunk.reshape(D, chunk.shape[-1])[:, begin:end]

    def bias_rows():
        return jnp.sum(bias_out[...].astype(full).reshape(-1, 16, D), 0)

    def wide_row(rows, begin, end):
        return jnp.concatenate([rows[k : k + 1] for k in range(begin, end)], 1)

    def conditions():
        rows = bias_rows()
        pre_time = contract(freq_low[...], matrix(3, 1408, 1664), 1, 1) + rows[11:12]
        hid_time = jax.nn.silu(pre_time).astype(low)
        cond = (
            product(hid_time, matrix(3, 1024, 1408))
            + rows[12:13]
            + contract(label_hot[...], matrix(3, 0, 1024), 1, 1)
        )
        act = jax.nn.silu(cond).astype(low)
        time_out[...] = pre_time
        cond_out[...] = cond
        mods_out[:, : 4 * D] = product(act, matrix(1, 0, 4 * D)) + wide_row(rows, 4, 8)
        mods_out[:, 4 * D :] = product(act, matrix(2, 0, 2 * D)) + wide_row(rows, 8, 10)
        fin_out[...] = product(act, matrix(2, 2 * D, 4 * D)) + wide_row(rows, 13, 15)

    def mod_row(start, number):
        return mods_out[pl.ds(start // PATCHES, 1), number * D : (number + 1) * D]

    def attention_in(start):
        rows = bias_rows()
        span = pl.ds(start, PATCHES)
        emb = contract(patches[span, :], matrix(2, 4 * D, 4 * D + 128), 1, 1)
        emb = emb + rows[10:11] + places[...]
        embedded[...] = emb
        normed, unused_std = layer_norm(emb)
        attn_in = (normed * (1.0 + mod_row(start, 1)) + mod_row(start, 0)).astype(low)
        qkv_out[span, :] = (
            product(attn_in, matrix(0, 0, 3 * D)) + wide_row(rows, 0, 3)
        ).astype(low)

    def attention_heads(start):
        span = pl.ds(start, PATCHES)
        lane = lax.broadcasted_iota(jnp.int32, (PATCHES, 2 * HD), 1)
        for pair in range(HEADS // 2):
            at = pair * 2 * HD
            queries = qkv_out[span, at : at + 2 * HD]
            keys = qkv_out[span, D + at : D + at + 2 * HD]
            values = qkv_out[span, 2 * D + at : 2 * D + at + 2 * HD]
            halves = []
            for half in range(2):
                mine = (lane < HD) if half == 0 else (lane >= HD)
                scores = contract(jnp.where(mine, queries, 0), keys, 1, 1) * HD ** (-0.5)
                powers = jnp.exp(scores - jnp.max(scores, 1, keepdims=True))
                probs = (powers / jnp.sum(powers, 1, keepdims=True)).astype(low)
                halves.append(product(probs, values))
            att_out[span, at : at + 2 * HD] = jnp.where(lane < HD, halves[0], halves[1]).astype(low)

    def attention_out(start):
        rows = bias_rows()
        span = pl.ds(start, PATCHES)
        attn = product(att_out[span, :], matrix(0, 3 * D, 4 * D)) + rows[3:4]
        middle = embedded[...] + mod_row(start, 2) * attn
        middle_out[span, :] = middle
        normed, unused_std = layer_norm(middle)
        moe_in = (normed * (1.0 + mod_row(start, 4)) + mod_row(start, 3)).astype(low)
        moe_out[span, :] = moe_in
        logits_out[span, :] = product(moe_in, matrix(0, 4 * D, 4 * D + 128))

    def fetch(shared_id):
        e = EXPERTS + shared_id
        first = pltpu.make_async_copy(down_out.at[e], down_here, here_sem.at[0])
        second = pltpu.make_async_copy(up_out.at[e], up_here, here_sem.at[1])
        first.start()
        second.start()
        first.wait()
        second.wait()

    def shared_block(shared_id, start):
        span = pl.ds(start, PATCHES)
        rows = moe_out[span, :]
        chunks = [up_here[n // 2, n % 2].reshape(D, D) for n in range(NARROW_PIECES)]
        down = down_here[...].reshape(FF, D)
        total = None
        for cut in range(0, FF, CUT):
            pre_act = product(rows, up_columns(chunks, cut))
            part = product(gelu_only(pre_act).astype(low), down[cut : cut + CUT])
            total = part if total is None else total + part
        if shared_id == 0:
            shared_out[span, :] = total
        else:
            shared_out[span, :] += total

    def tick(t, unused):
        @pl.when(t == 1)
        def _():
            for k in range(1, 4):
                bias_level(k).wait_recv()
            bias_x().start()

        @pl.when(t == 2)
        def _():
            bias_x().wait_recv()
            bias_y().start()

        @pl.when(t == 3)
        def _():
            bias_y().wait_recv()
            bias_core().start()

        @pl.when(t == 6)
        def _():
            own_up.wait()
            for k in range(1, 4):
                near_up(k).wait_recv()
            for n in range(NARROW_PIECES):
                up_wide[n] = up_got[n].astype(jnp.float32)

            for e in range(n_up):
                up_own[e] = jnp.concatenate(
                    [up_wide[n, e * ROWS : (e + 1) * ROWS] for n in range(NARROW_PIECES)], 0
                ).astype(jnp.bfloat16)

        for stage, lag in stages:
            s = t - lag

            @pl.when(s == 0)
            def _():
                stage(0, 0)

            @pl.when((s >= 1) & (s < 1 + n_down))
            def _():
                stage(1, jnp.clip(s, 1, n_down))

            @pl.when((s >= 1 + n_down) & (s < slabs))
            def _():
                stage(2, jnp.clip(s, 1 + n_down, slabs - 1))

        @pl.when(t == 5)
        def _():
            bias_core().wait_recv()
            conditions()

        for number, unit in enumerate((attention_in, attention_heads, attention_out)):

            @pl.when((t >= 6) & (t < 6 + 3 * lats) & ((t - 6) % 3 == number))
            def _():
                unit(pl.multiple_of(jnp.clip((t - 6) // 3, 0, lats - 1) * PATCHES, PATCHES))

        for shared_id in range(SHARED):
            begin = shared_at + shared_id * lats

            @pl.when(t == begin)
            def _():
                fetch(shared_id)

            @pl.when((t >= begin) & (t < begin + lats))
            def _():
                shared_block(
                    shared_id, pl.multiple_of(jnp.clip(t - begin, 0, lats - 1) * PATCHES, PATCHES)
                )

        return unused

    lax.fori_loop(0, slabs + 4, tick, 0)
    for k in range(1, 4):
        near_mats(k).wait_send()
        near_up(k).wait_send()
        bias_level(k).wait_send()
    bias_x().wait_send()
    bias_y().wait_send()
    bias_core().wait_send()


def gather_weights(
    mats, up_weights, down_weights, biases, patches, places, freq_low, label_hot
):
    low = jnp.bfloat16
    owner = lax.axis_index(AXES)
    m = mats.astype(low)
    rows = m.shape[0]

    thin = 13 * D

    def thin_part(at):
        return jnp.pad(m[:, at : at + 16], ((0, 0), (0, 112)))

    mats_in = jnp.stack(
        [
            jnp.concatenate([m[:, : 4 * D], thin_part(thin)], 1),
            jnp.concatenate([m[:, 4 * D : 8 * D], thin_part(thin + 16)], 1),
            jnp.concatenate(
                [m[:, 8 * D : 10 * D], m[:, 11 * D : 13 * D], thin_part(thin + 32)], 1
            ),
            jnp.concatenate(
                [
                    m[:, thin + 48 + FREQ :],
                    jnp.zeros((rows, 24), low),
                    m[:, 10 * D : 11 * D],
                    m[:, thin + 48 : thin + 48 + FREQ],
                ],
                1,
            ),
        ],
        0,
    )
    mats_in = jnp.pad(mats_in, ((0, 0), (0, 16 - rows), (0, 0)))
    line = lax.dynamic_update_slice(
        jnp.zeros((16 * D,), low), biases.astype(low), (owner * biases.shape[0],)
    )
    n_up = up_weights.shape[0]
    up_in = (
        up_weights.astype(low)
        .reshape(n_up, rows, NARROW_PIECES, D)
        .transpose(2, 0, 1, 3)
        .reshape(NARROW_PIECES, n_up * rows, D)
    )
    room = (n_up * rows + 15) // 16 * 16
    up_in = jnp.pad(up_in, ((0, 0), (0, room - n_up * rows), (0, 0)))
    slabs = 1 + 2 * n_up
    spread = mats_in.shape[2]
    dma = pltpu.SemaphoreType.DMA
    anywhere = pl.BlockSpec(memory_space=pl.ANY)
    tokens = patches.shape[0]
    full, vmem = jnp.float32, pl.BlockSpec(memory_space=pltpu.VMEM)
    outs = pl.pallas_call(
        gather_kernel,
        out_shape=[
            jax.ShapeDtypeStruct((2, 2, 4, 2, 3, 16, spread), low),
            jax.ShapeDtypeStruct((4, 2, 2, 2, 16, D), low),
            jax.ShapeDtypeStruct((n_up, 4, 2, 2, 2, PIECE, D), low),
            jax.ShapeDtypeStruct((n_up, 2, 2, 4, 2, PIECE, D), low),
            jax.ShapeDtypeStruct((8, 6 * D), full),
            jax.ShapeDtypeStruct((8, 2 * D), full),
            jax.ShapeDtypeStruct((8, D), full),
            jax.ShapeDtypeStruct((8, D), full),
            jax.ShapeDtypeStruct((tokens, 3 * D), low),
            jax.ShapeDtypeStruct((tokens, D), low),
            jax.ShapeDtypeStruct((tokens, D), full),
            jax.ShapeDtypeStruct((tokens, D), low),
            jax.ShapeDtypeStruct((tokens, 128), full),
            jax.ShapeDtypeStruct((tokens, D), full),
        ],
        in_specs=[anywhere] * 4 + [vmem] * 4,
        out_specs=[vmem] * 2 + [anywhere] * 2 + [vmem] * 10,
        scratch_shapes=[
            pltpu.VMEM((NARROW_PIECES, 16, spread), low),
            pltpu.VMEM((PIECE, spread), jnp.float32),
            pltpu.VMEM((NARROW_PIECES, room, D), low),
            pltpu.VMEM((NARROW_PIECES, room, D), jnp.float32),
            pltpu.VMEM((n_up, PIECE, D), low),
            pltpu.VMEM((PATCHES, D), full),
            pltpu.VMEM((4, 2, 2, 2, PIECE, D), low),
            pltpu.VMEM((2, 2, 4, 2, PIECE, D), low),
            dma((2, 4)),
            dma((2, 4)),
            dma((5,)),
            dma((4, 3)),
            dma((slabs, 3)),
            dma((4,)),
            dma((slabs,)),
            dma((4,)),
            dma((slabs,)),
            dma((4,)),
            dma((slabs,)),
            dma((6,)),
            dma((6,)),
            dma((2,)),
        ],
        compiler_params=pltpu.CompilerParams(
            collective_id=2, has_side_effects=True, vmem_limit_bytes=VMEM_ROOM
        ),
        name="gather_weights",
    )(
        mats_in,
        line.reshape(16, D),
        down_weights.astype(low),
        up_in,
        patches,
        places,
        freq_low,
        label_hot,
    )
    return outs


def split_weights(weights):
    mats_full, up_full, down_full, bias_full = weights
    matrices = cut_pieces(mats_full, column_widths(), 1)
    vectors = [member.astype(jnp.float32) for member in cut_pieces(bias_full, bias_widths(), 0)]
    up_full = up_full.reshape(-1, D, NARROW_PIECES, D).transpose(0, 2, 1, 3)
    return (matrices, vectors, up_full, down_full)


def forward(weights, latents, noise, timesteps, labels, routes):
    matrices, vectors, up_full, down_full = weights
    w_qkv, w_proj, w_mod, w_time2, w_final, w_router, w_head, w_patch, w_time1, w_table = matrices
    b_qkv, b_proj, b_mod, b_patch, b_time1, b_time2, b_final = vectors
    num_latents = latents.shape[0]
    rows_here = num_latents * PATCHES
    steps_f = timesteps.astype(jnp.float32)
    signal, spread = noise_level(steps_f)
    noisy = signal[:, None] * latents + spread[:, None] * noise
    patches = noisy.reshape(rows_here, PD).astype(jnp.bfloat16)
    embedded = (
        contract(patches, w_patch, 1, 1).reshape(num_latents, PATCHES, D)
        + b_patch
        + positions()[None]
    )
    freq_low = time_features(steps_f).astype(jnp.bfloat16)
    pre_time = contract(freq_low, w_time1, 1, 1) + b_time1
    hid_time = jax.nn.silu(pre_time).astype(jnp.bfloat16)
    label_hot = (labels[:, None] == jnp.arange(CLASSES, dtype=jnp.int32)[None, :]).astype(
        jnp.float32
    )
    label_emb = lax.dot_general(
        label_hot,
        w_table.astype(jnp.float32),
        (((1,), (1,)), ((), ())),
        precision=lax.Precision.HIGHEST,
        preferred_element_type=jnp.float32,
    )
    cond = product(hid_time, w_time2) + b_time2 + label_emb
    cond_act = jax.nn.silu(cond).astype(jnp.bfloat16)
    modulation = product(cond_act, w_mod) + b_mod
    final_mod = product(cond_act, w_final) + b_final
    shift_attn, scale_attn, gate_attn, shift_moe, scale_moe, gate_moe = [
        member[:, None, :] for member in jnp.split(modulation, 6, 1)
    ]
    shift_fin, scale_fin = [member[:, None, :] for member in jnp.split(final_mod, 2, 1)]
    normed_one, inv_one = layer_norm(embedded)
    attn_in = (
        (normed_one * (1.0 + scale_attn) + shift_attn).astype(jnp.bfloat16).reshape(rows_here, D)
    )
    qkv_out = (
        (product(attn_in, w_qkv) + b_qkv)
        .astype(jnp.bfloat16)
        .reshape(num_latents, PATCHES, 3, HEADS, HD)
    )
    scores = jnp.einsum(
        LQK, qkv_out[:, :, 0], qkv_out[:, :, 1], preferred_element_type=jnp.float32
    ) * HD ** (-0.5)
    log_totals = jax.nn.logsumexp(scores, -1)
    probs_low = jax.nn.softmax(scores, -1).astype(jnp.bfloat16)
    attended = (
        jnp.einsum(
            "lhqk,lkhd->lqhd", probs_low, qkv_out[:, :, 2], preferred_element_type=jnp.float32
        )
        .astype(jnp.bfloat16)
        .reshape(rows_here, D)
    )
    attn_out = (product(attended, w_proj) + b_proj).reshape(num_latents, PATCHES, D)
    middle = embedded + gate_attn * attn_out
    normed_two, inv_two = layer_norm(middle)
    moe_in = (normed_two * (1.0 + scale_moe) + shift_moe).astype(jnp.bfloat16).reshape(rows_here, D)
    logits = product(moe_in, w_router)
    route_hot = (routes[:, :, None] == jnp.arange(EXPERTS, dtype=jnp.int32)[None, None, :]).astype(
        jnp.float32
    )
    gate_vals = jax.nn.softmax(jnp.sum(route_hot * logits[:, None, :], 2), -1)
    slot_of, slot_meta = pack_slots(routes)
    routed = experts_forward(slot_of, slot_meta, moe_in, up_full, down_full)
    moe_out = gate_vals[:, 0:1] * routed[0] + gate_vals[:, 1:2] * routed[1]
    for shared_id in range(EXPERTS, EXPERTS + SHARED):
        for cut in range(0, FF, CUT):
            pre_act = product(moe_in, up_columns(up_full[shared_id], cut))
            activated = gelu_only(pre_act).astype(jnp.bfloat16)
            moe_out = moe_out + product(activated, down_full[shared_id, cut : cut + CUT])
    moe_out = moe_out.reshape(num_latents, PATCHES, D)
    final_state = middle + gate_moe * moe_out
    normed_fin, inv_fin = layer_norm(final_state)
    head_in = (
        (normed_fin * (1.0 + scale_fin) + shift_fin).astype(jnp.bfloat16).reshape(rows_here, D)
    )
    errors = product(head_in, w_head) - noise.reshape(rows_here, PD)
    return SimpleNamespace(
        patches=patches,
        freq_low=freq_low,
        pre_time=pre_time,
        hid_time=hid_time,
        label_hot=label_hot,
        cond=cond,
        cond_act=cond_act,
        scale_attn=scale_attn,
        gate_attn=gate_attn,
        scale_moe=scale_moe,
        gate_moe=gate_moe,
        scale_fin=scale_fin,
        normed_one=normed_one,
        inv_one=inv_one,
        attn_in=attn_in,
        qkv_out=qkv_out,
        log_totals=log_totals,
        attended=attended,
        attn_out=attn_out,
        normed_two=normed_two,
        inv_two=inv_two,
        moe_in=moe_in,
        route_hot=route_hot,
        gate_vals=gate_vals,
        slot_of=slot_of,
        slot_meta=slot_meta,
        routed=routed,
        moe_out=moe_out,
        normed_fin=normed_fin,
        inv_fin=inv_fin,
        head_in=head_in,
        errors=errors,
    )


def forward_fused(mats, up_weights, down_weights, biases, latents, noise, timesteps, labels):
    num_latents = latents.shape[0]
    rows_here = num_latents * PATCHES
    steps_f = timesteps.astype(jnp.float32)
    signal, spread = noise_level(steps_f)
    noisy = signal[:, None] * latents + spread[:, None] * noise
    patches = noisy.reshape(rows_here, PD).astype(jnp.bfloat16)
    freq_low = time_features(steps_f).astype(jnp.bfloat16)
    label_low = (labels[:, None] == jnp.arange(1024, dtype=jnp.int32)[None, :]).astype(jnp.bfloat16)
    less = ((0, 8 - num_latents), (0, 0))
    outs = gather_weights(
        mats,
        up_weights,
        down_weights,
        biases,
        jnp.pad(patches, ((0, 0), (0, 128 - PD))),
        positions(),
        jnp.pad(freq_low, less),
        jnp.pad(label_low, less),
    )
    n_up = outs[3].shape[0]
    return SimpleNamespace(
        patches=jnp.pad(patches, ((0, 0), (0, 128 - PD))),
        freq_low=jnp.pad(freq_low, less),
        mats_full=outs[0],
        bias_full=outs[1],
        down_full=outs[2].reshape(n_up, FF, D),
        up_full=outs[3].reshape(n_up, NARROW_PIECES, D, D),
        mods=outs[4],
        fin=outs[5],
        pre_time=outs[6],
        cond=outs[7],
        qkv=outs[8],
        attended=outs[9],
        middle=outs[10],
        moe_in=outs[11],
        logits=outs[12],
        shared_out=outs[13],
    )


def backward_fused(fused, latents, noise, labels, routes, total_tokens):
    num_latents = latents.shape[0]
    rows_here = num_latents * PATCHES
    less = ((0, 8 - num_latents), (0, 0))
    mods, fin = fused.mods[:num_latents], fused.fin[:num_latents]
    gate_moe = mods[:, None, 5 * D :]
    shift_fin, scale_fin = fin[:, None, :D], fin[:, None, D:]
    mats_full = fused.mats_full.reshape(NARROW_PIECES, D, -1)
    w_head = mats_full[1][:, 4 * D : 4 * D + PD]
    line = jnp.sum(fused.bias_full.reshape(-1, 16, D).astype(jnp.float32), 0)
    route_hot = (routes[:, :, None] == jnp.arange(EXPERTS, dtype=jnp.int32)[None, None, :]).astype(
        jnp.float32
    )
    logits = fused.logits[:, :EXPERTS]
    gate_vals = jax.nn.softmax(jnp.sum(route_hot * logits[:, None, :], 2), -1)
    slot_of, slot_meta = pack_slots(routes)
    routed = experts_forward(slot_of, slot_meta, fused.moe_in, fused.up_full, fused.down_full)
    moe_out = gate_vals[:, 0:1] * routed[0] + gate_vals[:, 1:2] * routed[1] + fused.shared_out
    moe_out = moe_out.reshape(num_latents, PATCHES, D)
    final_state = fused.middle.reshape(num_latents, PATCHES, D) + gate_moe * moe_out
    normed_fin, inv_fin = layer_norm(final_state)
    head_in = (
        (normed_fin * (1.0 + scale_fin) + shift_fin).astype(jnp.bfloat16).reshape(rows_here, D)
    )
    errors = product(head_in, w_head) - noise.reshape(rows_here, PD)
    grad_head, grad_head_in, unused = linear_back(errors * (2.0 / total_tokens), head_in, w_head)
    grad_head_in = grad_head_in.reshape(num_latents, PATCHES, D)
    grad_fin = jnp.concatenate(
        [jnp.sum(grad_head_in, 1), jnp.sum(grad_head_in * normed_fin, 1)], 1
    )
    grad_state = norm_back(grad_head_in * (1.0 + scale_fin), normed_fin, inv_fin)
    grad_gate = jnp.sum(moe_out * grad_state, 1)
    grad_moe = (gate_moe * grad_state).reshape(rows_here, D)
    grad_gates = jnp.stack([jnp.sum(routed[k] * grad_moe, 1) for k in range(2)], 1)
    grad_pair = jnp.stack(
        [(gate_vals[:, k : k + 1] * grad_moe).astype(jnp.bfloat16) for k in range(2)], 0
    )
    up_slabs, down_slabs, dx_routed = experts_backward(
        slot_of, slot_meta, fused.moe_in, grad_pair, fused.up_full, fused.down_full
    )
    grad_picked = gate_vals * (grad_gates - jnp.sum(gate_vals * grad_gates, 1, keepdims=True))
    grad_logits = jnp.sum(route_hot * grad_picked[:, :, None], 1)
    grad_router = contract(fused.moe_in, grad_logits.astype(jnp.bfloat16), 0, 0)
    thin = jnp.pad(jnp.concatenate([grad_router, grad_head], 1), ((0, 0), (0, 128 - 32)))
    label_parts = jnp.stack([labels // 32, labels % 32], 1).astype(jnp.bfloat16)
    members = (
        fused.moe_in,
        grad_moe.astype(jnp.bfloat16),
        dx_routed,
        jnp.pad(grad_logits, ((0, 0), (0, 128 - EXPERTS))),
        fused.middle,
        fused.qkv,
        fused.attended,
        grad_state.reshape(rows_here, D),
        fused.patches,
        positions(),
        fused.mods,
        fused.mats_full,
        line,
        fused.pre_time,
        fused.cond,
        fused.freq_low,
        jnp.pad(grad_gate, less),
        jnp.pad(grad_fin, less),
        thin,
        jnp.pad(label_parts, ((0, 8 - num_latents), (0, 126))),
    )
    return jnp.sum(errors * errors), reduce_slabs(
        down_slabs, up_slabs, fused.up_full, fused.down_full, members
    )


def backward(weights, kept, total_tokens):
    matrices, vectors, up_full, down_full = weights
    w_qkv, w_proj, w_mod, w_time2, w_final, w_router, w_head, w_patch, w_time1, w_table = matrices
    num_latents = kept.normed_one.shape[0]
    rows_here = num_latents * PATCHES
    grad_head, grad_head_in, unused = linear_back(
        kept.errors * (2.0 / total_tokens), kept.head_in, w_head
    )
    grad_head_in = grad_head_in.reshape(num_latents, PATCHES, D)
    grad_final_mod = jnp.concatenate(
        [jnp.sum(grad_head_in, 1), jnp.sum(grad_head_in * kept.normed_fin, 1)], 1
    )
    grad_state = norm_back(
        grad_head_in * (1.0 + kept.scale_fin), kept.normed_fin, kept.inv_fin
    )
    grad_gate_moe = jnp.sum(kept.moe_out * grad_state, 1)
    grad_moe = (kept.gate_moe * grad_state).reshape(rows_here, D)
    grad_moe_low = grad_moe.astype(jnp.bfloat16)
    moe_in = kept.moe_in
    gate_vals = kept.gate_vals
    routed = kept.routed
    grad_gates = jnp.stack([jnp.sum(routed[k] * grad_moe, 1) for k in range(2)], 1)
    grad_pair = jnp.stack(
        [(gate_vals[:, k : k + 1] * grad_moe).astype(jnp.bfloat16) for k in range(2)], 0
    )
    up_slabs, down_slabs, grad_moe_in = experts_backward(
        kept.slot_of, kept.slot_meta, moe_in, grad_pair, up_full, down_full
    )
    up_all = [up_slabs.transpose(0, 1, 3, 2, 4).reshape(-1, D, FF)]
    down_all = [down_slabs.reshape(-1, FF, D)]
    for shared_id in range(EXPERTS, EXPERTS + SHARED):
        up_part = jnp.concatenate([up_full[shared_id, k] for k in range(NARROW_PIECES)], 1)
        activated, slope = gelu_slope(product(moe_in, up_part))
        grad_act = contract(grad_moe_low, down_full[shared_id], 1, 1)
        grad_pre = (grad_act * slope).astype(jnp.bfloat16)
        down_all.append(contract(activated.astype(jnp.bfloat16), grad_moe_low, 0, 0)[None])
        up_all.append(contract(moe_in, grad_pre, 0, 0)[None])
        grad_moe_in = grad_moe_in + contract(grad_pre, up_part, 1, 1)
    up_slabs = jnp.concatenate([member.astype(jnp.float32) for member in up_all], 0)
    down_slabs = jnp.concatenate([member.astype(jnp.float32) for member in down_all], 0)
    grad_picked = gate_vals * (grad_gates - jnp.sum(gate_vals * grad_gates, 1, keepdims=True))
    grad_logits = jnp.sum(kept.route_hot * grad_picked[:, :, None], 1)
    grad_router, grad_from_router, unused = linear_back(grad_logits, moe_in, w_router)
    grad_moe_in = (grad_moe_in + grad_from_router).reshape(num_latents, PATCHES, D)
    grad_middle = grad_state + norm_back(
        grad_moe_in * (1.0 + kept.scale_moe), kept.normed_two, kept.inv_two
    )
    grad_gate_attn = jnp.sum(kept.attn_out * grad_middle, 1)
    grad_proj, grad_attended, grad_b_proj = linear_back(
        (kept.gate_attn * grad_middle).reshape(rows_here, D), kept.attended, w_proj
    )
    grad_att_low = grad_attended.astype(jnp.bfloat16).reshape(num_latents, PATCHES, HEADS, HD)
    qkv_out = kept.qkv_out
    queries = qkv_out[:, :, 0]
    key_rows = qkv_out[:, :, 1]
    values = qkv_out[:, :, 2]
    scores = jnp.einsum(
        LQK, queries, key_rows, preferred_element_type=jnp.float32
    ) * HD ** (-0.5)
    probs = jnp.exp(scores - kept.log_totals[..., None])
    probs_low = probs.astype(jnp.bfloat16)
    grad_values = jnp.einsum(
        "lhqk,lqhd->lkhd", probs_low, grad_att_low, preferred_element_type=jnp.float32
    )
    grad_probs = jnp.einsum(
        LQK, grad_att_low, values, preferred_element_type=jnp.float32
    )
    grad_scores = (
        probs * (grad_probs - jnp.sum(probs * grad_probs, -1, keepdims=True)) * HD ** (-0.5)
    ).astype(jnp.bfloat16)
    grad_queries = jnp.einsum(
        "lhqk,lkhd->lqhd", grad_scores, key_rows, preferred_element_type=jnp.float32
    )
    grad_keys = jnp.einsum(
        "lhqk,lqhd->lkhd", grad_scores, queries, preferred_element_type=jnp.float32
    )
    grad_qkv = jnp.stack([grad_queries, grad_keys, grad_values], 2).reshape(rows_here, 3 * D)
    grad_w_qkv, grad_attn_in, grad_b_qkv = linear_back(grad_qkv, kept.attn_in, w_qkv)
    grad_attn_in = grad_attn_in.reshape(num_latents, PATCHES, D)
    grad_embedded = grad_middle + norm_back(
        grad_attn_in * (1.0 + kept.scale_attn), kept.normed_one, kept.inv_one
    )
    grad_emb_flat = grad_embedded.reshape(rows_here, D)
    grad_patch = contract(grad_emb_flat.astype(jnp.bfloat16), kept.patches, 0, 0)
    grad_b_patch = jnp.sum(grad_emb_flat, 0)
    grad_modulation = jnp.concatenate(
        [
            jnp.sum(grad_attn_in, 1),
            jnp.sum(grad_attn_in * kept.normed_one, 1),
            grad_gate_attn,
            jnp.sum(grad_moe_in, 1),
            jnp.sum(grad_moe_in * kept.normed_two, 1),
            grad_gate_moe,
        ],
        1,
    )
    grad_mod_low = grad_modulation.astype(jnp.bfloat16)
    grad_fin_low = grad_final_mod.astype(jnp.bfloat16)
    grad_act = contract(grad_mod_low, w_mod, 1, 1) + contract(grad_fin_low, w_final, 1, 1)
    grad_cond = slope_back(jax.nn.silu, kept.cond, grad_act)
    grad_cond_low = grad_cond.astype(jnp.bfloat16)
    grad_hid_time = contract(grad_cond_low, w_time2, 1, 1)
    grad_pre_time = slope_back(jax.nn.silu, kept.pre_time, grad_hid_time)
    grad_time_low = grad_pre_time.astype(jnp.bfloat16)
    mats_slabs = jnp.concatenate([grad_w_qkv, grad_proj], 1)[None]
    thin = jnp.concatenate([grad_router, grad_head, grad_patch], 1)
    grad_bias = jnp.concatenate(
        [
            grad_b_qkv,
            grad_b_proj,
            jnp.sum(grad_modulation, 0),
            grad_b_patch,
            jnp.sum(grad_pre_time, 0),
            jnp.sum(grad_cond, 0),
            jnp.sum(grad_final_mod, 0),
        ]
    )
    lows = jnp.concatenate(
        [
            kept.cond_act,
            kept.hid_time,
            grad_mod_low,
            grad_fin_low,
            grad_cond_low,
            grad_time_low,
            kept.freq_low,
        ],
        1,
    )
    return (up_slabs, down_slabs, mats_slabs, thin, grad_bias, lows, grad_cond)


def latent_grads(lows, grad_cond, labels, row_start, row_count):
    lows = lax.all_gather(lows, AXES, axis=0, tiled=True)
    grad_cond = lax.all_gather(grad_cond, AXES, axis=0, tiled=True)
    labels = lax.all_gather(labels, AXES, axis=0, tiled=True)
    cond_act, hid_time, grad_mod, grad_fin, grad_low, grad_time, freq_low = cut_pieces(
        lows, [D, D, 6 * D, 2 * D, D, D, FREQ], 1
    )

    def rows_of(member):
        return lax.dynamic_slice_in_dim(member, row_start, row_count, 1)

    label_hot = (labels[:, None] == jnp.arange(CLASSES, dtype=jnp.int32)[None, :]).astype(
        jnp.float32
    )
    grad_table = lax.dot_general(
        rows_of(grad_cond),
        label_hot,
        (((0,), (0,)), ((), ())),
        precision=lax.Precision.HIGHEST,
        preferred_element_type=jnp.float32,
    )
    return (
        contract(rows_of(cond_act), grad_mod, 0, 0),
        contract(rows_of(hid_time), grad_low, 0, 0),
        contract(rows_of(cond_act), grad_fin, 0, 0),
        contract(rows_of(grad_time), freq_low, 0, 0),
        grad_table,
    )


def factor_start(grad, row_old):
    squares = grad * grad + eps_fact
    row_new = decay * row_old + (1.0 - decay) * jnp.mean(squares, 2)
    return (row_new, jnp.sum(squares, 1), jnp.sum(row_new, 1))


def factor_update(grad, row_new, col_total, row_total, col_old, row_count):
    col_new = decay * col_old + (1.0 - decay) * (col_total / row_count)
    row_mean = row_total / row_count
    update = grad * lax.rsqrt(row_new[:, :, None] * col_new[:, None, :] / row_mean[:, None, None])
    return (col_new, update, jnp.sum(update * update, (1, 2)))


def clip_apply(master, update, square_total, entry_count):
    update_rms = jnp.sqrt(square_total / entry_count)
    return master - learn_rate * (update / jnp.maximum(1.0, update_rms / clip_level)[:, None, None])


def update_plain(grads, masters, factors, loss_part):
    mats_grad, up_grad, down_grad, bias_grad = grads
    mats, up_weights, down_weights, biases = masters
    mats_row, mats_col, up_row, up_col, down_row, down_col, bias_state = factors
    widths = column_widths()
    grad_pieces = cut_pieces(mats_grad, widths, 1)
    starts = [
        factor_start(grad_pieces[k][None], mats_row[k][None]) for k in range(len(widths))
    ]
    up_row_new, up_col_part, up_row_part = factor_start(up_grad, up_row)
    down_row_new, down_col_part, down_row_part = factor_start(down_grad, down_row)
    col_totals, row_totals, up_cols, up_rows, down_cols, down_rows, loss_total = lax.psum(
        (
            jnp.concatenate([member[1] for member in starts], 1)[0],
            jnp.concatenate([member[2] for member in starts], 0),
            up_col_part,
            up_row_part,
            down_col_part,
            down_row_part,
            loss_part,
        ),
        AXES,
    )
    col_total_pieces = cut_pieces(col_totals, widths, 0)
    col_old_pieces = cut_pieces(mats_col, widths, 0)
    steps = [
        factor_update(
            grad_pieces[k][None],
            starts[k][0],
            col_total_pieces[k][None],
            row_totals[k][None],
            col_old_pieces[k][None],
            D,
        )
        for k in range(len(widths))
    ]
    up_col_new, up_update, up_square = factor_update(
        up_grad, up_row_new, up_cols, up_rows, up_col, D
    )
    down_col_new, down_update, down_square = factor_update(
        down_grad, down_row_new, down_cols, down_rows, down_col, FF
    )
    bias_state_new = decay * bias_state + (1.0 - decay) * (bias_grad * bias_grad + eps_fact)
    bias_update = bias_grad * lax.rsqrt(bias_state_new)
    square_mats, square_up, square_down, square_bias = lax.psum(
        (
            jnp.concatenate([member[2] for member in steps], 0),
            up_square,
            down_square,
            jnp.sum(bias_update * bias_update),
        ),
        AXES,
    )
    master_pieces = cut_pieces(mats, widths, 1)
    mats_new = jnp.concatenate(
        [
            clip_apply(
                master_pieces[k][None], steps[k][1], square_mats[k][None], D * widths[k]
            )[0]
            for k in range(len(widths))
        ],
        1,
    )
    up_new = clip_apply(up_weights, up_update, square_up, D * FF)
    down_new = clip_apply(down_weights, down_update, square_down, D * FF)
    bias_rms = jnp.sqrt(square_bias / (15 * D))
    bias_new = biases - learn_rate * (bias_update / jnp.maximum(1.0, bias_rms / clip_level))
    return (
        loss_total,
        mats_grad,
        mats_new,
        mats_new.astype(jnp.bfloat16),
        jnp.concatenate([member[0] for member in starts], 0),
        jnp.concatenate([member[0][0] for member in steps], 0),
        up_grad,
        up_new,
        up_new.astype(jnp.bfloat16),
        up_row_new,
        up_col_new,
        down_grad,
        down_new,
        down_new.astype(jnp.bfloat16),
        down_row_new,
        down_col_new,
        bias_grad,
        bias_new,
        bias_new.astype(jnp.bfloat16),
        bias_state_new,
    )


def body(
    latents,
    noise,
    timesteps,
    labels,
    routes,
    mats,
    up_weights,
    down_weights,
    biases,
    *factors,
):
    rows_here = mats.shape[0]
    total_tokens = latents.shape[0] * PATCHES * lax.axis_size(AXES)
    masters = (mats, up_weights, down_weights, biases)
    if lax.axis_size(WIDE) == WIDE_PIECES and lax.axis_size(NARROW) == NARROW_PIECES:
        fused = forward_fused(
            mats, up_weights, down_weights, biases, latents, noise, timesteps, labels
        )
        loss_part, (sums, turned, lat, bias_sum) = backward_fused(
            fused, latents, noise, labels, routes, total_tokens
        )
        outs = update_kernel_call(sums, turned, lat, bias_sum, masters, factors, loss_part)
    else:
        flat = jnp.concatenate([mats.reshape(-1), biases], 0).astype(jnp.bfloat16)
        flat = lax.all_gather(flat, AXES, axis=0, tiled=False)
        gathered = split_weights(
            (
                flat[:, : rows_here * mats.shape[1]].reshape(-1, mats.shape[1]),
                lax.all_gather(up_weights.astype(jnp.bfloat16), AXES, axis=1, tiled=True),
                lax.all_gather(down_weights.astype(jnp.bfloat16), AXES, axis=1, tiled=True),
                flat[:, rows_here * mats.shape[1] :].reshape(-1),
            )
        )
        kept = forward(gathered, latents, noise, timesteps, labels, routes)
        members = backward(gathered, kept, total_tokens)
        up_slabs, down_slabs, mats_slabs, thin, grad_bias, lows, grad_cond = members
        loss_part = jnp.sum(kept.errors * kept.errors)
        grads = plain_grads(
            down_slabs, up_slabs, mats_slabs, thin, grad_bias, lows, grad_cond, labels, rows_here
        )
        outs = update_plain(grads, masters, factors, loss_part)
    return (outs[0] / total_tokens,) + tuple(outs[1:])


def solution(mesh):
    rows = P(AXES, None)
    middle_rows = P(None, AXES, None)
    row_factor = P(None, AXES)
    line = P(AXES)
    in_specs = (
        (rows, rows, line, line, rows)
        + (rows, middle_rows, middle_rows, line)
        + (row_factor, P(), row_factor, P(), row_factor, P(), line)
    )
    out_specs = (
        (P(), rows, rows, rows, row_factor, P())
        + (middle_rows, middle_rows, middle_rows, row_factor, P()) * 2
        + (line, line, line, line)
    )
    return jax.shard_map(body, mesh=mesh, in_specs=in_specs, out_specs=out_specs, check_vma=False)
```

```python
import functools
import math
from types import SimpleNamespace

import jax
import jax.numpy as jnp
from jax import lax
from jax.experimental import pallas as pl
from jax.experimental.pallas import tpu as pltpu
from jax.sharding import PartitionSpec as P

WIDE = "wide"
NARROW = "narrow"
AXES = (WIDE, NARROW)
MESH_ID = pl.DeviceIdType.MESH

D = 384
HEADS = 6
HD = 64
FF = 1536
EXPERTS = 16
SHARED = 2
PD = 16
GRID = 16
FREQ = 256
CLASSES = 1000
BLK = 256
WIDE_PIECES = 8
NARROW_PIECES = 4
PIECE = 48
ROWS = 12
LAT_ROWS = 16
LQK = "lqhd,lkhd->lhqk"
CUT = 768
LAT_COLS = 1536
PATCHES = 256


eps_norm = 1e-06
eps_fact = 1e-30
decay = 0.5
clip_level = 0.1
learn_rate = 0.5

SQRT_2_PI = math.sqrt(2.0 / math.pi)
VMEM_ROOM = 56 * 1024 * 1024
REDUCE_ROOM = 60 * 1024 * 1024


def column_widths():
    return [3 * D, D, 6 * D, D, 2 * D, EXPERTS, PD, PD, FREQ, CLASSES]


def bias_widths():
    return [3 * D, D, 6 * D, D, D, D, 2 * D]


def cut_pieces(source, widths, along):
    pieces = []
    start = 0
    for width in widths:
        pieces.append(lax.slice_in_dim(source, start, start + width, axis=along))
        start = start + width
    return pieces


def product(left, right):
    return jnp.dot(left, right, preferred_element_type=jnp.float32)


def contract(left, right, left_dim, right_dim):
    return lax.dot_general(
        left, right, (((left_dim,), (right_dim,)), ((), ())), preferred_element_type=jnp.float32
    )


def gelu_tanh(values):
    return jax.nn.gelu(values, approximate=True)


def slope_back(function, source, grad_out):
    return jax.vjp(function, source)[1](grad_out)[0]


def layer_norm(source):
    centred = source - jnp.mean(source, -1, keepdims=True)
    inv_std = lax.rsqrt(jnp.mean(centred * centred, -1, keepdims=True) + eps_norm)
    return (centred * inv_std, inv_std)


def norm_back(grad_norm, normed, inv_std):
    return inv_std * (
        grad_norm
        - jnp.mean(grad_norm, -1, keepdims=True)
        - normed * jnp.mean(grad_norm * normed, -1, keepdims=True)
    )


def linear_back(grad_out, inputs, weight):
    grad_low = grad_out.astype(jnp.bfloat16)
    return (
        contract(inputs, grad_low, 0, 0),
        contract(grad_low, weight, 1, 1),
        jnp.sum(grad_out, 0),
    )


def sincos(coords, width):
    omegas = 1.0 / 10000.0 ** (jnp.arange(width // 2, dtype=jnp.float32) / (width / 2.0))
    angles = coords[:, None] * omegas[None, :]
    return jnp.concatenate([jnp.sin(angles), jnp.cos(angles)], 1)


def positions():
    places = jnp.arange(PATCHES, dtype=jnp.int32)
    grid_row = (places // GRID).astype(jnp.float32)
    grid_col = (places % GRID).astype(jnp.float32)
    return jnp.concatenate([sincos(grid_row, D // 2), sincos(grid_col, D // 2)], 1)


def time_features(steps_f):
    half_width = FREQ // 2
    freq_rates = jnp.exp(
        -math.log(10000.0) * jnp.arange(half_width, dtype=jnp.float32) / half_width
    )
    angles = steps_f[:, None] * freq_rates[None, :]
    return jnp.concatenate([jnp.cos(angles), jnp.sin(angles)], 1)


def noise_level(steps_f):
    alpha_bar = jnp.cos((steps_f / 1000.0 + 0.008) / 1.008 * (math.pi / 2)) ** 2
    return (jnp.sqrt(alpha_bar), jnp.sqrt(1.0 - alpha_bar))


def pack_slots(routes):
    ids = jnp.arange(EXPERTS, dtype=jnp.int32)[:, None]
    named = [(routes[:, k][None, :] == ids) for k in range(2)]
    either = (named[0] | named[1]).astype(jnp.bfloat16)
    rows_here = routes.shape[0]
    place = jnp.arange(rows_here, dtype=jnp.int32)
    before = (place[:, None] < place[None, :]).astype(jnp.bfloat16)
    rank_in = product(either, before)
    counts = jnp.sum(either.astype(jnp.float32), 1).astype(jnp.int32)
    padded = (counts + 7) // 8 * 8
    starts = jnp.sum(jnp.where(ids > ids.T, padded[None, :], 0), 1)
    slots = rank_in.astype(jnp.int32) + starts[:, None]
    slot_of = jnp.stack([jnp.sum(jnp.where(member, slots, 0), 0) for member in named], 0)
    return (slot_of, jnp.stack([starts, counts], 0))


def gelu_slope(values):
    inner = SQRT_2_PI * (values + 0.044715 * values * values * values)
    bend = jnp.tanh(inner)
    return (
        0.5 * values * (1.0 + bend),
        0.5 * (1.0 + bend)
        + 0.5
        * values
        * (1.0 - bend * bend)
        * SQRT_2_PI
        * (1.0 + 3.0 * 0.044715 * values * values),
    )


def gelu_only(values):
    inner = SQRT_2_PI * (values + 0.044715 * values * values * values)
    return 0.5 * values * (1.0 + jnp.tanh(inner))


def up_columns(chunks, cut):
    return jnp.concatenate([chunks[cut // D + k] for k in range(CUT // D)], 1)


def slot_pick(slots_ref, base, rows):
    place = base + lax.broadcasted_iota(jnp.int32, (rows, slots_ref.shape[1]), 0)
    return ((slots_ref[0:1, :] == place) | (slots_ref[1:2, :] == place)).astype(jnp.bfloat16)


def routed_blocks(meta, slots_ref, x_ref, up_ref, down_ref, y_ref):
    stack_id = pl.program_id(0)
    start = meta[0, stack_id]

    def block(number, unused):
        base = pl.multiple_of(start + number * BLK, 8)
        rows = product(slot_pick(slots_ref, base, BLK), x_ref[...]).astype(jnp.bfloat16)
        total = None
        for cut in range(0, FF, CUT):
            pre_act = product(rows, up_columns(up_ref[0], cut))
            part = product(gelu_only(pre_act).astype(jnp.bfloat16), down_ref[0, cut : cut + CUT])
            total = part if total is None else total + part
        y_ref[pl.ds(base, BLK), :] = total
        return unused

    lax.fori_loop(0, (meta[1, stack_id] + BLK - 1) // BLK, block, 0)


def forward_kernel(meta, slot_at, slots_ref, x_ref, up_ref, down_ref, routed_ref, y_ref):
    routed_blocks(meta, slots_ref, x_ref, up_ref, down_ref, y_ref)

    @pl.when(pl.program_id(0) == EXPERTS - 1)
    def _():
        def group(number, unused):
            for step in range(8):
                token = number * 8 + step
                for k in range(2):
                    routed_ref[k, pl.ds(token, 1), :] = y_ref[pl.ds(slot_at[k, token], 1), :]
            return unused

        lax.fori_loop(0, x_ref.shape[0] // 8, group, 0)


def head_kernel(
    token_scale,
    meta,
    slot_at,
    slots_ref,
    x_ref,
    up_ref,
    down_ref,
    logits_ref,
    routes_ref,
    shared_ref,
    middle_ref,
    noise_ref,
    mods_ref,
    fin_ref,
    head_ref,
    pair_out,
    both_out,
    state_out,
    logits_out,
    thin_out,
    gate_out,
    fin_out,
    loss_out,
    routed_ref,
    y_ref,
):
    routed_blocks(meta, slots_ref, x_ref, up_ref, down_ref, y_ref)
    low = jnp.bfloat16

    @pl.when(pl.program_id(0) == EXPERTS - 1)
    def _():
        gate_out[...] = jnp.zeros_like(gate_out)
        fin_out[...] = jnp.zeros_like(fin_out)
        thin_out[...] = jnp.zeros_like(thin_out)
        loss_out[...] = jnp.zeros_like(loss_out)
        lane = lax.broadcasted_iota(jnp.int32, (PATCHES, 128), 1)

        def latent(lat, unused):
            base = pl.multiple_of(lat * PATCHES, PATCHES)
            span = pl.ds(base, PATCHES)

            def group(number, unused):
                for step in range(8):
                    token = number * 8 + step
                    for k in range(2):
                        routed_ref[k, pl.ds(token, 1), :] = y_ref[
                            pl.ds(slot_at[k, base + token], 1), :
                        ]
                return unused

            lax.fori_loop(0, PATCHES // 8, group, 0)
            hot = [
                (lane == routes_ref[span, k : k + 1]).astype(jnp.float32) for k in range(2)
            ]
            picked = [jnp.sum(hot[k] * logits_ref[span, :], 1, keepdims=True) for k in range(2)]
            most = jnp.maximum(picked[0], picked[1])
            powers = [jnp.exp(picked[k] - most) for k in range(2)]
            gates = [powers[k] / (powers[0] + powers[1]) for k in range(2)]
            moe_out = gates[0] * routed_ref[0] + gates[1] * routed_ref[1] + shared_ref[span, :]
            gate_moe = mods_ref[pl.ds(lat, 1), 5 * D :]
            normed, inv_std = layer_norm(middle_ref[span, :] + gate_moe * moe_out)
            scale = 1.0 + fin_ref[pl.ds(lat, 1), D:]
            head_in = (normed * scale + fin_ref[pl.ds(lat, 1), :D]).astype(low)
            errors = product(head_in, head_ref[...]) - noise_ref[span, :]
            loss_out[...] += jnp.sum(jnp.sum(errors * errors, 1, keepdims=True), 0, keepdims=True)
            errors = (errors * token_scale).astype(low)
            grads = contract(errors, head_ref[...], 1, 1)
            fin_out[pl.ds(lat, 1), :D] = jnp.sum(grads, 0, keepdims=True)
            fin_out[pl.ds(lat, 1), D:] = jnp.sum(grads * normed, 0, keepdims=True)
            state = norm_back(grads * scale, normed, inv_std)
            state_out[span, :] = state
            gate_out[pl.ds(lat, 1), :] = jnp.sum(moe_out * state, 0, keepdims=True)
            grads = gate_moe * state
            both_out[span, :] = grads.astype(low)
            slopes = []
            for k in range(2):
                slopes.append(jnp.sum(routed_ref[k] * grads, 1, keepdims=True))
                pair_out[k, span, :] = (gates[k] * grads).astype(low)
            usual = gates[0] * slopes[0] + gates[1] * slopes[1]
            grad_logits = (
                hot[0] * (gates[0] * (slopes[0] - usual)) + hot[1] * (gates[1] * (slopes[1] - usual))
            )
            logits_out[span, :] = grad_logits
            thin_out[...] += contract(x_ref[span, :], grad_logits.astype(low), 0, 0) + pltpu.roll(
                contract(head_in, errors, 0, 0), EXPERTS, 1
            )
            return unused

        lax.fori_loop(0, x_ref.shape[0] // PATCHES, latent, 0)


def experts_and_head(slot_of, meta, moe_in, up_full, down_full, token_scale, members):
    tokens = moe_in.shape[0]
    full, low = jnp.float32, jnp.bfloat16
    shapes = (
        ((2, tokens, D), low),
        ((tokens, D), low),
        ((tokens, D), full),
        ((tokens, 128), full),
        ((D, 128), full),
        ((8, D), full),
        ((8, 2 * D), full),
        ((1, 1), full),
    )
    return pl.pallas_call(
        functools.partial(head_kernel, token_scale),
        grid_spec=pltpu.PrefetchScalarGridSpec(
            num_scalar_prefetch=2,
            grid=(EXPERTS,),
            in_specs=[
                whole_block((2, tokens)),
                whole_block((tokens, D)),
                pl.BlockSpec((1, NARROW_PIECES, D, D), lambda e, *unused: (e, 0, 0, 0)),
                pl.BlockSpec((1, FF, D), lambda e, *unused: (e, 0, 0)),
            ]
            + [whole_block(member.shape) for member in members],
            out_specs=[whole_block(shape) for shape, kind in shapes],
            scratch_shapes=[
                pltpu.VMEM((2, PATCHES, D), full),
                pltpu.VMEM((slot_room(tokens), D), full),
            ],
        ),
        out_shape=[jax.ShapeDtypeStruct(shape, kind) for shape, kind in shapes],
        compiler_params=pltpu.CompilerParams(vmem_limit_bytes=VMEM_ROOM),
        name="experts_and_head",
    )(meta, slot_of, slot_of, moe_in, up_full, down_full, *members)


def slot_room(tokens):
    return tokens * 2 + EXPERTS * 8 + BLK


def whole_block(shape):
    return pl.BlockSpec(shape, lambda e, *unused: (0,) * len(shape))


def experts_forward(slot_of, meta, moe_in, up_full, down_full):
    tokens = moe_in.shape[0]
    return pl.pallas_call(
        forward_kernel,
        grid_spec=pltpu.PrefetchScalarGridSpec(
            num_scalar_prefetch=2,
            grid=(EXPERTS,),
            in_specs=[
                whole_block((2, tokens)),
                whole_block((tokens, D)),
                pl.BlockSpec((1, NARROW_PIECES, D, D), lambda e, *unused: (e, 0, 0, 0)),
                pl.BlockSpec((1, FF, D), lambda e, *unused: (e, 0, 0)),
            ],
            out_specs=whole_block((2, tokens, D)),
            scratch_shapes=[pltpu.VMEM((slot_room(tokens), D), jnp.float32)],
        ),
        out_shape=jax.ShapeDtypeStruct((2, tokens, D), jnp.float32),
        compiler_params=pltpu.CompilerParams(vmem_limit_bytes=VMEM_ROOM),
        cost_estimate=pl.CostEstimate(
            flops=20_000_000_000, bytes_accessed=50_000_000, transcendentals=0
        ),
        name="experts_forward",
    )(meta, slot_of, slot_of, moe_in, up_full, down_full)


def backward_kernel(
    meta,
    slot_at,
    slots_ref,
    x_ref,
    pair_ref,
    up_ref,
    down_ref,
    up_out,
    down_out,
    dx_ref,
    up_sum,
    down_sum,
    dx_slots,
):
    stack_id = pl.program_id(0)
    tokens = x_ref.shape[0]
    up_sum[...] = jnp.zeros_like(up_sum)
    down_sum[...] = jnp.zeros_like(down_sum)

    def expert(rows, grads):
        total = None
        for cut in range(0, FF, CUT):
            up_part = up_columns(up_ref[0], cut)
            activated, slope = gelu_slope(product(rows, up_part))
            grad_act = contract(grads, down_ref[0, cut : cut + CUT], 1, 1)
            grad_pre = (grad_act * slope).astype(jnp.bfloat16)
            down_sum[cut : cut + CUT, :] += contract(activated.astype(jnp.bfloat16), grads, 0, 0)
            up_sum[:, cut : cut + CUT] += contract(rows, grad_pre, 0, 0)
            part = contract(grad_pre, up_part, 1, 1)
            total = part if total is None else total + part
        return total

    start = meta[0, stack_id]
    stop = start + meta[1, stack_id]

    def block(number, unused):
        base = pl.multiple_of(start + number * BLK, 8)
        rows = product(slot_pick(slots_ref, base, BLK), x_ref[...]).astype(jnp.bfloat16)
        place = base + lax.broadcasted_iota(jnp.int32, (BLK, tokens), 0)
        place = jnp.where(place < stop, place, -1)
        grads = None
        for k in range(2):
            part = product((slots_ref[k : k + 1, :] == place).astype(jnp.bfloat16), pair_ref[k])
            grads = part if grads is None else grads + part
        dx_slots[pl.ds(base, BLK), :] = expert(rows, grads.astype(jnp.bfloat16))
        return unused

    lax.fori_loop(0, (meta[1, stack_id] + BLK - 1) // BLK, block, 0)
    for n in range(NARROW_PIECES):
        up_out[0, :, n] = (
            up_sum[:, n * D : (n + 1) * D]
            .astype(jnp.bfloat16)
            .reshape(WIDE_PIECES, PIECE, D)
        )
    down_out[0] = down_sum[...].astype(jnp.bfloat16).reshape(WIDE_PIECES, NARROW_PIECES, PIECE, D)

    @pl.when(stack_id == EXPERTS - 1)
    def _():
        def group(number, unused):
            for step in range(8):
                token = number * 8 + step
                dx_ref[pl.ds(token, 1), :] = (
                    dx_slots[pl.ds(slot_at[0, token], 1), :]
                    + dx_slots[pl.ds(slot_at[1, token], 1), :]
                )
            return unused

        lax.fori_loop(0, tokens // 8, group, 0)


def experts_backward(slot_of, meta, moe_in, grad_pair, up_full, down_full):
    tokens = moe_in.shape[0]
    slabs = (EXPERTS, WIDE_PIECES, NARROW_PIECES, PIECE, D)
    slab_spec = pl.BlockSpec((1,) + slabs[1:], lambda e, *unused: (e, 0, 0, 0, 0))
    return pl.pallas_call(
        backward_kernel,
        grid_spec=pltpu.PrefetchScalarGridSpec(
            num_scalar_prefetch=2,
            grid=(EXPERTS,),
            in_specs=[
                whole_block((2, tokens)),
                whole_block((tokens, D)),
                whole_block((2, tokens, D)),
                pl.BlockSpec((1, NARROW_PIECES, D, D), lambda e, *unused: (e, 0, 0, 0)),
                pl.BlockSpec((1, FF, D), lambda e, *unused: (e, 0, 0)),
            ],
            out_specs=[slab_spec, slab_spec, whole_block((tokens, D))],
            scratch_shapes=[
                pltpu.VMEM((D, FF), jnp.float32),
                pltpu.VMEM((FF, D), jnp.float32),
                pltpu.VMEM((slot_room(tokens), D), jnp.float32),
            ],
        ),
        out_shape=[
            jax.ShapeDtypeStruct(slabs, jnp.bfloat16),
            jax.ShapeDtypeStruct(slabs, jnp.bfloat16),
            jax.ShapeDtypeStruct((tokens, D), jnp.float32),
        ],
        compiler_params=pltpu.CompilerParams(vmem_limit_bytes=VMEM_ROOM),
        cost_estimate=pl.CostEstimate(
            flops=45_000_000_000, bytes_accessed=90_000_000, transcendentals=0
        ),
        name="experts_backward",
    )(meta, slot_of, slot_of, moe_in, grad_pair, up_full, down_full)


def reduce_kernel(
    down_ref,
    up_ref,
    up_all,
    down_all,
    moe_in,
    grad_both,
    dx_routed,
    grad_logits,
    middle,
    qkv,
    attended,
    grad_state,
    patches,
    places,
    mods,
    mats_all,
    bias_rows,
    pre_time,
    cond,
    freq_low,
    grad_gate,
    grad_fin,
    thin_in,
    label_parts,
    out_ref,
    rows_ref,
    lat_ref,
    bias_ref,
    own,
    got_core,
    out_one,
    keep_one,
    got_one,
    out_two,
    keep_two,
    got_two,
    got_last,
    keep_z,
    out_z,
    got_z,
    row_parts,
    late,
    up_here,
    down_here,
    up_sum,
    down_sum,
    dx_sum,
    grad_mid,
    grad_att,
    grad_qkv,
    qkv_sum,
    proj_sum,
    patch_sum,
    grad_mods,
    lat_full,
    lat_low,
    own_sem,
    core_send,
    core_recv,
    one_send,
    one_recv,
    two_send,
    two_recv,
    z_send,
    z_recv,
    row_send,
    row_recv,
    lat_own,
    lat_send,
    lat_recv,
    here_sem,
    core_free,
    one_free,
):
    full, low = jnp.float32, jnp.bfloat16
    n_down, n_up, n_late = down_ref.shape[0], up_ref.shape[0], late.shape[0]
    slabs = n_down + n_up + n_late
    ahead, ring = 2, got_core.shape[0]
    wide, narrow = lax.axis_index(WIDE), lax.axis_index(NARROW)
    z, x = wide // 2, wide % 2
    y, c = narrow // 2, narrow % 2
    x_one, y_one = x + (1 - c) * (1 - 2 * x), y + c * (1 - 2 * y)
    x_two, y_two = x + c * (1 - 2 * x), y + (1 - c) * (1 - 2 * y)
    to_one = (z * 2 + x_one, y_one * 2 + c)
    to_two = (z * 2 + x_two, y_two * 2 + c)
    first_mine = x * (1 - c) + y * c
    second_mine = y * (1 - c) + x * c
    first_step, second_step = 2 - c, 1 + c
    mates = [
        (wide, (y + (k // 2) * (1 - 2 * y)) * 2 + c + (k % 2) * (1 - 2 * c)) for k in range(1, 4)
    ]
    levels = [(((z + k) % 4) * 2 + x, narrow) for k in range(1, 4)]
    to_x, to_core = (z * 2 + 1 - x, narrow), mates[0]
    barrier = pltpu.get_barrier_semaphore()
    for target in mates + levels + [to_x]:
        pl.semaphore_signal(barrier, inc=1, device_id=target, device_id_type=MESH_ID)
    pl.semaphore_wait(barrier, 7)

    def remote(source, target, send, recv, device):
        return pltpu.make_async_remote_copy(
            src_ref=source,
            dst_ref=target,
            send_sem=send,
            recv_sem=recv,
            device_id=device,
            device_id_type=MESH_ID,
        )

    def core_copy(source, s):
        return remote(
            source.at[:, 1 - c],
            got_core.at[s % ring],
            core_send.at[s % 4],
            core_recv.at[s % ring],
            to_core,
        )

    def own_copy(source, s):
        return pltpu.make_async_copy(source.at[:, c], own.at[s % 3], own_sem.at[s % 3])

    def one_copy(s):
        return remote(
            out_one.at[s % 2], got_one.at[s % ring], one_send.at[s % 2], one_recv.at[s % ring], to_one
        )

    def two_copy(s, turned=False):
        if turned:
            start, end = out_two.at[s % 2, 0], got_last.at[s // 2]
        else:
            start, end = out_two.at[s % 2], got_two.at[s // 2]
        return remote(start, end, two_send.at[s % 2], two_recv.at[s], to_two)

    def z_copy(s, k, turned=False):
        start, end = out_z.at[s % 2, (z + k) % 4], got_z.at[s, k - 1]
        if not turned:
            start, end = start.at[0], end.at[0]
        return remote(start, end, z_send.at[s % 2, k - 1], z_recv.at[s, k - 1], levels[k - 1])

    def by_order(s, run):
        turned = s % 2 == 1

        @pl.when(turned)
        def _():
            run(True)

        @pl.when(jnp.logical_not(turned))
        def _():
            run(False)

    def row_copy(r, k):
        mate = mates[k - 1]
        return remote(
            row_parts.at[r % 2, mate[1]],
            rows_ref.at[r, narrow],
            row_send.at[r % 2, k - 1],
            row_recv.at[r, k - 1],
            mate,
        )

    def lat_level(k):
        return remote(
            lat_low, lat_ref.at[z, x, y, c], lat_send.at[k - 1], lat_recv.at[k - 1], levels[k - 1]
        )

    def lat_x():
        spot = lat_ref.at[:, x, y, c]
        return remote(spot, spot, lat_send.at[3], lat_recv.at[3], to_x)

    def lat_y():
        spot = lat_ref.at[:, :, y, c]
        return remote(spot, spot, lat_send.at[4], lat_recv.at[4], mates[1])

    def lat_core():
        spot = lat_ref.at[:, :, :, c]
        return remote(spot, spot, lat_send.at[5], lat_recv.at[5], to_core)

    def lat_own_copy():
        return pltpu.make_async_copy(lat_low, lat_ref.at[z, x, y, c], lat_own.at[0])

    def begin(source, s):
        @pl.when(s >= 4)
        def _():
            core_copy(source, s).wait_send()

        @pl.when(s >= ring)
        def _():
            pl.semaphore_wait(core_free, 1)

        core_copy(source, s).start()
        own_copy(source, s).start()

    def stage_core(s):
        own_copy(down_ref.at[0], s).wait()
        core_copy(down_ref.at[0], s).wait_recv()

        @pl.when(s >= 2)
        def _():
            one_copy(s).wait_send()

        @pl.when(s >= ring)
        def _():
            pl.semaphore_wait(one_free, 1)

        for level in range(4):
            for other in range(2):
                place = level * 2 + other
                base = level * 4 + other * second_step
                send_at = base + (1 - first_mine) * first_step
                out_one[s % 2, place] = (
                    own[s % 3, send_at].astype(full) + got_core[s % ring, send_at].astype(full)
                ).astype(low)
        one_copy(s).start()
        for level in range(4):
            for other in range(2):
                place = level * 2 + other
                base = level * 4 + other * second_step
                keep_at = base + first_mine * first_step
                keep_one[s % 3, place] = own[s % 3, keep_at].astype(full) + got_core[
                    s % ring, keep_at
                ].astype(full)

        @pl.when(s < slabs - ring)
        def _():
            pl.semaphore_signal(core_free, inc=1, device_id=to_core, device_id_type=MESH_ID)

    def stage_one(s):
        one_copy(s).wait_recv()

        def run(turned):
            @pl.when(s >= 2)
            def _():
                sent(s, turned)

            if turned:
                for level in range(4):
                    for other in range(2):
                        out_z[s % 2, level, other] = (
                            keep_one[s % 3, level * 2 + other]
                            + got_one[s % ring, level * 2 + other].astype(full)
                        ).astype(low)
                for k in range(1, 4):
                    z_copy(s, k, True).start()
                for other in range(2):
                    keep_two[s % 3, other] = keep_one[s % 3, z * 2 + other] + got_one[
                        s % ring, z * 2 + other
                    ].astype(full)
            else:
                for level in range(4):
                    send_at = level * 2 + 1 - second_mine
                    out_two[s % 2, level] = (
                        keep_one[s % 3, send_at] + got_one[s % ring, send_at].astype(full)
                    ).astype(low)
                two_copy(s).start()
                for level in range(4):
                    keep_at = level * 2 + second_mine
                    keep_two[s % 3, level] = keep_one[s % 3, keep_at] + got_one[
                        s % ring, keep_at
                    ].astype(full)

        by_order(s, run)

        @pl.when(s < slabs - ring)
        def _():
            pl.semaphore_signal(one_free, inc=1, device_id=to_one, device_id_type=MESH_ID)

    def sent(s, turned):
        if turned:
            for k in range(1, 4):
                z_copy(s, k, True).wait_send()
        else:
            two_copy(s).wait_send()

    def sent_last(s, turned):
        if turned:
            two_copy(s, True).wait_send()
        else:
            for k in range(1, 4):
                z_copy(s, k).wait_send()

    def stage_two(s):
        def run(turned):
            if turned:
                for k in range(1, 4):
                    z_copy(s, k, True).wait_recv()
            else:
                two_copy(s).wait_recv()

            @pl.when(s >= 2)
            def _():
                sent_last(s, turned)

            if turned:

                def gathered(other):
                    total = keep_two[s % 3, other]
                    for k in range(3):
                        total = total + got_z[s, k, other].astype(full)
                    return total

                out_two[s % 2, 0] = gathered(1 - second_mine).astype(low)
                two_copy(s, True).start()
                keep_z[s % 3] = gathered(second_mine)
            else:
                for level in range(4):
                    out_z[s % 2, level, 0] = (
                        keep_two[s % 3, level] + got_two[s // 2, level].astype(full)
                    ).astype(low)
                for k in range(1, 4):
                    z_copy(s, k).start()
                keep_z[s % 3] = keep_two[s % 3, z] + got_two[s // 2, z].astype(full)

        by_order(s, run)

    def direct_place(s):
        late_at = s - n_down - n_up
        return (s < n_down) | ((late_at >= 0) & (late_at < SHARED))

    def row_place(s):
        return jnp.where(s < n_down + n_up, s - n_down, s - n_down - SHARED)

    def finish(s):
        def run(turned):
            if turned:
                two_copy(s, True).wait_recv()
                keep_z[s % 3] += got_last[s // 2].astype(full)
            else:
                for k in range(1, 4):
                    z_copy(s, k).wait_recv()
                total = keep_z[s % 3]
                for k in range(3):
                    total = total + got_z[s, k, 0].astype(full)
                keep_z[s % 3] = total

        by_order(s, run)
        total = keep_z[s % 3]

        @pl.when(direct_place(s))
        def _():
            out_ref[jnp.clip(jnp.where(s < n_down, s, s - n_up), 0, n_down + SHARED - 1)] = total

        @pl.when(jnp.logical_not(direct_place(s)))
        def _():
            r = row_place(s)

            @pl.when(r >= 2)
            def _():
                for k in range(1, 4):
                    row_copy(r, k).wait_send()

            for n in range(NARROW_PIECES):
                row_parts[r % 2, n] = total[n * ROWS : (n + 1) * ROWS]
            rows_ref[r, narrow] = row_parts[r % 2, narrow]
            for k in range(1, 4):
                row_copy(r, k).start()

    def rows_in(s):
        @pl.when(jnp.logical_not(direct_place(s)))
        def _():
            for k in range(1, 4):
                row_copy(row_place(s), k).wait_recv()

    tokens = moe_in.shape[0]
    lats = tokens // PATCHES

    def matrix(number, start, stop):
        chunk = mats_all[number // 2, number % 2]
        return chunk.reshape(D, chunk.shape[-1])[:, start:stop]

    def mod_row(start, number):
        return mods[pl.ds(start // PATCHES, 1), number * D : (number + 1) * D]

    def keep_mod(start, number, values):
        grad_mods[pl.ds(start // PATCHES, 1), number * D : (number + 1) * D] = jnp.sum(
            values, 0, keepdims=True
        )

    def add_bias(number, values):
        for k in range(values.shape[1] // D):
            bias_ref[number + k : number + k + 1, :] += jnp.sum(
                values[:, k * D : (k + 1) * D], 0, keepdims=True
            )

    def prepare():
        bias_ref[...] = jnp.zeros_like(bias_ref)
        qkv_sum[...] = jnp.zeros_like(qkv_sum)
        proj_sum[...] = jnp.zeros_like(proj_sum)
        patch_sum[...] = jnp.zeros_like(patch_sum)
        grad_mods[...] = jnp.zeros_like(grad_mods)

    def fetch(shared_id):
        e = EXPERTS + shared_id
        first = pltpu.make_async_copy(down_all.at[e], down_here, here_sem.at[0])
        second = pltpu.make_async_copy(up_all.at[e], up_here, here_sem.at[1])
        first.start()
        second.start()
        first.wait()
        second.wait()
        up_sum[...] = jnp.zeros_like(up_sum)
        down_sum[...] = jnp.zeros_like(down_sum)

    def shared_block(shared_id, start):
        span = pl.ds(start, PATCHES)
        rows, grads = moe_in[span, :], grad_both[span, :]
        total = dx_routed[span, :] if shared_id == 0 else dx_sum[span, :]
        for cut in range(0, FF, CUT):
            up_part = up_columns(up_here, cut)
            activated, slope = gelu_slope(product(rows, up_part))
            grad_act = contract(grads, down_here[cut : cut + CUT], 1, 1)
            grad_pre = (grad_act * slope).astype(low)
            down_sum[cut : cut + CUT, :] += contract(activated.astype(low), grads, 0, 0)
            up_sum[:, cut : cut + CUT] += contract(rows, grad_pre, 0, 0)
            total = total + contract(grad_pre, up_part, 1, 1)
        dx_sum[span, :] = total

    def shared_slabs(shared_id):
        for w in range(WIDE_PIECES):
            for n in range(NARROW_PIECES):
                at = (w * NARROW_PIECES + n) * PIECE
                late[shared_id, w * 2 + n // 2, n % 2] = down_sum[at : at + PIECE, :].astype(low)
                late[SHARED + shared_id, w * 2 + n // 2, n % 2] = up_sum[
                    w * PIECE : (w + 1) * PIECE, n * D : (n + 1) * D
                ].astype(low)

    def back_out(start):
        span = pl.ds(start, PATCHES)
        grads = dx_sum[span, :] + contract(
            grad_logits[span, :].astype(low), matrix(0, 4 * D, 4 * D + 128), 1, 1
        )
        normed, inv_std = layer_norm(middle[span, :])
        keep_mod(start, 3, grads)
        keep_mod(start, 4, grads * normed)
        grads = grad_state[span, :] + norm_back(
            grads * (1.0 + mod_row(start, 4)), normed, inv_std
        )
        grad_mid[...] = grads
        proj = matrix(0, 3 * D, 4 * D)
        rows = attended[span, :]
        keep_mod(start, 2, (product(rows, proj) + bias_rows[3:4, :]) * grads)
        grads = grads * mod_row(start, 2)
        add_bias(3, grads)
        grads = grads.astype(low)
        proj_sum[...] += contract(rows, grads, 0, 0)
        grad_att[...] = contract(grads, proj, 1, 1).astype(low)

    def back_pair(pair, start):
        span = pl.ds(start, PATCHES)
        lane = lax.broadcasted_iota(jnp.int32, (PATCHES, 2 * HD), 1)
        at = pair * 2 * HD
        queries = qkv[span, at : at + 2 * HD]
        keys = qkv[span, D + at : D + at + 2 * HD]
        values = qkv[span, 2 * D + at : 2 * D + at + 2 * HD]
        grads = grad_att[:, at : at + 2 * HD]
        sums = None
        for half in range(2):
            mine = (lane < HD) if half == 0 else (lane >= HD)
            scores = contract(jnp.where(mine, queries, 0), keys, 1, 1) * HD ** (-0.5)
            powers = jnp.exp(scores - jnp.max(scores, 1, keepdims=True))
            probs = powers / jnp.sum(powers, 1, keepdims=True)
            grad_mine = jnp.where(mine, grads, 0)
            grad_probs = contract(grad_mine, values, 1, 1)
            grad_scores = (
                probs
                * (grad_probs - jnp.sum(probs * grad_probs, 1, keepdims=True))
                * HD ** (-0.5)
            ).astype(low)
            parts = (
                product(grad_scores, jnp.where(mine, keys, 0)),
                contract(grad_scores, jnp.where(mine, queries, 0), 0, 0),
                contract(probs.astype(low), grad_mine, 0, 0),
            )
            sums = parts if sums is None else [a + b for a, b in zip(sums, parts)]
        for k in range(3):
            where = k * D + at
            grad_qkv[:, where : where + 2 * HD] = sums[k].astype(low)
            bias_ref[k : k + 1, at : at + 2 * HD] += jnp.sum(sums[k], 0, keepdims=True)

    def back_in(start):
        span = pl.ds(start, PATCHES)
        emb = contract(patches[span, :], matrix(2, 4 * D, 4 * D + 128), 1, 1)
        emb = emb + bias_rows[10:11, :] + places[...]
        normed, inv_std = layer_norm(emb)
        rows = (normed * (1.0 + mod_row(start, 1)) + mod_row(start, 0)).astype(low)
        qkv_sum[...] += contract(rows, grad_qkv[...], 0, 0)
        grads = contract(grad_qkv[...], matrix(0, 0, 3 * D), 1, 1)
        keep_mod(start, 0, grads)
        keep_mod(start, 1, grads * normed)
        grads = grad_mid[...] + norm_back(grads * (1.0 + mod_row(start, 1)), normed, inv_std)
        add_bias(10, grads)
        patch_sum[...] += contract(grads.astype(low), patches[span, :], 0, 0)

    def silu_slope(values):
        gate = jax.nn.sigmoid(values)
        return gate + values * gate * (1.0 - gate)

    def back_conditions():
        grad_mods[:, 5 * D :] = grad_gate[...]
        grads = grad_mods[...]
        mod_low, fin_low = grads.astype(low), grad_fin[...].astype(low)
        grad_act = (
            contract(mod_low[:, : 4 * D], matrix(1, 0, 4 * D), 1, 1)
            + contract(mod_low[:, 4 * D :], matrix(2, 0, 2 * D), 1, 1)
            + contract(fin_low, matrix(2, 2 * D, 4 * D), 1, 1)
        )
        grad_cond = silu_slope(cond[...]) * grad_act
        high = grad_cond.astype(low)
        grad_time = silu_slope(pre_time[...]) * contract(high, matrix(3, 1024, 1408), 1, 1)
        add_bias(4, grads)
        add_bias(11, grad_time)
        add_bias(12, grad_cond)
        add_bias(13, grad_fin[...])
        high = high.astype(full)
        rest = grad_cond - high
        middle_part = rest.astype(low).astype(full)
        act = jax.nn.silu(cond[...]).astype(low).astype(full)
        hid = jax.nn.silu(pre_time[...]).astype(low).astype(full)
        mod_low, fin_low = mod_low.astype(full), fin_low.astype(full)
        quarters = (
            jnp.concatenate([act, hid, mod_low[:, : 2 * D]], 1),
            mod_low[:, 2 * D :],
            jnp.concatenate([fin_low, high, grad_time.astype(low).astype(full)], 1),
            jnp.concatenate(
                [
                    freq_low[...].astype(full),
                    middle_part,
                    rest - middle_part,
                    label_parts[...].astype(full),
                    jnp.zeros((8, D), full),
                ],
                1,
            ),
        )
        for lat in range(lats):
            for k in range(4):
                lat_full[lat * 4 + k : lat * 4 + k + 1, :] = quarters[k][lat : lat + 1, :]
        lat_low[...] = lat_full[...].astype(low)

    def last_slabs():
        for w in range(WIDE_PIECES):
            span = slice(w * PIECE, (w + 1) * PIECE)
            for n in range(3):
                late[2 * SHARED, w * 2 + n // 2, n % 2] = qkv_sum[
                    span, n * D : (n + 1) * D
                ].astype(low)
            late[2 * SHARED, w * 2 + 1, 1] = proj_sum[span, :].astype(low)
            thin = thin_in[span, :] + pltpu.roll(patch_sum[span, :], EXPERTS + PD, 1)
            for n in range(NARROW_PIECES):
                late[2 * SHARED + 1, w * 2 + n // 2, n % 2] = jnp.zeros((PIECE, D), low)
            late[2 * SHARED + 1, w * 2, 0, :, :128] = thin.astype(low)

    first_lat = SHARED * lats
    units = (
        back_out,
        lambda start: back_pair(0, start),
        lambda start: back_pair(1, start),
        lambda start: back_pair(2, start),
        back_in,
    )
    after = first_lat + len(units) * lats

    def tick(t, unused):
        first = 0
        for source, count in ((down_ref, n_down), (up_ref, n_up), (late, n_late)):

            @pl.when((t >= first) & (t < first + count))
            def _():
                begin(source.at[jnp.clip(t - first, 0, count - 1)], t)

            first += count

        for lag, stage in enumerate((stage_core, stage_one, stage_two, finish, rows_in)):
            s = t - ahead - 2 * lag

            @pl.when((s >= 0) & (s < slabs))
            def _():
                stage(s)

        @pl.when(t == 0)
        def _():
            prepare()

        for shared_id in range(SHARED):
            start_at = shared_id * lats

            @pl.when(t == start_at)
            def _():
                fetch(shared_id)

            @pl.when((t >= start_at) & (t < start_at + lats))
            def _():
                shared_block(
                    shared_id,
                    pl.multiple_of(jnp.clip(t - start_at, 0, lats - 1) * PATCHES, PATCHES),
                )

            @pl.when(t == start_at + lats - 1)
            def _():
                shared_slabs(shared_id)

        for number, unit in enumerate(units):

            @pl.when((t >= first_lat) & (t < after) & ((t - first_lat) % len(units) == number))
            def _():
                lat = jnp.clip((t - first_lat) // len(units), 0, lats - 1)
                unit(pl.multiple_of(lat * PATCHES, PATCHES))

        @pl.when(t == after)
        def _():
            back_conditions()
            lat_own_copy().start()
            for k in range(1, 4):
                lat_level(k).start()
            lat_own_copy().wait()

        @pl.when(t == after + 1)
        def _():
            last_slabs()

        @pl.when(t == after + 3)
        def _():
            for k in range(1, 4):
                lat_level(k).wait_recv()
            lat_x().start()

        @pl.when(t == after + 5)
        def _():
            lat_x().wait_recv()
            lat_y().start()

        @pl.when(t == after + 7)
        def _():
            lat_y().wait_recv()
            lat_core().start()

        return unused

    lax.fori_loop(0, slabs + ahead + 8, tick, 0)
    for back in range(4):
        core_copy(down_ref.at[0], slabs - 1 - back).wait_send()
    turned = rows_ref.shape[0]
    for back in range(2):
        s = slabs - 1 - back
        one_copy(s).wait_send()
        sent(s, s % 2 == 1)
        sent_last(s, s % 2 == 1)
        for k in range(1, 4):
            row_copy(turned - 1 - back, k).wait_send()
    for k in range(1, 4):
        lat_level(k).wait_send()
    lat_x().wait_send()
    lat_y().wait_send()
    lat_core().wait()


def reduce_slabs(down_slabs, up_slabs, up_all, down_all, members):
    n_late = 2 * SHARED + 2
    routed = down_slabs.shape[0]
    slabs = 2 * routed + n_late
    direct, turned = routed + SHARED, routed + SHARED + 2
    ring = 4
    low, full = jnp.bfloat16, jnp.float32
    sources = [
        member.reshape(routed, WIDE_PIECES * NARROW_PIECES // 2, 2, PIECE, D)
        for member in (down_slabs, up_slabs)
    ]
    tokens = members[0].shape[0]
    dma, regular = pltpu.SemaphoreType.DMA, pltpu.SemaphoreType.REGULAR
    vmem, anywhere = pl.BlockSpec(memory_space=pltpu.VMEM), pl.BlockSpec(memory_space=pl.ANY)
    sums, rows, lats, bias_sum = pl.pallas_call(
        reduce_kernel,
        out_shape=[
            jax.ShapeDtypeStruct((direct, PIECE, D), full),
            jax.ShapeDtypeStruct((turned, NARROW_PIECES, ROWS, D), full),
            jax.ShapeDtypeStruct((4, 2, 2, 2, LAT_ROWS, LAT_COLS), low),
            jax.ShapeDtypeStruct((16, D), full),
        ],
        in_specs=[anywhere] * 4 + [vmem] * len(members),
        out_specs=[vmem, vmem, anywhere, vmem],
        scratch_shapes=[
            pltpu.VMEM((3, 16, PIECE, D), low),
            pltpu.VMEM((ring, 16, PIECE, D), low),
            pltpu.VMEM((2, 8, PIECE, D), low),
            pltpu.VMEM((3, 8, PIECE, D), full),
            pltpu.VMEM((ring, 8, PIECE, D), low),
            pltpu.VMEM((2, 4, PIECE, D), low),
            pltpu.VMEM((3, 4, PIECE, D), full),
            pltpu.VMEM(((slabs + 1) // 2, 4, PIECE, D), low),
            pltpu.VMEM(((slabs + 1) // 2, PIECE, D), low),
            pltpu.VMEM((3, PIECE, D), full),
            pltpu.VMEM((2, 4, 2, PIECE, D), low),
            pltpu.VMEM((slabs, 3, 2, PIECE, D), low),
            pltpu.VMEM((2, NARROW_PIECES, ROWS, D), full),
            pltpu.VMEM((n_late, 16, 2, PIECE, D), low),
            pltpu.VMEM((NARROW_PIECES, D, D), low),
            pltpu.VMEM((FF, D), low),
            pltpu.VMEM((D, FF), full),
            pltpu.VMEM((FF, D), full),
            pltpu.VMEM((tokens, D), full),
            pltpu.VMEM((PATCHES, D), full),
            pltpu.VMEM((PATCHES, D), low),
            pltpu.VMEM((PATCHES, 3 * D), low),
            pltpu.VMEM((D, 3 * D), full),
            pltpu.VMEM((D, D), full),
            pltpu.VMEM((D, 128), full),
            pltpu.VMEM((8, 6 * D), full),
            pltpu.VMEM((LAT_ROWS, LAT_COLS), full),
            pltpu.VMEM((LAT_ROWS, LAT_COLS), low),
            dma((3,)),
            dma((4,)),
            dma((ring,)),
            dma((2,)),
            dma((ring,)),
            dma((2,)),
            dma((slabs,)),
            dma((2, 3)),
            dma((slabs, 3)),
            dma((2, 3)),
            dma((turned, 3)),
            dma((1,)),
            dma((6,)),
            dma((6,)),
            dma((2,)),
            regular,
            regular,
        ],
        compiler_params=pltpu.CompilerParams(
            collective_id=0, has_side_effects=True, vmem_limit_bytes=REDUCE_ROOM
        ),
        name="reduce_slabs",
    )(*sources, up_all, down_all, *members)
    return sums, rows, lats.reshape(-1, LAT_COLS), bias_sum


def plain_grads(
    down_slabs, up_slabs, mats_slabs, thin, grad_bias, lows, grad_cond, labels, row_count
):
    def scattered(member):
        return lax.psum_scatter(member, AXES, scatter_dimension=1, tiled=True)

    proj_grad = scattered(mats_slabs)
    row_start = lax.axis_index(AXES) * row_count
    thin_grad = lax.psum_scatter(thin, AXES, scatter_dimension=0, tiled=True)
    bias_grad = lax.psum_scatter(grad_bias, AXES, scatter_dimension=0, tiled=True)
    grad_mod, grad_time2, grad_fin, grad_time1, grad_table = latent_grads(
        lows, grad_cond, labels, row_start, row_count
    )
    mats_grad = jnp.concatenate(
        [proj_grad[0], grad_mod, grad_time2, grad_fin, thin_grad, grad_time1, grad_table], 1
    )
    return (mats_grad, scattered(up_slabs), scattered(down_slabs), bias_grad)


def spread(value, place):
    lane = lax.broadcasted_iota(jnp.int32, (1, 128), 1)
    return jnp.where(lane == place, value, 0.0)


def pick(row, place):
    lane = lax.broadcasted_iota(jnp.int32, (1, 128), 1)
    return jnp.sum(jnp.where(lane == place, row, 0.0), 1, keepdims=True)


def total(values):
    return jnp.sum(jnp.sum(values, 1, keepdims=True), 0, keepdims=True)


def turn_line(values):
    count = max(values.shape)
    same = lax.broadcasted_iota(jnp.int32, (count, count), 0) == lax.broadcasted_iota(
        jnp.int32, (count, count), 1
    )
    across = 1 if values.shape[0] == 1 else 0
    return jnp.sum(jnp.where(same, values, 0.0), across, keepdims=True)


def joined(chunks):
    return jnp.concatenate([chunks[j] for j in range(NARROW_PIECES)], 1)


def by_piece(values, start_last, width_last):
    bounds = [sum(column_widths()[:k]) for k in range(len(column_widths()) + 1)]
    last_lane = lax.broadcasted_iota(jnp.int32, (ROWS, width_last), 1) + start_last
    chosen_value = values[0]
    for k in range(6, len(column_widths())):
        chosen_value = jnp.where(last_lane >= bounds[k], values[k - 5], chosen_value)
    return chosen_value


def factored(grad, row, col, mean):
    return grad * lax.rsqrt(row * col / mean)


def update_kernel(
    sums_ref,
    rows_ref,
    lat_ref,
    bias_sum,
    loss_ref,
    mats_row,
    mats_col,
    up_row,
    up_col,
    down_row,
    down_col,
    bias_state,
    mats_grad,
    mats_row_new,
    mats_col_new,
    up_row_new,
    up_col_new,
    down_row_new,
    down_col_new,
    bias_grad,
    bias_state_new,
    line_out,
    squares_out,
    part,
    got_plane,
    mine,
    got_level,
    column,
    result,
    squares_plane,
    squares_level,
    sems,
):
    full, low = jnp.float32, jnp.bfloat16
    wide, narrow = lax.axis_index(WIDE), lax.axis_index(NARROW)
    z, spot = wide // 2, (wide % 2) * 4 + narrow

    def plane_device(k):
        there = (spot + k) % 8
        return (z * 2 + there // 4, there % 4)

    def level_device(k):
        return (((z + k) % 4) * 2 + wide % 2, narrow)

    barrier = pltpu.get_barrier_semaphore()
    for k in range(1, 8):
        pl.semaphore_signal(barrier, inc=1, device_id=plane_device(k), device_id_type=MESH_ID)
    for k in range(1, 4):
        pl.semaphore_signal(barrier, inc=1, device_id=level_device(k), device_id_type=MESH_ID)
    pl.semaphore_wait(barrier, 10)

    def remote(source, target, phase, k, device):
        return pltpu.make_async_remote_copy(
            src_ref=source,
            dst_ref=target,
            send_sem=sems.at[0, phase, k],
            recv_sem=sems.at[1, phase, k],
            device_id=device,
            device_id_type=MESH_ID,
        )

    def exchange(copies):
        for copy in copies:
            copy.start()
        for copy in copies:
            copy.wait()

    count = lat_ref.shape[0] // 4
    order = lax.broadcasted_iota(jnp.int32, (count, count * 4), 0) * 4
    place = lax.broadcasted_iota(jnp.int32, (count, count * 4), 1)
    quarters = [
        product((place == order + k).astype(low), lat_ref[...]).astype(low) for k in range(4)
    ]
    owner_row = (wide * NARROW_PIECES + narrow) * ROWS
    chosen = (
        lax.broadcasted_iota(jnp.int32, (16, D), 1)
        == lax.broadcasted_iota(jnp.int32, (16, D), 0) + owner_row
    ).astype(low)

    def rows_of(member):
        return contract(chosen, member, 1, 1).astype(low)

    act_rows = rows_of(quarters[0][:, :D])
    hid_rows = rows_of(quarters[0][:, D : 2 * D])
    high = quarters[2][:, 2 * D : 3 * D]
    for j in range(NARROW_PIECES):
        mats_grad[:, j * D : (j + 1) * D] = rows_ref[EXPERTS + SHARED, j]
    mats_grad[:, 4 * D : 6 * D] = product(act_rows, quarters[0][:, 2 * D :])[:ROWS]
    mats_grad[:, 6 * D : 10 * D] = product(act_rows, quarters[1])[:ROWS]
    mats_grad[:, 10 * D : 11 * D] = product(hid_rows, high)[:ROWS]
    mats_grad[:, 11 * D : 13 * D] = product(act_rows, quarters[2][:, : 2 * D])[:ROWS]
    time_rows = rows_of(quarters[2][:, 3 * D :])
    time_one = product(time_rows, quarters[3][:, :FREQ])
    label_at = FREQ + 2 * D
    labels = quarters[3][:, label_at : label_at + 128].astype(full)
    label = labels[:, 0:1] * 32.0 + labels[:, 1:2]
    label_hot = (
        lax.broadcasted_iota(jnp.int32, (count, 1024), 1).astype(full) == label
    ).astype(low)
    table = (
        product(rows_of(high), label_hot)
        + product(rows_of(quarters[3][:, FREQ : FREQ + D]), label_hot)
        + product(rows_of(quarters[3][:, FREQ + D : FREQ + 2 * D]), label_hot)
    )
    start_last = 13 * D
    width_last = mats_grad.shape[1] - start_last
    room = 11 * 128
    thin = jnp.concatenate(
        [rows_ref[EXPERTS + SHARED + 1, 0][:, :128], jnp.zeros((4, 128), full)], 0
    )
    thin = jnp.where(
        lax.broadcasted_iota(jnp.int32, (16, 128), 1) < EXPERTS + 2 * PD, thin, 0.0
    )

    def padded(member):
        return jnp.concatenate(
            [member, jnp.zeros((16, room - member.shape[1]), full)], 1
        )

    last = (
        padded(thin)
        + pltpu.roll(padded(time_one), EXPERTS + 2 * PD, 1)
        + pltpu.roll(padded(table), EXPERTS + 2 * PD + FREQ, 1)
    )
    mats_grad[:, start_last:] = last[:ROWS, :width_last]

    part[...] = jnp.zeros_like(part)
    widths = column_widths()
    mats_at, line_at, bias_at = 360, 416, 432
    total_cols = mats_grad.shape[1]
    cuts = [(at, min(at + 128, total_cols)) for at in range(0, total_cols, 128)]
    for number, (begin, end) in enumerate(cuts):
        values = mats_grad[:, begin:end]
        part[mats_at + number : mats_at + number + 1, : end - begin] = jnp.sum(
            values * values + eps_fact, 0, keepdims=True
        )
    bounds = [sum(widths[:k]) for k in range(len(widths) + 1)]
    last_lane = lax.broadcasted_iota(jnp.int32, (ROWS, width_last), 1) + start_last
    last_sq = mats_grad[:, start_last:] * mats_grad[:, start_last:] + eps_fact
    line = spread(loss_ref[...], 46)
    for k in range(len(widths)):
        if k < 5:
            values = mats_grad[:, bounds[k] : bounds[k + 1]]
            sq = values * values + eps_fact
        else:
            sq = jnp.where((last_lane >= bounds[k]) & (last_lane < bounds[k + 1]), last_sq, 0.0)
        new = decay * turn_line(mats_row[k : k + 1, :]) + (1.0 - decay) * (
            jnp.sum(sq, 1, keepdims=True) / widths[k]
        )
        mats_row_new[k : k + 1, :] = turn_line(new)
        line = line + spread(jnp.sum(new, 0, keepdims=True), k)

    def begin_up(e, line):
        values = joined(rows_ref[e])
        sq = values * values + eps_fact
        new = decay * turn_line(up_row[pl.ds(e, 1), :]) + (1.0 - decay) * (jnp.sum(sq, 1, keepdims=True) / FF)
        up_row_new[pl.ds(e, 1), :] = turn_line(new)
        cols = jnp.sum(sq, 0, keepdims=True)
        for k in range(FF // 128):
            part[pl.ds(24 * k + e, 1), :] = cols[:, 128 * k : 128 * (k + 1)]
        return line + spread(jnp.sum(new, 0, keepdims=True), 10 + e)

    def begin_down(e, line):
        values = sums_ref[e]
        sq = values * values + eps_fact
        new = decay * turn_line(down_row[pl.ds(e, 1), :]) + (1.0 - decay) * (jnp.sum(sq, 1, keepdims=True) / D)
        down_row_new[pl.ds(e, 1), :] = turn_line(new)
        cols = jnp.sum(sq, 0, keepdims=True)
        for k in range(D // 128):
            part[pl.ds(24 * (12 + k) + e, 1), :] = cols[:, 128 * k : 128 * (k + 1)]
        return line + spread(jnp.sum(new, 0, keepdims=True), 28 + e)

    line = lax.fori_loop(0, EXPERTS + SHARED, begin_up, line)
    line = lax.fori_loop(0, EXPERTS + SHARED, begin_down, line)
    part[line_at : line_at + 1, :] = line
    for k in range(D // 128):
        part[bias_at + 16 * k : bias_at + 16 * (k + 1), :] = bias_sum[:, 128 * k : 128 * (k + 1)]

    exchange(
        [
            remote(
                part.at[pl.ds(((spot + k) % 8) * 64, 64)], got_plane.at[k], 0, k, plane_device(k)
            )
            for k in range(1, 8)
        ]
    )
    here = part[pl.ds(pl.multiple_of(spot * 64, 64), 64), :]
    for k in range(1, 8):
        here = here + got_plane[k]
    mine[...] = here.reshape(4, 16, 128)
    exchange(
        [
            remote(mine.at[(z + k) % 4], got_level.at[k], 1, k, level_device(k))
            for k in range(1, 4)
        ]
    )
    column[z] = mine[z] + got_level[1] + got_level[2] + got_level[3]
    exchange(
        [remote(column.at[z], column.at[z], 2, k, level_device(k)) for k in range(1, 4)]
    )
    result[spot] = column[...]
    exchange(
        [remote(result.at[spot], result.at[spot], 3, k, plane_device(k)) for k in range(1, 8)]
    )

    def sums_row(row, width=128):
        if isinstance(row, int):
            return result[row // 64, (row // 16) % 4, row % 16 : row % 16 + 1, :width]
        return result[row // 64, (row // 16) % 4, pl.ds(row % 16, 1), :width]

    line = sums_row(line_at)
    line_out[...] = line
    room = bias_grad.shape[1]
    begin = (wide * NARROW_PIECES + narrow) * room
    parts = []
    for k in range(3):
        block = jnp.minimum(begin // 128 + k, 47)
        parts.append(sums_row(bias_at + (block % 3) * 16 + block // 3))
    parts = jnp.broadcast_to(jnp.concatenate(parts, 1), (8, D))
    bias_grad[...] = pltpu.roll(parts, (D - begin % 128) % D, 1)[0:1, :room]
    for number, (begin, end) in enumerate(cuts):
        mats_col_new[:, begin:end] = decay * mats_col[:, begin:end] + (1.0 - decay) * (
            sums_row(mats_at + number, end - begin) / D
        )

    squares = jnp.zeros((1, 128), full)
    for k in range(5):
        begin, end = bounds[k], bounds[k + 1]
        step = factored(
            mats_grad[:, begin:end],
            turn_line(mats_row_new[k : k + 1, :]),
            mats_col_new[:, begin:end],
            pick(line, k) / D,
        )
        squares = squares + spread(total(step * step), k)
    last = range(5, len(widths))
    step_last = factored(
        mats_grad[:, start_last:],
        by_piece([turn_line(mats_row_new[k : k + 1, :]) for k in last], start_last, width_last),
        mats_col_new[:, start_last:],
        by_piece([pick(line, k) / D for k in last], start_last, width_last),
    )
    for k in last:
        inside = (last_lane >= bounds[k]) & (last_lane < bounds[k + 1])
        squares = squares + spread(total(jnp.where(inside, step_last * step_last, 0.0)), k)

    def step_up(e, squares):
        cols = jnp.concatenate([sums_row(24 * k + e) for k in range(FF // 128)], 1)
        new = decay * up_col[pl.ds(e, 1), :] + (1.0 - decay) * (cols / D)
        up_col_new[pl.ds(e, 1), :] = new
        row = turn_line(up_row_new[pl.ds(e, 1), :])
        step = factored(joined(rows_ref[e]), row, new, pick(line, 10 + e) / D)
        return squares + spread(total(step * step), 10 + e)

    def step_down(e, squares):
        cols = jnp.concatenate([sums_row(24 * (12 + k) + e) for k in range(D // 128)], 1)
        new = decay * down_col[pl.ds(e, 1), :] + (1.0 - decay) * (cols / FF)
        down_col_new[pl.ds(e, 1), :] = new
        row = turn_line(down_row_new[pl.ds(e, 1), :])
        step = factored(sums_ref[e], row, new, pick(line, 28 + e) / FF)
        return squares + spread(total(step * step), 28 + e)

    squares = lax.fori_loop(0, EXPERTS + SHARED, step_up, squares)
    squares = lax.fori_loop(0, EXPERTS + SHARED, step_down, squares)
    state = decay * bias_state[...] + (1.0 - decay) * (
        bias_grad[...] * bias_grad[...] + eps_fact
    )
    bias_state_new[...] = state
    bias_step = bias_grad[...] * lax.rsqrt(state)
    squares = squares + spread(total(bias_step * bias_step), 46)
    squares_plane[spot] = jnp.broadcast_to(squares, (8, 128))
    exchange(
        [
            remote(squares_plane.at[spot], squares_plane.at[spot], 4, k, plane_device(k))
            for k in range(1, 8)
        ]
    )
    squares_level[z] = jnp.sum(squares_plane[...], 0)
    exchange(
        [
            remote(squares_level.at[z], squares_level.at[z], 5, k, level_device(k))
            for k in range(1, 4)
        ]
    )
    squares_out[...] = jnp.sum(squares_level[...], 0)[0:1]


def settle_kernel(
    total_tokens,
    sums_ref,
    rows_ref,
    up_ref,
    down_ref,
    mats_ref,
    bias_ref,
    mats_grad,
    mats_row,
    mats_col,
    up_row,
    up_col,
    down_row,
    down_col,
    bias_grad,
    bias_state,
    line_ref,
    squares_ref,
    loss_out,
    mats_grad_out,
    mats_new,
    mats_copy,
    mats_row_out,
    mats_col_out,
    up_grad,
    up_new,
    up_copy,
    up_row_out,
    up_col_out,
    down_grad,
    down_new,
    down_copy,
    down_row_out,
    down_col_out,
    bias_grad_out,
    bias_new,
    bias_copy,
    bias_state_out,
):
    line, squares = line_ref[...], squares_ref[...]
    low = jnp.bfloat16
    group = up_ref.shape[0]

    def clipped(place, entries):
        rms = jnp.sqrt(pick(squares, place) / entries)
        return jnp.maximum(1.0, rms / clip_level)

    def settle(new_ref, copy_ref, index, master, step, limit):
        value = master - learn_rate * (step / limit)
        new_ref[index] = value
        copy_ref[index] = value.astype(low)

    for i in range(group):
        e = pl.program_id(0) * group + i
        grad = joined(rows_ref[i])
        up_grad[i] = grad
        step = factored(
            grad,
            turn_line(up_row[pl.ds(e, 1), :]),
            up_col[pl.ds(e, 1), :],
            pick(line, 10 + e) / D,
        )
        settle(up_new, up_copy, i, up_ref[i], step, clipped(10 + e, D * FF))
        grad = sums_ref[i]
        down_grad[i] = grad
        step = factored(
            grad,
            turn_line(down_row[pl.ds(e, 1), :]),
            down_col[pl.ds(e, 1), :],
            pick(line, 28 + e) / FF,
        )
        settle(down_new, down_copy, i, down_ref[i], step, clipped(28 + e, D * FF))

    @pl.when(pl.program_id(0) == 0)
    def _():
        widths = column_widths()
        bounds = [sum(widths[:k]) for k in range(len(widths) + 1)]
        start_last = bounds[5]
        width_last = bounds[-1] - start_last
        loss_out[...] = pick(line, 46) / total_tokens
        for given, out in (
            (mats_grad, mats_grad_out),
            (mats_row, mats_row_out),
            (mats_col, mats_col_out),
            (up_row, up_row_out),
            (up_col, up_col_out),
            (down_row, down_row_out),
            (down_col, down_col_out),
            (bias_grad, bias_grad_out),
            (bias_state, bias_state_out),
        ):
            out[...] = given[...]
        for k in range(6):
            if k < 5:
                index = (slice(None), slice(bounds[k], bounds[k + 1]))
                row, mean = turn_line(mats_row[k : k + 1, :]), pick(line, k) / D
                limit = clipped(k, D * widths[k])
            else:
                last = range(5, len(widths))
                index = (slice(None), slice(start_last, None))
                row, mean, limit = [
                    by_piece(values, start_last, width_last)
                    for values in (
                        [turn_line(mats_row[j : j + 1, :]) for j in last],
                        [pick(line, j) / D for j in last],
                        [clipped(j, D * widths[j]) for j in last],
                    )
                ]
            step = factored(mats_grad[index], row, mats_col[index], mean)
            settle(mats_new, mats_copy, index, mats_ref[index], step, limit)
        index = (slice(None), slice(None))
        step = bias_grad[...] * lax.rsqrt(bias_state[...])
        settle(bias_new, bias_copy, index, bias_ref[...], step, clipped(46, 15 * D))


def update_kernel_call(sums, rows, lat, bias_sum, masters, factors, loss_part, total_tokens):
    mats, up_weights, down_weights, biases = masters
    mats_row, mats_col, up_row, up_col, down_row, down_col, bias_state = factors
    full, low = jnp.float32, jnp.bfloat16
    mats_col, bias_state, biases = [
        member.reshape(1, -1) for member in (mats_col, bias_state, biases)
    ]

    def like(member, kind=full):
        return jax.ShapeDtypeStruct(member.shape, kind)

    row = jax.ShapeDtypeStruct((1, 128), full)
    rows_like = [mats_row, mats_col, up_row, up_col, down_row, down_col, bias_state, bias_state]
    vmem = pl.BlockSpec(memory_space=pltpu.VMEM)
    dma = pltpu.SemaphoreType.DMA
    found = pl.pallas_call(
        update_kernel,
        out_shape=[like(member) for member in [mats] + rows_like] + [row, row],
        in_specs=[vmem] * 12,
        out_specs=[vmem] * 11,
        scratch_shapes=[
            pltpu.VMEM((512, 128), full),
            pltpu.VMEM((8, 64, 128), full),
            pltpu.VMEM((4, 16, 128), full),
            pltpu.VMEM((4, 16, 128), full),
            pltpu.VMEM((4, 16, 128), full),
            pltpu.VMEM((8, 4, 16, 128), full),
            pltpu.VMEM((8, 8, 128), full),
            pltpu.VMEM((4, 8, 128), full),
            dma((2, 6, 8)),
        ],
        compiler_params=pltpu.CompilerParams(
            collective_id=1, has_side_effects=True, vmem_limit_bytes=VMEM_ROOM
        ),
        name="update",
    )(
        sums,
        rows,
        lat,
        bias_sum,
        loss_part.reshape(1, 1),
        mats_row,
        mats_col,
        up_row,
        up_col,
        down_row,
        down_col,
        bias_state,
    )
    group = 3
    wholes = [biases] + list(found)

    def whole(member):
        return pl.BlockSpec(member.shape, lambda g: (0,) * len(member.shape))

    def parts(member):
        rest = member.shape[1:]
        return pl.BlockSpec((group,) + rest, lambda g: (g,) + (0,) * len(rest))

    one = jax.ShapeDtypeStruct((1, 1), full)
    outs = (
        [(one, whole(one))]
        + [(like(mats, kind), whole(mats)) for kind in (full, full, low)]
        + [(like(member), whole(member)) for member in (mats_row, mats_col)]
        + [(like(up_weights, kind), parts(up_weights)) for kind in (full, full, low)]
        + [(like(member), whole(member)) for member in (up_row, up_col)]
        + [(like(down_weights, kind), parts(down_weights)) for kind in (full, full, low)]
        + [(like(member), whole(member)) for member in (down_row, down_col)]
        + [(like(biases, kind), whole(biases)) for kind in (full, full, low, full)]
    )
    outs = list(
        pl.pallas_call(
            functools.partial(settle_kernel, total_tokens),
            grid=(up_weights.shape[0] // group,),
            in_specs=[parts(member) for member in (sums, rows, up_weights, down_weights)]
            + [whole(member) for member in [mats] + wholes],
            out_shape=[shape for shape, spec in outs],
            out_specs=[spec for shape, spec in outs],
            compiler_params=pltpu.CompilerParams(vmem_limit_bytes=VMEM_ROOM),
            name="finish",
        )(sums, rows, up_weights, down_weights, mats, *wholes)
    )
    outs[0] = outs[0][0, 0]
    for at in (5, 16, 17, 18, 19):
        outs[at] = outs[at].reshape(-1)
    return tuple(outs)


def gather_kernel(
    mats_in,
    bias_in,
    down_in,
    up_in,
    patches,
    places,
    freq_low,
    label_hot,
    mats_out,
    bias_out,
    down_out,
    up_out,
    mods_out,
    fin_out,
    time_out,
    cond_out,
    qkv_out,
    att_out,
    middle_out,
    moe_out,
    logits_out,
    shared_out,
    mats_got,
    mats_own,
    up_got,
    up_wide,
    up_own,
    embedded,
    down_here,
    up_here,
    near_send,
    near_recv,
    own_sem,
    level_send,
    level_recv,
    one_send,
    one_recv,
    two_send,
    two_recv,
    core_send,
    core_recv,
    bias_send,
    bias_recv,
    here_sem,
):
    n_down, n_up = down_in.shape[0], up_own.shape[0]
    lead, n_mats = 3, mats_out.shape[4]
    after_mats = lead + n_mats
    first_up = n_down + n_mats
    slabs = first_up + n_up
    wide, narrow = lax.axis_index(WIDE), lax.axis_index(NARROW)
    z, x = wide // 2, wide % 2
    y, c = narrow // 2, narrow % 2
    mates = [
        (wide, (y + (k // 2) * (1 - 2 * y)) * 2 + c + (k % 2) * (1 - 2 * c)) for k in range(1, 4)
    ]
    levels = [(((z + k) % 4) * 2 + x, narrow) for k in range(1, 4)]
    to_x = (z * 2 + 1 - x, narrow)
    to_core, to_y = mates[0], mates[1]
    to_one = (z * 2 + x + (1 - c) * (1 - 2 * x), (y + c * (1 - 2 * y)) * 2 + c)
    to_two = (z * 2 + x + c * (1 - 2 * x), (y + (1 - c) * (1 - 2 * y)) * 2 + c)
    barrier = pltpu.get_barrier_semaphore()
    for target in mates + levels + [to_x]:
        pl.semaphore_signal(barrier, inc=1, device_id=target, device_id_type=MESH_ID)
    pl.semaphore_wait(barrier, 7)

    def remote(source, target, send, recv, device):
        return pltpu.make_async_remote_copy(
            src_ref=source,
            dst_ref=target,
            send_sem=send,
            recv_sem=recv,
            device_id=device,
            device_id_type=MESH_ID,
        )

    def near_mats(k):
        return remote(
            mats_in.at[mates[k - 1][1]],
            mats_got.at[narrow],
            near_send.at[0, k],
            near_recv.at[0, k],
            mates[k - 1],
        )

    def near_up(k):
        return remote(
            up_in.at[mates[k - 1][1]],
            up_got.at[narrow],
            near_send.at[1, k],
            near_recv.at[1, k],
            mates[k - 1],
        )

    own_mats = pltpu.make_async_copy(mats_in.at[narrow], mats_got.at[narrow], own_sem.at[0])
    own_up = pltpu.make_async_copy(up_in.at[narrow], up_got.at[narrow], own_sem.at[1])
    own_bias = pltpu.make_async_copy(bias_in, bias_out.at[z, x, y, c], own_sem.at[2])
    own_mats.start()
    own_up.start()
    own_bias.start()
    for k in range(1, 4):
        near_mats(k).start()

    def bias_level(k):
        return remote(
            bias_in, bias_out.at[z, x, y, c], bias_send.at[k - 1], bias_recv.at[k - 1], levels[k - 1]
        )

    def bias_x():
        part = bias_out.at[:, x, y, c]
        return remote(part, part, bias_send.at[3], bias_recv.at[3], to_x)

    def bias_y():
        part = bias_out.at[:, :, y, c]
        return remote(part, part, bias_send.at[4], bias_recv.at[4], to_y)

    def bias_core():
        part = bias_out.at[:, :, :, c]
        return remote(part, part, bias_send.at[5], bias_recv.at[5], to_core)

    for k in range(1, 4):
        bias_level(k).start()
    for k in range(1, 4):
        near_up(k).start()

    def mats_ready():
        own_mats.wait()
        for k in range(1, 4):
            near_mats(k).wait_recv()
        for n in range(NARROW_PIECES):
            mats_own[n * ROWS : (n + 1) * ROWS] = mats_got[n].astype(jnp.float32)[:ROWS]
        for n in range(n_mats):
            mats_got[n, :, :] = mats_own[16 * n : 16 * (n + 1)].astype(jnp.bfloat16)

    own_bias.wait()

    def turn(number):
        return (number + EXPERTS) % n_up

    def down_at(s):
        return turn(jnp.where(s < lead, s, s - n_mats))

    def source(kind, s):
        if kind == 0:
            return mats_got.at[s - lead]
        if kind == 1:
            return down_in.at[down_at(s)]
        return up_own.at[turn(s - first_up)]

    def piece(kind, s, at):
        z_at, x_at, y_at, c_at = at
        if kind == 0:
            return mats_out.at[y_at, c_at, z_at, x_at, s - lead]
        if kind == 1:
            return down_out.at[down_at(s), z_at, x_at, y_at, c_at]
        return up_out.at[turn(s - first_up), y_at, c_at, z_at, x_at]

    every = slice(None)

    def own_copy(kind, s):
        return pltpu.make_async_copy(
            source(kind, s), piece(kind, s, (z, x, y, c)), own_sem.at[3 + s % 4]
        )

    def level_copy(kind, s, k, turned=False, first=0):
        if turned:
            part = piece(kind, s, (z, x, every, c) if first == 0 else (z, every, y, c))
            start = part
        else:
            part = piece(kind, s, (z, x, y, c))
            start = source(kind, s)
        return remote(
            start, part, level_send.at[s % 8, k - 1], level_recv.at[s, k - 1], levels[k - 1]
        )

    def both_parts(kind, s, first):
        return piece(kind, s, (every, x, every, c) if first else (every, every, y, c))

    def one_copy(kind, s, turned=False, first=0):
        part = both_parts(kind, s, 1 - first) if turned else piece(kind, s, (every, x, y, c))
        return remote(part, part, one_send.at[s % 8], one_recv.at[s], to_one)

    def two_copy(kind, s, turned=False, first=0):
        if turned:
            part, start = piece(kind, s, (z, x, y, c)), source(kind, s)
        else:
            part = both_parts(kind, s, first)
            start = part
        return remote(start, part, two_send.at[s % 8], two_recv.at[s], to_two)

    def core_copy(kind, s):
        part = piece(kind, s, (every, every, every, c))
        return remote(part, part, core_send.at[s % 8], core_recv.at[s], to_core)

    def by_order(kind, s, run):
        if kind == 0:
            run(False)
            return
        turned = (s % 5 == 1) | (s % 5 == 3)

        @pl.when(turned)
        def _():
            run(True)

        @pl.when(jnp.logical_not(turned))
        def _():
            run(False)

    def by_core(run):
        for first in range(2):

            @pl.when(c == first)
            def _():
                run(first)

    def stage_level(kind, s):
        own_copy(kind, s).start()

        def run(turned):
            if turned:
                two_copy(kind, s, True).start()
            else:
                for k in range(1, 4):
                    level_copy(kind, s, k).start()

        by_order(kind, s, run)

    def stage_one(kind, s):
        own_copy(kind, s).wait()

        def run(turned):
            if turned:
                two_copy(kind, s, True).wait_recv()

                def send(first):
                    for k in range(1, 4):
                        level_copy(kind, s, k, True, first).start()

                by_core(send)
            else:
                for k in range(1, 4):
                    level_copy(kind, s, k).wait_recv()
                one_copy(kind, s).start()

        by_order(kind, s, run)

    def stage_two(kind, s):
        def run(turned):
            if turned:
                for k in range(1, 4):
                    level_copy(kind, s, k, True).wait_recv()
                by_core(lambda first: one_copy(kind, s, True, first).start())
            else:
                one_copy(kind, s).wait_recv()
                by_core(lambda first: two_copy(kind, s, False, first).start())

        by_order(kind, s, run)

    def stage_core(kind, s):
        def run(turned):
            if turned:
                one_copy(kind, s, True).wait_recv()
            else:
                two_copy(kind, s).wait_recv()

        by_order(kind, s, run)
        core_copy(kind, s).start()

    def stage_last(kind, s):
        core_copy(kind, s).wait_recv()

    def stage_sent(kind, s):
        def run(turned):
            for k in range(1, 4):
                level_copy(kind, s, k, turned).wait_send()
            one_copy(kind, s, turned).wait_send()
            two_copy(kind, s, turned).wait_send()

        by_order(kind, s, run)
        core_copy(kind, s).wait_send()

    stages = (
        (stage_sent, 8),
        (stage_level, 0),
        (stage_one, 2),
        (stage_two, 4),
        (stage_core, 6),
        (stage_last, 8),
    )

    lats = patches.shape[0] // PATCHES
    ready, shared_at = after_mats + 8, first_up + SHARED + 8
    low, full = jnp.bfloat16, jnp.float32

    def matrix(number, begin, end):
        chunk = mats_out[number // 2, number % 2]
        return chunk.reshape(D, chunk.shape[-1])[:, begin:end]

    def bias_rows():
        return jnp.sum(bias_out[...].astype(full).reshape(-1, 16, D), 0)

    def wide_row(rows, begin, end):
        return jnp.concatenate([rows[k : k + 1] for k in range(begin, end)], 1)

    def conditions():
        rows = bias_rows()
        pre_time = contract(freq_low[...], matrix(3, 1408, 1664), 1, 1) + rows[11:12]
        hid_time = jax.nn.silu(pre_time).astype(low)
        cond = (
            product(hid_time, matrix(3, 1024, 1408))
            + rows[12:13]
            + contract(label_hot[...], matrix(3, 0, 1024), 1, 1)
        )
        act = jax.nn.silu(cond).astype(low)
        time_out[...] = pre_time
        cond_out[...] = cond
        mods_out[:, : 4 * D] = product(act, matrix(1, 0, 4 * D)) + wide_row(rows, 4, 8)
        mods_out[:, 4 * D :] = product(act, matrix(2, 0, 2 * D)) + wide_row(rows, 8, 10)
        fin_out[...] = product(act, matrix(2, 2 * D, 4 * D)) + wide_row(rows, 13, 15)

    def mod_row(start, number):
        return mods_out[pl.ds(start // PATCHES, 1), number * D : (number + 1) * D]

    def attention_in(start):
        rows = bias_rows()
        span = pl.ds(start, PATCHES)
        emb = contract(patches[span, :], matrix(2, 4 * D, 4 * D + 128), 1, 1)
        emb = emb + rows[10:11] + places[...]
        embedded[...] = emb
        normed, unused_std = layer_norm(emb)
        attn_in = (normed * (1.0 + mod_row(start, 1)) + mod_row(start, 0)).astype(low)
        qkv_out[span, :] = (
            product(attn_in, matrix(0, 0, 3 * D)) + wide_row(rows, 0, 3)
        ).astype(low)

    def attention_heads(start):
        span = pl.ds(start, PATCHES)
        lane = lax.broadcasted_iota(jnp.int32, (PATCHES, 2 * HD), 1)
        for pair in range(HEADS // 2):
            at = pair * 2 * HD
            queries = qkv_out[span, at : at + 2 * HD]
            keys = qkv_out[span, D + at : D + at + 2 * HD]
            values = qkv_out[span, 2 * D + at : 2 * D + at + 2 * HD]
            halves = []
            for half in range(2):
                mine = (lane < HD) if half == 0 else (lane >= HD)
                scores = contract(jnp.where(mine, queries, 0), keys, 1, 1) * HD ** (-0.5)
                powers = jnp.exp(scores - jnp.max(scores, 1, keepdims=True))
                probs = (powers / jnp.sum(powers, 1, keepdims=True)).astype(low)
                halves.append(product(probs, values))
            att_out[span, at : at + 2 * HD] = jnp.where(lane < HD, halves[0], halves[1]).astype(low)

    def attention_out(start):
        rows = bias_rows()
        span = pl.ds(start, PATCHES)
        attn = product(att_out[span, :], matrix(0, 3 * D, 4 * D)) + rows[3:4]
        middle = embedded[...] + mod_row(start, 2) * attn
        middle_out[span, :] = middle
        normed, unused_std = layer_norm(middle)
        moe_in = (normed * (1.0 + mod_row(start, 4)) + mod_row(start, 3)).astype(low)
        moe_out[span, :] = moe_in
        logits_out[span, :] = product(moe_in, matrix(0, 4 * D, 4 * D + 128))

    def fetch(shared_id):
        e = EXPERTS + shared_id
        first = pltpu.make_async_copy(down_out.at[e], down_here, here_sem.at[0])
        second = pltpu.make_async_copy(up_out.at[e], up_here, here_sem.at[1])
        first.start()
        second.start()
        first.wait()
        second.wait()

    def shared_block(shared_id, start):
        span = pl.ds(start, PATCHES)
        rows = moe_out[span, :]
        chunks = [up_here[n // 2, n % 2].reshape(D, D) for n in range(NARROW_PIECES)]
        down = down_here[...].reshape(FF, D)
        total = None
        for cut in range(0, FF, CUT):
            pre_act = product(rows, up_columns(chunks, cut))
            part = product(gelu_only(pre_act).astype(low), down[cut : cut + CUT])
            total = part if total is None else total + part
        if shared_id == 0:
            shared_out[span, :] = total
        else:
            shared_out[span, :] += total

    def tick(t, unused):
        @pl.when(t == 1)
        def _():
            for k in range(1, 4):
                bias_level(k).wait_recv()
            bias_x().start()

        @pl.when(t == 2)
        def _():
            bias_x().wait_recv()
            bias_y().start()

        @pl.when(t == 3)
        def _():
            bias_y().wait_recv()
            bias_core().start()

        @pl.when(t == 6)
        def _():
            own_up.wait()
            for k in range(1, 4):
                near_up(k).wait_recv()
            for n in range(NARROW_PIECES):
                up_wide[n] = up_got[n].astype(jnp.float32)

            for e in range(n_up):
                up_own[e] = jnp.concatenate(
                    [up_wide[n, e * ROWS : (e + 1) * ROWS] for n in range(NARROW_PIECES)], 0
                ).astype(jnp.bfloat16)

        @pl.when(t == 2)
        def _():
            mats_ready()

        for stage, lag in stages:
            s = t - lag

            @pl.when((s >= lead) & (s < after_mats))
            def _():
                stage(0, jnp.clip(s, lead, after_mats - 1))

            @pl.when(((s >= 0) & (s < lead)) | ((s >= after_mats) & (s < first_up)))
            def _():
                stage(1, jnp.clip(s, 0, first_up - 1))

            @pl.when((s >= first_up) & (s < slabs))
            def _():
                stage(2, jnp.clip(s, first_up, slabs - 1))

        @pl.when(t == ready)
        def _():
            bias_core().wait_recv()
            conditions()

        for number, unit in enumerate((attention_in, attention_heads, attention_out)):

            @pl.when((t > ready) & (t <= ready + 3 * lats) & ((t - ready - 1) % 3 == number))
            def _():
                unit(pl.multiple_of(jnp.clip((t - ready - 1) // 3, 0, lats - 1) * PATCHES, PATCHES))

        for shared_id in range(SHARED):
            begin = shared_at + shared_id * lats

            @pl.when(t == begin)
            def _():
                fetch(shared_id)

            @pl.when((t >= begin) & (t < begin + lats))
            def _():
                shared_block(
                    shared_id, pl.multiple_of(jnp.clip(t - begin, 0, lats - 1) * PATCHES, PATCHES)
                )

        return unused

    lax.fori_loop(0, slabs + 8, tick, 0)
    for k in range(1, 4):
        near_mats(k).wait_send()
        near_up(k).wait_send()
        bias_level(k).wait_send()
    bias_x().wait_send()
    bias_y().wait_send()
    bias_core().wait_send()


def gather_weights(
    mats, up_weights, down_weights, biases, patches, places, freq_low, label_hot
):
    low = jnp.bfloat16
    owner = lax.axis_index(AXES)
    m = mats.astype(low)
    rows = m.shape[0]

    thin = 13 * D

    def thin_part(at):
        return jnp.pad(m[:, at : at + 16], ((0, 0), (0, 112)))

    mats_in = jnp.stack(
        [
            jnp.concatenate([m[:, : 4 * D], thin_part(thin)], 1),
            jnp.concatenate([m[:, 4 * D : 8 * D], thin_part(thin + 16)], 1),
            jnp.concatenate(
                [m[:, 8 * D : 10 * D], m[:, 11 * D : 13 * D], thin_part(thin + 32)], 1
            ),
            jnp.concatenate(
                [
                    m[:, thin + 48 + FREQ :],
                    jnp.zeros((rows, 24), low),
                    m[:, 10 * D : 11 * D],
                    m[:, thin + 48 : thin + 48 + FREQ],
                ],
                1,
            ),
        ],
        0,
    )
    mats_in = jnp.pad(mats_in, ((0, 0), (0, 16 - rows), (0, 0)))
    line = lax.dynamic_update_slice(
        jnp.zeros((16 * D,), low), biases.astype(low), (owner * biases.shape[0],)
    )
    n_up = up_weights.shape[0]
    up_in = (
        up_weights.astype(low)
        .reshape(n_up, rows, NARROW_PIECES, D)
        .transpose(2, 0, 1, 3)
        .reshape(NARROW_PIECES, n_up * rows, D)
    )
    room = (n_up * rows + 15) // 16 * 16
    up_in = jnp.pad(up_in, ((0, 0), (0, room - n_up * rows), (0, 0)))
    slabs = 3 + 2 * n_up
    spread = mats_in.shape[2]
    dma = pltpu.SemaphoreType.DMA
    anywhere = pl.BlockSpec(memory_space=pl.ANY)
    tokens = patches.shape[0]
    full, vmem = jnp.float32, pl.BlockSpec(memory_space=pltpu.VMEM)
    outs = pl.pallas_call(
        gather_kernel,
        out_shape=[
            jax.ShapeDtypeStruct((2, 2, 4, 2, 3, 16, spread), low),
            jax.ShapeDtypeStruct((4, 2, 2, 2, 16, D), low),
            jax.ShapeDtypeStruct((n_up, 4, 2, 2, 2, PIECE, D), low),
            jax.ShapeDtypeStruct((n_up, 2, 2, 4, 2, PIECE, D), low),
            jax.ShapeDtypeStruct((8, 6 * D), full),
            jax.ShapeDtypeStruct((8, 2 * D), full),
            jax.ShapeDtypeStruct((8, D), full),
            jax.ShapeDtypeStruct((8, D), full),
            jax.ShapeDtypeStruct((tokens, 3 * D), low),
            jax.ShapeDtypeStruct((tokens, D), low),
            jax.ShapeDtypeStruct((tokens, D), full),
            jax.ShapeDtypeStruct((tokens, D), low),
            jax.ShapeDtypeStruct((tokens, 128), full),
            jax.ShapeDtypeStruct((tokens, D), full),
        ],
        in_specs=[anywhere] * 4 + [vmem] * 4,
        out_specs=[vmem] * 2 + [anywhere] * 2 + [vmem] * 10,
        scratch_shapes=[
            pltpu.VMEM((NARROW_PIECES, 16, spread), low),
            pltpu.VMEM((PIECE, spread), jnp.float32),
            pltpu.VMEM((NARROW_PIECES, room, D), low),
            pltpu.VMEM((NARROW_PIECES, room, D), jnp.float32),
            pltpu.VMEM((n_up, PIECE, D), low),
            pltpu.VMEM((PATCHES, D), full),
            pltpu.VMEM((4, 2, 2, 2, PIECE, D), low),
            pltpu.VMEM((2, 2, 4, 2, PIECE, D), low),
            dma((2, 4)),
            dma((2, 4)),
            dma((7,)),
            dma((8, 3)),
            dma((slabs, 3)),
            dma((8,)),
            dma((slabs,)),
            dma((8,)),
            dma((slabs,)),
            dma((8,)),
            dma((slabs,)),
            dma((6,)),
            dma((6,)),
            dma((2,)),
        ],
        compiler_params=pltpu.CompilerParams(
            collective_id=2, has_side_effects=True, vmem_limit_bytes=VMEM_ROOM
        ),
        name="gather_weights",
    )(
        mats_in,
        line.reshape(16, D),
        down_weights.astype(low),
        up_in,
        patches,
        places,
        freq_low,
        label_hot,
    )
    return outs


def split_weights(weights):
    mats_full, up_full, down_full, bias_full = weights
    matrices = cut_pieces(mats_full, column_widths(), 1)
    vectors = [member.astype(jnp.float32) for member in cut_pieces(bias_full, bias_widths(), 0)]
    up_full = up_full.reshape(-1, D, NARROW_PIECES, D).transpose(0, 2, 1, 3)
    return (matrices, vectors, up_full, down_full)


def forward(weights, latents, noise, timesteps, labels, routes):
    matrices, vectors, up_full, down_full = weights
    w_qkv, w_proj, w_mod, w_time2, w_final, w_router, w_head, w_patch, w_time1, w_table = matrices
    b_qkv, b_proj, b_mod, b_patch, b_time1, b_time2, b_final = vectors
    num_latents = latents.shape[0]
    rows_here = num_latents * PATCHES
    steps_f = timesteps.astype(jnp.float32)
    signal, spread = noise_level(steps_f)
    noisy = signal[:, None] * latents + spread[:, None] * noise
    patches = noisy.reshape(rows_here, PD).astype(jnp.bfloat16)
    embedded = (
        contract(patches, w_patch, 1, 1).reshape(num_latents, PATCHES, D)
        + b_patch
        + positions()[None]
    )
    freq_low = time_features(steps_f).astype(jnp.bfloat16)
    pre_time = contract(freq_low, w_time1, 1, 1) + b_time1
    hid_time = jax.nn.silu(pre_time).astype(jnp.bfloat16)
    label_hot = (labels[:, None] == jnp.arange(CLASSES, dtype=jnp.int32)[None, :]).astype(
        jnp.float32
    )
    label_emb = lax.dot_general(
        label_hot,
        w_table.astype(jnp.float32),
        (((1,), (1,)), ((), ())),
        precision=lax.Precision.HIGHEST,
        preferred_element_type=jnp.float32,
    )
    cond = product(hid_time, w_time2) + b_time2 + label_emb
    cond_act = jax.nn.silu(cond).astype(jnp.bfloat16)
    modulation = product(cond_act, w_mod) + b_mod
    final_mod = product(cond_act, w_final) + b_final
    shift_attn, scale_attn, gate_attn, shift_moe, scale_moe, gate_moe = [
        member[:, None, :] for member in jnp.split(modulation, 6, 1)
    ]
    shift_fin, scale_fin = [member[:, None, :] for member in jnp.split(final_mod, 2, 1)]
    normed_one, inv_one = layer_norm(embedded)
    attn_in = (
        (normed_one * (1.0 + scale_attn) + shift_attn).astype(jnp.bfloat16).reshape(rows_here, D)
    )
    qkv_out = (
        (product(attn_in, w_qkv) + b_qkv)
        .astype(jnp.bfloat16)
        .reshape(num_latents, PATCHES, 3, HEADS, HD)
    )
    scores = jnp.einsum(
        LQK, qkv_out[:, :, 0], qkv_out[:, :, 1], preferred_element_type=jnp.float32
    ) * HD ** (-0.5)
    log_totals = jax.nn.logsumexp(scores, -1)
    probs_low = jax.nn.softmax(scores, -1).astype(jnp.bfloat16)
    attended = (
        jnp.einsum(
            "lhqk,lkhd->lqhd", probs_low, qkv_out[:, :, 2], preferred_element_type=jnp.float32
        )
        .astype(jnp.bfloat16)
        .reshape(rows_here, D)
    )
    attn_out = (product(attended, w_proj) + b_proj).reshape(num_latents, PATCHES, D)
    middle = embedded + gate_attn * attn_out
    normed_two, inv_two = layer_norm(middle)
    moe_in = (normed_two * (1.0 + scale_moe) + shift_moe).astype(jnp.bfloat16).reshape(rows_here, D)
    logits = product(moe_in, w_router)
    route_hot = (routes[:, :, None] == jnp.arange(EXPERTS, dtype=jnp.int32)[None, None, :]).astype(
        jnp.float32
    )
    gate_vals = jax.nn.softmax(jnp.sum(route_hot * logits[:, None, :], 2), -1)
    slot_of, slot_meta = pack_slots(routes)
    routed = experts_forward(slot_of, slot_meta, moe_in, up_full, down_full)
    moe_out = gate_vals[:, 0:1] * routed[0] + gate_vals[:, 1:2] * routed[1]
    for shared_id in range(EXPERTS, EXPERTS + SHARED):
        for cut in range(0, FF, CUT):
            pre_act = product(moe_in, up_columns(up_full[shared_id], cut))
            activated = gelu_only(pre_act).astype(jnp.bfloat16)
            moe_out = moe_out + product(activated, down_full[shared_id, cut : cut + CUT])
    moe_out = moe_out.reshape(num_latents, PATCHES, D)
    final_state = middle + gate_moe * moe_out
    normed_fin, inv_fin = layer_norm(final_state)
    head_in = (
        (normed_fin * (1.0 + scale_fin) + shift_fin).astype(jnp.bfloat16).reshape(rows_here, D)
    )
    errors = product(head_in, w_head) - noise.reshape(rows_here, PD)
    return SimpleNamespace(
        patches=patches,
        freq_low=freq_low,
        pre_time=pre_time,
        hid_time=hid_time,
        label_hot=label_hot,
        cond=cond,
        cond_act=cond_act,
        scale_attn=scale_attn,
        gate_attn=gate_attn,
        scale_moe=scale_moe,
        gate_moe=gate_moe,
        scale_fin=scale_fin,
        normed_one=normed_one,
        inv_one=inv_one,
        attn_in=attn_in,
        qkv_out=qkv_out,
        log_totals=log_totals,
        attended=attended,
        attn_out=attn_out,
        normed_two=normed_two,
        inv_two=inv_two,
        moe_in=moe_in,
        route_hot=route_hot,
        gate_vals=gate_vals,
        slot_of=slot_of,
        slot_meta=slot_meta,
        routed=routed,
        moe_out=moe_out,
        normed_fin=normed_fin,
        inv_fin=inv_fin,
        head_in=head_in,
        errors=errors,
    )


def forward_fused(mats, up_weights, down_weights, biases, latents, noise, timesteps, labels):
    num_latents = latents.shape[0]
    rows_here = num_latents * PATCHES
    steps_f = timesteps.astype(jnp.float32)
    signal, spread = noise_level(steps_f)
    noisy = signal[:, None] * latents + spread[:, None] * noise
    patches = noisy.reshape(rows_here, PD).astype(jnp.bfloat16)
    freq_low = time_features(steps_f).astype(jnp.bfloat16)
    label_low = (labels[:, None] == jnp.arange(1024, dtype=jnp.int32)[None, :]).astype(jnp.bfloat16)
    less = ((0, 8 - num_latents), (0, 0))
    outs = gather_weights(
        mats,
        up_weights,
        down_weights,
        biases,
        jnp.pad(patches, ((0, 0), (0, 128 - PD))),
        positions(),
        jnp.pad(freq_low, less),
        jnp.pad(label_low, less),
    )
    n_up = outs[3].shape[0]
    return SimpleNamespace(
        patches=jnp.pad(patches, ((0, 0), (0, 128 - PD))),
        freq_low=jnp.pad(freq_low, less),
        mats_full=outs[0],
        bias_full=outs[1],
        down_full=outs[2].reshape(n_up, FF, D),
        up_full=outs[3].reshape(n_up, NARROW_PIECES, D, D),
        mods=outs[4],
        fin=outs[5],
        pre_time=outs[6],
        cond=outs[7],
        qkv=outs[8],
        attended=outs[9],
        middle=outs[10],
        moe_in=outs[11],
        logits=outs[12],
        shared_out=outs[13],
    )


def backward_fused(fused, latents, noise, labels, routes, total_tokens):
    num_latents = latents.shape[0]
    rows_here = num_latents * PATCHES
    line = jnp.sum(fused.bias_full.reshape(-1, 16, D).astype(jnp.float32), 0)
    slot_of, slot_meta = pack_slots(routes)
    members = (
        fused.logits,
        routes,
        fused.shared_out,
        fused.middle,
        jnp.pad(noise.reshape(rows_here, PD), ((0, 0), (0, 128 - PD))),
        fused.mods,
        fused.fin,
        fused.mats_full[0, 1].reshape(D, -1)[:, 4 * D :],
    )
    grad_pair, grad_both, grad_state, grad_logits, thin, grad_gate, grad_fin, loss_part = (
        experts_and_head(
            slot_of,
            slot_meta,
            fused.moe_in,
            fused.up_full,
            fused.down_full,
            2.0 / total_tokens,
            members,
        )
    )
    up_slabs, down_slabs, dx_routed = experts_backward(
        slot_of, slot_meta, fused.moe_in, grad_pair, fused.up_full, fused.down_full
    )
    label_parts = jnp.stack([labels // 32, labels % 32], 1).astype(jnp.bfloat16)
    members = (
        fused.moe_in,
        grad_both,
        dx_routed,
        grad_logits,
        fused.middle,
        fused.qkv,
        fused.attended,
        grad_state,
        fused.patches,
        positions(),
        fused.mods,
        fused.mats_full,
        line,
        fused.pre_time,
        fused.cond,
        fused.freq_low,
        grad_gate,
        grad_fin,
        thin,
        jnp.pad(label_parts, ((0, 8 - num_latents), (0, 126))),
    )
    return loss_part, reduce_slabs(
        down_slabs, up_slabs, fused.up_full, fused.down_full, members
    )


def backward(weights, kept, total_tokens):
    matrices, vectors, up_full, down_full = weights
    w_qkv, w_proj, w_mod, w_time2, w_final, w_router, w_head, w_patch, w_time1, w_table = matrices
    num_latents = kept.normed_one.shape[0]
    rows_here = num_latents * PATCHES
    grad_head, grad_head_in, unused = linear_back(
        kept.errors * (2.0 / total_tokens), kept.head_in, w_head
    )
    grad_head_in = grad_head_in.reshape(num_latents, PATCHES, D)
    grad_final_mod = jnp.concatenate(
        [jnp.sum(grad_head_in, 1), jnp.sum(grad_head_in * kept.normed_fin, 1)], 1
    )
    grad_state = norm_back(
        grad_head_in * (1.0 + kept.scale_fin), kept.normed_fin, kept.inv_fin
    )
    grad_gate_moe = jnp.sum(kept.moe_out * grad_state, 1)
    grad_moe = (kept.gate_moe * grad_state).reshape(rows_here, D)
    grad_moe_low = grad_moe.astype(jnp.bfloat16)
    moe_in = kept.moe_in
    gate_vals = kept.gate_vals
    routed = kept.routed
    grad_gates = jnp.stack([jnp.sum(routed[k] * grad_moe, 1) for k in range(2)], 1)
    grad_pair = jnp.stack(
        [(gate_vals[:, k : k + 1] * grad_moe).astype(jnp.bfloat16) for k in range(2)], 0
    )
    up_slabs, down_slabs, grad_moe_in = experts_backward(
        kept.slot_of, kept.slot_meta, moe_in, grad_pair, up_full, down_full
    )
    up_all = [up_slabs.transpose(0, 1, 3, 2, 4).reshape(-1, D, FF)]
    down_all = [down_slabs.reshape(-1, FF, D)]
    for shared_id in range(EXPERTS, EXPERTS + SHARED):
        up_part = jnp.concatenate([up_full[shared_id, k] for k in range(NARROW_PIECES)], 1)
        activated, slope = gelu_slope(product(moe_in, up_part))
        grad_act = contract(grad_moe_low, down_full[shared_id], 1, 1)
        grad_pre = (grad_act * slope).astype(jnp.bfloat16)
        down_all.append(contract(activated.astype(jnp.bfloat16), grad_moe_low, 0, 0)[None])
        up_all.append(contract(moe_in, grad_pre, 0, 0)[None])
        grad_moe_in = grad_moe_in + contract(grad_pre, up_part, 1, 1)
    up_slabs = jnp.concatenate([member.astype(jnp.float32) for member in up_all], 0)
    down_slabs = jnp.concatenate([member.astype(jnp.float32) for member in down_all], 0)
    grad_picked = gate_vals * (grad_gates - jnp.sum(gate_vals * grad_gates, 1, keepdims=True))
    grad_logits = jnp.sum(kept.route_hot * grad_picked[:, :, None], 1)
    grad_router, grad_from_router, unused = linear_back(grad_logits, moe_in, w_router)
    grad_moe_in = (grad_moe_in + grad_from_router).reshape(num_latents, PATCHES, D)
    grad_middle = grad_state + norm_back(
        grad_moe_in * (1.0 + kept.scale_moe), kept.normed_two, kept.inv_two
    )
    grad_gate_attn = jnp.sum(kept.attn_out * grad_middle, 1)
    grad_proj, grad_attended, grad_b_proj = linear_back(
        (kept.gate_attn * grad_middle).reshape(rows_here, D), kept.attended, w_proj
    )
    grad_att_low = grad_attended.astype(jnp.bfloat16).reshape(num_latents, PATCHES, HEADS, HD)
    qkv_out = kept.qkv_out
    queries = qkv_out[:, :, 0]
    key_rows = qkv_out[:, :, 1]
    values = qkv_out[:, :, 2]
    scores = jnp.einsum(
        LQK, queries, key_rows, preferred_element_type=jnp.float32
    ) * HD ** (-0.5)
    probs = jnp.exp(scores - kept.log_totals[..., None])
    probs_low = probs.astype(jnp.bfloat16)
    grad_values = jnp.einsum(
        "lhqk,lqhd->lkhd", probs_low, grad_att_low, preferred_element_type=jnp.float32
    )
    grad_probs = jnp.einsum(
        LQK, grad_att_low, values, preferred_element_type=jnp.float32
    )
    grad_scores = (
        probs * (grad_probs - jnp.sum(probs * grad_probs, -1, keepdims=True)) * HD ** (-0.5)
    ).astype(jnp.bfloat16)
    grad_queries = jnp.einsum(
        "lhqk,lkhd->lqhd", grad_scores, key_rows, preferred_element_type=jnp.float32
    )
    grad_keys = jnp.einsum(
        "lhqk,lqhd->lkhd", grad_scores, queries, preferred_element_type=jnp.float32
    )
    grad_qkv = jnp.stack([grad_queries, grad_keys, grad_values], 2).reshape(rows_here, 3 * D)
    grad_w_qkv, grad_attn_in, grad_b_qkv = linear_back(grad_qkv, kept.attn_in, w_qkv)
    grad_attn_in = grad_attn_in.reshape(num_latents, PATCHES, D)
    grad_embedded = grad_middle + norm_back(
        grad_attn_in * (1.0 + kept.scale_attn), kept.normed_one, kept.inv_one
    )
    grad_emb_flat = grad_embedded.reshape(rows_here, D)
    grad_patch = contract(grad_emb_flat.astype(jnp.bfloat16), kept.patches, 0, 0)
    grad_b_patch = jnp.sum(grad_emb_flat, 0)
    grad_modulation = jnp.concatenate(
        [
            jnp.sum(grad_attn_in, 1),
            jnp.sum(grad_attn_in * kept.normed_one, 1),
            grad_gate_attn,
            jnp.sum(grad_moe_in, 1),
            jnp.sum(grad_moe_in * kept.normed_two, 1),
            grad_gate_moe,
        ],
        1,
    )
    grad_mod_low = grad_modulation.astype(jnp.bfloat16)
    grad_fin_low = grad_final_mod.astype(jnp.bfloat16)
    grad_act = contract(grad_mod_low, w_mod, 1, 1) + contract(grad_fin_low, w_final, 1, 1)
    grad_cond = slope_back(jax.nn.silu, kept.cond, grad_act)
    grad_cond_low = grad_cond.astype(jnp.bfloat16)
    grad_hid_time = contract(grad_cond_low, w_time2, 1, 1)
    grad_pre_time = slope_back(jax.nn.silu, kept.pre_time, grad_hid_time)
    grad_time_low = grad_pre_time.astype(jnp.bfloat16)
    mats_slabs = jnp.concatenate([grad_w_qkv, grad_proj], 1)[None]
    thin = jnp.concatenate([grad_router, grad_head, grad_patch], 1)
    grad_bias = jnp.concatenate(
        [
            grad_b_qkv,
            grad_b_proj,
            jnp.sum(grad_modulation, 0),
            grad_b_patch,
            jnp.sum(grad_pre_time, 0),
            jnp.sum(grad_cond, 0),
            jnp.sum(grad_final_mod, 0),
        ]
    )
    lows = jnp.concatenate(
        [
            kept.cond_act,
            kept.hid_time,
            grad_mod_low,
            grad_fin_low,
            grad_cond_low,
            grad_time_low,
            kept.freq_low,
        ],
        1,
    )
    return (up_slabs, down_slabs, mats_slabs, thin, grad_bias, lows, grad_cond)


def latent_grads(lows, grad_cond, labels, row_start, row_count):
    lows = lax.all_gather(lows, AXES, axis=0, tiled=True)
    grad_cond = lax.all_gather(grad_cond, AXES, axis=0, tiled=True)
    labels = lax.all_gather(labels, AXES, axis=0, tiled=True)
    cond_act, hid_time, grad_mod, grad_fin, grad_low, grad_time, freq_low = cut_pieces(
        lows, [D, D, 6 * D, 2 * D, D, D, FREQ], 1
    )

    def rows_of(member):
        return lax.dynamic_slice_in_dim(member, row_start, row_count, 1)

    label_hot = (labels[:, None] == jnp.arange(CLASSES, dtype=jnp.int32)[None, :]).astype(
        jnp.float32
    )
    grad_table = lax.dot_general(
        rows_of(grad_cond),
        label_hot,
        (((0,), (0,)), ((), ())),
        precision=lax.Precision.HIGHEST,
        preferred_element_type=jnp.float32,
    )
    return (
        contract(rows_of(cond_act), grad_mod, 0, 0),
        contract(rows_of(hid_time), grad_low, 0, 0),
        contract(rows_of(cond_act), grad_fin, 0, 0),
        contract(rows_of(grad_time), freq_low, 0, 0),
        grad_table,
    )


def factor_start(grad, row_old):
    squares = grad * grad + eps_fact
    row_new = decay * row_old + (1.0 - decay) * jnp.mean(squares, 2)
    return (row_new, jnp.sum(squares, 1), jnp.sum(row_new, 1))


def factor_update(grad, row_new, col_total, row_total, col_old, row_count):
    col_new = decay * col_old + (1.0 - decay) * (col_total / row_count)
    row_mean = row_total / row_count
    update = grad * lax.rsqrt(row_new[:, :, None] * col_new[:, None, :] / row_mean[:, None, None])
    return (col_new, update, jnp.sum(update * update, (1, 2)))


def clip_apply(master, update, square_total, entry_count):
    update_rms = jnp.sqrt(square_total / entry_count)
    return master - learn_rate * (update / jnp.maximum(1.0, update_rms / clip_level)[:, None, None])


def update_plain(grads, masters, factors, loss_part):
    mats_grad, up_grad, down_grad, bias_grad = grads
    mats, up_weights, down_weights, biases = masters
    mats_row, mats_col, up_row, up_col, down_row, down_col, bias_state = factors
    widths = column_widths()
    grad_pieces = cut_pieces(mats_grad, widths, 1)
    starts = [
        factor_start(grad_pieces[k][None], mats_row[k][None]) for k in range(len(widths))
    ]
    up_row_new, up_col_part, up_row_part = factor_start(up_grad, up_row)
    down_row_new, down_col_part, down_row_part = factor_start(down_grad, down_row)
    col_totals, row_totals, up_cols, up_rows, down_cols, down_rows, loss_total = lax.psum(
        (
            jnp.concatenate([member[1] for member in starts], 1)[0],
            jnp.concatenate([member[2] for member in starts], 0),
            up_col_part,
            up_row_part,
            down_col_part,
            down_row_part,
            loss_part,
        ),
        AXES,
    )
    col_total_pieces = cut_pieces(col_totals, widths, 0)
    col_old_pieces = cut_pieces(mats_col, widths, 0)
    steps = [
        factor_update(
            grad_pieces[k][None],
            starts[k][0],
            col_total_pieces[k][None],
            row_totals[k][None],
            col_old_pieces[k][None],
            D,
        )
        for k in range(len(widths))
    ]
    up_col_new, up_update, up_square = factor_update(
        up_grad, up_row_new, up_cols, up_rows, up_col, D
    )
    down_col_new, down_update, down_square = factor_update(
        down_grad, down_row_new, down_cols, down_rows, down_col, FF
    )
    bias_state_new = decay * bias_state + (1.0 - decay) * (bias_grad * bias_grad + eps_fact)
    bias_update = bias_grad * lax.rsqrt(bias_state_new)
    square_mats, square_up, square_down, square_bias = lax.psum(
        (
            jnp.concatenate([member[2] for member in steps], 0),
            up_square,
            down_square,
            jnp.sum(bias_update * bias_update),
        ),
        AXES,
    )
    master_pieces = cut_pieces(mats, widths, 1)
    mats_new = jnp.concatenate(
        [
            clip_apply(
                master_pieces[k][None], steps[k][1], square_mats[k][None], D * widths[k]
            )[0]
            for k in range(len(widths))
        ],
        1,
    )
    up_new = clip_apply(up_weights, up_update, square_up, D * FF)
    down_new = clip_apply(down_weights, down_update, square_down, D * FF)
    bias_rms = jnp.sqrt(square_bias / (15 * D))
    bias_new = biases - learn_rate * (bias_update / jnp.maximum(1.0, bias_rms / clip_level))
    return (
        loss_total,
        mats_grad,
        mats_new,
        mats_new.astype(jnp.bfloat16),
        jnp.concatenate([member[0] for member in starts], 0),
        jnp.concatenate([member[0][0] for member in steps], 0),
        up_grad,
        up_new,
        up_new.astype(jnp.bfloat16),
        up_row_new,
        up_col_new,
        down_grad,
        down_new,
        down_new.astype(jnp.bfloat16),
        down_row_new,
        down_col_new,
        bias_grad,
        bias_new,
        bias_new.astype(jnp.bfloat16),
        bias_state_new,
    )


def body(
    latents,
    noise,
    timesteps,
    labels,
    routes,
    mats,
    up_weights,
    down_weights,
    biases,
    *factors,
):
    rows_here = mats.shape[0]
    total_tokens = latents.shape[0] * PATCHES * lax.axis_size(AXES)
    masters = (mats, up_weights, down_weights, biases)
    if lax.axis_size(WIDE) == WIDE_PIECES and lax.axis_size(NARROW) == NARROW_PIECES:
        fused = forward_fused(
            mats, up_weights, down_weights, biases, latents, noise, timesteps, labels
        )
        loss_part, (sums, turned, lat, bias_sum) = backward_fused(
            fused, latents, noise, labels, routes, total_tokens
        )
        return update_kernel_call(
            sums, turned, lat, bias_sum, masters, factors, loss_part, total_tokens
        )
    else:
        flat = jnp.concatenate([mats.reshape(-1), biases], 0).astype(jnp.bfloat16)
        flat = lax.all_gather(flat, AXES, axis=0, tiled=False)
        gathered = split_weights(
            (
                flat[:, : rows_here * mats.shape[1]].reshape(-1, mats.shape[1]),
                lax.all_gather(up_weights.astype(jnp.bfloat16), AXES, axis=1, tiled=True),
                lax.all_gather(down_weights.astype(jnp.bfloat16), AXES, axis=1, tiled=True),
                flat[:, rows_here * mats.shape[1] :].reshape(-1),
            )
        )
        kept = forward(gathered, latents, noise, timesteps, labels, routes)
        members = backward(gathered, kept, total_tokens)
        up_slabs, down_slabs, mats_slabs, thin, grad_bias, lows, grad_cond = members
        loss_part = jnp.sum(kept.errors * kept.errors)
        grads = plain_grads(
            down_slabs, up_slabs, mats_slabs, thin, grad_bias, lows, grad_cond, labels, rows_here
        )
        outs = update_plain(grads, masters, factors, loss_part)
    return (outs[0] / total_tokens,) + tuple(outs[1:])


def solution(mesh):
    rows = P(AXES, None)
    middle_rows = P(None, AXES, None)
    row_factor = P(None, AXES)
    line = P(AXES)
    in_specs = (
        (rows, rows, line, line, rows)
        + (rows, middle_rows, middle_rows, line)
        + (row_factor, P(), row_factor, P(), row_factor, P(), line)
    )
    out_specs = (
        (P(), rows, rows, rows, row_factor, P())
        + (middle_rows, middle_rows, middle_rows, row_factor, P()) * 2
        + (line, line, line, line)
    )
    return jax.shard_map(body, mesh=mesh, in_specs=in_specs, out_specs=out_specs, check_vma=False)
```

```python
import functools
import math
from types import SimpleNamespace

import jax
import jax.numpy as jnp
from jax import lax
from jax.experimental import pallas as pl
from jax.experimental.pallas import tpu as pltpu
from jax.sharding import PartitionSpec as P

WIDE = "wide"
NARROW = "narrow"
AXES = (WIDE, NARROW)
MESH_ID = pl.DeviceIdType.MESH

D = 384
HEADS = 6
HD = 64
FF = 1536
EXPERTS = 16
SHARED = 2
PD = 16
GRID = 16
FREQ = 256
CLASSES = 1000
BLK = 256
WIDE_PIECES = 8
NARROW_PIECES = 4
PIECE = 48
ROWS = 12
LAT_ROWS = 16
LQK = "lqhd,lkhd->lhqk"
CUT = 768
LAT_COLS = 1536
PATCHES = 256


eps_norm = 1e-06
eps_fact = 1e-30
decay = 0.5
clip_level = 0.1
learn_rate = 0.5

SQRT_2_PI = math.sqrt(2.0 / math.pi)
VMEM_ROOM = 56 * 1024 * 1024
REDUCE_ROOM = 60 * 1024 * 1024


def column_widths():
    return [3 * D, D, 6 * D, D, 2 * D, EXPERTS, PD, PD, FREQ, CLASSES]


def bias_widths():
    return [3 * D, D, 6 * D, D, D, D, 2 * D]


def cut_pieces(source, widths, along):
    pieces = []
    start = 0
    for width in widths:
        pieces.append(lax.slice_in_dim(source, start, start + width, axis=along))
        start = start + width
    return pieces


def product(left, right):
    return jnp.dot(left, right, preferred_element_type=jnp.float32)


def contract(left, right, left_dim, right_dim):
    return lax.dot_general(
        left, right, (((left_dim,), (right_dim,)), ((), ())), preferred_element_type=jnp.float32
    )


def gelu_tanh(values):
    return jax.nn.gelu(values, approximate=True)


def slope_back(function, source, grad_out):
    return jax.vjp(function, source)[1](grad_out)[0]


def layer_norm(source):
    centred = source - jnp.mean(source, -1, keepdims=True)
    inv_std = lax.rsqrt(jnp.mean(centred * centred, -1, keepdims=True) + eps_norm)
    return (centred * inv_std, inv_std)


def norm_back(grad_norm, normed, inv_std):
    return inv_std * (
        grad_norm
        - jnp.mean(grad_norm, -1, keepdims=True)
        - normed * jnp.mean(grad_norm * normed, -1, keepdims=True)
    )


def linear_back(grad_out, inputs, weight):
    grad_low = grad_out.astype(jnp.bfloat16)
    return (
        contract(inputs, grad_low, 0, 0),
        contract(grad_low, weight, 1, 1),
        jnp.sum(grad_out, 0),
    )


def sincos(coords, width):
    omegas = 1.0 / 10000.0 ** (jnp.arange(width // 2, dtype=jnp.float32) / (width / 2.0))
    angles = coords[:, None] * omegas[None, :]
    return jnp.concatenate([jnp.sin(angles), jnp.cos(angles)], 1)


def positions():
    places = jnp.arange(PATCHES, dtype=jnp.int32)
    grid_row = (places // GRID).astype(jnp.float32)
    grid_col = (places % GRID).astype(jnp.float32)
    return jnp.concatenate([sincos(grid_row, D // 2), sincos(grid_col, D // 2)], 1)


def time_features(steps_f):
    half_width = FREQ // 2
    freq_rates = jnp.exp(
        -math.log(10000.0) * jnp.arange(half_width, dtype=jnp.float32) / half_width
    )
    angles = steps_f[:, None] * freq_rates[None, :]
    return jnp.concatenate([jnp.cos(angles), jnp.sin(angles)], 1)


def noise_level(steps_f):
    alpha_bar = jnp.cos((steps_f / 1000.0 + 0.008) / 1.008 * (math.pi / 2)) ** 2
    return (jnp.sqrt(alpha_bar), jnp.sqrt(1.0 - alpha_bar))


def pack_slots(routes):
    ids = jnp.arange(EXPERTS, dtype=jnp.int32)[:, None]
    named = [(routes[:, k][None, :] == ids) for k in range(2)]
    either = (named[0] | named[1]).astype(jnp.bfloat16)
    rows_here = routes.shape[0]
    place = jnp.arange(rows_here, dtype=jnp.int32)
    before = (place[:, None] < place[None, :]).astype(jnp.bfloat16)
    rank_in = product(either, before)
    counts = jnp.sum(either.astype(jnp.float32), 1).astype(jnp.int32)
    padded = (counts + 15) // 16 * 16
    starts = jnp.sum(jnp.where(ids > ids.T, padded[None, :], 0), 1)
    slots = rank_in.astype(jnp.int32) + starts[:, None]
    slot_of = jnp.stack([jnp.sum(jnp.where(member, slots, 0), 0) for member in named], 0)
    return (slot_of, jnp.stack([starts, counts], 0))


def gelu_slope(values):
    inner = SQRT_2_PI * (values + 0.044715 * values * values * values)
    bend = jnp.tanh(inner)
    return (
        0.5 * values * (1.0 + bend),
        0.5 * (1.0 + bend)
        + 0.5
        * values
        * (1.0 - bend * bend)
        * SQRT_2_PI
        * (1.0 + 3.0 * 0.044715 * values * values),
    )


def gelu_only(values):
    inner = SQRT_2_PI * (values + 0.044715 * values * values * values)
    return 0.5 * values * (1.0 + jnp.tanh(inner))


def up_columns(chunks, cut):
    return jnp.concatenate([chunks[cut // D + k] for k in range(CUT // D)], 1)


def slot_pick(slots_ref, base, rows):
    place = base + lax.broadcasted_iota(jnp.int32, (rows, slots_ref.shape[1]), 0)
    return ((slots_ref[0:1, :] == place) | (slots_ref[1:2, :] == place)).astype(jnp.bfloat16)


def over_blocks(meta, run):
    start, count = meta[0, pl.program_id(0)], meta[1, pl.program_id(0)]
    blocks = (count + BLK // 2 - 1) // BLK
    rest = count - blocks * BLK

    def block(number, unused):
        run(pl.multiple_of(start + number * BLK, 16), BLK)
        return unused

    lax.fori_loop(0, blocks, block, 0)

    @pl.when(rest > BLK // 4)
    def _():
        run(pl.multiple_of(start + blocks * BLK, 16), BLK // 2)

    @pl.when((rest > 0) & (rest <= BLK // 4))
    def _():
        run(pl.multiple_of(start + blocks * BLK, 16), BLK // 4)


def routed_blocks(meta, slots_ref, x_ref, up_ref, down_ref, x_out, y_ref):
    def run(base, size):
        rows = product(slot_pick(slots_ref, base, size), x_ref[...]).astype(jnp.bfloat16)
        x_out[pl.ds(base, size), :] = rows
        total = None
        for cut in range(0, FF, CUT):
            pre_act = product(rows, up_columns(up_ref[0], cut))
            part = product(gelu_only(pre_act).astype(jnp.bfloat16), down_ref[0, cut : cut + CUT])
            total = part if total is None else total + part
        y_ref[pl.ds(base, size), :] = total

    over_blocks(meta, run)


def forward_kernel(
    meta, slot_at, slots_ref, x_ref, up_ref, down_ref, routed_ref, x_out, y_ref
):
    routed_blocks(meta, slots_ref, x_ref, up_ref, down_ref, x_out, y_ref)

    @pl.when(pl.program_id(0) == EXPERTS - 1)
    def _():
        def group(number, unused):
            for step in range(8):
                token = number * 8 + step
                for k in range(2):
                    routed_ref[k, pl.ds(token, 1), :] = y_ref[pl.ds(slot_at[k, token], 1), :]
            return unused

        lax.fori_loop(0, x_ref.shape[0] // 8, group, 0)


def head_kernel(
    token_scale,
    meta,
    slot_at,
    slots_ref,
    x_ref,
    up_ref,
    down_ref,
    logits_ref,
    routes_ref,
    shared_ref,
    middle_ref,
    noise_ref,
    mods_ref,
    fin_ref,
    head_ref,
    pair_out,
    both_out,
    state_out,
    logits_out,
    thin_out,
    gate_out,
    fin_out,
    loss_out,
    x_out,
    routed_ref,
    y_ref,
):
    routed_blocks(meta, slots_ref, x_ref, up_ref, down_ref, x_out, y_ref)
    low = jnp.bfloat16

    @pl.when(pl.program_id(0) == EXPERTS - 1)
    def _():
        gate_out[...] = jnp.zeros_like(gate_out)
        fin_out[...] = jnp.zeros_like(fin_out)
        thin_out[...] = jnp.zeros_like(thin_out)
        loss_out[...] = jnp.zeros_like(loss_out)
        lane = lax.broadcasted_iota(jnp.int32, (PATCHES, 128), 1)

        def latent(lat, unused):
            base = pl.multiple_of(lat * PATCHES, PATCHES)
            span = pl.ds(base, PATCHES)

            def group(number, unused):
                for step in range(8):
                    token = number * 8 + step
                    for k in range(2):
                        routed_ref[k, pl.ds(token, 1), :] = y_ref[
                            pl.ds(slot_at[k, base + token], 1), :
                        ]
                return unused

            lax.fori_loop(0, PATCHES // 8, group, 0)
            hot = [
                (lane == routes_ref[span, k : k + 1]).astype(jnp.float32) for k in range(2)
            ]
            picked = [jnp.sum(hot[k] * logits_ref[span, :], 1, keepdims=True) for k in range(2)]
            most = jnp.maximum(picked[0], picked[1])
            powers = [jnp.exp(picked[k] - most) for k in range(2)]
            gates = [powers[k] / (powers[0] + powers[1]) for k in range(2)]
            moe_out = gates[0] * routed_ref[0] + gates[1] * routed_ref[1] + shared_ref[span, :]
            gate_moe = mods_ref[pl.ds(lat, 1), 5 * D :]
            normed, inv_std = layer_norm(middle_ref[span, :] + gate_moe * moe_out)
            scale = 1.0 + fin_ref[pl.ds(lat, 1), D:]
            head_in = (normed * scale + fin_ref[pl.ds(lat, 1), :D]).astype(low)
            errors = product(head_in, head_ref[...]) - noise_ref[span, :]
            loss_out[...] += jnp.sum(jnp.sum(errors * errors, 1, keepdims=True), 0, keepdims=True)
            errors = (errors * token_scale).astype(low)
            grads = contract(errors, head_ref[...], 1, 1)
            fin_out[pl.ds(lat, 1), :D] = jnp.sum(grads, 0, keepdims=True)
            fin_out[pl.ds(lat, 1), D:] = jnp.sum(grads * normed, 0, keepdims=True)
            state = norm_back(grads * scale, normed, inv_std)
            state_out[span, :] = state
            gate_out[pl.ds(lat, 1), :] = jnp.sum(moe_out * state, 0, keepdims=True)
            grads = gate_moe * state
            both_out[span, :] = grads.astype(low)
            slopes = []
            for k in range(2):
                slopes.append(jnp.sum(routed_ref[k] * grads, 1, keepdims=True))
                pair_out[k, span, :] = (gates[k] * grads).astype(low)
            usual = gates[0] * slopes[0] + gates[1] * slopes[1]
            grad_logits = (
                hot[0] * (gates[0] * (slopes[0] - usual)) + hot[1] * (gates[1] * (slopes[1] - usual))
            )
            logits_out[span, :] = grad_logits
            thin_out[...] += contract(x_ref[span, :], grad_logits.astype(low), 0, 0) + pltpu.roll(
                contract(head_in, errors, 0, 0), EXPERTS, 1
            )
            return unused

        lax.fori_loop(0, x_ref.shape[0] // PATCHES, latent, 0)


def experts_and_head(slot_of, meta, moe_in, up_full, down_full, token_scale, members):
    tokens = moe_in.shape[0]
    full, low = jnp.float32, jnp.bfloat16
    shapes = (
        ((2, tokens, D), low),
        ((tokens, D), low),
        ((tokens, D), full),
        ((tokens, 128), full),
        ((D, 128), full),
        ((8, D), full),
        ((8, 2 * D), full),
        ((1, 1), full),
        ((slot_room(tokens), D), low),
    )
    return pl.pallas_call(
        functools.partial(head_kernel, token_scale),
        grid_spec=pltpu.PrefetchScalarGridSpec(
            num_scalar_prefetch=2,
            grid=(EXPERTS,),
            in_specs=[
                whole_block((2, tokens)),
                whole_block((tokens, D)),
                pl.BlockSpec((1, NARROW_PIECES, D, D), lambda e, *unused: (e, 0, 0, 0)),
                pl.BlockSpec((1, FF, D), lambda e, *unused: (e, 0, 0)),
            ]
            + [whole_block(member.shape) for member in members],
            out_specs=[whole_block(shape) for shape, kind in shapes],
            scratch_shapes=[
                pltpu.VMEM((2, PATCHES, D), full),
                pltpu.VMEM((slot_room(tokens), D), full),
            ],
        ),
        out_shape=[jax.ShapeDtypeStruct(shape, kind) for shape, kind in shapes],
        compiler_params=pltpu.CompilerParams(vmem_limit_bytes=VMEM_ROOM),
        name="experts_and_head",
    )(meta, slot_of, slot_of, moe_in, up_full, down_full, *members)


def slot_room(tokens):
    return tokens * 2 + EXPERTS * 16 + BLK


def whole_block(shape):
    return pl.BlockSpec(shape, lambda e, *unused: (0,) * len(shape))


def experts_forward(slot_of, meta, moe_in, up_full, down_full):
    tokens = moe_in.shape[0]
    return pl.pallas_call(
        forward_kernel,
        grid_spec=pltpu.PrefetchScalarGridSpec(
            num_scalar_prefetch=2,
            grid=(EXPERTS,),
            in_specs=[
                whole_block((2, tokens)),
                whole_block((tokens, D)),
                pl.BlockSpec((1, NARROW_PIECES, D, D), lambda e, *unused: (e, 0, 0, 0)),
                pl.BlockSpec((1, FF, D), lambda e, *unused: (e, 0, 0)),
            ],
            out_specs=[whole_block((2, tokens, D)), whole_block((slot_room(tokens), D))],
            scratch_shapes=[pltpu.VMEM((slot_room(tokens), D), jnp.float32)],
        ),
        out_shape=[
            jax.ShapeDtypeStruct((2, tokens, D), jnp.float32),
            jax.ShapeDtypeStruct((slot_room(tokens), D), jnp.bfloat16),
        ],
        compiler_params=pltpu.CompilerParams(vmem_limit_bytes=VMEM_ROOM),
        cost_estimate=pl.CostEstimate(
            flops=20_000_000_000, bytes_accessed=50_000_000, transcendentals=0
        ),
        name="experts_forward",
    )(meta, slot_of, slot_of, moe_in, up_full, down_full)


def backward_kernel(
    meta,
    slot_at,
    slots_ref,
    x_ref,
    pair_ref,
    up_ref,
    down_ref,
    up_out,
    down_out,
    dx_ref,
    up_sum,
    down_sum,
    dx_slots,
):
    stack_id = pl.program_id(0)
    tokens = pair_ref.shape[1]
    up_sum[...] = jnp.zeros_like(up_sum)
    down_sum[...] = jnp.zeros_like(down_sum)

    def expert(rows, grads):
        total = None
        for cut in range(0, FF, CUT):
            up_part = up_columns(up_ref[0], cut)
            activated, slope = gelu_slope(product(rows, up_part))
            grad_act = contract(grads, down_ref[0, cut : cut + CUT], 1, 1)
            grad_pre = (grad_act * slope).astype(jnp.bfloat16)
            down_sum[cut : cut + CUT, :] += contract(activated.astype(jnp.bfloat16), grads, 0, 0)
            up_sum[:, cut : cut + CUT] += contract(rows, grad_pre, 0, 0)
            part = contract(grad_pre, up_part, 1, 1)
            total = part if total is None else total + part
        return total

    stop = meta[0, stack_id] + meta[1, stack_id]

    def run(base, size):
        place = base + lax.broadcasted_iota(jnp.int32, (size, tokens), 0)
        place = jnp.where(place < stop, place, -1)
        grads = None
        for k in range(2):
            part = product((slots_ref[k : k + 1, :] == place).astype(jnp.bfloat16), pair_ref[k])
            grads = part if grads is None else grads + part
        dx_slots[pl.ds(base, size), :] = expert(
            x_ref[pl.ds(base, size), :], grads.astype(jnp.bfloat16)
        )

    over_blocks(meta, run)
    for n in range(NARROW_PIECES):
        up_out[0, :, n] = (
            up_sum[:, n * D : (n + 1) * D]
            .astype(jnp.bfloat16)
            .reshape(WIDE_PIECES, PIECE, D)
        )
    down_out[0] = down_sum[...].astype(jnp.bfloat16).reshape(WIDE_PIECES, NARROW_PIECES, PIECE, D)

    @pl.when(stack_id == EXPERTS - 1)
    def _():
        def group(number, unused):
            for step in range(8):
                token = number * 8 + step
                dx_ref[pl.ds(token, 1), :] = (
                    dx_slots[pl.ds(slot_at[0, token], 1), :]
                    + dx_slots[pl.ds(slot_at[1, token], 1), :]
                )
            return unused

        lax.fori_loop(0, tokens // 8, group, 0)


def experts_backward(slot_of, meta, slot_rows, grad_pair, up_full, down_full):
    tokens = slot_of.shape[1]
    slabs = (EXPERTS, WIDE_PIECES, NARROW_PIECES, PIECE, D)
    slab_spec = pl.BlockSpec((1,) + slabs[1:], lambda e, *unused: (e, 0, 0, 0, 0))
    return pl.pallas_call(
        backward_kernel,
        grid_spec=pltpu.PrefetchScalarGridSpec(
            num_scalar_prefetch=2,
            grid=(EXPERTS,),
            in_specs=[
                whole_block((2, tokens)),
                whole_block(slot_rows.shape),
                whole_block((2, tokens, D)),
                pl.BlockSpec((1, NARROW_PIECES, D, D), lambda e, *unused: (e, 0, 0, 0)),
                pl.BlockSpec((1, FF, D), lambda e, *unused: (e, 0, 0)),
            ],
            out_specs=[slab_spec, slab_spec, whole_block((tokens, D))],
            scratch_shapes=[
                pltpu.VMEM((D, FF), jnp.float32),
                pltpu.VMEM((FF, D), jnp.float32),
                pltpu.VMEM((slot_room(tokens), D), jnp.float32),
            ],
        ),
        out_shape=[
            jax.ShapeDtypeStruct(slabs, jnp.bfloat16),
            jax.ShapeDtypeStruct(slabs, jnp.bfloat16),
            jax.ShapeDtypeStruct((tokens, D), jnp.float32),
        ],
        compiler_params=pltpu.CompilerParams(vmem_limit_bytes=VMEM_ROOM),
        cost_estimate=pl.CostEstimate(
            flops=45_000_000_000, bytes_accessed=90_000_000, transcendentals=0
        ),
        name="experts_backward",
    )(meta, slot_of, slot_of, slot_rows, grad_pair, up_full, down_full)


def reduce_kernel(
    down_ref,
    up_ref,
    up_all,
    down_all,
    moe_in_far,
    grad_both_far,
    dx_routed_far,
    grad_logits_far,
    middle_far,
    qkv_far,
    attended_far,
    grad_state_far,
    patches_far,
    places_far,
    mods_far,
    mats_all_far,
    bias_rows_far,
    pre_time_far,
    cond_far,
    freq_low_far,
    grad_gate_far,
    grad_fin_far,
    thin_in_far,
    label_parts_far,
    out_ref,
    rows_ref,
    lat_ref,
    bias_ref,
    own,
    got_core,
    out_one,
    keep_one,
    got_one,
    out_two,
    keep_two,
    got_two,
    got_last,
    keep_z,
    out_z,
    got_z,
    row_parts,
    late,
    up_here,
    down_here,
    up_sum,
    down_sum,
    dx_sum,
    grad_mid,
    grad_att,
    grad_qkv,
    qkv_sum,
    proj_sum,
    patch_sum,
    grad_mods,
    lat_full,
    lat_low,
    own_sem,
    core_send,
    core_recv,
    one_send,
    one_recv,
    two_send,
    two_recv,
    z_send,
    z_recv,
    row_send,
    row_recv,
    lat_own,
    lat_send,
    lat_recv,
    here_sem,
    core_free,
    one_free,
    load_sem,
    moe_in,
    grad_both,
    dx_routed,
    grad_logits,
    middle,
    qkv,
    attended,
    grad_state,
    patches,
    places,
    mods,
    mats_all,
    bias_rows,
    pre_time,
    cond,
    freq_low,
    grad_gate,
    grad_fin,
    thin_in,
    label_parts,
):
    full, low = jnp.float32, jnp.bfloat16
    loads = [
        pltpu.make_async_copy(far, near, load_sem.at[number])
        for number, (far, near) in enumerate(
            (
                (moe_in_far, moe_in),
                (grad_both_far, grad_both),
                (dx_routed_far, dx_routed),
                (grad_logits_far, grad_logits),
                (middle_far, middle),
                (qkv_far, qkv),
                (attended_far, attended),
                (grad_state_far, grad_state),
                (patches_far, patches),
                (places_far, places),
                (mods_far, mods),
                (mats_all_far, mats_all),
                (bias_rows_far, bias_rows),
                (pre_time_far, pre_time),
                (cond_far, cond),
                (freq_low_far, freq_low),
                (grad_gate_far, grad_gate),
                (grad_fin_far, grad_fin),
                (thin_in_far, thin_in),
                (label_parts_far, label_parts),
            )
        )
    ]
    for load in loads:
        load.start()
    n_down, n_up, n_late = down_ref.shape[0], up_ref.shape[0], late.shape[0]
    slabs = n_down + n_up + n_late
    ahead, ring = 2, got_core.shape[0]
    wide, narrow = lax.axis_index(WIDE), lax.axis_index(NARROW)
    z, x = wide // 2, wide % 2
    y, c = narrow // 2, narrow % 2
    x_one, y_one = x + (1 - c) * (1 - 2 * x), y + c * (1 - 2 * y)
    x_two, y_two = x + c * (1 - 2 * x), y + (1 - c) * (1 - 2 * y)
    to_one = (z * 2 + x_one, y_one * 2 + c)
    to_two = (z * 2 + x_two, y_two * 2 + c)
    first_mine = x * (1 - c) + y * c
    second_mine = y * (1 - c) + x * c
    first_step, second_step = 2 - c, 1 + c
    mates = [
        (wide, (y + (k // 2) * (1 - 2 * y)) * 2 + c + (k % 2) * (1 - 2 * c)) for k in range(1, 4)
    ]
    levels = [(((z + k) % 4) * 2 + x, narrow) for k in range(1, 4)]
    to_x, to_core = (z * 2 + 1 - x, narrow), mates[0]
    barrier = pltpu.get_barrier_semaphore()
    for target in mates + levels + [to_x]:
        pl.semaphore_signal(barrier, inc=1, device_id=target, device_id_type=MESH_ID)
    pl.semaphore_wait(barrier, 7)

    def remote(source, target, send, recv, device):
        return pltpu.make_async_remote_copy(
            src_ref=source,
            dst_ref=target,
            send_sem=send,
            recv_sem=recv,
            device_id=device,
            device_id_type=MESH_ID,
        )

    def core_copy(source, s):
        return remote(
            source.at[:, 1 - c],
            got_core.at[s % ring],
            core_send.at[s % 4],
            core_recv.at[s % ring],
            to_core,
        )

    def own_copy(source, s):
        return pltpu.make_async_copy(source.at[:, c], own.at[s % 3], own_sem.at[s % 3])

    def one_copy(s):
        return remote(
            out_one.at[s % 2], got_one.at[s % ring], one_send.at[s % 2], one_recv.at[s % ring], to_one
        )

    def two_copy(s, turned=False):
        if turned:
            start, end = out_two.at[s % 2, 0], got_last.at[s // 2]
        else:
            start, end = out_two.at[s % 2], got_two.at[s // 2]
        return remote(start, end, two_send.at[s % 2], two_recv.at[s], to_two)

    def z_copy(s, k, turned=False):
        start, end = out_z.at[s % 2, (z + k) % 4], got_z.at[s, k - 1]
        if not turned:
            start, end = start.at[0], end.at[0]
        return remote(start, end, z_send.at[s % 2, k - 1], z_recv.at[s, k - 1], levels[k - 1])

    def by_order(s, run):
        turned = s % 2 == 1

        @pl.when(turned)
        def _():
            run(True)

        @pl.when(jnp.logical_not(turned))
        def _():
            run(False)

    def row_copy(r, k):
        mate = mates[k - 1]
        return remote(
            row_parts.at[r % 2, mate[1]],
            rows_ref.at[r, narrow],
            row_send.at[r % 2, k - 1],
            row_recv.at[r, k - 1],
            mate,
        )

    def lat_level(k):
        return remote(
            lat_low, lat_ref.at[z, x, y, c], lat_send.at[k - 1], lat_recv.at[k - 1], levels[k - 1]
        )

    def lat_x():
        spot = lat_ref.at[:, x, y, c]
        return remote(spot, spot, lat_send.at[3], lat_recv.at[3], to_x)

    def lat_y():
        spot = lat_ref.at[:, :, y, c]
        return remote(spot, spot, lat_send.at[4], lat_recv.at[4], mates[1])

    def lat_core():
        spot = lat_ref.at[:, :, :, c]
        return remote(spot, spot, lat_send.at[5], lat_recv.at[5], to_core)

    def lat_own_copy():
        return pltpu.make_async_copy(lat_low, lat_ref.at[z, x, y, c], lat_own.at[0])

    def begin(source, s):
        @pl.when(s >= 4)
        def _():
            core_copy(source, s).wait_send()

        @pl.when(s >= ring)
        def _():
            pl.semaphore_wait(core_free, 1)

        core_copy(source, s).start()
        own_copy(source, s).start()

    def stage_core(s):
        own_copy(down_ref.at[0], s).wait()
        core_copy(down_ref.at[0], s).wait_recv()

        @pl.when(s >= 2)
        def _():
            one_copy(s).wait_send()

        @pl.when(s >= ring)
        def _():
            pl.semaphore_wait(one_free, 1)

        for level in range(4):
            for other in range(2):
                place = level * 2 + other
                base = level * 4 + other * second_step
                send_at = base + (1 - first_mine) * first_step
                out_one[s % 2, place] = (
                    own[s % 3, send_at].astype(full) + got_core[s % ring, send_at].astype(full)
                ).astype(low)
        one_copy(s).start()
        for level in range(4):
            for other in range(2):
                place = level * 2 + other
                base = level * 4 + other * second_step
                keep_at = base + first_mine * first_step
                keep_one[s % 3, place] = own[s % 3, keep_at].astype(full) + got_core[
                    s % ring, keep_at
                ].astype(full)

        @pl.when(s < slabs - ring)
        def _():
            pl.semaphore_signal(core_free, inc=1, device_id=to_core, device_id_type=MESH_ID)

    def stage_one(s):
        one_copy(s).wait_recv()

        def run(turned):
            @pl.when(s >= 2)
            def _():
                sent(s, turned)

            if turned:
                for level in range(4):
                    for other in range(2):
                        out_z[s % 2, level, other] = (
                            keep_one[s % 3, level * 2 + other]
                            + got_one[s % ring, level * 2 + other].astype(full)
                        ).astype(low)
                for k in range(1, 4):
                    z_copy(s, k, True).start()
                for other in range(2):
                    keep_two[s % 3, other] = keep_one[s % 3, z * 2 + other] + got_one[
                        s % ring, z * 2 + other
                    ].astype(full)
            else:
                for level in range(4):
                    send_at = level * 2 + 1 - second_mine
                    out_two[s % 2, level] = (
                        keep_one[s % 3, send_at] + got_one[s % ring, send_at].astype(full)
                    ).astype(low)
                two_copy(s).start()
                for level in range(4):
                    keep_at = level * 2 + second_mine
                    keep_two[s % 3, level] = keep_one[s % 3, keep_at] + got_one[
                        s % ring, keep_at
                    ].astype(full)

        by_order(s, run)

        @pl.when(s < slabs - ring)
        def _():
            pl.semaphore_signal(one_free, inc=1, device_id=to_one, device_id_type=MESH_ID)

    def sent(s, turned):
        if turned:
            for k in range(1, 4):
                z_copy(s, k, True).wait_send()
        else:
            two_copy(s).wait_send()

    def sent_last(s, turned):
        if turned:
            two_copy(s, True).wait_send()
        else:
            for k in range(1, 4):
                z_copy(s, k).wait_send()

    def stage_two(s):
        def run(turned):
            if turned:
                for k in range(1, 4):
                    z_copy(s, k, True).wait_recv()
            else:
                two_copy(s).wait_recv()

            @pl.when(s >= 2)
            def _():
                sent_last(s, turned)

            if turned:

                def gathered(other):
                    total = keep_two[s % 3, other]
                    for k in range(3):
                        total = total + got_z[s, k, other].astype(full)
                    return total

                out_two[s % 2, 0] = gathered(1 - second_mine).astype(low)
                two_copy(s, True).start()
                keep_z[s % 3] = gathered(second_mine)
            else:
                for level in range(4):
                    out_z[s % 2, level, 0] = (
                        keep_two[s % 3, level] + got_two[s // 2, level].astype(full)
                    ).astype(low)
                for k in range(1, 4):
                    z_copy(s, k).start()
                keep_z[s % 3] = keep_two[s % 3, z] + got_two[s // 2, z].astype(full)

        by_order(s, run)

    def direct_place(s):
        late_at = s - n_down - n_up
        return (s < n_down) | ((late_at >= 0) & (late_at < SHARED))

    def row_place(s):
        return jnp.where(s < n_down + n_up, s - n_down, s - n_down - SHARED)

    def finish(s):
        def run(turned):
            if turned:
                two_copy(s, True).wait_recv()
                keep_z[s % 3] += got_last[s // 2].astype(full)
            else:
                for k in range(1, 4):
                    z_copy(s, k).wait_recv()
                total = keep_z[s % 3]
                for k in range(3):
                    total = total + got_z[s, k, 0].astype(full)
                keep_z[s % 3] = total

        by_order(s, run)
        total = keep_z[s % 3]

        @pl.when(direct_place(s))
        def _():
            out_ref[jnp.clip(jnp.where(s < n_down, s, s - n_up), 0, n_down + SHARED - 1)] = total

        @pl.when(jnp.logical_not(direct_place(s)))
        def _():
            r = row_place(s)

            @pl.when(r >= 2)
            def _():
                for k in range(1, 4):
                    row_copy(r, k).wait_send()

            for n in range(NARROW_PIECES):
                row_parts[r % 2, n] = total[n * ROWS : (n + 1) * ROWS]
            rows_ref[r, narrow] = row_parts[r % 2, narrow]
            for k in range(1, 4):
                row_copy(r, k).start()

    def rows_in(s):
        @pl.when(jnp.logical_not(direct_place(s)))
        def _():
            for k in range(1, 4):
                row_copy(row_place(s), k).wait_recv()

    tokens = moe_in.shape[0]
    lats = tokens // PATCHES

    def matrix(number, start, stop):
        chunk = mats_all[number // 2, number % 2]
        return chunk.reshape(D, chunk.shape[-1])[:, start:stop]

    def mod_row(start, number):
        return mods[pl.ds(start // PATCHES, 1), number * D : (number + 1) * D]

    def keep_mod(start, number, values):
        grad_mods[pl.ds(start // PATCHES, 1), number * D : (number + 1) * D] = jnp.sum(
            values, 0, keepdims=True
        )

    def add_bias(number, values):
        for k in range(values.shape[1] // D):
            bias_ref[number + k : number + k + 1, :] += jnp.sum(
                values[:, k * D : (k + 1) * D], 0, keepdims=True
            )

    def prepare():
        bias_ref[...] = jnp.zeros_like(bias_ref)
        qkv_sum[...] = jnp.zeros_like(qkv_sum)
        proj_sum[...] = jnp.zeros_like(proj_sum)
        patch_sum[...] = jnp.zeros_like(patch_sum)
        grad_mods[...] = jnp.zeros_like(grad_mods)

    def fetch(shared_id):
        e = EXPERTS + shared_id
        first = pltpu.make_async_copy(down_all.at[e], down_here, here_sem.at[0])
        second = pltpu.make_async_copy(up_all.at[e], up_here, here_sem.at[1])
        first.start()
        second.start()
        first.wait()
        second.wait()
        up_sum[...] = jnp.zeros_like(up_sum)
        down_sum[...] = jnp.zeros_like(down_sum)

    def shared_block(shared_id, start):
        span = pl.ds(start, PATCHES)
        rows, grads = moe_in[span, :], grad_both[span, :]
        total = dx_routed[span, :] if shared_id == 0 else dx_sum[span, :]
        for cut in range(0, FF, CUT):
            up_part = up_columns(up_here, cut)
            activated, slope = gelu_slope(product(rows, up_part))
            grad_act = contract(grads, down_here[cut : cut + CUT], 1, 1)
            grad_pre = (grad_act * slope).astype(low)
            down_sum[cut : cut + CUT, :] += contract(activated.astype(low), grads, 0, 0)
            up_sum[:, cut : cut + CUT] += contract(rows, grad_pre, 0, 0)
            total = total + contract(grad_pre, up_part, 1, 1)
        dx_sum[span, :] = total

    def shared_slabs(shared_id):
        for w in range(WIDE_PIECES):
            for n in range(NARROW_PIECES):
                at = (w * NARROW_PIECES + n) * PIECE
                late[shared_id, w * 2 + n // 2, n % 2] = down_sum[at : at + PIECE, :].astype(low)
                late[SHARED + shared_id, w * 2 + n // 2, n % 2] = up_sum[
                    w * PIECE : (w + 1) * PIECE, n * D : (n + 1) * D
                ].astype(low)

    def back_out(start):
        span = pl.ds(start, PATCHES)
        grads = dx_sum[span, :] + contract(
            grad_logits[span, :].astype(low), matrix(0, 4 * D, 4 * D + 128), 1, 1
        )
        normed, inv_std = layer_norm(middle[span, :])
        keep_mod(start, 3, grads)
        keep_mod(start, 4, grads * normed)
        grads = grad_state[span, :] + norm_back(
            grads * (1.0 + mod_row(start, 4)), normed, inv_std
        )
        grad_mid[...] = grads
        proj = matrix(0, 3 * D, 4 * D)
        rows = attended[span, :]
        keep_mod(start, 2, (product(rows, proj) + bias_rows[3:4, :]) * grads)
        grads = grads * mod_row(start, 2)
        add_bias(3, grads)
        grads = grads.astype(low)
        proj_sum[...] += contract(rows, grads, 0, 0)
        grad_att[...] = contract(grads, proj, 1, 1).astype(low)

    def back_pair(pair, start):
        span = pl.ds(start, PATCHES)
        lane = lax.broadcasted_iota(jnp.int32, (PATCHES, 2 * HD), 1)
        at = pair * 2 * HD
        queries = qkv[span, at : at + 2 * HD]
        keys = qkv[span, D + at : D + at + 2 * HD]
        values = qkv[span, 2 * D + at : 2 * D + at + 2 * HD]
        grads = grad_att[:, at : at + 2 * HD]
        sums = None
        for half in range(2):
            mine = (lane < HD) if half == 0 else (lane >= HD)
            scores = contract(jnp.where(mine, queries, 0), keys, 1, 1) * HD ** (-0.5)
            powers = jnp.exp(scores - jnp.max(scores, 1, keepdims=True))
            probs = powers / jnp.sum(powers, 1, keepdims=True)
            grad_mine = jnp.where(mine, grads, 0)
            grad_probs = contract(grad_mine, values, 1, 1)
            grad_scores = (
                probs
                * (grad_probs - jnp.sum(probs * grad_probs, 1, keepdims=True))
                * HD ** (-0.5)
            ).astype(low)
            parts = (
                product(grad_scores, jnp.where(mine, keys, 0)),
                contract(grad_scores, jnp.where(mine, queries, 0), 0, 0),
                contract(probs.astype(low), grad_mine, 0, 0),
            )
            sums = parts if sums is None else [a + b for a, b in zip(sums, parts)]
        for k in range(3):
            where = k * D + at
            grad_qkv[:, where : where + 2 * HD] = sums[k].astype(low)
            bias_ref[k : k + 1, at : at + 2 * HD] += jnp.sum(sums[k], 0, keepdims=True)

    def back_in(start):
        span = pl.ds(start, PATCHES)
        emb = contract(patches[span, :], matrix(2, 4 * D, 4 * D + 128), 1, 1)
        emb = emb + bias_rows[10:11, :] + places[...]
        normed, inv_std = layer_norm(emb)
        rows = (normed * (1.0 + mod_row(start, 1)) + mod_row(start, 0)).astype(low)
        qkv_sum[...] += contract(rows, grad_qkv[...], 0, 0)
        grads = contract(grad_qkv[...], matrix(0, 0, 3 * D), 1, 1)
        keep_mod(start, 0, grads)
        keep_mod(start, 1, grads * normed)
        grads = grad_mid[...] + norm_back(grads * (1.0 + mod_row(start, 1)), normed, inv_std)
        add_bias(10, grads)
        patch_sum[...] += contract(grads.astype(low), patches[span, :], 0, 0)

    def silu_slope(values):
        gate = jax.nn.sigmoid(values)
        return gate + values * gate * (1.0 - gate)

    def back_conditions():
        grad_mods[:, 5 * D :] = grad_gate[...]
        grads = grad_mods[...]
        mod_low, fin_low = grads.astype(low), grad_fin[...].astype(low)
        grad_act = (
            contract(mod_low[:, : 4 * D], matrix(1, 0, 4 * D), 1, 1)
            + contract(mod_low[:, 4 * D :], matrix(2, 0, 2 * D), 1, 1)
            + contract(fin_low, matrix(2, 2 * D, 4 * D), 1, 1)
        )
        grad_cond = silu_slope(cond[...]) * grad_act
        high = grad_cond.astype(low)
        grad_time = silu_slope(pre_time[...]) * contract(high, matrix(3, 1024, 1408), 1, 1)
        add_bias(4, grads)
        add_bias(11, grad_time)
        add_bias(12, grad_cond)
        add_bias(13, grad_fin[...])
        high = high.astype(full)
        rest = grad_cond - high
        middle_part = rest.astype(low).astype(full)
        act = jax.nn.silu(cond[...]).astype(low).astype(full)
        hid = jax.nn.silu(pre_time[...]).astype(low).astype(full)
        mod_low, fin_low = mod_low.astype(full), fin_low.astype(full)
        quarters = (
            jnp.concatenate([act, hid, mod_low[:, : 2 * D]], 1),
            mod_low[:, 2 * D :],
            jnp.concatenate([fin_low, high, grad_time.astype(low).astype(full)], 1),
            jnp.concatenate(
                [
                    freq_low[...].astype(full),
                    middle_part,
                    rest - middle_part,
                    label_parts[...].astype(full),
                    jnp.zeros((8, D), full),
                ],
                1,
            ),
        )
        for lat in range(lats):
            for k in range(4):
                lat_full[lat * 4 + k : lat * 4 + k + 1, :] = quarters[k][lat : lat + 1, :]
        lat_low[...] = lat_full[...].astype(low)

    def last_slabs():
        for w in range(WIDE_PIECES):
            span = slice(w * PIECE, (w + 1) * PIECE)
            for n in range(3):
                late[2 * SHARED, w * 2 + n // 2, n % 2] = qkv_sum[
                    span, n * D : (n + 1) * D
                ].astype(low)
            late[2 * SHARED, w * 2 + 1, 1] = proj_sum[span, :].astype(low)
            thin = thin_in[span, :] + pltpu.roll(patch_sum[span, :], EXPERTS + PD, 1)
            for n in range(NARROW_PIECES):
                late[2 * SHARED + 1, w * 2 + n // 2, n % 2] = jnp.zeros((PIECE, D), low)
            late[2 * SHARED + 1, w * 2, 0, :, :128] = thin.astype(low)

    first_lat = SHARED * lats
    units = (
        back_out,
        lambda start: back_pair(0, start),
        lambda start: back_pair(1, start),
        lambda start: back_pair(2, start),
        back_in,
    )
    after = first_lat + len(units) * lats

    def tick(t, unused):
        first = 0
        for source, count in ((down_ref, n_down), (up_ref, n_up), (late, n_late)):

            @pl.when((t >= first) & (t < first + count))
            def _():
                begin(source.at[jnp.clip(t - first, 0, count - 1)], t)

            first += count

        for lag, stage in enumerate((stage_core, stage_one, stage_two, finish, rows_in)):
            s = t - ahead - 2 * lag

            @pl.when((s >= 0) & (s < slabs))
            def _():
                stage(s)

        @pl.when(t == 0)
        def _():
            prepare()
            for load in loads[:3]:
                load.wait()

        @pl.when(t == first_lat)
        def _():
            for load in loads[3:]:
                load.wait()

        for shared_id in range(SHARED):
            start_at = shared_id * lats

            @pl.when(t == start_at)
            def _():
                fetch(shared_id)

            @pl.when((t >= start_at) & (t < start_at + lats))
            def _():
                shared_block(
                    shared_id,
                    pl.multiple_of(jnp.clip(t - start_at, 0, lats - 1) * PATCHES, PATCHES),
                )

            @pl.when(t == start_at + lats - 1)
            def _():
                shared_slabs(shared_id)

        for number, unit in enumerate(units):

            @pl.when((t >= first_lat) & (t < after) & ((t - first_lat) % len(units) == number))
            def _():
                lat = jnp.clip((t - first_lat) // len(units), 0, lats - 1)
                unit(pl.multiple_of(lat * PATCHES, PATCHES))

        @pl.when(t == after)
        def _():
            back_conditions()
            lat_own_copy().start()
            for k in range(1, 4):
                lat_level(k).start()
            lat_own_copy().wait()

        @pl.when(t == after + 1)
        def _():
            last_slabs()

        @pl.when(t == after + 3)
        def _():
            for k in range(1, 4):
                lat_level(k).wait_recv()
            lat_x().start()

        @pl.when(t == after + 5)
        def _():
            lat_x().wait_recv()
            lat_y().start()

        @pl.when(t == after + 7)
        def _():
            lat_y().wait_recv()
            lat_core().start()

        return unused

    lax.fori_loop(0, slabs + ahead + 8, tick, 0)
    for back in range(4):
        core_copy(down_ref.at[0], slabs - 1 - back).wait_send()
    turned = rows_ref.shape[0]
    for back in range(2):
        s = slabs - 1 - back
        one_copy(s).wait_send()
        sent(s, s % 2 == 1)
        sent_last(s, s % 2 == 1)
        for k in range(1, 4):
            row_copy(turned - 1 - back, k).wait_send()
    for k in range(1, 4):
        lat_level(k).wait_send()
    lat_x().wait_send()
    lat_y().wait_send()
    lat_core().wait()


def reduce_slabs(down_slabs, up_slabs, up_all, down_all, members):
    n_late = 2 * SHARED + 2
    routed = down_slabs.shape[0]
    slabs = 2 * routed + n_late
    direct, turned = routed + SHARED, routed + SHARED + 2
    ring = 4
    low, full = jnp.bfloat16, jnp.float32
    sources = [
        member.reshape(routed, WIDE_PIECES * NARROW_PIECES // 2, 2, PIECE, D)
        for member in (down_slabs, up_slabs)
    ]
    tokens = members[0].shape[0]
    dma, regular = pltpu.SemaphoreType.DMA, pltpu.SemaphoreType.REGULAR
    vmem, anywhere = pl.BlockSpec(memory_space=pltpu.VMEM), pl.BlockSpec(memory_space=pl.ANY)
    sums, rows, lats, bias_sum = pl.pallas_call(
        reduce_kernel,
        out_shape=[
            jax.ShapeDtypeStruct((direct, PIECE, D), full),
            jax.ShapeDtypeStruct((turned, NARROW_PIECES, ROWS, D), full),
            jax.ShapeDtypeStruct((4, 2, 2, 2, LAT_ROWS, LAT_COLS), low),
            jax.ShapeDtypeStruct((16, D), full),
        ],
        in_specs=[anywhere] * (4 + len(members)),
        out_specs=[vmem, vmem, anywhere, vmem],
        scratch_shapes=[
            pltpu.VMEM((3, 16, PIECE, D), low),
            pltpu.VMEM((ring, 16, PIECE, D), low),
            pltpu.VMEM((2, 8, PIECE, D), low),
            pltpu.VMEM((3, 8, PIECE, D), full),
            pltpu.VMEM((ring, 8, PIECE, D), low),
            pltpu.VMEM((2, 4, PIECE, D), low),
            pltpu.VMEM((3, 4, PIECE, D), full),
            pltpu.VMEM(((slabs + 1) // 2, 4, PIECE, D), low),
            pltpu.VMEM(((slabs + 1) // 2, PIECE, D), low),
            pltpu.VMEM((3, PIECE, D), full),
            pltpu.VMEM((2, 4, 2, PIECE, D), low),
            pltpu.VMEM((slabs, 3, 2, PIECE, D), low),
            pltpu.VMEM((2, NARROW_PIECES, ROWS, D), full),
            pltpu.VMEM((n_late, 16, 2, PIECE, D), low),
            pltpu.VMEM((NARROW_PIECES, D, D), low),
            pltpu.VMEM((FF, D), low),
            pltpu.VMEM((D, FF), full),
            pltpu.VMEM((FF, D), full),
            pltpu.VMEM((tokens, D), full),
            pltpu.VMEM((PATCHES, D), full),
            pltpu.VMEM((PATCHES, D), low),
            pltpu.VMEM((PATCHES, 3 * D), low),
            pltpu.VMEM((D, 3 * D), full),
            pltpu.VMEM((D, D), full),
            pltpu.VMEM((D, 128), full),
            pltpu.VMEM((8, 6 * D), full),
            pltpu.VMEM((LAT_ROWS, LAT_COLS), full),
            pltpu.VMEM((LAT_ROWS, LAT_COLS), low),
            dma((3,)),
            dma((4,)),
            dma((ring,)),
            dma((2,)),
            dma((ring,)),
            dma((2,)),
            dma((slabs,)),
            dma((2, 3)),
            dma((slabs, 3)),
            dma((2, 3)),
            dma((turned, 3)),
            dma((1,)),
            dma((6,)),
            dma((6,)),
            dma((2,)),
            regular,
            regular,
            dma((len(members),)),
        ]
        + [pltpu.VMEM(member.shape, member.dtype) for member in members],
        compiler_params=pltpu.CompilerParams(
            collective_id=0, has_side_effects=True, vmem_limit_bytes=REDUCE_ROOM
        ),
        name="reduce_slabs",
    )(*sources, up_all, down_all, *members)
    return sums, rows, lats.reshape(-1, LAT_COLS), bias_sum


def plain_grads(
    down_slabs, up_slabs, mats_slabs, thin, grad_bias, lows, grad_cond, labels, row_count
):
    def scattered(member):
        return lax.psum_scatter(member, AXES, scatter_dimension=1, tiled=True)

    proj_grad = scattered(mats_slabs)
    row_start = lax.axis_index(AXES) * row_count
    thin_grad = lax.psum_scatter(thin, AXES, scatter_dimension=0, tiled=True)
    bias_grad = lax.psum_scatter(grad_bias, AXES, scatter_dimension=0, tiled=True)
    grad_mod, grad_time2, grad_fin, grad_time1, grad_table = latent_grads(
        lows, grad_cond, labels, row_start, row_count
    )
    mats_grad = jnp.concatenate(
        [proj_grad[0], grad_mod, grad_time2, grad_fin, thin_grad, grad_time1, grad_table], 1
    )
    return (mats_grad, scattered(up_slabs), scattered(down_slabs), bias_grad)


def spread(value, place):
    lane = lax.broadcasted_iota(jnp.int32, (1, 128), 1)
    return jnp.where(lane == place, value, 0.0)


def pick(row, place):
    lane = lax.broadcasted_iota(jnp.int32, (1, 128), 1)
    return jnp.sum(jnp.where(lane == place, row, 0.0), 1, keepdims=True)


def total(values):
    return jnp.sum(jnp.sum(values, 1, keepdims=True), 0, keepdims=True)


def turn_line(values):
    count = max(values.shape)
    same = lax.broadcasted_iota(jnp.int32, (count, count), 0) == lax.broadcasted_iota(
        jnp.int32, (count, count), 1
    )
    across = 1 if values.shape[0] == 1 else 0
    return jnp.sum(jnp.where(same, values, 0.0), across, keepdims=True)


def joined(chunks):
    return jnp.concatenate([chunks[j] for j in range(NARROW_PIECES)], 1)


def by_piece(values, start_last, width_last):
    bounds = [sum(column_widths()[:k]) for k in range(len(column_widths()) + 1)]
    last_lane = lax.broadcasted_iota(jnp.int32, (ROWS, width_last), 1) + start_last
    chosen_value = values[0]
    for k in range(6, len(column_widths())):
        chosen_value = jnp.where(last_lane >= bounds[k], values[k - 5], chosen_value)
    return chosen_value


def factored(grad, row, col, mean):
    return grad * lax.rsqrt(row * col / mean)


def update_kernel(
    sums_ref,
    rows_ref,
    lat_ref,
    bias_sum,
    loss_ref,
    mats_row,
    mats_col,
    up_row,
    up_col,
    down_row,
    down_col,
    bias_state,
    mats_grad,
    mats_row_new,
    mats_col_new,
    up_row_new,
    up_col_new,
    down_row_new,
    down_col_new,
    bias_grad,
    bias_state_new,
    line_out,
    squares_out,
    part,
    got_plane,
    got_level,
    result,
    squares_plane,
    squares_level,
    sems,
):
    full, low = jnp.float32, jnp.bfloat16
    wide, narrow = lax.axis_index(WIDE), lax.axis_index(NARROW)
    z, spot = wide // 2, (wide % 2) * 4 + narrow

    def plane_device(k):
        there = (spot + k) % 8
        return (z * 2 + there // 4, there % 4)

    def level_device(k):
        return (((z + k) % 4) * 2 + wide % 2, narrow)

    barrier = pltpu.get_barrier_semaphore()
    for k in range(1, 8):
        pl.semaphore_signal(barrier, inc=1, device_id=plane_device(k), device_id_type=MESH_ID)
    for k in range(1, 4):
        pl.semaphore_signal(barrier, inc=1, device_id=level_device(k), device_id_type=MESH_ID)
    pl.semaphore_wait(barrier, 10)

    def remote(source, target, phase, k, device):
        return pltpu.make_async_remote_copy(
            src_ref=source,
            dst_ref=target,
            send_sem=sems.at[0, phase, k],
            recv_sem=sems.at[1, phase, k],
            device_id=device,
            device_id_type=MESH_ID,
        )

    def exchange(copies):
        for copy in copies:
            copy.start()
        for copy in copies:
            copy.wait()

    count = lat_ref.shape[0] // 4
    order = lax.broadcasted_iota(jnp.int32, (count, count * 4), 0) * 4
    place = lax.broadcasted_iota(jnp.int32, (count, count * 4), 1)
    quarters = [
        product((place == order + k).astype(low), lat_ref[...]).astype(low) for k in range(4)
    ]
    owner_row = (wide * NARROW_PIECES + narrow) * ROWS
    chosen = (
        lax.broadcasted_iota(jnp.int32, (16, D), 1)
        == lax.broadcasted_iota(jnp.int32, (16, D), 0) + owner_row
    ).astype(low)

    def rows_of(member):
        return contract(chosen, member, 1, 1).astype(low)

    act_rows = rows_of(quarters[0][:, :D])
    hid_rows = rows_of(quarters[0][:, D : 2 * D])
    high = quarters[2][:, 2 * D : 3 * D]
    for j in range(NARROW_PIECES):
        mats_grad[:, j * D : (j + 1) * D] = rows_ref[EXPERTS + SHARED, j]
    mats_grad[:, 4 * D : 6 * D] = product(act_rows, quarters[0][:, 2 * D :])[:ROWS]
    mats_grad[:, 6 * D : 10 * D] = product(act_rows, quarters[1])[:ROWS]
    mats_grad[:, 10 * D : 11 * D] = product(hid_rows, high)[:ROWS]
    mats_grad[:, 11 * D : 13 * D] = product(act_rows, quarters[2][:, : 2 * D])[:ROWS]
    time_rows = rows_of(quarters[2][:, 3 * D :])
    time_one = product(time_rows, quarters[3][:, :FREQ])
    label_at = FREQ + 2 * D
    labels = quarters[3][:, label_at : label_at + 128].astype(full)
    label = labels[:, 0:1] * 32.0 + labels[:, 1:2]
    label_hot = (
        lax.broadcasted_iota(jnp.int32, (count, 1024), 1).astype(full) == label
    ).astype(low)
    table = (
        product(rows_of(high), label_hot)
        + product(rows_of(quarters[3][:, FREQ : FREQ + D]), label_hot)
        + product(rows_of(quarters[3][:, FREQ + D : FREQ + 2 * D]), label_hot)
    )
    start_last = 13 * D
    width_last = mats_grad.shape[1] - start_last
    room = 11 * 128
    thin = jnp.concatenate(
        [rows_ref[EXPERTS + SHARED + 1, 0][:, :128], jnp.zeros((4, 128), full)], 0
    )
    thin = jnp.where(
        lax.broadcasted_iota(jnp.int32, (16, 128), 1) < EXPERTS + 2 * PD, thin, 0.0
    )

    def padded(member):
        return jnp.concatenate(
            [member, jnp.zeros((16, room - member.shape[1]), full)], 1
        )

    last = (
        padded(thin)
        + pltpu.roll(padded(time_one), EXPERTS + 2 * PD, 1)
        + pltpu.roll(padded(table), EXPERTS + 2 * PD + FREQ, 1)
    )
    mats_grad[:, start_last:] = last[:ROWS, :width_last]

    part[...] = jnp.zeros_like(part)
    widths = column_widths()
    mats_at, line_at, bias_at = 360, 416, 432
    total_cols = mats_grad.shape[1]
    cuts = [(at, min(at + 128, total_cols)) for at in range(0, total_cols, 128)]
    for number, (begin, end) in enumerate(cuts):
        values = mats_grad[:, begin:end]
        part[mats_at + number : mats_at + number + 1, : end - begin] = jnp.sum(
            values * values + eps_fact, 0, keepdims=True
        )
    bounds = [sum(widths[:k]) for k in range(len(widths) + 1)]
    last_lane = lax.broadcasted_iota(jnp.int32, (ROWS, width_last), 1) + start_last
    last_sq = mats_grad[:, start_last:] * mats_grad[:, start_last:] + eps_fact
    line = spread(loss_ref[...], 46)
    for k in range(len(widths)):
        if k < 5:
            values = mats_grad[:, bounds[k] : bounds[k + 1]]
            sq = values * values + eps_fact
        else:
            sq = jnp.where((last_lane >= bounds[k]) & (last_lane < bounds[k + 1]), last_sq, 0.0)
        new = decay * turn_line(mats_row[k : k + 1, :]) + (1.0 - decay) * (
            jnp.sum(sq, 1, keepdims=True) / widths[k]
        )
        mats_row_new[k : k + 1, :] = turn_line(new)
        line = line + spread(jnp.sum(new, 0, keepdims=True), k)

    def begin_up(e, line):
        values = joined(rows_ref[e])
        sq = values * values + eps_fact
        new = decay * turn_line(up_row[pl.ds(e, 1), :]) + (1.0 - decay) * (jnp.sum(sq, 1, keepdims=True) / FF)
        up_row_new[pl.ds(e, 1), :] = turn_line(new)
        cols = jnp.sum(sq, 0, keepdims=True)
        for k in range(FF // 128):
            part[pl.ds(24 * k + e, 1), :] = cols[:, 128 * k : 128 * (k + 1)]
        return line + spread(jnp.sum(new, 0, keepdims=True), 10 + e)

    def begin_down(e, line):
        values = sums_ref[e]
        sq = values * values + eps_fact
        new = decay * turn_line(down_row[pl.ds(e, 1), :]) + (1.0 - decay) * (jnp.sum(sq, 1, keepdims=True) / D)
        down_row_new[pl.ds(e, 1), :] = turn_line(new)
        cols = jnp.sum(sq, 0, keepdims=True)
        for k in range(D // 128):
            part[pl.ds(24 * (12 + k) + e, 1), :] = cols[:, 128 * k : 128 * (k + 1)]
        return line + spread(jnp.sum(new, 0, keepdims=True), 28 + e)

    line = lax.fori_loop(0, EXPERTS + SHARED, begin_up, line)
    line = lax.fori_loop(0, EXPERTS + SHARED, begin_down, line)
    part[line_at : line_at + 1, :] = line
    for k in range(D // 128):
        part[bias_at + 16 * k : bias_at + 16 * (k + 1), :] = bias_sum[:, 128 * k : 128 * (k + 1)]

    exchange(
        [
            remote(
                part.at[pl.ds(((spot + k) % 8) * 64, 64)], got_plane.at[k], 0, k, plane_device(k)
            )
            for k in range(1, 8)
        ]
    )
    here = part[pl.ds(pl.multiple_of(spot * 64, 64), 64), :]
    for k in range(1, 8):
        here = here + got_plane[k]
    got_level[z] = here.reshape(4, 16, 128)
    exchange(
        [remote(got_level.at[z], got_level.at[z], 1, k, level_device(k)) for k in range(1, 4)]
    )
    result[spot] = got_level[0] + got_level[1] + got_level[2] + got_level[3]
    exchange(
        [remote(result.at[spot], result.at[spot], 3, k, plane_device(k)) for k in range(1, 8)]
    )

    def sums_row(row, width=128):
        if isinstance(row, int):
            return result[row // 64, (row // 16) % 4, row % 16 : row % 16 + 1, :width]
        return result[row // 64, (row // 16) % 4, pl.ds(row % 16, 1), :width]

    line = sums_row(line_at)
    line_out[...] = line
    room = bias_grad.shape[1]
    begin = (wide * NARROW_PIECES + narrow) * room
    parts = []
    for k in range(3):
        block = jnp.minimum(begin // 128 + k, 47)
        parts.append(sums_row(bias_at + (block % 3) * 16 + block // 3))
    parts = jnp.broadcast_to(jnp.concatenate(parts, 1), (8, D))
    bias_grad[...] = pltpu.roll(parts, (D - begin % 128) % D, 1)[0:1, :room]
    for number, (begin, end) in enumerate(cuts):
        mats_col_new[:, begin:end] = decay * mats_col[:, begin:end] + (1.0 - decay) * (
            sums_row(mats_at + number, end - begin) / D
        )

    squares = jnp.zeros((1, 128), full)
    for k in range(5):
        begin, end = bounds[k], bounds[k + 1]
        step = factored(
            mats_grad[:, begin:end],
            turn_line(mats_row_new[k : k + 1, :]),
            mats_col_new[:, begin:end],
            pick(line, k) / D,
        )
        squares = squares + spread(total(step * step), k)
    last = range(5, len(widths))
    step_last = factored(
        mats_grad[:, start_last:],
        by_piece([turn_line(mats_row_new[k : k + 1, :]) for k in last], start_last, width_last),
        mats_col_new[:, start_last:],
        by_piece([pick(line, k) / D for k in last], start_last, width_last),
    )
    for k in last:
        inside = (last_lane >= bounds[k]) & (last_lane < bounds[k + 1])
        squares = squares + spread(total(jnp.where(inside, step_last * step_last, 0.0)), k)

    def step_up(e, squares):
        cols = jnp.concatenate([sums_row(24 * k + e) for k in range(FF // 128)], 1)
        new = decay * up_col[pl.ds(e, 1), :] + (1.0 - decay) * (cols / D)
        up_col_new[pl.ds(e, 1), :] = new
        row = turn_line(up_row_new[pl.ds(e, 1), :])
        step = factored(joined(rows_ref[e]), row, new, pick(line, 10 + e) / D)
        return squares + spread(total(step * step), 10 + e)

    def step_down(e, squares):
        cols = jnp.concatenate([sums_row(24 * (12 + k) + e) for k in range(D // 128)], 1)
        new = decay * down_col[pl.ds(e, 1), :] + (1.0 - decay) * (cols / FF)
        down_col_new[pl.ds(e, 1), :] = new
        row = turn_line(down_row_new[pl.ds(e, 1), :])
        step = factored(sums_ref[e], row, new, pick(line, 28 + e) / FF)
        return squares + spread(total(step * step), 28 + e)

    squares = lax.fori_loop(0, EXPERTS + SHARED, step_up, squares)
    squares = lax.fori_loop(0, EXPERTS + SHARED, step_down, squares)
    state = decay * bias_state[...] + (1.0 - decay) * (
        bias_grad[...] * bias_grad[...] + eps_fact
    )
    bias_state_new[...] = state
    bias_step = bias_grad[...] * lax.rsqrt(state)
    squares = squares + spread(total(bias_step * bias_step), 46)
    squares_plane[spot] = jnp.broadcast_to(squares, (8, 128))
    exchange(
        [
            remote(squares_plane.at[spot], squares_plane.at[spot], 4, k, plane_device(k))
            for k in range(1, 8)
        ]
    )
    squares_level[z] = jnp.sum(squares_plane[...], 0)
    exchange(
        [
            remote(squares_level.at[z], squares_level.at[z], 5, k, level_device(k))
            for k in range(1, 4)
        ]
    )
    squares_out[...] = jnp.sum(squares_level[...], 0)[0:1]


def settle_kernel(
    total_tokens,
    sums_ref,
    rows_ref,
    up_ref,
    down_ref,
    mats_ref,
    bias_ref,
    mats_grad,
    mats_row,
    mats_col,
    up_row,
    up_col,
    down_row,
    down_col,
    bias_grad,
    bias_state,
    line_ref,
    squares_ref,
    loss_out,
    mats_grad_out,
    mats_new,
    mats_copy,
    mats_row_out,
    mats_col_out,
    up_grad,
    up_new,
    up_copy,
    up_row_out,
    up_col_out,
    down_grad,
    down_new,
    down_copy,
    down_row_out,
    down_col_out,
    bias_grad_out,
    bias_new,
    bias_copy,
    bias_state_out,
):
    line, squares = line_ref[...], squares_ref[...]
    low = jnp.bfloat16
    group = up_ref.shape[0]

    def clipped(place, entries):
        rms = jnp.sqrt(pick(squares, place) / entries)
        return jnp.maximum(1.0, rms / clip_level)

    def settle(new_ref, copy_ref, index, master, step, limit):
        value = master - learn_rate * (step / limit)
        new_ref[index] = value
        copy_ref[index] = value.astype(low)

    for i in range(group):
        e = pl.program_id(0) * group + i
        grad = joined(rows_ref[i])
        up_grad[i] = grad
        step = factored(
            grad,
            turn_line(up_row[pl.ds(e, 1), :]),
            up_col[pl.ds(e, 1), :],
            pick(line, 10 + e) / D,
        )
        settle(up_new, up_copy, i, up_ref[i], step, clipped(10 + e, D * FF))
        grad = sums_ref[i]
        down_grad[i] = grad
        step = factored(
            grad,
            turn_line(down_row[pl.ds(e, 1), :]),
            down_col[pl.ds(e, 1), :],
            pick(line, 28 + e) / FF,
        )
        settle(down_new, down_copy, i, down_ref[i], step, clipped(28 + e, D * FF))

    @pl.when(pl.program_id(0) == 0)
    def _():
        widths = column_widths()
        bounds = [sum(widths[:k]) for k in range(len(widths) + 1)]
        start_last = bounds[5]
        width_last = bounds[-1] - start_last
        loss_out[...] = pick(line, 46) / total_tokens
        for given, out in (
            (mats_grad, mats_grad_out),
            (mats_row, mats_row_out),
            (mats_col, mats_col_out),
            (up_row, up_row_out),
            (up_col, up_col_out),
            (down_row, down_row_out),
            (down_col, down_col_out),
            (bias_grad, bias_grad_out),
            (bias_state, bias_state_out),
        ):
            out[...] = given[...]
        for k in range(6):
            if k < 5:
                index = (slice(None), slice(bounds[k], bounds[k + 1]))
                row, mean = turn_line(mats_row[k : k + 1, :]), pick(line, k) / D
                limit = clipped(k, D * widths[k])
            else:
                last = range(5, len(widths))
                index = (slice(None), slice(start_last, None))
                row, mean, limit = [
                    by_piece(values, start_last, width_last)
                    for values in (
                        [turn_line(mats_row[j : j + 1, :]) for j in last],
                        [pick(line, j) / D for j in last],
                        [clipped(j, D * widths[j]) for j in last],
                    )
                ]
            step = factored(mats_grad[index], row, mats_col[index], mean)
            settle(mats_new, mats_copy, index, mats_ref[index], step, limit)
        index = (slice(None), slice(None))
        step = bias_grad[...] * lax.rsqrt(bias_state[...])
        settle(bias_new, bias_copy, index, bias_ref[...], step, clipped(46, 15 * D))


def update_kernel_call(sums, rows, lat, bias_sum, masters, factors, loss_part, total_tokens):
    mats, up_weights, down_weights, biases = masters
    mats_row, mats_col, up_row, up_col, down_row, down_col, bias_state = factors
    full, low = jnp.float32, jnp.bfloat16
    mats_col, bias_state, biases = [
        member.reshape(1, -1) for member in (mats_col, bias_state, biases)
    ]

    def like(member, kind=full):
        return jax.ShapeDtypeStruct(member.shape, kind)

    row = jax.ShapeDtypeStruct((1, 128), full)
    rows_like = [mats_row, mats_col, up_row, up_col, down_row, down_col, bias_state, bias_state]
    vmem = pl.BlockSpec(memory_space=pltpu.VMEM)
    dma = pltpu.SemaphoreType.DMA
    found = pl.pallas_call(
        update_kernel,
        out_shape=[like(member) for member in [mats] + rows_like] + [row, row],
        in_specs=[vmem] * 12,
        out_specs=[vmem] * 11,
        scratch_shapes=[
            pltpu.VMEM((512, 128), full),
            pltpu.VMEM((8, 64, 128), full),
            pltpu.VMEM((4, 4, 16, 128), full),
            pltpu.VMEM((8, 4, 16, 128), full),
            pltpu.VMEM((8, 8, 128), full),
            pltpu.VMEM((4, 8, 128), full),
            dma((2, 6, 8)),
        ],
        compiler_params=pltpu.CompilerParams(
            collective_id=1, has_side_effects=True, vmem_limit_bytes=VMEM_ROOM
        ),
        name="update",
    )(
        sums,
        rows,
        lat,
        bias_sum,
        loss_part.reshape(1, 1),
        mats_row,
        mats_col,
        up_row,
        up_col,
        down_row,
        down_col,
        bias_state,
    )
    group = 3
    wholes = [biases] + list(found)

    def whole(member):
        return pl.BlockSpec(member.shape, lambda g: (0,) * len(member.shape))

    def parts(member):
        rest = member.shape[1:]
        return pl.BlockSpec((group,) + rest, lambda g: (g,) + (0,) * len(rest))

    one = jax.ShapeDtypeStruct((1, 1), full)
    outs = (
        [(one, whole(one))]
        + [(like(mats, kind), whole(mats)) for kind in (full, full, low)]
        + [(like(member), whole(member)) for member in (mats_row, mats_col)]
        + [(like(up_weights, kind), parts(up_weights)) for kind in (full, full, low)]
        + [(like(member), whole(member)) for member in (up_row, up_col)]
        + [(like(down_weights, kind), parts(down_weights)) for kind in (full, full, low)]
        + [(like(member), whole(member)) for member in (down_row, down_col)]
        + [(like(biases, kind), whole(biases)) for kind in (full, full, low, full)]
    )
    outs = list(
        pl.pallas_call(
            functools.partial(settle_kernel, total_tokens),
            grid=(up_weights.shape[0] // group,),
            in_specs=[parts(member) for member in (sums, rows, up_weights, down_weights)]
            + [whole(member) for member in [mats] + wholes],
            out_shape=[shape for shape, spec in outs],
            out_specs=[spec for shape, spec in outs],
            compiler_params=pltpu.CompilerParams(vmem_limit_bytes=VMEM_ROOM),
            name="finish",
        )(sums, rows, up_weights, down_weights, mats, *wholes)
    )
    outs[0] = outs[0][0, 0]
    for at in (5, 16, 17, 18, 19):
        outs[at] = outs[at].reshape(-1)
    return tuple(outs)


def gather_kernel(
    mats_in,
    bias_in,
    down_in,
    up_in,
    patches,
    places,
    freq_low,
    label_hot,
    mats_far,
    bias_out,
    down_out,
    up_out,
    mods_out,
    fin_out,
    time_out,
    cond_out,
    qkv_out_far,
    att_out_far,
    middle_out_far,
    moe_out_far,
    logits_out_far,
    shared_out_far,
    mats_got,
    mats_own,
    up_got,
    up_wide,
    up_own,
    embedded,
    down_here,
    up_here,
    near_send,
    near_recv,
    own_sem,
    level_send,
    level_recv,
    one_send,
    one_recv,
    two_send,
    two_recv,
    core_send,
    core_recv,
    bias_send,
    bias_recv,
    here_sem,
    mats_sem,
    mats_out,
    qkv_out,
    att_out,
    middle_out,
    moe_out,
    logits_out,
    shared_out,
):
    leaves = [
        pltpu.make_async_copy(near, far, mats_sem.at[number])
        for number, (near, far) in enumerate(
            (
                (mats_out, mats_far),
                (qkv_out, qkv_out_far),
                (att_out, att_out_far),
                (middle_out, middle_out_far),
                (moe_out, moe_out_far),
                (logits_out, logits_out_far),
                (shared_out, shared_out_far),
            )
        )
    ]
    n_down, n_up = down_in.shape[0], up_own.shape[0]
    lead, n_mats = 3, mats_out.shape[4]
    after_mats = lead + n_mats
    first_up = n_down + n_mats
    slabs = first_up + n_up
    wide, narrow = lax.axis_index(WIDE), lax.axis_index(NARROW)
    z, x = wide // 2, wide % 2
    y, c = narrow // 2, narrow % 2
    mates = [
        (wide, (y + (k // 2) * (1 - 2 * y)) * 2 + c + (k % 2) * (1 - 2 * c)) for k in range(1, 4)
    ]
    levels = [(((z + k) % 4) * 2 + x, narrow) for k in range(1, 4)]
    to_x = (z * 2 + 1 - x, narrow)
    to_core, to_y = mates[0], mates[1]
    to_one = (z * 2 + x + (1 - c) * (1 - 2 * x), (y + c * (1 - 2 * y)) * 2 + c)
    to_two = (z * 2 + x + c * (1 - 2 * x), (y + (1 - c) * (1 - 2 * y)) * 2 + c)
    barrier = pltpu.get_barrier_semaphore()
    for target in mates + levels + [to_x]:
        pl.semaphore_signal(barrier, inc=1, device_id=target, device_id_type=MESH_ID)
    pl.semaphore_wait(barrier, 7)

    def remote(source, target, send, recv, device):
        return pltpu.make_async_remote_copy(
            src_ref=source,
            dst_ref=target,
            send_sem=send,
            recv_sem=recv,
            device_id=device,
            device_id_type=MESH_ID,
        )

    def near_mats(k):
        return remote(
            mats_in.at[mates[k - 1][1]],
            mats_got.at[narrow],
            near_send.at[0, k],
            near_recv.at[0, k],
            mates[k - 1],
        )

    def near_up(k):
        return remote(
            up_in.at[mates[k - 1][1]],
            up_got.at[narrow],
            near_send.at[1, k],
            near_recv.at[1, k],
            mates[k - 1],
        )

    own_mats = pltpu.make_async_copy(mats_in.at[narrow], mats_got.at[narrow], own_sem.at[0])
    own_up = pltpu.make_async_copy(up_in.at[narrow], up_got.at[narrow], own_sem.at[1])
    own_bias = pltpu.make_async_copy(bias_in, bias_out.at[z, x, y, c], own_sem.at[2])
    own_mats.start()
    own_up.start()
    own_bias.start()
    for k in range(1, 4):
        near_mats(k).start()

    def bias_level(k):
        return remote(
            bias_in, bias_out.at[z, x, y, c], bias_send.at[k - 1], bias_recv.at[k - 1], levels[k - 1]
        )

    def bias_x():
        part = bias_out.at[:, x, y, c]
        return remote(part, part, bias_send.at[3], bias_recv.at[3], to_x)

    def bias_y():
        part = bias_out.at[:, :, y, c]
        return remote(part, part, bias_send.at[4], bias_recv.at[4], to_y)

    def bias_core():
        part = bias_out.at[:, :, :, c]
        return remote(part, part, bias_send.at[5], bias_recv.at[5], to_core)

    for k in range(1, 4):
        bias_level(k).start()
    for k in range(1, 4):
        near_up(k).start()

    def mats_ready():
        own_mats.wait()
        for k in range(1, 4):
            near_mats(k).wait_recv()
        for n in range(NARROW_PIECES):
            mats_own[n * ROWS : (n + 1) * ROWS] = mats_got[n].astype(jnp.float32)[:ROWS]
        for n in range(n_mats):
            mats_got[n, :, :] = mats_own[16 * n : 16 * (n + 1)].astype(jnp.bfloat16)

    own_bias.wait()

    def turn(number):
        return (number + EXPERTS) % n_up

    def down_at(s):
        return turn(jnp.where(s < lead, s, s - n_mats))

    def source(kind, s):
        if kind == 0:
            return mats_got.at[s - lead]
        if kind == 1:
            return down_in.at[down_at(s)]
        return up_own.at[turn(s - first_up)]

    def piece(kind, s, at):
        z_at, x_at, y_at, c_at = at
        if kind == 0:
            return mats_out.at[y_at, c_at, z_at, x_at, s - lead]
        if kind == 1:
            return down_out.at[down_at(s), z_at, x_at, y_at, c_at]
        return up_out.at[turn(s - first_up), y_at, c_at, z_at, x_at]

    every = slice(None)

    def own_copy(kind, s):
        return pltpu.make_async_copy(
            source(kind, s), piece(kind, s, (z, x, y, c)), own_sem.at[3 + s % 4]
        )

    def level_copy(kind, s, k, turned=False, first=0):
        if turned:
            part = piece(kind, s, (z, x, every, c) if first == 0 else (z, every, y, c))
            start = part
        else:
            part = piece(kind, s, (z, x, y, c))
            start = source(kind, s)
        return remote(
            start, part, level_send.at[s % 12, k - 1], level_recv.at[s, k - 1], levels[k - 1]
        )

    def both_parts(kind, s, first):
        return piece(kind, s, (every, x, every, c) if first else (every, every, y, c))

    def one_copy(kind, s, turned=False, first=0):
        part = both_parts(kind, s, 1 - first) if turned else piece(kind, s, (every, x, y, c))
        return remote(part, part, one_send.at[s % 12], one_recv.at[s], to_one)

    def two_copy(kind, s, turned=False, first=0):
        if turned:
            part, start = piece(kind, s, (z, x, y, c)), source(kind, s)
        else:
            part = both_parts(kind, s, first)
            start = part
        return remote(start, part, two_send.at[s % 12], two_recv.at[s], to_two)

    def core_copy(kind, s):
        part = piece(kind, s, (every, every, every, c))
        return remote(part, part, core_send.at[s % 12], core_recv.at[s], to_core)

    def by_order(kind, s, run):
        if kind == 0:
            run(False)
            return
        turned = (s % 5 == 1) | (s % 5 == 3)

        @pl.when(turned)
        def _():
            run(True)

        @pl.when(jnp.logical_not(turned))
        def _():
            run(False)

    def by_core(run):
        for first in range(2):

            @pl.when(c == first)
            def _():
                run(first)

    def stage_level(kind, s):
        own_copy(kind, s).start()

        def run(turned):
            if turned:
                two_copy(kind, s, True).start()
            else:
                for k in range(1, 4):
                    level_copy(kind, s, k).start()

        by_order(kind, s, run)

    def stage_one(kind, s):
        own_copy(kind, s).wait()

        def run(turned):
            if turned:
                two_copy(kind, s, True).wait_recv()

                def send(first):
                    for k in range(1, 4):
                        level_copy(kind, s, k, True, first).start()

                by_core(send)
            else:
                for k in range(1, 4):
                    level_copy(kind, s, k).wait_recv()
                one_copy(kind, s).start()

        by_order(kind, s, run)

    def stage_two(kind, s):
        def run(turned):
            if turned:
                for k in range(1, 4):
                    level_copy(kind, s, k, True).wait_recv()
                by_core(lambda first: one_copy(kind, s, True, first).start())
            else:
                one_copy(kind, s).wait_recv()
                by_core(lambda first: two_copy(kind, s, False, first).start())

        by_order(kind, s, run)

    def stage_core(kind, s):
        def run(turned):
            if turned:
                one_copy(kind, s, True).wait_recv()
            else:
                two_copy(kind, s).wait_recv()

        by_order(kind, s, run)
        core_copy(kind, s).start()

    def stage_last(kind, s):
        core_copy(kind, s).wait_recv()

    def stage_sent(kind, s):
        def run(turned):
            for k in range(1, 4):
                level_copy(kind, s, k, turned).wait_send()
            one_copy(kind, s, turned).wait_send()
            two_copy(kind, s, turned).wait_send()

        by_order(kind, s, run)
        core_copy(kind, s).wait_send()

    stages = (
        (stage_sent, 12),
        (stage_level, 0),
        (stage_one, 3),
        (stage_two, 6),
        (stage_core, 9),
        (stage_last, 12),
    )

    lats = patches.shape[0] // PATCHES
    ready, shared_at = after_mats + 12, first_up + SHARED + 12
    low, full = jnp.bfloat16, jnp.float32

    def matrix(number, begin, end):
        chunk = mats_out[number // 2, number % 2]
        return chunk.reshape(D, chunk.shape[-1])[:, begin:end]

    def bias_rows():
        return jnp.sum(bias_out[...].astype(full).reshape(-1, 16, D), 0)

    def wide_row(rows, begin, end):
        return jnp.concatenate([rows[k : k + 1] for k in range(begin, end)], 1)

    def conditions():
        rows = bias_rows()
        pre_time = contract(freq_low[...], matrix(3, 1408, 1664), 1, 1) + rows[11:12]
        hid_time = jax.nn.silu(pre_time).astype(low)
        cond = (
            product(hid_time, matrix(3, 1024, 1408))
            + rows[12:13]
            + contract(label_hot[...], matrix(3, 0, 1024), 1, 1)
        )
        act = jax.nn.silu(cond).astype(low)
        time_out[...] = pre_time
        cond_out[...] = cond
        mods_out[:, : 4 * D] = product(act, matrix(1, 0, 4 * D)) + wide_row(rows, 4, 8)
        mods_out[:, 4 * D :] = product(act, matrix(2, 0, 2 * D)) + wide_row(rows, 8, 10)
        fin_out[...] = product(act, matrix(2, 2 * D, 4 * D)) + wide_row(rows, 13, 15)

    def mod_row(start, number):
        return mods_out[pl.ds(start // PATCHES, 1), number * D : (number + 1) * D]

    def attention_in(start):
        rows = bias_rows()
        span = pl.ds(start, PATCHES)
        emb = contract(patches[span, :], matrix(2, 4 * D, 4 * D + 128), 1, 1)
        emb = emb + rows[10:11] + places[...]
        embedded[...] = emb
        normed, unused_std = layer_norm(emb)
        attn_in = (normed * (1.0 + mod_row(start, 1)) + mod_row(start, 0)).astype(low)
        qkv_out[span, :] = (
            product(attn_in, matrix(0, 0, 3 * D)) + wide_row(rows, 0, 3)
        ).astype(low)

    def attention_heads(start):
        span = pl.ds(start, PATCHES)
        lane = lax.broadcasted_iota(jnp.int32, (PATCHES, 2 * HD), 1)
        for pair in range(HEADS // 2):
            at = pair * 2 * HD
            queries = qkv_out[span, at : at + 2 * HD]
            keys = qkv_out[span, D + at : D + at + 2 * HD]
            values = qkv_out[span, 2 * D + at : 2 * D + at + 2 * HD]
            halves = []
            for half in range(2):
                mine = (lane < HD) if half == 0 else (lane >= HD)
                scores = contract(jnp.where(mine, queries, 0), keys, 1, 1) * HD ** (-0.5)
                powers = jnp.exp(scores - jnp.max(scores, 1, keepdims=True))
                probs = (powers / jnp.sum(powers, 1, keepdims=True)).astype(low)
                halves.append(product(probs, values))
            att_out[span, at : at + 2 * HD] = jnp.where(lane < HD, halves[0], halves[1]).astype(low)

    def attention_out(start):
        rows = bias_rows()
        span = pl.ds(start, PATCHES)
        attn = product(att_out[span, :], matrix(0, 3 * D, 4 * D)) + rows[3:4]
        middle = embedded[...] + mod_row(start, 2) * attn
        middle_out[span, :] = middle
        normed, unused_std = layer_norm(middle)
        moe_in = (normed * (1.0 + mod_row(start, 4)) + mod_row(start, 3)).astype(low)
        moe_out[span, :] = moe_in
        logits_out[span, :] = product(moe_in, matrix(0, 4 * D, 4 * D + 128))

    def fetch(shared_id):
        e = EXPERTS + shared_id
        first = pltpu.make_async_copy(down_out.at[e], down_here, here_sem.at[0])
        second = pltpu.make_async_copy(up_out.at[e], up_here, here_sem.at[1])
        first.start()
        second.start()
        first.wait()
        second.wait()

    def shared_block(shared_id, start):
        span = pl.ds(start, PATCHES)
        rows = moe_out[span, :]
        chunks = [up_here[n // 2, n % 2].reshape(D, D) for n in range(NARROW_PIECES)]
        down = down_here[...].reshape(FF, D)
        total = None
        for cut in range(0, FF, CUT):
            pre_act = product(rows, up_columns(chunks, cut))
            part = product(gelu_only(pre_act).astype(low), down[cut : cut + CUT])
            total = part if total is None else total + part
        if shared_id == 0:
            shared_out[span, :] = total
        else:
            shared_out[span, :] += total

    def tick(t, unused):
        @pl.when(t == 1)
        def _():
            for k in range(1, 4):
                bias_level(k).wait_recv()
            bias_x().start()

        @pl.when(t == 2)
        def _():
            bias_x().wait_recv()
            bias_y().start()

        @pl.when(t == 3)
        def _():
            bias_y().wait_recv()
            bias_core().start()

        @pl.when(t == 6)
        def _():
            own_up.wait()
            for k in range(1, 4):
                near_up(k).wait_recv()
            for n in range(NARROW_PIECES):
                up_wide[n] = up_got[n].astype(jnp.float32)

            for e in range(n_up):
                up_own[e] = jnp.concatenate(
                    [up_wide[n, e * ROWS : (e + 1) * ROWS] for n in range(NARROW_PIECES)], 0
                ).astype(jnp.bfloat16)

        @pl.when(t == 2)
        def _():
            mats_ready()

        for stage, lag in stages:
            s = t - lag

            @pl.when((s >= lead) & (s < after_mats))
            def _():
                stage(0, jnp.clip(s, lead, after_mats - 1))

            @pl.when(((s >= 0) & (s < lead)) | ((s >= after_mats) & (s < first_up)))
            def _():
                stage(1, jnp.clip(s, 0, first_up - 1))

            @pl.when((s >= first_up) & (s < slabs))
            def _():
                stage(2, jnp.clip(s, first_up, slabs - 1))

        @pl.when(t == ready)
        def _():
            bias_core().wait_recv()
            conditions()

        for number, unit in enumerate((attention_in, attention_heads, attention_out)):

            @pl.when((t > ready) & (t <= ready + 3 * lats) & ((t - ready - 1) % 3 == number))
            def _():
                unit(pl.multiple_of(jnp.clip((t - ready - 1) // 3, 0, lats - 1) * PATCHES, PATCHES))

        @pl.when(t == ready + 3 * lats + 1)
        def _():
            for leave in leaves[:-1]:
                leave.start()

        for shared_id in range(SHARED):
            begin = shared_at + shared_id * lats

            @pl.when(t == begin)
            def _():
                fetch(shared_id)

            @pl.when((t >= begin) & (t < begin + lats))
            def _():
                shared_block(
                    shared_id, pl.multiple_of(jnp.clip(t - begin, 0, lats - 1) * PATCHES, PATCHES)
                )

        @pl.when(t == shared_at + SHARED * lats)
        def _():
            leaves[-1].start()

        return unused

    lax.fori_loop(0, slabs + 12, tick, 0)
    for leave in leaves:
        leave.wait()
    for k in range(1, 4):
        near_mats(k).wait_send()
        near_up(k).wait_send()
        bias_level(k).wait_send()
    bias_x().wait_send()
    bias_y().wait_send()
    bias_core().wait_send()


def gather_weights(
    mats, up_weights, down_weights, biases, patches, places, freq_low, label_hot
):
    low = jnp.bfloat16
    owner = lax.axis_index(AXES)
    m = mats.astype(low)
    rows = m.shape[0]

    thin = 13 * D

    def thin_part(at):
        return jnp.pad(m[:, at : at + 16], ((0, 0), (0, 112)))

    mats_in = jnp.stack(
        [
            jnp.concatenate([m[:, : 4 * D], thin_part(thin)], 1),
            jnp.concatenate([m[:, 4 * D : 8 * D], thin_part(thin + 16)], 1),
            jnp.concatenate(
                [m[:, 8 * D : 10 * D], m[:, 11 * D : 13 * D], thin_part(thin + 32)], 1
            ),
            jnp.concatenate(
                [
                    m[:, thin + 48 + FREQ :],
                    jnp.zeros((rows, 24), low),
                    m[:, 10 * D : 11 * D],
                    m[:, thin + 48 : thin + 48 + FREQ],
                ],
                1,
            ),
        ],
        0,
    )
    mats_in = jnp.pad(mats_in, ((0, 0), (0, 16 - rows), (0, 0)))
    line = lax.dynamic_update_slice(
        jnp.zeros((16 * D,), low), biases.astype(low), (owner * biases.shape[0],)
    )
    n_up = up_weights.shape[0]
    up_in = (
        up_weights.astype(low)
        .reshape(n_up, rows, NARROW_PIECES, D)
        .transpose(2, 0, 1, 3)
        .reshape(NARROW_PIECES, n_up * rows, D)
    )
    room = (n_up * rows + 15) // 16 * 16
    up_in = jnp.pad(up_in, ((0, 0), (0, room - n_up * rows), (0, 0)))
    slabs = 3 + 2 * n_up
    spread = mats_in.shape[2]
    dma = pltpu.SemaphoreType.DMA
    anywhere = pl.BlockSpec(memory_space=pl.ANY)
    tokens = patches.shape[0]
    full, vmem = jnp.float32, pl.BlockSpec(memory_space=pltpu.VMEM)
    outs = pl.pallas_call(
        gather_kernel,
        out_shape=[
            jax.ShapeDtypeStruct((2, 2, 4, 2, 3, 16, spread), low),
            jax.ShapeDtypeStruct((4, 2, 2, 2, 16, D), low),
            jax.ShapeDtypeStruct((n_up, 4, 2, 2, 2, PIECE, D), low),
            jax.ShapeDtypeStruct((n_up, 2, 2, 4, 2, PIECE, D), low),
            jax.ShapeDtypeStruct((8, 6 * D), full),
            jax.ShapeDtypeStruct((8, 2 * D), full),
            jax.ShapeDtypeStruct((8, D), full),
            jax.ShapeDtypeStruct((8, D), full),
            jax.ShapeDtypeStruct((tokens, 3 * D), low),
            jax.ShapeDtypeStruct((tokens, D), low),
            jax.ShapeDtypeStruct((tokens, D), full),
            jax.ShapeDtypeStruct((tokens, D), low),
            jax.ShapeDtypeStruct((tokens, 128), full),
            jax.ShapeDtypeStruct((tokens, D), full),
        ],
        in_specs=[anywhere] * 4 + [vmem] * 4,
        out_specs=[anywhere, vmem] + [anywhere] * 2 + [vmem] * 4 + [anywhere] * 6,
        scratch_shapes=[
            pltpu.VMEM((NARROW_PIECES, 16, spread), low),
            pltpu.VMEM((PIECE, spread), jnp.float32),
            pltpu.VMEM((NARROW_PIECES, room, D), low),
            pltpu.VMEM((NARROW_PIECES, room, D), jnp.float32),
            pltpu.VMEM((n_up, PIECE, D), low),
            pltpu.VMEM((PATCHES, D), full),
            pltpu.VMEM((4, 2, 2, 2, PIECE, D), low),
            pltpu.VMEM((2, 2, 4, 2, PIECE, D), low),
            dma((2, 4)),
            dma((2, 4)),
            dma((7,)),
            dma((12, 3)),
            dma((slabs, 3)),
            dma((12,)),
            dma((slabs,)),
            dma((12,)),
            dma((slabs,)),
            dma((12,)),
            dma((slabs,)),
            dma((6,)),
            dma((6,)),
            dma((2,)),
            dma((7,)),
            pltpu.VMEM((2, 2, 4, 2, 3, 16, spread), low),
            pltpu.VMEM((tokens, 3 * D), low),
            pltpu.VMEM((tokens, D), low),
            pltpu.VMEM((tokens, D), full),
            pltpu.VMEM((tokens, D), low),
            pltpu.VMEM((tokens, 128), full),
            pltpu.VMEM((tokens, D), full),
        ],
        compiler_params=pltpu.CompilerParams(
            collective_id=2, has_side_effects=True, vmem_limit_bytes=VMEM_ROOM
        ),
        name="gather_weights",
    )(
        mats_in,
        line.reshape(16, D),
        down_weights.astype(low),
        up_in,
        patches,
        places,
        freq_low,
        label_hot,
    )
    return outs


def split_weights(weights):
    mats_full, up_full, down_full, bias_full = weights
    matrices = cut_pieces(mats_full, column_widths(), 1)
    vectors = [member.astype(jnp.float32) for member in cut_pieces(bias_full, bias_widths(), 0)]
    up_full = up_full.reshape(-1, D, NARROW_PIECES, D).transpose(0, 2, 1, 3)
    return (matrices, vectors, up_full, down_full)


def forward(weights, latents, noise, timesteps, labels, routes):
    matrices, vectors, up_full, down_full = weights
    w_qkv, w_proj, w_mod, w_time2, w_final, w_router, w_head, w_patch, w_time1, w_table = matrices
    b_qkv, b_proj, b_mod, b_patch, b_time1, b_time2, b_final = vectors
    num_latents = latents.shape[0]
    rows_here = num_latents * PATCHES
    steps_f = timesteps.astype(jnp.float32)
    signal, spread = noise_level(steps_f)
    noisy = signal[:, None] * latents + spread[:, None] * noise
    patches = noisy.reshape(rows_here, PD).astype(jnp.bfloat16)
    embedded = (
        contract(patches, w_patch, 1, 1).reshape(num_latents, PATCHES, D)
        + b_patch
        + positions()[None]
    )
    freq_low = time_features(steps_f).astype(jnp.bfloat16)
    pre_time = contract(freq_low, w_time1, 1, 1) + b_time1
    hid_time = jax.nn.silu(pre_time).astype(jnp.bfloat16)
    label_hot = (labels[:, None] == jnp.arange(CLASSES, dtype=jnp.int32)[None, :]).astype(
        jnp.float32
    )
    label_emb = lax.dot_general(
        label_hot,
        w_table.astype(jnp.float32),
        (((1,), (1,)), ((), ())),
        precision=lax.Precision.HIGHEST,
        preferred_element_type=jnp.float32,
    )
    cond = product(hid_time, w_time2) + b_time2 + label_emb
    cond_act = jax.nn.silu(cond).astype(jnp.bfloat16)
    modulation = product(cond_act, w_mod) + b_mod
    final_mod = product(cond_act, w_final) + b_final
    shift_attn, scale_attn, gate_attn, shift_moe, scale_moe, gate_moe = [
        member[:, None, :] for member in jnp.split(modulation, 6, 1)
    ]
    shift_fin, scale_fin = [member[:, None, :] for member in jnp.split(final_mod, 2, 1)]
    normed_one, inv_one = layer_norm(embedded)
    attn_in = (
        (normed_one * (1.0 + scale_attn) + shift_attn).astype(jnp.bfloat16).reshape(rows_here, D)
    )
    qkv_out = (
        (product(attn_in, w_qkv) + b_qkv)
        .astype(jnp.bfloat16)
        .reshape(num_latents, PATCHES, 3, HEADS, HD)
    )
    scores = jnp.einsum(
        LQK, qkv_out[:, :, 0], qkv_out[:, :, 1], preferred_element_type=jnp.float32
    ) * HD ** (-0.5)
    log_totals = jax.nn.logsumexp(scores, -1)
    probs_low = jax.nn.softmax(scores, -1).astype(jnp.bfloat16)
    attended = (
        jnp.einsum(
            "lhqk,lkhd->lqhd", probs_low, qkv_out[:, :, 2], preferred_element_type=jnp.float32
        )
        .astype(jnp.bfloat16)
        .reshape(rows_here, D)
    )
    attn_out = (product(attended, w_proj) + b_proj).reshape(num_latents, PATCHES, D)
    middle = embedded + gate_attn * attn_out
    normed_two, inv_two = layer_norm(middle)
    moe_in = (normed_two * (1.0 + scale_moe) + shift_moe).astype(jnp.bfloat16).reshape(rows_here, D)
    logits = product(moe_in, w_router)
    route_hot = (routes[:, :, None] == jnp.arange(EXPERTS, dtype=jnp.int32)[None, None, :]).astype(
        jnp.float32
    )
    gate_vals = jax.nn.softmax(jnp.sum(route_hot * logits[:, None, :], 2), -1)
    slot_of, slot_meta = pack_slots(routes)
    routed, slot_rows = experts_forward(slot_of, slot_meta, moe_in, up_full, down_full)
    moe_out = gate_vals[:, 0:1] * routed[0] + gate_vals[:, 1:2] * routed[1]
    for shared_id in range(EXPERTS, EXPERTS + SHARED):
        for cut in range(0, FF, CUT):
            pre_act = product(moe_in, up_columns(up_full[shared_id], cut))
            activated = gelu_only(pre_act).astype(jnp.bfloat16)
            moe_out = moe_out + product(activated, down_full[shared_id, cut : cut + CUT])
    moe_out = moe_out.reshape(num_latents, PATCHES, D)
    final_state = middle + gate_moe * moe_out
    normed_fin, inv_fin = layer_norm(final_state)
    head_in = (
        (normed_fin * (1.0 + scale_fin) + shift_fin).astype(jnp.bfloat16).reshape(rows_here, D)
    )
    errors = product(head_in, w_head) - noise.reshape(rows_here, PD)
    return SimpleNamespace(
        patches=patches,
        freq_low=freq_low,
        pre_time=pre_time,
        hid_time=hid_time,
        label_hot=label_hot,
        cond=cond,
        cond_act=cond_act,
        scale_attn=scale_attn,
        gate_attn=gate_attn,
        scale_moe=scale_moe,
        gate_moe=gate_moe,
        scale_fin=scale_fin,
        normed_one=normed_one,
        inv_one=inv_one,
        attn_in=attn_in,
        qkv_out=qkv_out,
        log_totals=log_totals,
        attended=attended,
        attn_out=attn_out,
        normed_two=normed_two,
        inv_two=inv_two,
        moe_in=moe_in,
        route_hot=route_hot,
        gate_vals=gate_vals,
        slot_of=slot_of,
        slot_meta=slot_meta,
        slot_rows=slot_rows,
        routed=routed,
        moe_out=moe_out,
        normed_fin=normed_fin,
        inv_fin=inv_fin,
        head_in=head_in,
        errors=errors,
    )


def forward_fused(mats, up_weights, down_weights, biases, latents, noise, timesteps, labels):
    num_latents = latents.shape[0]
    rows_here = num_latents * PATCHES
    steps_f = timesteps.astype(jnp.float32)
    signal, spread = noise_level(steps_f)
    noisy = signal[:, None] * latents + spread[:, None] * noise
    patches = noisy.reshape(rows_here, PD).astype(jnp.bfloat16)
    freq_low = time_features(steps_f).astype(jnp.bfloat16)
    label_low = (labels[:, None] == jnp.arange(1024, dtype=jnp.int32)[None, :]).astype(jnp.bfloat16)
    less = ((0, 8 - num_latents), (0, 0))
    outs = gather_weights(
        mats,
        up_weights,
        down_weights,
        biases,
        jnp.pad(patches, ((0, 0), (0, 128 - PD))),
        positions(),
        jnp.pad(freq_low, less),
        jnp.pad(label_low, less),
    )
    n_up = outs[3].shape[0]
    return SimpleNamespace(
        patches=jnp.pad(patches, ((0, 0), (0, 128 - PD))),
        freq_low=jnp.pad(freq_low, less),
        mats_full=outs[0],
        bias_full=outs[1],
        down_full=outs[2].reshape(n_up, FF, D),
        up_full=outs[3].reshape(n_up, NARROW_PIECES, D, D),
        mods=outs[4],
        fin=outs[5],
        pre_time=outs[6],
        cond=outs[7],
        qkv=outs[8],
        attended=outs[9],
        middle=outs[10],
        moe_in=outs[11],
        logits=outs[12],
        shared_out=outs[13],
    )


def backward_fused(fused, latents, noise, labels, routes, total_tokens):
    num_latents = latents.shape[0]
    rows_here = num_latents * PATCHES
    line = jnp.sum(fused.bias_full.reshape(-1, 16, D).astype(jnp.float32), 0)
    slot_of, slot_meta = pack_slots(routes)
    members = (
        fused.logits,
        routes,
        fused.shared_out,
        fused.middle,
        jnp.pad(noise.reshape(rows_here, PD), ((0, 0), (0, 128 - PD))),
        fused.mods,
        fused.fin,
        fused.mats_full[0, 1].reshape(D, -1)[:, 4 * D :],
    )
    (
        grad_pair,
        grad_both,
        grad_state,
        grad_logits,
        thin,
        grad_gate,
        grad_fin,
        loss_part,
        slot_rows,
    ) = (
        experts_and_head(
            slot_of,
            slot_meta,
            fused.moe_in,
            fused.up_full,
            fused.down_full,
            2.0 / total_tokens,
            members,
        )
    )
    up_slabs, down_slabs, dx_routed = experts_backward(
        slot_of, slot_meta, slot_rows, grad_pair, fused.up_full, fused.down_full
    )
    label_parts = jnp.stack([labels // 32, labels % 32], 1).astype(jnp.bfloat16)
    members = (
        fused.moe_in,
        grad_both,
        dx_routed,
        grad_logits,
        fused.middle,
        fused.qkv,
        fused.attended,
        grad_state,
        fused.patches,
        positions(),
        fused.mods,
        fused.mats_full,
        line,
        fused.pre_time,
        fused.cond,
        fused.freq_low,
        grad_gate,
        grad_fin,
        thin,
        jnp.pad(label_parts, ((0, 8 - num_latents), (0, 126))),
    )
    return loss_part, reduce_slabs(
        down_slabs, up_slabs, fused.up_full, fused.down_full, members
    )


def backward(weights, kept, total_tokens):
    matrices, vectors, up_full, down_full = weights
    w_qkv, w_proj, w_mod, w_time2, w_final, w_router, w_head, w_patch, w_time1, w_table = matrices
    num_latents = kept.normed_one.shape[0]
    rows_here = num_latents * PATCHES
    grad_head, grad_head_in, unused = linear_back(
        kept.errors * (2.0 / total_tokens), kept.head_in, w_head
    )
    grad_head_in = grad_head_in.reshape(num_latents, PATCHES, D)
    grad_final_mod = jnp.concatenate(
        [jnp.sum(grad_head_in, 1), jnp.sum(grad_head_in * kept.normed_fin, 1)], 1
    )
    grad_state = norm_back(
        grad_head_in * (1.0 + kept.scale_fin), kept.normed_fin, kept.inv_fin
    )
    grad_gate_moe = jnp.sum(kept.moe_out * grad_state, 1)
    grad_moe = (kept.gate_moe * grad_state).reshape(rows_here, D)
    grad_moe_low = grad_moe.astype(jnp.bfloat16)
    moe_in = kept.moe_in
    gate_vals = kept.gate_vals
    routed = kept.routed
    grad_gates = jnp.stack([jnp.sum(routed[k] * grad_moe, 1) for k in range(2)], 1)
    grad_pair = jnp.stack(
        [(gate_vals[:, k : k + 1] * grad_moe).astype(jnp.bfloat16) for k in range(2)], 0
    )
    up_slabs, down_slabs, grad_moe_in = experts_backward(
        kept.slot_of, kept.slot_meta, kept.slot_rows, grad_pair, up_full, down_full
    )
    up_all = [up_slabs.transpose(0, 1, 3, 2, 4).reshape(-1, D, FF)]
    down_all = [down_slabs.reshape(-1, FF, D)]
    for shared_id in range(EXPERTS, EXPERTS + SHARED):
        up_part = jnp.concatenate([up_full[shared_id, k] for k in range(NARROW_PIECES)], 1)
        activated, slope = gelu_slope(product(moe_in, up_part))
        grad_act = contract(grad_moe_low, down_full[shared_id], 1, 1)
        grad_pre = (grad_act * slope).astype(jnp.bfloat16)
        down_all.append(contract(activated.astype(jnp.bfloat16), grad_moe_low, 0, 0)[None])
        up_all.append(contract(moe_in, grad_pre, 0, 0)[None])
        grad_moe_in = grad_moe_in + contract(grad_pre, up_part, 1, 1)
    up_slabs = jnp.concatenate([member.astype(jnp.float32) for member in up_all], 0)
    down_slabs = jnp.concatenate([member.astype(jnp.float32) for member in down_all], 0)
    grad_picked = gate_vals * (grad_gates - jnp.sum(gate_vals * grad_gates, 1, keepdims=True))
    grad_logits = jnp.sum(kept.route_hot * grad_picked[:, :, None], 1)
    grad_router, grad_from_router, unused = linear_back(grad_logits, moe_in, w_router)
    grad_moe_in = (grad_moe_in + grad_from_router).reshape(num_latents, PATCHES, D)
    grad_middle = grad_state + norm_back(
        grad_moe_in * (1.0 + kept.scale_moe), kept.normed_two, kept.inv_two
    )
    grad_gate_attn = jnp.sum(kept.attn_out * grad_middle, 1)
    grad_proj, grad_attended, grad_b_proj = linear_back(
        (kept.gate_attn * grad_middle).reshape(rows_here, D), kept.attended, w_proj
    )
    grad_att_low = grad_attended.astype(jnp.bfloat16).reshape(num_latents, PATCHES, HEADS, HD)
    qkv_out = kept.qkv_out
    queries = qkv_out[:, :, 0]
    key_rows = qkv_out[:, :, 1]
    values = qkv_out[:, :, 2]
    scores = jnp.einsum(
        LQK, queries, key_rows, preferred_element_type=jnp.float32
    ) * HD ** (-0.5)
    probs = jnp.exp(scores - kept.log_totals[..., None])
    probs_low = probs.astype(jnp.bfloat16)
    grad_values = jnp.einsum(
        "lhqk,lqhd->lkhd", probs_low, grad_att_low, preferred_element_type=jnp.float32
    )
    grad_probs = jnp.einsum(
        LQK, grad_att_low, values, preferred_element_type=jnp.float32
    )
    grad_scores = (
        probs * (grad_probs - jnp.sum(probs * grad_probs, -1, keepdims=True)) * HD ** (-0.5)
    ).astype(jnp.bfloat16)
    grad_queries = jnp.einsum(
        "lhqk,lkhd->lqhd", grad_scores, key_rows, preferred_element_type=jnp.float32
    )
    grad_keys = jnp.einsum(
        "lhqk,lqhd->lkhd", grad_scores, queries, preferred_element_type=jnp.float32
    )
    grad_qkv = jnp.stack([grad_queries, grad_keys, grad_values], 2).reshape(rows_here, 3 * D)
    grad_w_qkv, grad_attn_in, grad_b_qkv = linear_back(grad_qkv, kept.attn_in, w_qkv)
    grad_attn_in = grad_attn_in.reshape(num_latents, PATCHES, D)
    grad_embedded = grad_middle + norm_back(
        grad_attn_in * (1.0 + kept.scale_attn), kept.normed_one, kept.inv_one
    )
    grad_emb_flat = grad_embedded.reshape(rows_here, D)
    grad_patch = contract(grad_emb_flat.astype(jnp.bfloat16), kept.patches, 0, 0)
    grad_b_patch = jnp.sum(grad_emb_flat, 0)
    grad_modulation = jnp.concatenate(
        [
            jnp.sum(grad_attn_in, 1),
            jnp.sum(grad_attn_in * kept.normed_one, 1),
            grad_gate_attn,
            jnp.sum(grad_moe_in, 1),
            jnp.sum(grad_moe_in * kept.normed_two, 1),
            grad_gate_moe,
        ],
        1,
    )
    grad_mod_low = grad_modulation.astype(jnp.bfloat16)
    grad_fin_low = grad_final_mod.astype(jnp.bfloat16)
    grad_act = contract(grad_mod_low, w_mod, 1, 1) + contract(grad_fin_low, w_final, 1, 1)
    grad_cond = slope_back(jax.nn.silu, kept.cond, grad_act)
    grad_cond_low = grad_cond.astype(jnp.bfloat16)
    grad_hid_time = contract(grad_cond_low, w_time2, 1, 1)
    grad_pre_time = slope_back(jax.nn.silu, kept.pre_time, grad_hid_time)
    grad_time_low = grad_pre_time.astype(jnp.bfloat16)
    mats_slabs = jnp.concatenate([grad_w_qkv, grad_proj], 1)[None]
    thin = jnp.concatenate([grad_router, grad_head, grad_patch], 1)
    grad_bias = jnp.concatenate(
        [
            grad_b_qkv,
            grad_b_proj,
            jnp.sum(grad_modulation, 0),
            grad_b_patch,
            jnp.sum(grad_pre_time, 0),
            jnp.sum(grad_cond, 0),
            jnp.sum(grad_final_mod, 0),
        ]
    )
    lows = jnp.concatenate(
        [
            kept.cond_act,
            kept.hid_time,
            grad_mod_low,
            grad_fin_low,
            grad_cond_low,
            grad_time_low,
            kept.freq_low,
        ],
        1,
    )
    return (up_slabs, down_slabs, mats_slabs, thin, grad_bias, lows, grad_cond)


def latent_grads(lows, grad_cond, labels, row_start, row_count):
    lows = lax.all_gather(lows, AXES, axis=0, tiled=True)
    grad_cond = lax.all_gather(grad_cond, AXES, axis=0, tiled=True)
    labels = lax.all_gather(labels, AXES, axis=0, tiled=True)
    cond_act, hid_time, grad_mod, grad_fin, grad_low, grad_time, freq_low = cut_pieces(
        lows, [D, D, 6 * D, 2 * D, D, D, FREQ], 1
    )

    def rows_of(member):
        return lax.dynamic_slice_in_dim(member, row_start, row_count, 1)

    label_hot = (labels[:, None] == jnp.arange(CLASSES, dtype=jnp.int32)[None, :]).astype(
        jnp.float32
    )
    grad_table = lax.dot_general(
        rows_of(grad_cond),
        label_hot,
        (((0,), (0,)), ((), ())),
        precision=lax.Precision.HIGHEST,
        preferred_element_type=jnp.float32,
    )
    return (
        contract(rows_of(cond_act), grad_mod, 0, 0),
        contract(rows_of(hid_time), grad_low, 0, 0),
        contract(rows_of(cond_act), grad_fin, 0, 0),
        contract(rows_of(grad_time), freq_low, 0, 0),
        grad_table,
    )


def factor_start(grad, row_old):
    squares = grad * grad + eps_fact
    row_new = decay * row_old + (1.0 - decay) * jnp.mean(squares, 2)
    return (row_new, jnp.sum(squares, 1), jnp.sum(row_new, 1))


def factor_update(grad, row_new, col_total, row_total, col_old, row_count):
    col_new = decay * col_old + (1.0 - decay) * (col_total / row_count)
    row_mean = row_total / row_count
    update = grad * lax.rsqrt(row_new[:, :, None] * col_new[:, None, :] / row_mean[:, None, None])
    return (col_new, update, jnp.sum(update * update, (1, 2)))


def clip_apply(master, update, square_total, entry_count):
    update_rms = jnp.sqrt(square_total / entry_count)
    return master - learn_rate * (update / jnp.maximum(1.0, update_rms / clip_level)[:, None, None])


def update_plain(grads, masters, factors, loss_part):
    mats_grad, up_grad, down_grad, bias_grad = grads
    mats, up_weights, down_weights, biases = masters
    mats_row, mats_col, up_row, up_col, down_row, down_col, bias_state = factors
    widths = column_widths()
    grad_pieces = cut_pieces(mats_grad, widths, 1)
    starts = [
        factor_start(grad_pieces[k][None], mats_row[k][None]) for k in range(len(widths))
    ]
    up_row_new, up_col_part, up_row_part = factor_start(up_grad, up_row)
    down_row_new, down_col_part, down_row_part = factor_start(down_grad, down_row)
    col_totals, row_totals, up_cols, up_rows, down_cols, down_rows, loss_total = lax.psum(
        (
            jnp.concatenate([member[1] for member in starts], 1)[0],
            jnp.concatenate([member[2] for member in starts], 0),
            up_col_part,
            up_row_part,
            down_col_part,
            down_row_part,
            loss_part,
        ),
        AXES,
    )
    col_total_pieces = cut_pieces(col_totals, widths, 0)
    col_old_pieces = cut_pieces(mats_col, widths, 0)
    steps = [
        factor_update(
            grad_pieces[k][None],
            starts[k][0],
            col_total_pieces[k][None],
            row_totals[k][None],
            col_old_pieces[k][None],
            D,
        )
        for k in range(len(widths))
    ]
    up_col_new, up_update, up_square = factor_update(
        up_grad, up_row_new, up_cols, up_rows, up_col, D
    )
    down_col_new, down_update, down_square = factor_update(
        down_grad, down_row_new, down_cols, down_rows, down_col, FF
    )
    bias_state_new = decay * bias_state + (1.0 - decay) * (bias_grad * bias_grad + eps_fact)
    bias_update = bias_grad * lax.rsqrt(bias_state_new)
    square_mats, square_up, square_down, square_bias = lax.psum(
        (
            jnp.concatenate([member[2] for member in steps], 0),
            up_square,
            down_square,
            jnp.sum(bias_update * bias_update),
        ),
        AXES,
    )
    master_pieces = cut_pieces(mats, widths, 1)
    mats_new = jnp.concatenate(
        [
            clip_apply(
                master_pieces[k][None], steps[k][1], square_mats[k][None], D * widths[k]
            )[0]
            for k in range(len(widths))
        ],
        1,
    )
    up_new = clip_apply(up_weights, up_update, square_up, D * FF)
    down_new = clip_apply(down_weights, down_update, square_down, D * FF)
    bias_rms = jnp.sqrt(square_bias / (15 * D))
    bias_new = biases - learn_rate * (bias_update / jnp.maximum(1.0, bias_rms / clip_level))
    return (
        loss_total,
        mats_grad,
        mats_new,
        mats_new.astype(jnp.bfloat16),
        jnp.concatenate([member[0] for member in starts], 0),
        jnp.concatenate([member[0][0] for member in steps], 0),
        up_grad,
        up_new,
        up_new.astype(jnp.bfloat16),
        up_row_new,
        up_col_new,
        down_grad,
        down_new,
        down_new.astype(jnp.bfloat16),
        down_row_new,
        down_col_new,
        bias_grad,
        bias_new,
        bias_new.astype(jnp.bfloat16),
        bias_state_new,
    )


def body(
    latents,
    noise,
    timesteps,
    labels,
    routes,
    mats,
    up_weights,
    down_weights,
    biases,
    *factors,
):
    rows_here = mats.shape[0]
    total_tokens = latents.shape[0] * PATCHES * lax.axis_size(AXES)
    masters = (mats, up_weights, down_weights, biases)
    if lax.axis_size(WIDE) == WIDE_PIECES and lax.axis_size(NARROW) == NARROW_PIECES:
        fused = forward_fused(
            mats, up_weights, down_weights, biases, latents, noise, timesteps, labels
        )
        loss_part, (sums, turned, lat, bias_sum) = backward_fused(
            fused, latents, noise, labels, routes, total_tokens
        )
        return update_kernel_call(
            sums, turned, lat, bias_sum, masters, factors, loss_part, total_tokens
        )
    else:
        flat = jnp.concatenate([mats.reshape(-1), biases], 0).astype(jnp.bfloat16)
        flat = lax.all_gather(flat, AXES, axis=0, tiled=False)
        gathered = split_weights(
            (
                flat[:, : rows_here * mats.shape[1]].reshape(-1, mats.shape[1]),
                lax.all_gather(up_weights.astype(jnp.bfloat16), AXES, axis=1, tiled=True),
                lax.all_gather(down_weights.astype(jnp.bfloat16), AXES, axis=1, tiled=True),
                flat[:, rows_here * mats.shape[1] :].reshape(-1),
            )
        )
        kept = forward(gathered, latents, noise, timesteps, labels, routes)
        members = backward(gathered, kept, total_tokens)
        up_slabs, down_slabs, mats_slabs, thin, grad_bias, lows, grad_cond = members
        loss_part = jnp.sum(kept.errors * kept.errors)
        grads = plain_grads(
            down_slabs, up_slabs, mats_slabs, thin, grad_bias, lows, grad_cond, labels, rows_here
        )
        outs = update_plain(grads, masters, factors, loss_part)
    return (outs[0] / total_tokens,) + tuple(outs[1:])


def solution(mesh):
    rows = P(AXES, None)
    middle_rows = P(None, AXES, None)
    row_factor = P(None, AXES)
    line = P(AXES)
    in_specs = (
        (rows, rows, line, line, rows)
        + (rows, middle_rows, middle_rows, line)
        + (row_factor, P(), row_factor, P(), row_factor, P(), line)
    )
    out_specs = (
        (P(), rows, rows, rows, row_factor, P())
        + (middle_rows, middle_rows, middle_rows, row_factor, P()) * 2
        + (line, line, line, line)
    )
    return jax.shard_map(body, mesh=mesh, in_specs=in_specs, out_specs=out_specs, check_vma=False)
```

```python
import functools
import math
from types import SimpleNamespace

import jax
import jax.numpy as jnp
from jax import lax
from jax.experimental import pallas as pl
from jax.experimental.pallas import tpu as pltpu
from jax.sharding import PartitionSpec as P

WIDE = "wide"
NARROW = "narrow"
AXES = (WIDE, NARROW)
MESH_ID = pl.DeviceIdType.MESH

D = 384
HEADS = 6
HD = 64
FF = 1536
EXPERTS = 16
SHARED = 2
PD = 16
GRID = 16
FREQ = 256
CLASSES = 1000
BLK = 256
WIDE_PIECES = 8
NARROW_PIECES = 4
PIECE = 48
ROWS = 12
LAT_ROWS = 16
LQK = "lqhd,lkhd->lhqk"
CUT = 768
LAT_COLS = 1536
PATCHES = 256


eps_norm = 1e-06
eps_fact = 1e-30
decay = 0.5
clip_level = 0.1
learn_rate = 0.5

SQRT_2_PI = math.sqrt(2.0 / math.pi)
VMEM_ROOM = 56 * 1024 * 1024
REDUCE_ROOM = 61 * 1024 * 1024


def column_widths():
    return [3 * D, D, 6 * D, D, 2 * D, EXPERTS, PD, PD, FREQ, CLASSES]


def bias_widths():
    return [3 * D, D, 6 * D, D, D, D, 2 * D]


def cut_pieces(source, widths, along):
    pieces = []
    start = 0
    for width in widths:
        pieces.append(lax.slice_in_dim(source, start, start + width, axis=along))
        start = start + width
    return pieces


def product(left, right):
    return jnp.dot(left, right, preferred_element_type=jnp.float32)


def contract(left, right, left_dim, right_dim):
    return lax.dot_general(
        left, right, (((left_dim,), (right_dim,)), ((), ())), preferred_element_type=jnp.float32
    )


def gelu_tanh(values):
    return jax.nn.gelu(values, approximate=True)


def slope_back(function, source, grad_out):
    return jax.vjp(function, source)[1](grad_out)[0]


def layer_norm(source):
    centred = source - jnp.mean(source, -1, keepdims=True)
    inv_std = lax.rsqrt(jnp.mean(centred * centred, -1, keepdims=True) + eps_norm)
    return (centred * inv_std, inv_std)


def norm_back(grad_norm, normed, inv_std):
    return inv_std * (
        grad_norm
        - jnp.mean(grad_norm, -1, keepdims=True)
        - normed * jnp.mean(grad_norm * normed, -1, keepdims=True)
    )


def linear_back(grad_out, inputs, weight):
    grad_low = grad_out.astype(jnp.bfloat16)
    return (
        contract(inputs, grad_low, 0, 0),
        contract(grad_low, weight, 1, 1),
        jnp.sum(grad_out, 0),
    )


def sincos(coords, width):
    omegas = 1.0 / 10000.0 ** (jnp.arange(width // 2, dtype=jnp.float32) / (width / 2.0))
    angles = coords[:, None] * omegas[None, :]
    return jnp.concatenate([jnp.sin(angles), jnp.cos(angles)], 1)


def positions():
    places = jnp.arange(PATCHES, dtype=jnp.int32)
    grid_row = (places // GRID).astype(jnp.float32)
    grid_col = (places % GRID).astype(jnp.float32)
    return jnp.concatenate([sincos(grid_row, D // 2), sincos(grid_col, D // 2)], 1)


def time_features(steps_f):
    half_width = FREQ // 2
    freq_rates = jnp.exp(
        -math.log(10000.0) * jnp.arange(half_width, dtype=jnp.float32) / half_width
    )
    angles = steps_f[:, None] * freq_rates[None, :]
    return jnp.concatenate([jnp.cos(angles), jnp.sin(angles)], 1)


def noise_level(steps_f):
    alpha_bar = jnp.cos((steps_f / 1000.0 + 0.008) / 1.008 * (math.pi / 2)) ** 2
    return (jnp.sqrt(alpha_bar), jnp.sqrt(1.0 - alpha_bar))


def pack_slots(routes):
    ids = jnp.arange(EXPERTS, dtype=jnp.int32)[:, None]
    named = [(routes[:, k][None, :] == ids) for k in range(2)]
    either = (named[0] | named[1]).astype(jnp.bfloat16)
    rows_here = routes.shape[0]
    place = jnp.arange(rows_here, dtype=jnp.int32)
    before = (place[:, None] < place[None, :]).astype(jnp.bfloat16)
    rank_in = product(either, before)
    counts = jnp.sum(either.astype(jnp.float32), 1).astype(jnp.int32)
    padded = (counts + 15) // 16 * 16
    starts = jnp.sum(jnp.where(ids > ids.T, padded[None, :], 0), 1)
    slots = rank_in.astype(jnp.int32) + starts[:, None]
    slot_of = jnp.stack([jnp.sum(jnp.where(member, slots, 0), 0) for member in named], 0)
    return (slot_of, jnp.stack([starts, counts], 0))


def gelu_slope(values):
    inner = SQRT_2_PI * (values + 0.044715 * values * values * values)
    bend = jnp.tanh(inner)
    return (
        0.5 * values * (1.0 + bend),
        0.5 * (1.0 + bend)
        + 0.5
        * values
        * (1.0 - bend * bend)
        * SQRT_2_PI
        * (1.0 + 3.0 * 0.044715 * values * values),
    )


def gelu_only(values):
    inner = SQRT_2_PI * (values + 0.044715 * values * values * values)
    return 0.5 * values * (1.0 + jnp.tanh(inner))


def up_columns(chunks, cut):
    return jnp.concatenate([chunks[cut // D + k] for k in range(CUT // D)], 1)


def slot_pick(slots_ref, base, rows):
    place = base + lax.broadcasted_iota(jnp.int32, (rows, slots_ref.shape[1]), 0)
    return ((slots_ref[0:1, :] == place) | (slots_ref[1:2, :] == place)).astype(jnp.bfloat16)


def over_blocks(meta, run):
    start, count = meta[0, pl.program_id(0)], meta[1, pl.program_id(0)]
    blocks = (count + BLK // 2 - 1) // BLK
    rest = count - blocks * BLK

    def block(number, unused):
        run(pl.multiple_of(start + number * BLK, 16), BLK, number > 0)
        return unused

    lax.fori_loop(0, blocks, block, 0)

    @pl.when(rest > BLK // 4)
    def _():
        run(pl.multiple_of(start + blocks * BLK, 16), BLK // 2, blocks > 0)

    @pl.when((rest > 0) & (rest <= BLK // 4))
    def _():
        run(pl.multiple_of(start + blocks * BLK, 16), BLK // 4, blocks > 0)


def routed_blocks(meta, slots_ref, x_ref, up_ref, down_ref, x_out, y_ref):
    def run(base, size, unused):
        rows = product(slot_pick(slots_ref, base, size), x_ref[...]).astype(jnp.bfloat16)
        x_out[pl.ds(base, size), :] = rows
        total = None
        for cut in range(0, FF, CUT):
            pre_act = product(rows, up_columns(up_ref[0], cut))
            part = product(gelu_only(pre_act).astype(jnp.bfloat16), down_ref[0, cut : cut + CUT])
            total = part if total is None else total + part
        y_ref[pl.ds(base, size), :] = total

    over_blocks(meta, run)


def forward_kernel(
    meta, slot_at, slots_ref, x_ref, up_ref, down_ref, routed_ref, x_out, y_ref
):
    routed_blocks(meta, slots_ref, x_ref, up_ref, down_ref, x_out, y_ref)

    @pl.when(pl.program_id(0) == EXPERTS - 1)
    def _():
        def group(number, unused):
            for step in range(8):
                token = number * 8 + step
                for k in range(2):
                    routed_ref[k, pl.ds(token, 1), :] = y_ref[pl.ds(slot_at[k, token], 1), :]
            return unused

        lax.fori_loop(0, x_ref.shape[0] // 8, group, 0)


def head_kernel(
    token_scale,
    meta,
    slot_at,
    slots_ref,
    x_ref,
    up_ref,
    down_ref,
    logits_ref,
    routes_ref,
    shared_ref,
    middle_ref,
    noise_ref,
    mods_ref,
    fin_ref,
    head_ref,
    pair_out,
    both_out,
    state_out,
    logits_out,
    thin_out,
    gate_out,
    fin_out,
    loss_out,
    x_out,
    routed_ref,
    y_ref,
):
    routed_blocks(meta, slots_ref, x_ref, up_ref, down_ref, x_out, y_ref)
    low = jnp.bfloat16

    @pl.when(pl.program_id(0) == EXPERTS - 1)
    def _():
        gate_out[...] = jnp.zeros_like(gate_out)
        fin_out[...] = jnp.zeros_like(fin_out)
        thin_out[...] = jnp.zeros_like(thin_out)
        loss_out[...] = jnp.zeros_like(loss_out)
        lane = lax.broadcasted_iota(jnp.int32, (PATCHES, 128), 1)

        def latent(lat, unused):
            base = pl.multiple_of(lat * PATCHES, PATCHES)
            span = pl.ds(base, PATCHES)

            def group(number, unused):
                for step in range(8):
                    token = number * 8 + step
                    for k in range(2):
                        routed_ref[k, pl.ds(token, 1), :] = y_ref[
                            pl.ds(slot_at[k, base + token], 1), :
                        ]
                return unused

            lax.fori_loop(0, PATCHES // 8, group, 0)
            hot = [
                (lane == routes_ref[span, k : k + 1]).astype(jnp.float32) for k in range(2)
            ]
            picked = [jnp.sum(hot[k] * logits_ref[span, :], 1, keepdims=True) for k in range(2)]
            most = jnp.maximum(picked[0], picked[1])
            powers = [jnp.exp(picked[k] - most) for k in range(2)]
            gates = [powers[k] / (powers[0] + powers[1]) for k in range(2)]
            moe_out = gates[0] * routed_ref[0] + gates[1] * routed_ref[1] + shared_ref[span, :]
            gate_moe = mods_ref[pl.ds(lat, 1), 5 * D :]
            normed, inv_std = layer_norm(middle_ref[span, :] + gate_moe * moe_out)
            scale = 1.0 + fin_ref[pl.ds(lat, 1), D:]
            head_in = (normed * scale + fin_ref[pl.ds(lat, 1), :D]).astype(low)
            errors = product(head_in, head_ref[...]) - noise_ref[span, :]
            loss_out[...] += jnp.sum(jnp.sum(errors * errors, 1, keepdims=True), 0, keepdims=True)
            errors = (errors * token_scale).astype(low)
            grads = contract(errors, head_ref[...], 1, 1)
            fin_out[pl.ds(lat, 1), :D] = jnp.sum(grads, 0, keepdims=True)
            fin_out[pl.ds(lat, 1), D:] = jnp.sum(grads * normed, 0, keepdims=True)
            state = norm_back(grads * scale, normed, inv_std)
            state_out[span, :] = state
            gate_out[pl.ds(lat, 1), :] = jnp.sum(moe_out * state, 0, keepdims=True)
            grads = gate_moe * state
            both_out[span, :] = grads.astype(low)
            slopes = []
            for k in range(2):
                slopes.append(jnp.sum(routed_ref[k] * grads, 1, keepdims=True))
                pair_out[k, span, :] = (gates[k] * grads).astype(low)
            usual = gates[0] * slopes[0] + gates[1] * slopes[1]
            grad_logits = (
                hot[0] * (gates[0] * (slopes[0] - usual)) + hot[1] * (gates[1] * (slopes[1] - usual))
            )
            logits_out[span, :] = grad_logits
            thin_out[...] += contract(x_ref[span, :], grad_logits.astype(low), 0, 0) + pltpu.roll(
                contract(head_in, errors, 0, 0), EXPERTS, 1
            )
            return unused

        lax.fori_loop(0, x_ref.shape[0] // PATCHES, latent, 0)


def experts_and_head(slot_of, meta, moe_in, up_full, down_full, token_scale, members):
    tokens = moe_in.shape[0]
    full, low = jnp.float32, jnp.bfloat16
    shapes = (
        ((2, tokens, D), low),
        ((tokens, D), low),
        ((tokens, D), full),
        ((tokens, 128), full),
        ((D, 128), full),
        ((8, D), full),
        ((8, 2 * D), full),
        ((1, 1), full),
        ((slot_room(tokens), D), low),
    )
    return pl.pallas_call(
        functools.partial(head_kernel, token_scale),
        grid_spec=pltpu.PrefetchScalarGridSpec(
            num_scalar_prefetch=2,
            grid=(EXPERTS,),
            in_specs=[
                whole_block((2, tokens)),
                whole_block((tokens, D)),
                pl.BlockSpec((1, NARROW_PIECES, D, D), lambda e, *unused: (e, 0, 0, 0)),
                pl.BlockSpec((1, FF, D), lambda e, *unused: (e, 0, 0)),
            ]
            + [whole_block(member.shape) for member in members],
            out_specs=[whole_block(shape) for shape, kind in shapes],
            scratch_shapes=[
                pltpu.VMEM((2, PATCHES, D), full),
                pltpu.VMEM((slot_room(tokens), D), full),
            ],
        ),
        out_shape=[jax.ShapeDtypeStruct(shape, kind) for shape, kind in shapes],
        compiler_params=pltpu.CompilerParams(vmem_limit_bytes=VMEM_ROOM),
        name="experts_and_head",
    )(meta, slot_of, slot_of, moe_in, up_full, down_full, *members)


def slot_room(tokens):
    return tokens * 2 + EXPERTS * 16 + BLK


def whole_block(shape):
    return pl.BlockSpec(shape, lambda e, *unused: (0,) * len(shape))


def experts_forward(slot_of, meta, moe_in, up_full, down_full):
    tokens = moe_in.shape[0]
    return pl.pallas_call(
        forward_kernel,
        grid_spec=pltpu.PrefetchScalarGridSpec(
            num_scalar_prefetch=2,
            grid=(EXPERTS,),
            in_specs=[
                whole_block((2, tokens)),
                whole_block((tokens, D)),
                pl.BlockSpec((1, NARROW_PIECES, D, D), lambda e, *unused: (e, 0, 0, 0)),
                pl.BlockSpec((1, FF, D), lambda e, *unused: (e, 0, 0)),
            ],
            out_specs=[whole_block((2, tokens, D)), whole_block((slot_room(tokens), D))],
            scratch_shapes=[pltpu.VMEM((slot_room(tokens), D), jnp.float32)],
        ),
        out_shape=[
            jax.ShapeDtypeStruct((2, tokens, D), jnp.float32),
            jax.ShapeDtypeStruct((slot_room(tokens), D), jnp.bfloat16),
        ],
        compiler_params=pltpu.CompilerParams(vmem_limit_bytes=VMEM_ROOM),
        cost_estimate=pl.CostEstimate(
            flops=20_000_000_000, bytes_accessed=50_000_000, transcendentals=0
        ),
        name="experts_forward",
    )(meta, slot_of, slot_of, moe_in, up_full, down_full)


def backward_kernel(
    meta,
    slot_at,
    slots_ref,
    x_ref,
    pair_ref,
    up_ref,
    down_ref,
    up_out,
    down_out,
    dx_slots,
    up_sum,
    down_sum,
):
    stack_id = pl.program_id(0)
    tokens = pair_ref.shape[1]

    @pl.when(meta[1, stack_id] == 0)
    def _():
        up_sum[...] = jnp.zeros_like(up_sum)
        down_sum[...] = jnp.zeros_like(down_sum)

    def expert(rows, grads, later):
        total = None
        for cut in range(0, FF, CUT):
            up_part = up_columns(up_ref[0], cut)
            activated, slope = gelu_slope(product(rows, up_part))
            grad_act = contract(grads, down_ref[0, cut : cut + CUT], 1, 1)
            grad_pre = (grad_act * slope).astype(jnp.bfloat16)
            down_part = contract(activated.astype(jnp.bfloat16), grads, 0, 0)
            up_grad = contract(rows, grad_pre, 0, 0)
            down_sum[cut : cut + CUT, :] = down_part + jnp.where(
                later, down_sum[cut : cut + CUT, :], 0.0
            )
            up_sum[:, cut : cut + CUT] = up_grad + jnp.where(
                later, up_sum[:, cut : cut + CUT], 0.0
            )
            part = contract(grad_pre, up_part, 1, 1)
            total = part if total is None else total + part
        return total

    stop = meta[0, stack_id] + meta[1, stack_id]

    def run(base, size, later):
        place = base + lax.broadcasted_iota(jnp.int32, (size, tokens), 0)
        place = jnp.where(place < stop, place, -1)
        grads = None
        for k in range(2):
            part = product((slots_ref[k : k + 1, :] == place).astype(jnp.bfloat16), pair_ref[k])
            grads = part if grads is None else grads + part
        dx_slots[pl.ds(base, size), :] = expert(
            x_ref[pl.ds(base, size), :], grads.astype(jnp.bfloat16), later
        )

    over_blocks(meta, run)
    for n in range(NARROW_PIECES):
        up_out[0, :, n] = (
            up_sum[:, n * D : (n + 1) * D]
            .astype(jnp.bfloat16)
            .reshape(WIDE_PIECES, PIECE, D)
        )
    down_out[0] = down_sum[...].astype(jnp.bfloat16).reshape(WIDE_PIECES, NARROW_PIECES, PIECE, D)


def experts_backward(slot_of, meta, slot_rows, grad_pair, up_full, down_full):
    tokens = slot_of.shape[1]
    slabs = (EXPERTS, WIDE_PIECES, NARROW_PIECES, PIECE, D)
    slab_spec = pl.BlockSpec((1,) + slabs[1:], lambda e, *unused: (e, 0, 0, 0, 0))
    return pl.pallas_call(
        backward_kernel,
        grid_spec=pltpu.PrefetchScalarGridSpec(
            num_scalar_prefetch=2,
            grid=(EXPERTS,),
            in_specs=[
                whole_block((2, tokens)),
                whole_block(slot_rows.shape),
                whole_block((2, tokens, D)),
                pl.BlockSpec((1, NARROW_PIECES, D, D), lambda e, *unused: (e, 0, 0, 0)),
                pl.BlockSpec((1, FF, D), lambda e, *unused: (e, 0, 0)),
            ],
            out_specs=[slab_spec, slab_spec, whole_block(slot_rows.shape)],
            scratch_shapes=[
                pltpu.VMEM((D, FF), jnp.float32),
                pltpu.VMEM((FF, D), jnp.float32),
            ],
        ),
        out_shape=[
            jax.ShapeDtypeStruct(slabs, jnp.bfloat16),
            jax.ShapeDtypeStruct(slabs, jnp.bfloat16),
            jax.ShapeDtypeStruct(slot_rows.shape, jnp.float32),
        ],
        compiler_params=pltpu.CompilerParams(vmem_limit_bytes=VMEM_ROOM),
        cost_estimate=pl.CostEstimate(
            flops=45_000_000_000, bytes_accessed=90_000_000, transcendentals=0
        ),
        name="experts_backward",
    )(meta, slot_of, slot_of, slot_rows, grad_pair, up_full, down_full)


def reduce_kernel(
    slot_at,
    down_ref,
    up_ref,
    up_all,
    down_all,
    moe_in_far,
    grad_both_far,
    dx_routed_far,
    grad_logits_far,
    middle_far,
    qkv_far,
    attended_far,
    grad_state_far,
    patches_far,
    places_far,
    mods_far,
    mats_all_far,
    bias_rows_far,
    pre_time_far,
    cond_far,
    freq_low_far,
    grad_gate_far,
    grad_fin_far,
    thin_in_far,
    label_parts_far,
    out_ref,
    rows_ref,
    lat_ref,
    bias_ref,
    own,
    got_core,
    out_one,
    keep_one,
    got_one,
    out_two,
    keep_two,
    got_two,
    got_last,
    keep_z,
    out_z,
    got_z,
    got_pair,
    row_parts,
    late,
    up_here,
    down_here,
    up_sum,
    down_sum,
    dx_sum,
    grad_mid,
    grad_att,
    grad_qkv,
    qkv_sum,
    proj_sum,
    patch_sum,
    grad_mods,
    lat_full,
    lat_low,
    own_sem,
    core_send,
    core_recv,
    one_send,
    one_recv,
    two_send,
    two_recv,
    z_send,
    z_recv,
    row_send,
    row_recv,
    lat_own,
    lat_send,
    lat_recv,
    here_sem,
    core_free,
    one_free,
    load_sem,
    moe_in,
    grad_both,
    dx_routed,
    grad_logits,
    middle,
    qkv,
    attended,
    grad_state,
    patches,
    places,
    mods,
    mats_all,
    bias_rows,
    pre_time,
    cond,
    freq_low,
    grad_gate,
    grad_fin,
    thin_in,
    label_parts,
):
    full, low = jnp.float32, jnp.bfloat16
    loads = [
        pltpu.make_async_copy(far, near, load_sem.at[number])
        for number, (far, near) in enumerate(
            (
                (moe_in_far, moe_in),
                (grad_both_far, grad_both),
                (dx_routed_far, dx_routed),
                (grad_logits_far, grad_logits),
                (middle_far, middle),
                (qkv_far, qkv),
                (attended_far, attended),
                (grad_state_far, grad_state),
                (patches_far, patches),
                (places_far, places),
                (mods_far, mods),
                (mats_all_far, mats_all),
                (bias_rows_far, bias_rows),
                (pre_time_far, pre_time),
                (cond_far, cond),
                (freq_low_far, freq_low),
                (grad_gate_far, grad_gate),
                (grad_fin_far, grad_fin),
                (thin_in_far, thin_in),
                (label_parts_far, label_parts),
            )
        )
    ]
    for load in loads:
        load.start()
    n_down, n_up, n_late = down_ref.shape[0], up_ref.shape[0], late.shape[0]
    slabs = n_down + n_up + n_late
    ahead, ring = 2, got_core.shape[0]
    wide, narrow = lax.axis_index(WIDE), lax.axis_index(NARROW)
    z, x = wide // 2, wide % 2
    y, c = narrow // 2, narrow % 2
    x_one, y_one = x + (1 - c) * (1 - 2 * x), y + c * (1 - 2 * y)
    x_two, y_two = x + c * (1 - 2 * x), y + (1 - c) * (1 - 2 * y)
    to_one = (z * 2 + x_one, y_one * 2 + c)
    to_two = (z * 2 + x_two, y_two * 2 + c)
    first_mine = x * (1 - c) + y * c
    second_mine = y * (1 - c) + x * c
    first_step, second_step = 2 - c, 1 + c
    mates = [
        (wide, (y + (k // 2) * (1 - 2 * y)) * 2 + c + (k % 2) * (1 - 2 * c)) for k in range(1, 4)
    ]
    levels = [(((z + k) % 4) * 2 + x, narrow) for k in range(1, 4)]
    to_x, to_core = (z * 2 + 1 - x, narrow), mates[0]
    barrier = pltpu.get_barrier_semaphore()
    for target in mates + levels + [to_x]:
        pl.semaphore_signal(barrier, inc=1, device_id=target, device_id_type=MESH_ID)
    pl.semaphore_wait(barrier, 7)

    def remote(source, target, send, recv, device):
        return pltpu.make_async_remote_copy(
            src_ref=source,
            dst_ref=target,
            send_sem=send,
            recv_sem=recv,
            device_id=device,
            device_id_type=MESH_ID,
        )

    def core_copy(source, s):
        return remote(
            source.at[:, 1 - c],
            got_core.at[s % ring],
            core_send.at[s % 4],
            core_recv.at[s % ring],
            to_core,
        )

    def own_copy(source, s):
        return pltpu.make_async_copy(source.at[:, c], own.at[s % 3], own_sem.at[s % 3])

    def one_copy(s):
        return remote(
            out_one.at[s % 2], got_one.at[s % ring], one_send.at[s % 2], one_recv.at[s % ring], to_one
        )

    def two_copy(s, turned=False):
        if turned:
            start, end = out_two.at[s % 2, 0], got_last.at[s // 2]
        else:
            start, end = out_two.at[s % 2], got_two.at[s // 2]
        return remote(start, end, two_send.at[s % 2], two_recv.at[s], to_two)

    def z_copy(s, k, turned=False):
        start, end = out_z.at[s % 2, (z + k) % 4], got_pair.at[s // 2, k - 1]
        if not turned:
            start, end = start.at[0], got_z.at[s // 2, k - 1]
        return remote(start, end, z_send.at[s % 2, k - 1], z_recv.at[s, k - 1], levels[k - 1])

    def by_order(s, run):
        turned = s % 2 == 1

        @pl.when(turned)
        def _():
            run(True)

        @pl.when(jnp.logical_not(turned))
        def _():
            run(False)

    def row_copy(r, k):
        mate = mates[k - 1]
        return remote(
            row_parts.at[r % 2, mate[1]],
            rows_ref.at[r, narrow],
            row_send.at[r % 2, k - 1],
            row_recv.at[r, k - 1],
            mate,
        )

    def lat_level(k):
        return remote(
            lat_low, lat_ref.at[z, x, y, c], lat_send.at[k - 1], lat_recv.at[k - 1], levels[k - 1]
        )

    def lat_x():
        spot = lat_ref.at[:, x, y, c]
        return remote(spot, spot, lat_send.at[3], lat_recv.at[3], to_x)

    def lat_y():
        spot = lat_ref.at[:, :, y, c]
        return remote(spot, spot, lat_send.at[4], lat_recv.at[4], mates[1])

    def lat_core():
        spot = lat_ref.at[:, :, :, c]
        return remote(spot, spot, lat_send.at[5], lat_recv.at[5], to_core)

    def lat_own_copy():
        return pltpu.make_async_copy(lat_low, lat_ref.at[z, x, y, c], lat_own.at[0])

    def begin(source, s):
        @pl.when(s >= 4)
        def _():
            core_copy(source, s).wait_send()

        @pl.when(s >= ring)
        def _():
            pl.semaphore_wait(core_free, 1)

        core_copy(source, s).start()
        own_copy(source, s).start()

    def stage_core(s):
        own_copy(down_ref.at[0], s).wait()
        core_copy(down_ref.at[0], s).wait_recv()

        @pl.when(s >= 2)
        def _():
            one_copy(s).wait_send()

        @pl.when(s >= ring)
        def _():
            pl.semaphore_wait(one_free, 1)

        for level in range(4):
            for other in range(2):
                place = level * 2 + other
                base = level * 4 + other * second_step
                send_at = base + (1 - first_mine) * first_step
                out_one[s % 2, place] = (
                    own[s % 3, send_at].astype(full) + got_core[s % ring, send_at].astype(full)
                ).astype(low)
        one_copy(s).start()
        for level in range(4):
            for other in range(2):
                place = level * 2 + other
                base = level * 4 + other * second_step
                keep_at = base + first_mine * first_step
                keep_one[s % 3, place] = own[s % 3, keep_at].astype(full) + got_core[
                    s % ring, keep_at
                ].astype(full)

        @pl.when(s < slabs - ring)
        def _():
            pl.semaphore_signal(core_free, inc=1, device_id=to_core, device_id_type=MESH_ID)

    def stage_one(s):
        one_copy(s).wait_recv()

        def run(turned):
            @pl.when(s >= 2)
            def _():
                sent(s, turned)

            if turned:
                for level in range(4):
                    for other in range(2):
                        out_z[s % 2, level, other] = (
                            keep_one[s % 3, level * 2 + other]
                            + got_one[s % ring, level * 2 + other].astype(full)
                        ).astype(low)
                for k in range(1, 4):
                    z_copy(s, k, True).start()
                for other in range(2):
                    keep_two[s % 3, other] = keep_one[s % 3, z * 2 + other] + got_one[
                        s % ring, z * 2 + other
                    ].astype(full)
            else:
                for level in range(4):
                    send_at = level * 2 + 1 - second_mine
                    out_two[s % 2, level] = (
                        keep_one[s % 3, send_at] + got_one[s % ring, send_at].astype(full)
                    ).astype(low)
                two_copy(s).start()
                for level in range(4):
                    keep_at = level * 2 + second_mine
                    keep_two[s % 3, level] = keep_one[s % 3, keep_at] + got_one[
                        s % ring, keep_at
                    ].astype(full)

        by_order(s, run)

        @pl.when(s < slabs - ring)
        def _():
            pl.semaphore_signal(one_free, inc=1, device_id=to_one, device_id_type=MESH_ID)

    def sent(s, turned):
        if turned:
            for k in range(1, 4):
                z_copy(s, k, True).wait_send()
        else:
            two_copy(s).wait_send()

    def sent_last(s, turned):
        if turned:
            two_copy(s, True).wait_send()
        else:
            for k in range(1, 4):
                z_copy(s, k).wait_send()

    def stage_two(s):
        def run(turned):
            if turned:
                for k in range(1, 4):
                    z_copy(s, k, True).wait_recv()
            else:
                two_copy(s).wait_recv()

            @pl.when(s >= 2)
            def _():
                sent_last(s, turned)

            if turned:

                def gathered(other):
                    total = keep_two[s % 3, other]
                    for k in range(3):
                        total = total + got_pair[s // 2, k, other].astype(full)
                    return total

                out_two[s % 2, 0] = gathered(1 - second_mine).astype(low)
                two_copy(s, True).start()
                keep_z[s % 3] = gathered(second_mine)
            else:
                for level in range(4):
                    out_z[s % 2, level, 0] = (
                        keep_two[s % 3, level] + got_two[s // 2, level].astype(full)
                    ).astype(low)
                for k in range(1, 4):
                    z_copy(s, k).start()
                keep_z[s % 3] = keep_two[s % 3, z] + got_two[s // 2, z].astype(full)

        by_order(s, run)

    def direct_place(s):
        late_at = s - n_down - n_up
        return (s < n_down) | ((late_at >= 0) & (late_at < SHARED))

    def row_place(s):
        return jnp.where(s < n_down + n_up, s - n_down, s - n_down - SHARED)

    def finish(s):
        def run(turned):
            if turned:
                two_copy(s, True).wait_recv()
                keep_z[s % 3] += got_last[s // 2].astype(full)
            else:
                for k in range(1, 4):
                    z_copy(s, k).wait_recv()
                total = keep_z[s % 3]
                for k in range(3):
                    total = total + got_z[s // 2, k].astype(full)
                keep_z[s % 3] = total

        by_order(s, run)
        total = keep_z[s % 3]

        @pl.when(direct_place(s))
        def _():
            out_ref[jnp.clip(jnp.where(s < n_down, s, s - n_up), 0, n_down + SHARED - 1)] = total

        @pl.when(jnp.logical_not(direct_place(s)))
        def _():
            r = row_place(s)

            @pl.when(r >= 2)
            def _():
                for k in range(1, 4):
                    row_copy(r, k).wait_send()

            for n in range(NARROW_PIECES):
                row_parts[r % 2, n] = total[n * ROWS : (n + 1) * ROWS]
            rows_ref[r, narrow] = row_parts[r % 2, narrow]
            for k in range(1, 4):
                row_copy(r, k).start()

    def rows_in(s):
        @pl.when(jnp.logical_not(direct_place(s)))
        def _():
            for k in range(1, 4):
                row_copy(row_place(s), k).wait_recv()

    tokens = moe_in.shape[0]
    lats = tokens // PATCHES

    def matrix(number, start, stop):
        chunk = mats_all[number // 2, number % 2]
        return chunk.reshape(D, chunk.shape[-1])[:, start:stop]

    def mod_row(start, number):
        return mods[pl.ds(start // PATCHES, 1), number * D : (number + 1) * D]

    def keep_mod(start, number, values):
        grad_mods[pl.ds(start // PATCHES, 1), number * D : (number + 1) * D] = jnp.sum(
            values, 0, keepdims=True
        )

    def add_bias(number, values):
        for k in range(values.shape[1] // D):
            bias_ref[number + k : number + k + 1, :] += jnp.sum(
                values[:, k * D : (k + 1) * D], 0, keepdims=True
            )

    def prepare():
        bias_ref[...] = jnp.zeros_like(bias_ref)
        qkv_sum[...] = jnp.zeros_like(qkv_sum)
        proj_sum[...] = jnp.zeros_like(proj_sum)
        patch_sum[...] = jnp.zeros_like(patch_sum)
        grad_mods[...] = jnp.zeros_like(grad_mods)

    def fetch(shared_id):
        e = EXPERTS + shared_id
        first = pltpu.make_async_copy(down_all.at[e], down_here, here_sem.at[0])
        second = pltpu.make_async_copy(up_all.at[e], up_here, here_sem.at[1])
        first.start()
        second.start()
        first.wait()
        second.wait()
        up_sum[...] = jnp.zeros_like(up_sum)
        down_sum[...] = jnp.zeros_like(down_sum)

    def shared_block(shared_id, start):
        span = pl.ds(start, PATCHES)
        rows, grads = moe_in[span, :], grad_both[span, :]
        total = jnp.zeros((PATCHES, D), full) if shared_id == 0 else dx_sum[span, :]
        for cut in range(0, FF, CUT):
            up_part = up_columns(up_here, cut)
            activated, slope = gelu_slope(product(rows, up_part))
            grad_act = contract(grads, down_here[cut : cut + CUT], 1, 1)
            grad_pre = (grad_act * slope).astype(low)
            down_sum[cut : cut + CUT, :] += contract(activated.astype(low), grads, 0, 0)
            up_sum[:, cut : cut + CUT] += contract(rows, grad_pre, 0, 0)
            total = total + contract(grad_pre, up_part, 1, 1)
        dx_sum[span, :] = total

    def shared_slabs(shared_id):
        for w in range(WIDE_PIECES):
            for n in range(NARROW_PIECES):
                at = (w * NARROW_PIECES + n) * PIECE
                late[shared_id, w * 2 + n // 2, n % 2] = down_sum[at : at + PIECE, :].astype(low)
                late[SHARED + shared_id, w * 2 + n // 2, n % 2] = up_sum[
                    w * PIECE : (w + 1) * PIECE, n * D : (n + 1) * D
                ].astype(low)

    def back_rows(start):
        def group(number, unused):
            for step in range(8):
                token = start + number * 8 + step
                dx_sum[pl.ds(token, 1), :] += (
                    dx_routed[pl.ds(slot_at[0, token], 1), :]
                    + dx_routed[pl.ds(slot_at[1, token], 1), :]
                )
            return unused

        lax.fori_loop(0, PATCHES // 8, group, 0)

    def back_out(start):
        span = pl.ds(start, PATCHES)
        grads = dx_sum[span, :] + contract(
            grad_logits[span, :].astype(low), matrix(0, 4 * D, 4 * D + 128), 1, 1
        )
        normed, inv_std = layer_norm(middle[span, :])
        keep_mod(start, 3, grads)
        keep_mod(start, 4, grads * normed)
        grads = grad_state[span, :] + norm_back(
            grads * (1.0 + mod_row(start, 4)), normed, inv_std
        )
        grad_mid[...] = grads
        proj = matrix(0, 3 * D, 4 * D)
        rows = attended[span, :]
        keep_mod(start, 2, (product(rows, proj) + bias_rows[3:4, :]) * grads)
        grads = grads * mod_row(start, 2)
        add_bias(3, grads)
        grads = grads.astype(low)
        proj_sum[...] += contract(rows, grads, 0, 0)
        grad_att[...] = contract(grads, proj, 1, 1).astype(low)

    def back_pair(pair, start):
        span = pl.ds(start, PATCHES)
        lane = lax.broadcasted_iota(jnp.int32, (PATCHES, 2 * HD), 1)
        at = pair * 2 * HD
        queries = qkv[span, at : at + 2 * HD]
        keys = qkv[span, D + at : D + at + 2 * HD]
        values = qkv[span, 2 * D + at : 2 * D + at + 2 * HD]
        grads = grad_att[:, at : at + 2 * HD]
        sums = None
        for half in range(2):
            mine = (lane < HD) if half == 0 else (lane >= HD)
            scores = contract(jnp.where(mine, queries, 0), keys, 1, 1) * HD ** (-0.5)
            powers = jnp.exp(scores - jnp.max(scores, 1, keepdims=True))
            probs = powers / jnp.sum(powers, 1, keepdims=True)
            grad_mine = jnp.where(mine, grads, 0)
            grad_probs = contract(grad_mine, values, 1, 1)
            grad_scores = (
                probs
                * (grad_probs - jnp.sum(probs * grad_probs, 1, keepdims=True))
                * HD ** (-0.5)
            ).astype(low)
            parts = (
                product(grad_scores, jnp.where(mine, keys, 0)),
                contract(grad_scores, jnp.where(mine, queries, 0), 0, 0),
                contract(probs.astype(low), grad_mine, 0, 0),
            )
            sums = parts if sums is None else [a + b for a, b in zip(sums, parts)]
        for k in range(3):
            where = k * D + at
            grad_qkv[:, where : where + 2 * HD] = sums[k].astype(low)
            bias_ref[k : k + 1, at : at + 2 * HD] += jnp.sum(sums[k], 0, keepdims=True)

    def back_in(start):
        span = pl.ds(start, PATCHES)
        emb = contract(patches[span, :], matrix(2, 4 * D, 4 * D + 128), 1, 1)
        emb = emb + bias_rows[10:11, :] + places[...]
        normed, inv_std = layer_norm(emb)
        rows = (normed * (1.0 + mod_row(start, 1)) + mod_row(start, 0)).astype(low)
        qkv_sum[...] += contract(rows, grad_qkv[...], 0, 0)
        grads = contract(grad_qkv[...], matrix(0, 0, 3 * D), 1, 1)
        keep_mod(start, 0, grads)
        keep_mod(start, 1, grads * normed)
        grads = grad_mid[...] + norm_back(grads * (1.0 + mod_row(start, 1)), normed, inv_std)
        add_bias(10, grads)
        patch_sum[...] += contract(grads.astype(low), patches[span, :], 0, 0)

    def silu_slope(values):
        gate = jax.nn.sigmoid(values)
        return gate + values * gate * (1.0 - gate)

    def back_conditions():
        grad_mods[:, 5 * D :] = grad_gate[...]
        grads = grad_mods[...]
        mod_low, fin_low = grads.astype(low), grad_fin[...].astype(low)
        grad_act = (
            contract(mod_low[:, : 4 * D], matrix(1, 0, 4 * D), 1, 1)
            + contract(mod_low[:, 4 * D :], matrix(2, 0, 2 * D), 1, 1)
            + contract(fin_low, matrix(2, 2 * D, 4 * D), 1, 1)
        )
        grad_cond = silu_slope(cond[...]) * grad_act
        high = grad_cond.astype(low)
        grad_time = silu_slope(pre_time[...]) * contract(high, matrix(3, 1024, 1408), 1, 1)
        add_bias(4, grads)
        add_bias(11, grad_time)
        add_bias(12, grad_cond)
        add_bias(13, grad_fin[...])
        high = high.astype(full)
        rest = grad_cond - high
        middle_part = rest.astype(low).astype(full)
        act = jax.nn.silu(cond[...]).astype(low).astype(full)
        hid = jax.nn.silu(pre_time[...]).astype(low).astype(full)
        mod_low, fin_low = mod_low.astype(full), fin_low.astype(full)
        quarters = (
            jnp.concatenate([act, hid, mod_low[:, : 2 * D]], 1),
            mod_low[:, 2 * D :],
            jnp.concatenate([fin_low, high, grad_time.astype(low).astype(full)], 1),
            jnp.concatenate(
                [
                    freq_low[...].astype(full),
                    middle_part,
                    rest - middle_part,
                    label_parts[...].astype(full),
                    jnp.zeros((8, D), full),
                ],
                1,
            ),
        )
        for lat in range(lats):
            for k in range(4):
                lat_full[lat * 4 + k : lat * 4 + k + 1, :] = quarters[k][lat : lat + 1, :]
        lat_low[...] = lat_full[...].astype(low)

    def last_slabs():
        for w in range(WIDE_PIECES):
            span = slice(w * PIECE, (w + 1) * PIECE)
            for n in range(3):
                late[2 * SHARED, w * 2 + n // 2, n % 2] = qkv_sum[
                    span, n * D : (n + 1) * D
                ].astype(low)
            late[2 * SHARED, w * 2 + 1, 1] = proj_sum[span, :].astype(low)
            thin = thin_in[span, :] + pltpu.roll(patch_sum[span, :], EXPERTS + PD, 1)
            for n in range(NARROW_PIECES):
                late[2 * SHARED + 1, w * 2 + n // 2, n % 2] = jnp.zeros((PIECE, D), low)
            late[2 * SHARED + 1, w * 2, 0, :, :128] = thin.astype(low)

    first_lat = SHARED * lats
    units = (
        back_rows,
        back_out,
        lambda start: back_pair(0, start),
        lambda start: back_pair(1, start),
        lambda start: back_pair(2, start),
        back_in,
    )
    after = first_lat + len(units) * lats

    def tick(t, unused):
        first = 0
        for source, count in ((down_ref, n_down), (up_ref, n_up), (late, n_late)):

            @pl.when((t >= first) & (t < first + count))
            def _():
                begin(source.at[jnp.clip(t - first, 0, count - 1)], t)

            first += count

        for lag, stage in enumerate((stage_core, stage_one, stage_two, finish, rows_in)):
            s = t - ahead - 2 * lag

            @pl.when((s >= 0) & (s < slabs))
            def _():
                stage(s)

        @pl.when(t == 0)
        def _():
            prepare()
            for load in loads[:3]:
                load.wait()

        @pl.when(t == first_lat)
        def _():
            for load in loads[3:]:
                load.wait()

        for shared_id in range(SHARED):
            start_at = shared_id * lats

            @pl.when(t == start_at)
            def _():
                fetch(shared_id)

            @pl.when((t >= start_at) & (t < start_at + lats))
            def _():
                shared_block(
                    shared_id,
                    pl.multiple_of(jnp.clip(t - start_at, 0, lats - 1) * PATCHES, PATCHES),
                )

            @pl.when(t == start_at + lats - 1)
            def _():
                shared_slabs(shared_id)

        for number, unit in enumerate(units):

            @pl.when((t >= first_lat) & (t < after) & ((t - first_lat) % len(units) == number))
            def _():
                lat = jnp.clip((t - first_lat) // len(units), 0, lats - 1)
                unit(pl.multiple_of(lat * PATCHES, PATCHES))

        @pl.when(t == after)
        def _():
            back_conditions()
            lat_own_copy().start()
            for k in range(1, 4):
                lat_level(k).start()
            lat_own_copy().wait()

        @pl.when(t == after + 1)
        def _():
            last_slabs()

        @pl.when(t == after + 3)
        def _():
            for k in range(1, 4):
                lat_level(k).wait_recv()
            lat_x().start()

        @pl.when(t == after + 5)
        def _():
            lat_x().wait_recv()
            lat_y().start()

        @pl.when(t == after + 7)
        def _():
            lat_y().wait_recv()
            lat_core().start()

        return unused

    lax.fori_loop(0, slabs + ahead + 8, tick, 0)
    for back in range(4):
        core_copy(down_ref.at[0], slabs - 1 - back).wait_send()
    turned = rows_ref.shape[0]
    for back in range(2):
        s = slabs - 1 - back
        one_copy(s).wait_send()
        sent(s, s % 2 == 1)
        sent_last(s, s % 2 == 1)
        for k in range(1, 4):
            row_copy(turned - 1 - back, k).wait_send()
    for k in range(1, 4):
        lat_level(k).wait_send()
    lat_x().wait_send()
    lat_y().wait_send()
    lat_core().wait()


def reduce_slabs(slot_of, down_slabs, up_slabs, up_all, down_all, members):
    n_late = 2 * SHARED + 2
    routed = down_slabs.shape[0]
    slabs = 2 * routed + n_late
    direct, turned = routed + SHARED, routed + SHARED + 2
    ring = 4
    low, full = jnp.bfloat16, jnp.float32
    sources = [
        member.reshape(routed, WIDE_PIECES * NARROW_PIECES // 2, 2, PIECE, D)
        for member in (down_slabs, up_slabs)
    ]
    tokens = members[0].shape[0]
    dma, regular = pltpu.SemaphoreType.DMA, pltpu.SemaphoreType.REGULAR
    vmem, anywhere = pl.BlockSpec(memory_space=pltpu.VMEM), pl.BlockSpec(memory_space=pl.ANY)
    sums, rows, lats, bias_sum = pl.pallas_call(
        reduce_kernel,
        out_shape=[
            jax.ShapeDtypeStruct((direct, PIECE, D), full),
            jax.ShapeDtypeStruct((turned, NARROW_PIECES, ROWS, D), full),
            jax.ShapeDtypeStruct((4, 2, 2, 2, LAT_ROWS, LAT_COLS), low),
            jax.ShapeDtypeStruct((16, D), full),
        ],
        in_specs=[pl.BlockSpec(memory_space=pltpu.SMEM)] + [anywhere] * (4 + len(members)),
        out_specs=[vmem, vmem, anywhere, vmem],
        scratch_shapes=[
            pltpu.VMEM((3, 16, PIECE, D), low),
            pltpu.VMEM((ring, 16, PIECE, D), low),
            pltpu.VMEM((2, 8, PIECE, D), low),
            pltpu.VMEM((3, 8, PIECE, D), full),
            pltpu.VMEM((ring, 8, PIECE, D), low),
            pltpu.VMEM((2, 4, PIECE, D), low),
            pltpu.VMEM((3, 4, PIECE, D), full),
            pltpu.VMEM(((slabs + 1) // 2, 4, PIECE, D), low),
            pltpu.VMEM(((slabs + 1) // 2, PIECE, D), low),
            pltpu.VMEM((3, PIECE, D), full),
            pltpu.VMEM((2, 4, 2, PIECE, D), low),
            pltpu.VMEM(((slabs + 1) // 2, 3, PIECE, D), low),
            pltpu.VMEM((slabs // 2, 3, 2, PIECE, D), low),
            pltpu.VMEM((2, NARROW_PIECES, ROWS, D), full),
            pltpu.VMEM((n_late, 16, 2, PIECE, D), low),
            pltpu.VMEM((NARROW_PIECES, D, D), low),
            pltpu.VMEM((FF, D), low),
            pltpu.VMEM((D, FF), full),
            pltpu.VMEM((FF, D), full),
            pltpu.VMEM((tokens, D), full),
            pltpu.VMEM((PATCHES, D), full),
            pltpu.VMEM((PATCHES, D), low),
            pltpu.VMEM((PATCHES, 3 * D), low),
            pltpu.VMEM((D, 3 * D), full),
            pltpu.VMEM((D, D), full),
            pltpu.VMEM((D, 128), full),
            pltpu.VMEM((8, 6 * D), full),
            pltpu.VMEM((LAT_ROWS, LAT_COLS), full),
            pltpu.VMEM((LAT_ROWS, LAT_COLS), low),
            dma((3,)),
            dma((4,)),
            dma((ring,)),
            dma((2,)),
            dma((ring,)),
            dma((2,)),
            dma((slabs,)),
            dma((2, 3)),
            dma((slabs, 3)),
            dma((2, 3)),
            dma((turned, 3)),
            dma((1,)),
            dma((6,)),
            dma((6,)),
            dma((2,)),
            regular,
            regular,
            dma((len(members),)),
        ]
        + [pltpu.VMEM(member.shape, member.dtype) for member in members],
        compiler_params=pltpu.CompilerParams(
            collective_id=0, has_side_effects=True, vmem_limit_bytes=REDUCE_ROOM
        ),
        name="reduce_slabs",
    )(slot_of, *sources, up_all, down_all, *members)
    return sums, rows, lats.reshape(-1, LAT_COLS), bias_sum


def plain_grads(
    down_slabs, up_slabs, mats_slabs, thin, grad_bias, lows, grad_cond, labels, row_count
):
    def scattered(member):
        return lax.psum_scatter(member, AXES, scatter_dimension=1, tiled=True)

    proj_grad = scattered(mats_slabs)
    row_start = lax.axis_index(AXES) * row_count
    thin_grad = lax.psum_scatter(thin, AXES, scatter_dimension=0, tiled=True)
    bias_grad = lax.psum_scatter(grad_bias, AXES, scatter_dimension=0, tiled=True)
    grad_mod, grad_time2, grad_fin, grad_time1, grad_table = latent_grads(
        lows, grad_cond, labels, row_start, row_count
    )
    mats_grad = jnp.concatenate(
        [proj_grad[0], grad_mod, grad_time2, grad_fin, thin_grad, grad_time1, grad_table], 1
    )
    return (mats_grad, scattered(up_slabs), scattered(down_slabs), bias_grad)


def spread(value, place):
    lane = lax.broadcasted_iota(jnp.int32, (1, 128), 1)
    return jnp.where(lane == place, value, 0.0)


def pick(row, place):
    lane = lax.broadcasted_iota(jnp.int32, (1, 128), 1)
    return jnp.sum(jnp.where(lane == place, row, 0.0), 1, keepdims=True)


def total(values):
    return jnp.sum(jnp.sum(values, 1, keepdims=True), 0, keepdims=True)


def turn_line(values):
    count = max(values.shape)
    same = lax.broadcasted_iota(jnp.int32, (count, count), 0) == lax.broadcasted_iota(
        jnp.int32, (count, count), 1
    )
    across = 1 if values.shape[0] == 1 else 0
    return jnp.sum(jnp.where(same, values, 0.0), across, keepdims=True)


def joined(chunks):
    return jnp.concatenate([chunks[j] for j in range(NARROW_PIECES)], 1)


def by_piece(values, start_last, width_last):
    bounds = [sum(column_widths()[:k]) for k in range(len(column_widths()) + 1)]
    last_lane = lax.broadcasted_iota(jnp.int32, (ROWS, width_last), 1) + start_last
    chosen_value = values[0]
    for k in range(6, len(column_widths())):
        chosen_value = jnp.where(last_lane >= bounds[k], values[k - 5], chosen_value)
    return chosen_value


def factored(grad, row, col, mean):
    return grad * lax.rsqrt(row * col / mean)


def update_kernel(
    sums_ref,
    rows_ref,
    lat_ref,
    bias_sum,
    loss_ref,
    mats_row,
    mats_col,
    up_row,
    up_col,
    down_row,
    down_col,
    bias_state,
    mats_grad,
    mats_row_new,
    mats_col_new,
    up_row_new,
    up_col_new,
    down_row_new,
    down_col_new,
    bias_grad,
    bias_state_new,
    line_out,
    squares_out,
    part,
    got_plane,
    got_level,
    result,
    squares_plane,
    squares_level,
    sems,
):
    full, low = jnp.float32, jnp.bfloat16
    wide, narrow = lax.axis_index(WIDE), lax.axis_index(NARROW)
    z, spot = wide // 2, (wide % 2) * 4 + narrow

    def plane_device(k):
        there = (spot + k) % 8
        return (z * 2 + there // 4, there % 4)

    def level_device(k):
        return (((z + k) % 4) * 2 + wide % 2, narrow)

    barrier = pltpu.get_barrier_semaphore()
    for k in range(1, 8):
        pl.semaphore_signal(barrier, inc=1, device_id=plane_device(k), device_id_type=MESH_ID)
    for k in range(1, 4):
        pl.semaphore_signal(barrier, inc=1, device_id=level_device(k), device_id_type=MESH_ID)
    pl.semaphore_wait(barrier, 10)

    def remote(source, target, phase, k, device):
        return pltpu.make_async_remote_copy(
            src_ref=source,
            dst_ref=target,
            send_sem=sems.at[0, phase, k],
            recv_sem=sems.at[1, phase, k],
            device_id=device,
            device_id_type=MESH_ID,
        )

    def exchange(copies):
        for copy in copies:
            copy.start()
        for copy in copies:
            copy.wait()

    count = lat_ref.shape[0] // 4
    order = lax.broadcasted_iota(jnp.int32, (count, count * 4), 0) * 4
    place = lax.broadcasted_iota(jnp.int32, (count, count * 4), 1)
    quarters = [
        product((place == order + k).astype(low), lat_ref[...]).astype(low) for k in range(4)
    ]
    owner_row = (wide * NARROW_PIECES + narrow) * ROWS
    chosen = (
        lax.broadcasted_iota(jnp.int32, (16, D), 1)
        == lax.broadcasted_iota(jnp.int32, (16, D), 0) + owner_row
    ).astype(low)

    def rows_of(member):
        return contract(chosen, member, 1, 1).astype(low)

    act_rows = rows_of(quarters[0][:, :D])
    hid_rows = rows_of(quarters[0][:, D : 2 * D])
    high = quarters[2][:, 2 * D : 3 * D]
    for j in range(NARROW_PIECES):
        mats_grad[:, j * D : (j + 1) * D] = rows_ref[EXPERTS + SHARED, j]
    mats_grad[:, 4 * D : 6 * D] = product(act_rows, quarters[0][:, 2 * D :])[:ROWS]
    mats_grad[:, 6 * D : 10 * D] = product(act_rows, quarters[1])[:ROWS]
    mats_grad[:, 10 * D : 11 * D] = product(hid_rows, high)[:ROWS]
    mats_grad[:, 11 * D : 13 * D] = product(act_rows, quarters[2][:, : 2 * D])[:ROWS]
    time_rows = rows_of(quarters[2][:, 3 * D :])
    time_one = product(time_rows, quarters[3][:, :FREQ])
    label_at = FREQ + 2 * D
    labels = quarters[3][:, label_at : label_at + 128].astype(full)
    label = labels[:, 0:1] * 32.0 + labels[:, 1:2]
    label_hot = (
        lax.broadcasted_iota(jnp.int32, (count, 1024), 1).astype(full) == label
    ).astype(low)
    table = (
        product(rows_of(high), label_hot)
        + product(rows_of(quarters[3][:, FREQ : FREQ + D]), label_hot)
        + product(rows_of(quarters[3][:, FREQ + D : FREQ + 2 * D]), label_hot)
    )
    start_last = 13 * D
    width_last = mats_grad.shape[1] - start_last
    room = 11 * 128
    thin = jnp.concatenate(
        [rows_ref[EXPERTS + SHARED + 1, 0][:, :128], jnp.zeros((4, 128), full)], 0
    )
    thin = jnp.where(
        lax.broadcasted_iota(jnp.int32, (16, 128), 1) < EXPERTS + 2 * PD, thin, 0.0
    )

    def padded(member):
        return jnp.concatenate(
            [member, jnp.zeros((16, room - member.shape[1]), full)], 1
        )

    last = (
        padded(thin)
        + pltpu.roll(padded(time_one), EXPERTS + 2 * PD, 1)
        + pltpu.roll(padded(table), EXPERTS + 2 * PD + FREQ, 1)
    )
    mats_grad[:, start_last:] = last[:ROWS, :width_last]

    part[...] = jnp.zeros_like(part)
    widths = column_widths()
    mats_at, line_at, bias_at = 360, 416, 432
    total_cols = mats_grad.shape[1]
    cuts = [(at, min(at + 128, total_cols)) for at in range(0, total_cols, 128)]
    for number, (begin, end) in enumerate(cuts):
        values = mats_grad[:, begin:end]
        part[mats_at + number : mats_at + number + 1, : end - begin] = jnp.sum(
            values * values + eps_fact, 0, keepdims=True
        )
    bounds = [sum(widths[:k]) for k in range(len(widths) + 1)]
    last_lane = lax.broadcasted_iota(jnp.int32, (ROWS, width_last), 1) + start_last
    last_sq = mats_grad[:, start_last:] * mats_grad[:, start_last:] + eps_fact
    line = spread(loss_ref[...], 46)
    for k in range(len(widths)):
        if k < 5:
            values = mats_grad[:, bounds[k] : bounds[k + 1]]
            sq = values * values + eps_fact
        else:
            sq = jnp.where((last_lane >= bounds[k]) & (last_lane < bounds[k + 1]), last_sq, 0.0)
        new = decay * turn_line(mats_row[k : k + 1, :]) + (1.0 - decay) * (
            jnp.sum(sq, 1, keepdims=True) / widths[k]
        )
        mats_row_new[k : k + 1, :] = turn_line(new)
        line = line + spread(jnp.sum(new, 0, keepdims=True), k)

    def begin_up(e, line):
        values = joined(rows_ref[e])
        sq = values * values + eps_fact
        new = decay * turn_line(up_row[pl.ds(e, 1), :]) + (1.0 - decay) * (jnp.sum(sq, 1, keepdims=True) / FF)
        up_row_new[pl.ds(e, 1), :] = turn_line(new)
        cols = jnp.sum(sq, 0, keepdims=True)
        for k in range(FF // 128):
            part[pl.ds(24 * k + e, 1), :] = cols[:, 128 * k : 128 * (k + 1)]
        return line + spread(jnp.sum(new, 0, keepdims=True), 10 + e)

    def begin_down(e, line):
        values = sums_ref[e]
        sq = values * values + eps_fact
        new = decay * turn_line(down_row[pl.ds(e, 1), :]) + (1.0 - decay) * (jnp.sum(sq, 1, keepdims=True) / D)
        down_row_new[pl.ds(e, 1), :] = turn_line(new)
        cols = jnp.sum(sq, 0, keepdims=True)
        for k in range(D // 128):
            part[pl.ds(24 * (12 + k) + e, 1), :] = cols[:, 128 * k : 128 * (k + 1)]
        return line + spread(jnp.sum(new, 0, keepdims=True), 28 + e)

    line = lax.fori_loop(0, EXPERTS + SHARED, begin_up, line, unroll=True)
    line = lax.fori_loop(0, EXPERTS + SHARED, begin_down, line, unroll=True)
    part[line_at : line_at + 1, :] = line
    for k in range(D // 128):
        part[bias_at + 16 * k : bias_at + 16 * (k + 1), :] = bias_sum[:, 128 * k : 128 * (k + 1)]

    exchange(
        [
            remote(
                part.at[pl.ds(((spot + k) % 8) * 64, 64)], got_plane.at[k], 0, k, plane_device(k)
            )
            for k in range(1, 8)
        ]
    )
    here = part[pl.ds(pl.multiple_of(spot * 64, 64), 64), :]
    for k in range(1, 8):
        here = here + got_plane[k]
    got_level[z] = here.reshape(4, 16, 128)
    exchange(
        [remote(got_level.at[z], got_level.at[z], 1, k, level_device(k)) for k in range(1, 4)]
    )
    result[spot] = got_level[0] + got_level[1] + got_level[2] + got_level[3]
    exchange(
        [remote(result.at[spot], result.at[spot], 3, k, plane_device(k)) for k in range(1, 8)]
    )

    def sums_row(row, width=128):
        if isinstance(row, int):
            return result[row // 64, (row // 16) % 4, row % 16 : row % 16 + 1, :width]
        return result[row // 64, (row // 16) % 4, pl.ds(row % 16, 1), :width]

    line = sums_row(line_at)
    line_out[...] = line
    room = bias_grad.shape[1]
    begin = (wide * NARROW_PIECES + narrow) * room
    parts = []
    for k in range(3):
        block = jnp.minimum(begin // 128 + k, 47)
        parts.append(sums_row(bias_at + (block % 3) * 16 + block // 3))
    parts = jnp.broadcast_to(jnp.concatenate(parts, 1), (8, D))
    bias_grad[...] = pltpu.roll(parts, (D - begin % 128) % D, 1)[0:1, :room]
    for number, (begin, end) in enumerate(cuts):
        mats_col_new[:, begin:end] = decay * mats_col[:, begin:end] + (1.0 - decay) * (
            sums_row(mats_at + number, end - begin) / D
        )

    squares = jnp.zeros((1, 128), full)
    for k in range(5):
        begin, end = bounds[k], bounds[k + 1]
        step = factored(
            mats_grad[:, begin:end],
            turn_line(mats_row_new[k : k + 1, :]),
            mats_col_new[:, begin:end],
            pick(line, k) / D,
        )
        squares = squares + spread(total(step * step), k)
    last = range(5, len(widths))
    step_last = factored(
        mats_grad[:, start_last:],
        by_piece([turn_line(mats_row_new[k : k + 1, :]) for k in last], start_last, width_last),
        mats_col_new[:, start_last:],
        by_piece([pick(line, k) / D for k in last], start_last, width_last),
    )
    for k in last:
        inside = (last_lane >= bounds[k]) & (last_lane < bounds[k + 1])
        squares = squares + spread(total(jnp.where(inside, step_last * step_last, 0.0)), k)

    def step_up(e, squares):
        cols = jnp.concatenate([sums_row(24 * k + e) for k in range(FF // 128)], 1)
        new = decay * up_col[pl.ds(e, 1), :] + (1.0 - decay) * (cols / D)
        up_col_new[pl.ds(e, 1), :] = new
        row = turn_line(up_row_new[pl.ds(e, 1), :])
        step = factored(joined(rows_ref[e]), row, new, pick(line, 10 + e) / D)
        return squares + spread(total(step * step), 10 + e)

    def step_down(e, squares):
        cols = jnp.concatenate([sums_row(24 * (12 + k) + e) for k in range(D // 128)], 1)
        new = decay * down_col[pl.ds(e, 1), :] + (1.0 - decay) * (cols / FF)
        down_col_new[pl.ds(e, 1), :] = new
        row = turn_line(down_row_new[pl.ds(e, 1), :])
        step = factored(sums_ref[e], row, new, pick(line, 28 + e) / FF)
        return squares + spread(total(step * step), 28 + e)

    squares = lax.fori_loop(0, EXPERTS + SHARED, step_up, squares, unroll=True)
    squares = lax.fori_loop(0, EXPERTS + SHARED, step_down, squares, unroll=True)
    state = decay * bias_state[...] + (1.0 - decay) * (
        bias_grad[...] * bias_grad[...] + eps_fact
    )
    bias_state_new[...] = state
    bias_step = bias_grad[...] * lax.rsqrt(state)
    squares = squares + spread(total(bias_step * bias_step), 46)
    squares_plane[spot] = jnp.broadcast_to(squares, (8, 128))
    exchange(
        [
            remote(squares_plane.at[spot], squares_plane.at[spot], 4, k, plane_device(k))
            for k in range(1, 8)
        ]
    )
    squares_level[z] = jnp.sum(squares_plane[...], 0)
    exchange(
        [
            remote(squares_level.at[z], squares_level.at[z], 5, k, level_device(k))
            for k in range(1, 4)
        ]
    )
    squares_out[...] = jnp.sum(squares_level[...], 0)[0:1]


def settle_kernel(
    total_tokens,
    sums_ref,
    rows_ref,
    up_ref,
    down_ref,
    mats_ref,
    bias_ref,
    mats_grad,
    mats_row,
    mats_col,
    up_row,
    up_col,
    down_row,
    down_col,
    bias_grad,
    bias_state,
    line_ref,
    squares_ref,
    loss_out,
    mats_grad_out,
    mats_new,
    mats_copy,
    mats_row_out,
    mats_col_out,
    up_grad,
    up_new,
    up_copy,
    up_row_out,
    up_col_out,
    down_grad,
    down_new,
    down_copy,
    down_row_out,
    down_col_out,
    bias_grad_out,
    bias_new,
    bias_copy,
    bias_state_out,
):
    line, squares = line_ref[...], squares_ref[...]
    low = jnp.bfloat16
    group = up_ref.shape[0]

    def clipped(place, entries):
        rms = jnp.sqrt(pick(squares, place) / entries)
        return jnp.maximum(1.0, rms / clip_level)

    def settle(new_ref, copy_ref, index, master, step, limit):
        value = master - learn_rate * (step / limit)
        new_ref[index] = value
        copy_ref[index] = value.astype(low)

    for i in range(group):
        e = pl.program_id(0) * group + i
        grad = joined(rows_ref[i])
        up_grad[i] = grad
        step = factored(
            grad,
            turn_line(up_row[pl.ds(e, 1), :]),
            up_col[pl.ds(e, 1), :],
            pick(line, 10 + e) / D,
        )
        settle(up_new, up_copy, i, up_ref[i], step, clipped(10 + e, D * FF))
        grad = sums_ref[i]
        down_grad[i] = grad
        step = factored(
            grad,
            turn_line(down_row[pl.ds(e, 1), :]),
            down_col[pl.ds(e, 1), :],
            pick(line, 28 + e) / FF,
        )
        settle(down_new, down_copy, i, down_ref[i], step, clipped(28 + e, D * FF))

    @pl.when(pl.program_id(0) == 0)
    def _():
        widths = column_widths()
        bounds = [sum(widths[:k]) for k in range(len(widths) + 1)]
        start_last = bounds[5]
        width_last = bounds[-1] - start_last
        loss_out[...] = pick(line, 46) / total_tokens
        for given, out in (
            (mats_grad, mats_grad_out),
            (mats_row, mats_row_out),
            (mats_col, mats_col_out),
            (up_row, up_row_out),
            (up_col, up_col_out),
            (down_row, down_row_out),
            (down_col, down_col_out),
            (bias_grad, bias_grad_out),
            (bias_state, bias_state_out),
        ):
            out[...] = given[...]
        for k in range(6):
            if k < 5:
                index = (slice(None), slice(bounds[k], bounds[k + 1]))
                row, mean = turn_line(mats_row[k : k + 1, :]), pick(line, k) / D
                limit = clipped(k, D * widths[k])
            else:
                last = range(5, len(widths))
                index = (slice(None), slice(start_last, None))
                row, mean, limit = [
                    by_piece(values, start_last, width_last)
                    for values in (
                        [turn_line(mats_row[j : j + 1, :]) for j in last],
                        [pick(line, j) / D for j in last],
                        [clipped(j, D * widths[j]) for j in last],
                    )
                ]
            step = factored(mats_grad[index], row, mats_col[index], mean)
            settle(mats_new, mats_copy, index, mats_ref[index], step, limit)
        index = (slice(None), slice(None))
        step = bias_grad[...] * lax.rsqrt(bias_state[...])
        settle(bias_new, bias_copy, index, bias_ref[...], step, clipped(46, 15 * D))


def update_kernel_call(sums, rows, lat, bias_sum, masters, factors, loss_part, total_tokens):
    mats, up_weights, down_weights, biases = masters
    mats_row, mats_col, up_row, up_col, down_row, down_col, bias_state = factors
    full, low = jnp.float32, jnp.bfloat16
    mats_col, bias_state, biases = [
        member.reshape(1, -1) for member in (mats_col, bias_state, biases)
    ]

    def like(member, kind=full):
        return jax.ShapeDtypeStruct(member.shape, kind)

    row = jax.ShapeDtypeStruct((1, 128), full)
    rows_like = [mats_row, mats_col, up_row, up_col, down_row, down_col, bias_state, bias_state]
    vmem = pl.BlockSpec(memory_space=pltpu.VMEM)
    dma = pltpu.SemaphoreType.DMA
    found = pl.pallas_call(
        update_kernel,
        out_shape=[like(member) for member in [mats] + rows_like] + [row, row],
        in_specs=[vmem] * 12,
        out_specs=[vmem] * 11,
        scratch_shapes=[
            pltpu.VMEM((512, 128), full),
            pltpu.VMEM((8, 64, 128), full),
            pltpu.VMEM((4, 4, 16, 128), full),
            pltpu.VMEM((8, 4, 16, 128), full),
            pltpu.VMEM((8, 8, 128), full),
            pltpu.VMEM((4, 8, 128), full),
            dma((2, 6, 8)),
        ],
        compiler_params=pltpu.CompilerParams(
            collective_id=1, has_side_effects=True, vmem_limit_bytes=VMEM_ROOM
        ),
        name="update",
    )(
        sums,
        rows,
        lat,
        bias_sum,
        loss_part.reshape(1, 1),
        mats_row,
        mats_col,
        up_row,
        up_col,
        down_row,
        down_col,
        bias_state,
    )
    group = 3
    wholes = [biases] + list(found)

    def whole(member):
        return pl.BlockSpec(member.shape, lambda g: (0,) * len(member.shape))

    def parts(member):
        rest = member.shape[1:]
        return pl.BlockSpec((group,) + rest, lambda g: (g,) + (0,) * len(rest))

    one = jax.ShapeDtypeStruct((1, 1), full)
    outs = (
        [(one, whole(one))]
        + [(like(mats, kind), whole(mats)) for kind in (full, full, low)]
        + [(like(member), whole(member)) for member in (mats_row, mats_col)]
        + [(like(up_weights, kind), parts(up_weights)) for kind in (full, full, low)]
        + [(like(member), whole(member)) for member in (up_row, up_col)]
        + [(like(down_weights, kind), parts(down_weights)) for kind in (full, full, low)]
        + [(like(member), whole(member)) for member in (down_row, down_col)]
        + [(like(biases, kind), whole(biases)) for kind in (full, full, low, full)]
    )
    outs = list(
        pl.pallas_call(
            functools.partial(settle_kernel, total_tokens),
            grid=(up_weights.shape[0] // group,),
            in_specs=[parts(member) for member in (sums, rows, up_weights, down_weights)]
            + [whole(member) for member in [mats] + wholes],
            out_shape=[shape for shape, spec in outs],
            out_specs=[spec for shape, spec in outs],
            compiler_params=pltpu.CompilerParams(vmem_limit_bytes=VMEM_ROOM),
            name="finish",
        )(sums, rows, up_weights, down_weights, mats, *wholes)
    )
    outs[0] = outs[0][0, 0]
    for at in (5, 16, 17, 18, 19):
        outs[at] = outs[at].reshape(-1)
    return tuple(outs)


def gather_kernel(
    mats_in,
    bias_in,
    down_in,
    up_in,
    patches,
    places,
    freq_low,
    label_hot,
    mats_far,
    bias_out,
    down_out,
    up_out,
    mods_out,
    fin_out,
    time_out,
    cond_out,
    qkv_out_far,
    att_out_far,
    middle_out_far,
    moe_out_far,
    logits_out_far,
    shared_out_far,
    mats_got,
    mats_own,
    up_got,
    up_wide,
    up_own,
    embedded,
    down_here,
    up_here,
    near_send,
    near_recv,
    own_sem,
    level_send,
    level_recv,
    one_send,
    one_recv,
    two_send,
    two_recv,
    core_send,
    core_recv,
    bias_send,
    bias_recv,
    here_sem,
    mats_sem,
    mats_out,
    qkv_out,
    att_out,
    middle_out,
    moe_out,
    logits_out,
    shared_out,
):
    leaves = [
        pltpu.make_async_copy(near, far, mats_sem.at[number])
        for number, (near, far) in enumerate(
            (
                (mats_out, mats_far),
                (qkv_out, qkv_out_far),
                (att_out, att_out_far),
                (middle_out, middle_out_far),
                (moe_out, moe_out_far),
                (logits_out, logits_out_far),
                (shared_out, shared_out_far),
            )
        )
    ]
    n_down, n_up = down_in.shape[0], up_own.shape[0]
    lead, n_mats = 3, mats_out.shape[4]
    after_mats = lead + n_mats
    first_up = n_down + n_mats
    slabs = first_up + n_up
    wide, narrow = lax.axis_index(WIDE), lax.axis_index(NARROW)
    z, x = wide // 2, wide % 2
    y, c = narrow // 2, narrow % 2
    mates = [
        (wide, (y + (k // 2) * (1 - 2 * y)) * 2 + c + (k % 2) * (1 - 2 * c)) for k in range(1, 4)
    ]
    levels = [(((z + k) % 4) * 2 + x, narrow) for k in range(1, 4)]
    to_x = (z * 2 + 1 - x, narrow)
    to_core, to_y = mates[0], mates[1]
    to_one = (z * 2 + x + (1 - c) * (1 - 2 * x), (y + c * (1 - 2 * y)) * 2 + c)
    to_two = (z * 2 + x + c * (1 - 2 * x), (y + (1 - c) * (1 - 2 * y)) * 2 + c)
    barrier = pltpu.get_barrier_semaphore()
    for target in mates + levels + [to_x]:
        pl.semaphore_signal(barrier, inc=1, device_id=target, device_id_type=MESH_ID)
    pl.semaphore_wait(barrier, 7)

    def remote(source, target, send, recv, device):
        return pltpu.make_async_remote_copy(
            src_ref=source,
            dst_ref=target,
            send_sem=send,
            recv_sem=recv,
            device_id=device,
            device_id_type=MESH_ID,
        )

    def near_mats(k):
        return remote(
            mats_in.at[mates[k - 1][1]],
            mats_got.at[narrow],
            near_send.at[0, k],
            near_recv.at[0, k],
            mates[k - 1],
        )

    def near_up(k):
        return remote(
            up_in.at[mates[k - 1][1]],
            up_got.at[narrow],
            near_send.at[1, k],
            near_recv.at[1, k],
            mates[k - 1],
        )

    own_mats = pltpu.make_async_copy(mats_in.at[narrow], mats_got.at[narrow], own_sem.at[0])
    own_up = pltpu.make_async_copy(up_in.at[narrow], up_got.at[narrow], own_sem.at[1])
    own_bias = pltpu.make_async_copy(bias_in, bias_out.at[z, x, y, c], own_sem.at[2])
    own_mats.start()
    own_up.start()
    own_bias.start()
    for k in range(1, 4):
        near_mats(k).start()

    def bias_level(k):
        return remote(
            bias_in, bias_out.at[z, x, y, c], bias_send.at[k - 1], bias_recv.at[k - 1], levels[k - 1]
        )

    def bias_x():
        part = bias_out.at[:, x, y, c]
        return remote(part, part, bias_send.at[3], bias_recv.at[3], to_x)

    def bias_y():
        part = bias_out.at[:, :, y, c]
        return remote(part, part, bias_send.at[4], bias_recv.at[4], to_y)

    def bias_core():
        part = bias_out.at[:, :, :, c]
        return remote(part, part, bias_send.at[5], bias_recv.at[5], to_core)

    for k in range(1, 4):
        bias_level(k).start()
    for k in range(1, 4):
        near_up(k).start()

    def mats_ready():
        own_mats.wait()
        for k in range(1, 4):
            near_mats(k).wait_recv()
        for n in range(NARROW_PIECES):
            mats_own[n * ROWS : (n + 1) * ROWS] = mats_got[n].astype(jnp.float32)[:ROWS]
        for n in range(n_mats):
            mats_got[n, :, :] = mats_own[16 * n : 16 * (n + 1)].astype(jnp.bfloat16)

    own_bias.wait()

    def turn(number):
        return (number + EXPERTS) % n_up

    def down_at(s):
        return turn(jnp.where(s < lead, s, s - n_mats))

    def source(kind, s):
        if kind == 0:
            return mats_got.at[s - lead]
        if kind == 1:
            return down_in.at[down_at(s)]
        return up_own.at[turn(s - first_up)]

    def piece(kind, s, at):
        z_at, x_at, y_at, c_at = at
        if kind == 0:
            return mats_out.at[y_at, c_at, z_at, x_at, s - lead]
        if kind == 1:
            return down_out.at[down_at(s), z_at, x_at, y_at, c_at]
        return up_out.at[turn(s - first_up), y_at, c_at, z_at, x_at]

    every = slice(None)

    def own_copy(kind, s):
        return pltpu.make_async_copy(
            source(kind, s), piece(kind, s, (z, x, y, c)), own_sem.at[3 + s % 4]
        )

    def level_copy(kind, s, k, turned=False, first=0):
        if turned:
            part = piece(kind, s, (z, x, every, c) if first == 0 else (z, every, y, c))
            start = part
        else:
            part = piece(kind, s, (z, x, y, c))
            start = source(kind, s)
        return remote(
            start, part, level_send.at[s % 12, k - 1], level_recv.at[s, k - 1], levels[k - 1]
        )

    def both_parts(kind, s, first):
        return piece(kind, s, (every, x, every, c) if first else (every, every, y, c))

    def one_copy(kind, s, turned=False, first=0):
        part = both_parts(kind, s, 1 - first) if turned else piece(kind, s, (every, x, y, c))
        return remote(part, part, one_send.at[s % 12], one_recv.at[s], to_one)

    def two_copy(kind, s, turned=False, first=0):
        if turned:
            part, start = piece(kind, s, (z, x, y, c)), source(kind, s)
        else:
            part = both_parts(kind, s, first)
            start = part
        return remote(start, part, two_send.at[s % 12], two_recv.at[s], to_two)

    def core_copy(kind, s):
        part = piece(kind, s, (every, every, every, c))
        return remote(part, part, core_send.at[s % 12], core_recv.at[s], to_core)

    def by_order(kind, s, run):
        if kind == 0:
            run(False)
            return
        turned = (s % 5 == 1) | (s % 5 == 3)

        @pl.when(turned)
        def _():
            run(True)

        @pl.when(jnp.logical_not(turned))
        def _():
            run(False)

    def by_core(run):
        for first in range(2):

            @pl.when(c == first)
            def _():
                run(first)

    def stage_level(kind, s):
        own_copy(kind, s).start()

        def run(turned):
            if turned:
                two_copy(kind, s, True).start()
            else:
                for k in range(1, 4):
                    level_copy(kind, s, k).start()

        by_order(kind, s, run)

    def stage_one(kind, s):
        own_copy(kind, s).wait()

        def run(turned):
            if turned:
                two_copy(kind, s, True).wait_recv()

                def send(first):
                    for k in range(1, 4):
                        level_copy(kind, s, k, True, first).start()

                by_core(send)
            else:
                for k in range(1, 4):
                    level_copy(kind, s, k).wait_recv()
                one_copy(kind, s).start()

        by_order(kind, s, run)

    def stage_two(kind, s):
        def run(turned):
            if turned:
                for k in range(1, 4):
                    level_copy(kind, s, k, True).wait_recv()
                by_core(lambda first: one_copy(kind, s, True, first).start())
            else:
                one_copy(kind, s).wait_recv()
                by_core(lambda first: two_copy(kind, s, False, first).start())

        by_order(kind, s, run)

    def stage_core(kind, s):
        def run(turned):
            if turned:
                one_copy(kind, s, True).wait_recv()
            else:
                two_copy(kind, s).wait_recv()

        by_order(kind, s, run)
        core_copy(kind, s).start()

    def stage_last(kind, s):
        core_copy(kind, s).wait_recv()

    def stage_sent(kind, s):
        def run(turned):
            for k in range(1, 4):
                level_copy(kind, s, k, turned).wait_send()
            one_copy(kind, s, turned).wait_send()
            two_copy(kind, s, turned).wait_send()

        by_order(kind, s, run)
        core_copy(kind, s).wait_send()

    stages = (
        (stage_sent, 12),
        (stage_level, 0),
        (stage_one, 3),
        (stage_two, 6),
        (stage_core, 9),
        (stage_last, 12),
    )

    lats = patches.shape[0] // PATCHES
    ready, shared_at = after_mats + 12, first_up + SHARED + 12
    low, full = jnp.bfloat16, jnp.float32

    def matrix(number, begin, end):
        chunk = mats_out[number // 2, number % 2]
        return chunk.reshape(D, chunk.shape[-1])[:, begin:end]

    def bias_rows():
        return jnp.sum(bias_out[...].astype(full).reshape(-1, 16, D), 0)

    def wide_row(rows, begin, end):
        return jnp.concatenate([rows[k : k + 1] for k in range(begin, end)], 1)

    def conditions():
        rows = bias_rows()
        pre_time = contract(freq_low[...], matrix(3, 1408, 1664), 1, 1) + rows[11:12]
        hid_time = jax.nn.silu(pre_time).astype(low)
        cond = (
            product(hid_time, matrix(3, 1024, 1408))
            + rows[12:13]
            + contract(label_hot[...], matrix(3, 0, 1024), 1, 1)
        )
        act = jax.nn.silu(cond).astype(low)
        time_out[...] = pre_time
        cond_out[...] = cond
        mods_out[:, : 4 * D] = product(act, matrix(1, 0, 4 * D)) + wide_row(rows, 4, 8)
        mods_out[:, 4 * D :] = product(act, matrix(2, 0, 2 * D)) + wide_row(rows, 8, 10)
        fin_out[...] = product(act, matrix(2, 2 * D, 4 * D)) + wide_row(rows, 13, 15)

    def mod_row(start, number):
        return mods_out[pl.ds(start // PATCHES, 1), number * D : (number + 1) * D]

    def attention_in(start):
        rows = bias_rows()
        span = pl.ds(start, PATCHES)
        emb = contract(patches[span, :], matrix(2, 4 * D, 4 * D + 128), 1, 1)
        emb = emb + rows[10:11] + places[...]
        embedded[...] = emb
        normed, unused_std = layer_norm(emb)
        attn_in = (normed * (1.0 + mod_row(start, 1)) + mod_row(start, 0)).astype(low)
        qkv_out[span, :] = (
            product(attn_in, matrix(0, 0, 3 * D)) + wide_row(rows, 0, 3)
        ).astype(low)

    def attention_heads(start):
        span = pl.ds(start, PATCHES)
        lane = lax.broadcasted_iota(jnp.int32, (PATCHES, 2 * HD), 1)
        for pair in range(HEADS // 2):
            at = pair * 2 * HD
            queries = qkv_out[span, at : at + 2 * HD]
            keys = qkv_out[span, D + at : D + at + 2 * HD]
            values = qkv_out[span, 2 * D + at : 2 * D + at + 2 * HD]
            halves = []
            for half in range(2):
                mine = (lane < HD) if half == 0 else (lane >= HD)
                scores = contract(jnp.where(mine, queries, 0), keys, 1, 1) * HD ** (-0.5)
                powers = jnp.exp(scores - jnp.max(scores, 1, keepdims=True))
                probs = (powers / jnp.sum(powers, 1, keepdims=True)).astype(low)
                halves.append(product(probs, values))
            att_out[span, at : at + 2 * HD] = jnp.where(lane < HD, halves[0], halves[1]).astype(low)

    def attention_out(start):
        rows = bias_rows()
        span = pl.ds(start, PATCHES)
        attn = product(att_out[span, :], matrix(0, 3 * D, 4 * D)) + rows[3:4]
        middle = embedded[...] + mod_row(start, 2) * attn
        middle_out[span, :] = middle
        normed, unused_std = layer_norm(middle)
        moe_in = (normed * (1.0 + mod_row(start, 4)) + mod_row(start, 3)).astype(low)
        moe_out[span, :] = moe_in
        logits_out[span, :] = product(moe_in, matrix(0, 4 * D, 4 * D + 128))

    def fetch(shared_id):
        e = EXPERTS + shared_id
        first = pltpu.make_async_copy(down_out.at[e], down_here, here_sem.at[0])
        second = pltpu.make_async_copy(up_out.at[e], up_here, here_sem.at[1])
        first.start()
        second.start()
        first.wait()
        second.wait()

    def shared_block(shared_id, start):
        span = pl.ds(start, PATCHES)
        rows = moe_out[span, :]
        chunks = [up_here[n // 2, n % 2].reshape(D, D) for n in range(NARROW_PIECES)]
        down = down_here[...].reshape(FF, D)
        total = None
        for cut in range(0, FF, CUT):
            pre_act = product(rows, up_columns(chunks, cut))
            part = product(gelu_only(pre_act).astype(low), down[cut : cut + CUT])
            total = part if total is None else total + part
        if shared_id == 0:
            shared_out[span, :] = total
        else:
            shared_out[span, :] += total

    def tick(t, unused):
        @pl.when(t == 1)
        def _():
            for k in range(1, 4):
                bias_level(k).wait_recv()
            bias_x().start()

        @pl.when(t == 2)
        def _():
            bias_x().wait_recv()
            bias_y().start()

        @pl.when(t == 3)
        def _():
            bias_y().wait_recv()
            bias_core().start()

        @pl.when(t == 6)
        def _():
            own_up.wait()
            for k in range(1, 4):
                near_up(k).wait_recv()
            for n in range(NARROW_PIECES):
                up_wide[n] = up_got[n].astype(jnp.float32)

            for e in range(n_up):
                up_own[e] = jnp.concatenate(
                    [up_wide[n, e * ROWS : (e + 1) * ROWS] for n in range(NARROW_PIECES)], 0
                ).astype(jnp.bfloat16)

        @pl.when(t == 2)
        def _():
            mats_ready()

        for stage, lag in stages:
            s = t - lag

            @pl.when((s >= lead) & (s < after_mats))
            def _():
                stage(0, jnp.clip(s, lead, after_mats - 1))

            @pl.when(((s >= 0) & (s < lead)) | ((s >= after_mats) & (s < first_up)))
            def _():
                stage(1, jnp.clip(s, 0, first_up - 1))

            @pl.when((s >= first_up) & (s < slabs))
            def _():
                stage(2, jnp.clip(s, first_up, slabs - 1))

        @pl.when(t == ready)
        def _():
            bias_core().wait_recv()
            conditions()

        for number, unit in enumerate((attention_in, attention_heads, attention_out)):

            @pl.when((t > ready) & (t <= ready + 3 * lats) & ((t - ready - 1) % 3 == number))
            def _():
                unit(pl.multiple_of(jnp.clip((t - ready - 1) // 3, 0, lats - 1) * PATCHES, PATCHES))

        @pl.when(t == ready + 3 * lats + 1)
        def _():
            for leave in leaves[:-1]:
                leave.start()

        for shared_id in range(SHARED):
            begin = shared_at + shared_id * lats

            @pl.when(t == begin)
            def _():
                fetch(shared_id)

            @pl.when((t >= begin) & (t < begin + lats))
            def _():
                shared_block(
                    shared_id, pl.multiple_of(jnp.clip(t - begin, 0, lats - 1) * PATCHES, PATCHES)
                )

        @pl.when(t == shared_at + SHARED * lats)
        def _():
            leaves[-1].start()

        return unused

    lax.fori_loop(0, slabs + 12, tick, 0)
    for leave in leaves:
        leave.wait()
    for k in range(1, 4):
        near_mats(k).wait_send()
        near_up(k).wait_send()
        bias_level(k).wait_send()
    bias_x().wait_send()
    bias_y().wait_send()
    bias_core().wait_send()


def gather_weights(
    mats, up_weights, down_weights, biases, patches, places, freq_low, label_hot
):
    low = jnp.bfloat16
    owner = lax.axis_index(AXES)
    m = mats.astype(low)
    rows = m.shape[0]

    thin = 13 * D

    def thin_part(at):
        return jnp.pad(m[:, at : at + 16], ((0, 0), (0, 112)))

    mats_in = jnp.stack(
        [
            jnp.concatenate([m[:, : 4 * D], thin_part(thin)], 1),
            jnp.concatenate([m[:, 4 * D : 8 * D], thin_part(thin + 16)], 1),
            jnp.concatenate(
                [m[:, 8 * D : 10 * D], m[:, 11 * D : 13 * D], thin_part(thin + 32)], 1
            ),
            jnp.concatenate(
                [
                    m[:, thin + 48 + FREQ :],
                    jnp.zeros((rows, 24), low),
                    m[:, 10 * D : 11 * D],
                    m[:, thin + 48 : thin + 48 + FREQ],
                ],
                1,
            ),
        ],
        0,
    )
    mats_in = jnp.pad(mats_in, ((0, 0), (0, 16 - rows), (0, 0)))
    line = lax.dynamic_update_slice(
        jnp.zeros((16 * D,), low), biases.astype(low), (owner * biases.shape[0],)
    )
    n_up = up_weights.shape[0]
    up_in = (
        up_weights.astype(low)
        .reshape(n_up, rows, NARROW_PIECES, D)
        .transpose(2, 0, 1, 3)
        .reshape(NARROW_PIECES, n_up * rows, D)
    )
    room = (n_up * rows + 15) // 16 * 16
    up_in = jnp.pad(up_in, ((0, 0), (0, room - n_up * rows), (0, 0)))
    slabs = 3 + 2 * n_up
    spread = mats_in.shape[2]
    dma = pltpu.SemaphoreType.DMA
    anywhere = pl.BlockSpec(memory_space=pl.ANY)
    tokens = patches.shape[0]
    full, vmem = jnp.float32, pl.BlockSpec(memory_space=pltpu.VMEM)
    outs = pl.pallas_call(
        gather_kernel,
        out_shape=[
            jax.ShapeDtypeStruct((2, 2, 4, 2, 3, 16, spread), low),
            jax.ShapeDtypeStruct((4, 2, 2, 2, 16, D), low),
            jax.ShapeDtypeStruct((n_up, 4, 2, 2, 2, PIECE, D), low),
            jax.ShapeDtypeStruct((n_up, 2, 2, 4, 2, PIECE, D), low),
            jax.ShapeDtypeStruct((8, 6 * D), full),
            jax.ShapeDtypeStruct((8, 2 * D), full),
            jax.ShapeDtypeStruct((8, D), full),
            jax.ShapeDtypeStruct((8, D), full),
            jax.ShapeDtypeStruct((tokens, 3 * D), low),
            jax.ShapeDtypeStruct((tokens, D), low),
            jax.ShapeDtypeStruct((tokens, D), full),
            jax.ShapeDtypeStruct((tokens, D), low),
            jax.ShapeDtypeStruct((tokens, 128), full),
            jax.ShapeDtypeStruct((tokens, D), full),
        ],
        in_specs=[anywhere] * 4 + [vmem] * 4,
        out_specs=[anywhere, vmem] + [anywhere] * 2 + [vmem] * 4 + [anywhere] * 6,
        scratch_shapes=[
            pltpu.VMEM((NARROW_PIECES, 16, spread), low),
            pltpu.VMEM((PIECE, spread), jnp.float32),
            pltpu.VMEM((NARROW_PIECES, room, D), low),
            pltpu.VMEM((NARROW_PIECES, room, D), jnp.float32),
            pltpu.VMEM((n_up, PIECE, D), low),
            pltpu.VMEM((PATCHES, D), full),
            pltpu.VMEM((4, 2, 2, 2, PIECE, D), low),
            pltpu.VMEM((2, 2, 4, 2, PIECE, D), low),
            dma((2, 4)),
            dma((2, 4)),
            dma((7,)),
            dma((12, 3)),
            dma((slabs, 3)),
            dma((12,)),
            dma((slabs,)),
            dma((12,)),
            dma((slabs,)),
            dma((12,)),
            dma((slabs,)),
            dma((6,)),
            dma((6,)),
            dma((2,)),
            dma((7,)),
            pltpu.VMEM((2, 2, 4, 2, 3, 16, spread), low),
            pltpu.VMEM((tokens, 3 * D), low),
            pltpu.VMEM((tokens, D), low),
            pltpu.VMEM((tokens, D), full),
            pltpu.VMEM((tokens, D), low),
            pltpu.VMEM((tokens, 128), full),
            pltpu.VMEM((tokens, D), full),
        ],
        compiler_params=pltpu.CompilerParams(
            collective_id=2, has_side_effects=True, vmem_limit_bytes=VMEM_ROOM
        ),
        name="gather_weights",
    )(
        mats_in,
        line.reshape(16, D),
        down_weights.astype(low),
        up_in,
        patches,
        places,
        freq_low,
        label_hot,
    )
    return outs


def split_weights(weights):
    mats_full, up_full, down_full, bias_full = weights
    matrices = cut_pieces(mats_full, column_widths(), 1)
    vectors = [member.astype(jnp.float32) for member in cut_pieces(bias_full, bias_widths(), 0)]
    up_full = up_full.reshape(-1, D, NARROW_PIECES, D).transpose(0, 2, 1, 3)
    return (matrices, vectors, up_full, down_full)


def forward(weights, latents, noise, timesteps, labels, routes):
    matrices, vectors, up_full, down_full = weights
    w_qkv, w_proj, w_mod, w_time2, w_final, w_router, w_head, w_patch, w_time1, w_table = matrices
    b_qkv, b_proj, b_mod, b_patch, b_time1, b_time2, b_final = vectors
    num_latents = latents.shape[0]
    rows_here = num_latents * PATCHES
    steps_f = timesteps.astype(jnp.float32)
    signal, spread = noise_level(steps_f)
    noisy = signal[:, None] * latents + spread[:, None] * noise
    patches = noisy.reshape(rows_here, PD).astype(jnp.bfloat16)
    embedded = (
        contract(patches, w_patch, 1, 1).reshape(num_latents, PATCHES, D)
        + b_patch
        + positions()[None]
    )
    freq_low = time_features(steps_f).astype(jnp.bfloat16)
    pre_time = contract(freq_low, w_time1, 1, 1) + b_time1
    hid_time = jax.nn.silu(pre_time).astype(jnp.bfloat16)
    label_hot = (labels[:, None] == jnp.arange(CLASSES, dtype=jnp.int32)[None, :]).astype(
        jnp.float32
    )
    label_emb = lax.dot_general(
        label_hot,
        w_table.astype(jnp.float32),
        (((1,), (1,)), ((), ())),
        precision=lax.Precision.HIGHEST,
        preferred_element_type=jnp.float32,
    )
    cond = product(hid_time, w_time2) + b_time2 + label_emb
    cond_act = jax.nn.silu(cond).astype(jnp.bfloat16)
    modulation = product(cond_act, w_mod) + b_mod
    final_mod = product(cond_act, w_final) + b_final
    shift_attn, scale_attn, gate_attn, shift_moe, scale_moe, gate_moe = [
        member[:, None, :] for member in jnp.split(modulation, 6, 1)
    ]
    shift_fin, scale_fin = [member[:, None, :] for member in jnp.split(final_mod, 2, 1)]
    normed_one, inv_one = layer_norm(embedded)
    attn_in = (
        (normed_one * (1.0 + scale_attn) + shift_attn).astype(jnp.bfloat16).reshape(rows_here, D)
    )
    qkv_out = (
        (product(attn_in, w_qkv) + b_qkv)
        .astype(jnp.bfloat16)
        .reshape(num_latents, PATCHES, 3, HEADS, HD)
    )
    scores = jnp.einsum(
        LQK, qkv_out[:, :, 0], qkv_out[:, :, 1], preferred_element_type=jnp.float32
    ) * HD ** (-0.5)
    log_totals = jax.nn.logsumexp(scores, -1)
    probs_low = jax.nn.softmax(scores, -1).astype(jnp.bfloat16)
    attended = (
        jnp.einsum(
            "lhqk,lkhd->lqhd", probs_low, qkv_out[:, :, 2], preferred_element_type=jnp.float32
        )
        .astype(jnp.bfloat16)
        .reshape(rows_here, D)
    )
    attn_out = (product(attended, w_proj) + b_proj).reshape(num_latents, PATCHES, D)
    middle = embedded + gate_attn * attn_out
    normed_two, inv_two = layer_norm(middle)
    moe_in = (normed_two * (1.0 + scale_moe) + shift_moe).astype(jnp.bfloat16).reshape(rows_here, D)
    logits = product(moe_in, w_router)
    route_hot = (routes[:, :, None] == jnp.arange(EXPERTS, dtype=jnp.int32)[None, None, :]).astype(
        jnp.float32
    )
    gate_vals = jax.nn.softmax(jnp.sum(route_hot * logits[:, None, :], 2), -1)
    slot_of, slot_meta = pack_slots(routes)
    routed, slot_rows = experts_forward(slot_of, slot_meta, moe_in, up_full, down_full)
    moe_out = gate_vals[:, 0:1] * routed[0] + gate_vals[:, 1:2] * routed[1]
    for shared_id in range(EXPERTS, EXPERTS + SHARED):
        for cut in range(0, FF, CUT):
            pre_act = product(moe_in, up_columns(up_full[shared_id], cut))
            activated = gelu_only(pre_act).astype(jnp.bfloat16)
            moe_out = moe_out + product(activated, down_full[shared_id, cut : cut + CUT])
    moe_out = moe_out.reshape(num_latents, PATCHES, D)
    final_state = middle + gate_moe * moe_out
    normed_fin, inv_fin = layer_norm(final_state)
    head_in = (
        (normed_fin * (1.0 + scale_fin) + shift_fin).astype(jnp.bfloat16).reshape(rows_here, D)
    )
    errors = product(head_in, w_head) - noise.reshape(rows_here, PD)
    return SimpleNamespace(
        patches=patches,
        freq_low=freq_low,
        pre_time=pre_time,
        hid_time=hid_time,
        label_hot=label_hot,
        cond=cond,
        cond_act=cond_act,
        scale_attn=scale_attn,
        gate_attn=gate_attn,
        scale_moe=scale_moe,
        gate_moe=gate_moe,
        scale_fin=scale_fin,
        normed_one=normed_one,
        inv_one=inv_one,
        attn_in=attn_in,
        qkv_out=qkv_out,
        log_totals=log_totals,
        attended=attended,
        attn_out=attn_out,
        normed_two=normed_two,
        inv_two=inv_two,
        moe_in=moe_in,
        route_hot=route_hot,
        gate_vals=gate_vals,
        slot_of=slot_of,
        slot_meta=slot_meta,
        slot_rows=slot_rows,
        routed=routed,
        moe_out=moe_out,
        normed_fin=normed_fin,
        inv_fin=inv_fin,
        head_in=head_in,
        errors=errors,
    )


def forward_fused(mats, up_weights, down_weights, biases, latents, noise, timesteps, labels):
    num_latents = latents.shape[0]
    rows_here = num_latents * PATCHES
    steps_f = timesteps.astype(jnp.float32)
    signal, spread = noise_level(steps_f)
    noisy = signal[:, None] * latents + spread[:, None] * noise
    patches = noisy.reshape(rows_here, PD).astype(jnp.bfloat16)
    freq_low = time_features(steps_f).astype(jnp.bfloat16)
    label_low = (labels[:, None] == jnp.arange(1024, dtype=jnp.int32)[None, :]).astype(jnp.bfloat16)
    less = ((0, 8 - num_latents), (0, 0))
    outs = gather_weights(
        mats,
        up_weights,
        down_weights,
        biases,
        jnp.pad(patches, ((0, 0), (0, 128 - PD))),
        positions(),
        jnp.pad(freq_low, less),
        jnp.pad(label_low, less),
    )
    n_up = outs[3].shape[0]
    return SimpleNamespace(
        patches=jnp.pad(patches, ((0, 0), (0, 128 - PD))),
        freq_low=jnp.pad(freq_low, less),
        mats_full=outs[0],
        bias_full=outs[1],
        down_full=outs[2].reshape(n_up, FF, D),
        up_full=outs[3].reshape(n_up, NARROW_PIECES, D, D),
        mods=outs[4],
        fin=outs[5],
        pre_time=outs[6],
        cond=outs[7],
        qkv=outs[8],
        attended=outs[9],
        middle=outs[10],
        moe_in=outs[11],
        logits=outs[12],
        shared_out=outs[13],
    )


def backward_fused(fused, latents, noise, labels, routes, total_tokens):
    num_latents = latents.shape[0]
    rows_here = num_latents * PATCHES
    line = jnp.sum(fused.bias_full.reshape(-1, 16, D).astype(jnp.float32), 0)
    slot_of, slot_meta = pack_slots(routes)
    members = (
        fused.logits,
        routes,
        fused.shared_out,
        fused.middle,
        jnp.pad(noise.reshape(rows_here, PD), ((0, 0), (0, 128 - PD))),
        fused.mods,
        fused.fin,
        fused.mats_full[0, 1].reshape(D, -1)[:, 4 * D :],
    )
    (
        grad_pair,
        grad_both,
        grad_state,
        grad_logits,
        thin,
        grad_gate,
        grad_fin,
        loss_part,
        slot_rows,
    ) = (
        experts_and_head(
            slot_of,
            slot_meta,
            fused.moe_in,
            fused.up_full,
            fused.down_full,
            2.0 / total_tokens,
            members,
        )
    )
    up_slabs, down_slabs, dx_routed = experts_backward(
        slot_of, slot_meta, slot_rows, grad_pair, fused.up_full, fused.down_full
    )
    label_parts = jnp.stack([labels // 32, labels % 32], 1).astype(jnp.bfloat16)
    members = (
        fused.moe_in,
        grad_both,
        dx_routed,
        grad_logits,
        fused.middle,
        fused.qkv,
        fused.attended,
        grad_state,
        fused.patches,
        positions(),
        fused.mods,
        fused.mats_full,
        line,
        fused.pre_time,
        fused.cond,
        fused.freq_low,
        grad_gate,
        grad_fin,
        thin,
        jnp.pad(label_parts, ((0, 8 - num_latents), (0, 126))),
    )
    return loss_part, reduce_slabs(
        slot_of, down_slabs, up_slabs, fused.up_full, fused.down_full, members
    )


def backward(weights, kept, total_tokens):
    matrices, vectors, up_full, down_full = weights
    w_qkv, w_proj, w_mod, w_time2, w_final, w_router, w_head, w_patch, w_time1, w_table = matrices
    num_latents = kept.normed_one.shape[0]
    rows_here = num_latents * PATCHES
    grad_head, grad_head_in, unused = linear_back(
        kept.errors * (2.0 / total_tokens), kept.head_in, w_head
    )
    grad_head_in = grad_head_in.reshape(num_latents, PATCHES, D)
    grad_final_mod = jnp.concatenate(
        [jnp.sum(grad_head_in, 1), jnp.sum(grad_head_in * kept.normed_fin, 1)], 1
    )
    grad_state = norm_back(
        grad_head_in * (1.0 + kept.scale_fin), kept.normed_fin, kept.inv_fin
    )
    grad_gate_moe = jnp.sum(kept.moe_out * grad_state, 1)
    grad_moe = (kept.gate_moe * grad_state).reshape(rows_here, D)
    grad_moe_low = grad_moe.astype(jnp.bfloat16)
    moe_in = kept.moe_in
    gate_vals = kept.gate_vals
    routed = kept.routed
    grad_gates = jnp.stack([jnp.sum(routed[k] * grad_moe, 1) for k in range(2)], 1)
    grad_pair = jnp.stack(
        [(gate_vals[:, k : k + 1] * grad_moe).astype(jnp.bfloat16) for k in range(2)], 0
    )
    up_slabs, down_slabs, dx_slots = experts_backward(
        kept.slot_of, kept.slot_meta, kept.slot_rows, grad_pair, up_full, down_full
    )
    place = jnp.arange(dx_slots.shape[0], dtype=jnp.int32)[None, :]
    used = place < jnp.max(kept.slot_meta[0] + kept.slot_meta[1])
    dx_slots = jnp.where(used.T, dx_slots, 0.0)
    slot_hot = [(kept.slot_of[k][:, None] == place).astype(jnp.float32) for k in range(2)]
    grad_moe_in = jnp.dot(slot_hot[0] + slot_hot[1], dx_slots, precision=lax.Precision.HIGHEST)
    up_all = [up_slabs.transpose(0, 1, 3, 2, 4).reshape(-1, D, FF)]
    down_all = [down_slabs.reshape(-1, FF, D)]
    for shared_id in range(EXPERTS, EXPERTS + SHARED):
        up_part = jnp.concatenate([up_full[shared_id, k] for k in range(NARROW_PIECES)], 1)
        activated, slope = gelu_slope(product(moe_in, up_part))
        grad_act = contract(grad_moe_low, down_full[shared_id], 1, 1)
        grad_pre = (grad_act * slope).astype(jnp.bfloat16)
        down_all.append(contract(activated.astype(jnp.bfloat16), grad_moe_low, 0, 0)[None])
        up_all.append(contract(moe_in, grad_pre, 0, 0)[None])
        grad_moe_in = grad_moe_in + contract(grad_pre, up_part, 1, 1)
    up_slabs = jnp.concatenate([member.astype(jnp.float32) for member in up_all], 0)
    down_slabs = jnp.concatenate([member.astype(jnp.float32) for member in down_all], 0)
    grad_picked = gate_vals * (grad_gates - jnp.sum(gate_vals * grad_gates, 1, keepdims=True))
    grad_logits = jnp.sum(kept.route_hot * grad_picked[:, :, None], 1)
    grad_router, grad_from_router, unused = linear_back(grad_logits, moe_in, w_router)
    grad_moe_in = (grad_moe_in + grad_from_router).reshape(num_latents, PATCHES, D)
    grad_middle = grad_state + norm_back(
        grad_moe_in * (1.0 + kept.scale_moe), kept.normed_two, kept.inv_two
    )
    grad_gate_attn = jnp.sum(kept.attn_out * grad_middle, 1)
    grad_proj, grad_attended, grad_b_proj = linear_back(
        (kept.gate_attn * grad_middle).reshape(rows_here, D), kept.attended, w_proj
    )
    grad_att_low = grad_attended.astype(jnp.bfloat16).reshape(num_latents, PATCHES, HEADS, HD)
    qkv_out = kept.qkv_out
    queries = qkv_out[:, :, 0]
    key_rows = qkv_out[:, :, 1]
    values = qkv_out[:, :, 2]
    scores = jnp.einsum(
        LQK, queries, key_rows, preferred_element_type=jnp.float32
    ) * HD ** (-0.5)
    probs = jnp.exp(scores - kept.log_totals[..., None])
    probs_low = probs.astype(jnp.bfloat16)
    grad_values = jnp.einsum(
        "lhqk,lqhd->lkhd", probs_low, grad_att_low, preferred_element_type=jnp.float32
    )
    grad_probs = jnp.einsum(
        LQK, grad_att_low, values, preferred_element_type=jnp.float32
    )
    grad_scores = (
        probs * (grad_probs - jnp.sum(probs * grad_probs, -1, keepdims=True)) * HD ** (-0.5)
    ).astype(jnp.bfloat16)
    grad_queries = jnp.einsum(
        "lhqk,lkhd->lqhd", grad_scores, key_rows, preferred_element_type=jnp.float32
    )
    grad_keys = jnp.einsum(
        "lhqk,lqhd->lkhd", grad_scores, queries, preferred_element_type=jnp.float32
    )
    grad_qkv = jnp.stack([grad_queries, grad_keys, grad_values], 2).reshape(rows_here, 3 * D)
    grad_w_qkv, grad_attn_in, grad_b_qkv = linear_back(grad_qkv, kept.attn_in, w_qkv)
    grad_attn_in = grad_attn_in.reshape(num_latents, PATCHES, D)
    grad_embedded = grad_middle + norm_back(
        grad_attn_in * (1.0 + kept.scale_attn), kept.normed_one, kept.inv_one
    )
    grad_emb_flat = grad_embedded.reshape(rows_here, D)
    grad_patch = contract(grad_emb_flat.astype(jnp.bfloat16), kept.patches, 0, 0)
    grad_b_patch = jnp.sum(grad_emb_flat, 0)
    grad_modulation = jnp.concatenate(
        [
            jnp.sum(grad_attn_in, 1),
            jnp.sum(grad_attn_in * kept.normed_one, 1),
            grad_gate_attn,
            jnp.sum(grad_moe_in, 1),
            jnp.sum(grad_moe_in * kept.normed_two, 1),
            grad_gate_moe,
        ],
        1,
    )
    grad_mod_low = grad_modulation.astype(jnp.bfloat16)
    grad_fin_low = grad_final_mod.astype(jnp.bfloat16)
    grad_act = contract(grad_mod_low, w_mod, 1, 1) + contract(grad_fin_low, w_final, 1, 1)
    grad_cond = slope_back(jax.nn.silu, kept.cond, grad_act)
    grad_cond_low = grad_cond.astype(jnp.bfloat16)
    grad_hid_time = contract(grad_cond_low, w_time2, 1, 1)
    grad_pre_time = slope_back(jax.nn.silu, kept.pre_time, grad_hid_time)
    grad_time_low = grad_pre_time.astype(jnp.bfloat16)
    mats_slabs = jnp.concatenate([grad_w_qkv, grad_proj], 1)[None]
    thin = jnp.concatenate([grad_router, grad_head, grad_patch], 1)
    grad_bias = jnp.concatenate(
        [
            grad_b_qkv,
            grad_b_proj,
            jnp.sum(grad_modulation, 0),
            grad_b_patch,
            jnp.sum(grad_pre_time, 0),
            jnp.sum(grad_cond, 0),
            jnp.sum(grad_final_mod, 0),
        ]
    )
    lows = jnp.concatenate(
        [
            kept.cond_act,
            kept.hid_time,
            grad_mod_low,
            grad_fin_low,
            grad_cond_low,
            grad_time_low,
            kept.freq_low,
        ],
        1,
    )
    return (up_slabs, down_slabs, mats_slabs, thin, grad_bias, lows, grad_cond)


def latent_grads(lows, grad_cond, labels, row_start, row_count):
    lows = lax.all_gather(lows, AXES, axis=0, tiled=True)
    grad_cond = lax.all_gather(grad_cond, AXES, axis=0, tiled=True)
    labels = lax.all_gather(labels, AXES, axis=0, tiled=True)
    cond_act, hid_time, grad_mod, grad_fin, grad_low, grad_time, freq_low = cut_pieces(
        lows, [D, D, 6 * D, 2 * D, D, D, FREQ], 1
    )

    def rows_of(member):
        return lax.dynamic_slice_in_dim(member, row_start, row_count, 1)

    label_hot = (labels[:, None] == jnp.arange(CLASSES, dtype=jnp.int32)[None, :]).astype(
        jnp.float32
    )
    grad_table = lax.dot_general(
        rows_of(grad_cond),
        label_hot,
        (((0,), (0,)), ((), ())),
        precision=lax.Precision.HIGHEST,
        preferred_element_type=jnp.float32,
    )
    return (
        contract(rows_of(cond_act), grad_mod, 0, 0),
        contract(rows_of(hid_time), grad_low, 0, 0),
        contract(rows_of(cond_act), grad_fin, 0, 0),
        contract(rows_of(grad_time), freq_low, 0, 0),
        grad_table,
    )


def factor_start(grad, row_old):
    squares = grad * grad + eps_fact
    row_new = decay * row_old + (1.0 - decay) * jnp.mean(squares, 2)
    return (row_new, jnp.sum(squares, 1), jnp.sum(row_new, 1))


def factor_update(grad, row_new, col_total, row_total, col_old, row_count):
    col_new = decay * col_old + (1.0 - decay) * (col_total / row_count)
    row_mean = row_total / row_count
    update = grad * lax.rsqrt(row_new[:, :, None] * col_new[:, None, :] / row_mean[:, None, None])
    return (col_new, update, jnp.sum(update * update, (1, 2)))


def clip_apply(master, update, square_total, entry_count):
    update_rms = jnp.sqrt(square_total / entry_count)
    return master - learn_rate * (update / jnp.maximum(1.0, update_rms / clip_level)[:, None, None])


def update_plain(grads, masters, factors, loss_part):
    mats_grad, up_grad, down_grad, bias_grad = grads
    mats, up_weights, down_weights, biases = masters
    mats_row, mats_col, up_row, up_col, down_row, down_col, bias_state = factors
    widths = column_widths()
    grad_pieces = cut_pieces(mats_grad, widths, 1)
    starts = [
        factor_start(grad_pieces[k][None], mats_row[k][None]) for k in range(len(widths))
    ]
    up_row_new, up_col_part, up_row_part = factor_start(up_grad, up_row)
    down_row_new, down_col_part, down_row_part = factor_start(down_grad, down_row)
    col_totals, row_totals, up_cols, up_rows, down_cols, down_rows, loss_total = lax.psum(
        (
            jnp.concatenate([member[1] for member in starts], 1)[0],
            jnp.concatenate([member[2] for member in starts], 0),
            up_col_part,
            up_row_part,
            down_col_part,
            down_row_part,
            loss_part,
        ),
        AXES,
    )
    col_total_pieces = cut_pieces(col_totals, widths, 0)
    col_old_pieces = cut_pieces(mats_col, widths, 0)
    steps = [
        factor_update(
            grad_pieces[k][None],
            starts[k][0],
            col_total_pieces[k][None],
            row_totals[k][None],
            col_old_pieces[k][None],
            D,
        )
        for k in range(len(widths))
    ]
    up_col_new, up_update, up_square = factor_update(
        up_grad, up_row_new, up_cols, up_rows, up_col, D
    )
    down_col_new, down_update, down_square = factor_update(
        down_grad, down_row_new, down_cols, down_rows, down_col, FF
    )
    bias_state_new = decay * bias_state + (1.0 - decay) * (bias_grad * bias_grad + eps_fact)
    bias_update = bias_grad * lax.rsqrt(bias_state_new)
    square_mats, square_up, square_down, square_bias = lax.psum(
        (
            jnp.concatenate([member[2] for member in steps], 0),
            up_square,
            down_square,
            jnp.sum(bias_update * bias_update),
        ),
        AXES,
    )
    master_pieces = cut_pieces(mats, widths, 1)
    mats_new = jnp.concatenate(
        [
            clip_apply(
                master_pieces[k][None], steps[k][1], square_mats[k][None], D * widths[k]
            )[0]
            for k in range(len(widths))
        ],
        1,
    )
    up_new = clip_apply(up_weights, up_update, square_up, D * FF)
    down_new = clip_apply(down_weights, down_update, square_down, D * FF)
    bias_rms = jnp.sqrt(square_bias / (15 * D))
    bias_new = biases - learn_rate * (bias_update / jnp.maximum(1.0, bias_rms / clip_level))
    return (
        loss_total,
        mats_grad,
        mats_new,
        mats_new.astype(jnp.bfloat16),
        jnp.concatenate([member[0] for member in starts], 0),
        jnp.concatenate([member[0][0] for member in steps], 0),
        up_grad,
        up_new,
        up_new.astype(jnp.bfloat16),
        up_row_new,
        up_col_new,
        down_grad,
        down_new,
        down_new.astype(jnp.bfloat16),
        down_row_new,
        down_col_new,
        bias_grad,
        bias_new,
        bias_new.astype(jnp.bfloat16),
        bias_state_new,
    )


def body(
    latents,
    noise,
    timesteps,
    labels,
    routes,
    mats,
    up_weights,
    down_weights,
    biases,
    *factors,
):
    rows_here = mats.shape[0]
    total_tokens = latents.shape[0] * PATCHES * lax.axis_size(AXES)
    masters = (mats, up_weights, down_weights, biases)
    if lax.axis_size(WIDE) == WIDE_PIECES and lax.axis_size(NARROW) == NARROW_PIECES:
        fused = forward_fused(
            mats, up_weights, down_weights, biases, latents, noise, timesteps, labels
        )
        loss_part, (sums, turned, lat, bias_sum) = backward_fused(
            fused, latents, noise, labels, routes, total_tokens
        )
        return update_kernel_call(
            sums, turned, lat, bias_sum, masters, factors, loss_part, total_tokens
        )
    else:
        flat = jnp.concatenate([mats.reshape(-1), biases], 0).astype(jnp.bfloat16)
        flat = lax.all_gather(flat, AXES, axis=0, tiled=False)
        gathered = split_weights(
            (
                flat[:, : rows_here * mats.shape[1]].reshape(-1, mats.shape[1]),
                lax.all_gather(up_weights.astype(jnp.bfloat16), AXES, axis=1, tiled=True),
                lax.all_gather(down_weights.astype(jnp.bfloat16), AXES, axis=1, tiled=True),
                flat[:, rows_here * mats.shape[1] :].reshape(-1),
            )
        )
        kept = forward(gathered, latents, noise, timesteps, labels, routes)
        members = backward(gathered, kept, total_tokens)
        up_slabs, down_slabs, mats_slabs, thin, grad_bias, lows, grad_cond = members
        loss_part = jnp.sum(kept.errors * kept.errors)
        grads = plain_grads(
            down_slabs, up_slabs, mats_slabs, thin, grad_bias, lows, grad_cond, labels, rows_here
        )
        outs = update_plain(grads, masters, factors, loss_part)
    return (outs[0] / total_tokens,) + tuple(outs[1:])


def solution(mesh):
    rows = P(AXES, None)
    middle_rows = P(None, AXES, None)
    row_factor = P(None, AXES)
    line = P(AXES)
    in_specs = (
        (rows, rows, line, line, rows)
        + (rows, middle_rows, middle_rows, line)
        + (row_factor, P(), row_factor, P(), row_factor, P(), line)
    )
    out_specs = (
        (P(), rows, rows, rows, row_factor, P())
        + (middle_rows, middle_rows, middle_rows, row_factor, P()) * 2
        + (line, line, line, line)
    )
    return jax.shard_map(body, mesh=mesh, in_specs=in_specs, out_specs=out_specs, check_vma=False)
```

```python
import functools
import math
from types import SimpleNamespace

import jax
import jax.numpy as jnp
from jax import lax
from jax.experimental import pallas as pl
from jax.experimental.pallas import tpu as pltpu
from jax.sharding import PartitionSpec as P

WIDE = "wide"
NARROW = "narrow"
AXES = (WIDE, NARROW)
MESH_ID = pl.DeviceIdType.MESH

D = 384
HEADS = 6
HD = 64
FF = 1536
EXPERTS = 16
SHARED = 2
PD = 16
GRID = 16
FREQ = 256
CLASSES = 1000
BLK = 256
WIDE_PIECES = 8
NARROW_PIECES = 4
PIECE = 48
ROWS = 12
LAT_ROWS = 16
LQK = "lqhd,lkhd->lhqk"
CUT = 768
LAT_COLS = 1536
PATCHES = 256


eps_norm = 1e-06
eps_fact = 1e-30
decay = 0.5
clip_level = 0.1
learn_rate = 0.5

SQRT_2_PI = math.sqrt(2.0 / math.pi)
VMEM_ROOM = 56 * 1024 * 1024
REDUCE_ROOM = 61 * 1024 * 1024


def column_widths():
    return [3 * D, D, 6 * D, D, 2 * D, EXPERTS, PD, PD, FREQ, CLASSES]


def bias_widths():
    return [3 * D, D, 6 * D, D, D, D, 2 * D]


def cut_pieces(source, widths, along):
    pieces = []
    start = 0
    for width in widths:
        pieces.append(lax.slice_in_dim(source, start, start + width, axis=along))
        start = start + width
    return pieces


def product(left, right):
    return jnp.dot(left, right, preferred_element_type=jnp.float32)


def contract(left, right, left_dim, right_dim):
    return lax.dot_general(
        left, right, (((left_dim,), (right_dim,)), ((), ())), preferred_element_type=jnp.float32
    )


def gelu_tanh(values):
    return jax.nn.gelu(values, approximate=True)


def slope_back(function, source, grad_out):
    return jax.vjp(function, source)[1](grad_out)[0]


def layer_norm(source):
    centred = source - jnp.mean(source, -1, keepdims=True)
    inv_std = lax.rsqrt(jnp.mean(centred * centred, -1, keepdims=True) + eps_norm)
    return (centred * inv_std, inv_std)


def norm_back(grad_norm, normed, inv_std):
    return inv_std * (
        grad_norm
        - jnp.mean(grad_norm, -1, keepdims=True)
        - normed * jnp.mean(grad_norm * normed, -1, keepdims=True)
    )


def linear_back(grad_out, inputs, weight):
    grad_low = grad_out.astype(jnp.bfloat16)
    return (
        contract(inputs, grad_low, 0, 0),
        contract(grad_low, weight, 1, 1),
        jnp.sum(grad_out, 0),
    )


def sincos(coords, width):
    omegas = 1.0 / 10000.0 ** (jnp.arange(width // 2, dtype=jnp.float32) / (width / 2.0))
    angles = coords[:, None] * omegas[None, :]
    return jnp.concatenate([jnp.sin(angles), jnp.cos(angles)], 1)


def positions():
    places = jnp.arange(PATCHES, dtype=jnp.int32)
    grid_row = (places // GRID).astype(jnp.float32)
    grid_col = (places % GRID).astype(jnp.float32)
    return jnp.concatenate([sincos(grid_row, D // 2), sincos(grid_col, D // 2)], 1)


def time_features(steps_f):
    half_width = FREQ // 2
    freq_rates = jnp.exp(
        -math.log(10000.0) * jnp.arange(half_width, dtype=jnp.float32) / half_width
    )
    angles = steps_f[:, None] * freq_rates[None, :]
    return jnp.concatenate([jnp.cos(angles), jnp.sin(angles)], 1)


def noise_level(steps_f):
    alpha_bar = jnp.cos((steps_f / 1000.0 + 0.008) / 1.008 * (math.pi / 2)) ** 2
    return (jnp.sqrt(alpha_bar), jnp.sqrt(1.0 - alpha_bar))


def pack_slots(routes):
    ids = jnp.arange(EXPERTS, dtype=jnp.int32)[:, None]
    named = [(routes[:, k][None, :] == ids) for k in range(2)]
    either = (named[0] | named[1]).astype(jnp.bfloat16)
    rows_here = routes.shape[0]
    place = jnp.arange(rows_here, dtype=jnp.int32)
    before = (place[:, None] < place[None, :]).astype(jnp.bfloat16)
    rank_in = product(either, before)
    counts = jnp.sum(either.astype(jnp.float32), 1).astype(jnp.int32)
    padded = (counts + 15) // 16 * 16
    starts = jnp.sum(jnp.where(ids > ids.T, padded[None, :], 0), 1)
    slots = rank_in.astype(jnp.int32) + starts[:, None]
    slot_of = jnp.stack([jnp.sum(jnp.where(member, slots, 0), 0) for member in named], 0)
    return (slot_of, jnp.stack([starts, counts], 0))


def gelu_slope(values):
    inner = SQRT_2_PI * (values + 0.044715 * values * values * values)
    bend = jnp.tanh(inner)
    return (
        0.5 * values * (1.0 + bend),
        0.5 * (1.0 + bend)
        + 0.5
        * values
        * (1.0 - bend * bend)
        * SQRT_2_PI
        * (1.0 + 3.0 * 0.044715 * values * values),
    )


def gelu_only(values):
    inner = SQRT_2_PI * (values + 0.044715 * values * values * values)
    return 0.5 * values * (1.0 + jnp.tanh(inner))


def up_columns(chunks, cut):
    return jnp.concatenate([chunks[cut // D + k] for k in range(CUT // D)], 1)


def slot_pick(slots_ref, base, rows):
    place = base + lax.broadcasted_iota(jnp.int32, (rows, slots_ref.shape[1]), 0)
    return ((slots_ref[0:1, :] == place) | (slots_ref[1:2, :] == place)).astype(jnp.bfloat16)


def over_blocks(meta, run):
    start, count = meta[0, pl.program_id(0)], meta[1, pl.program_id(0)]
    blocks = (count + BLK // 2 - 1) // BLK
    rest = count - blocks * BLK

    def block(number, unused):
        run(pl.multiple_of(start + number * BLK, 16), BLK, number > 0)
        return unused

    lax.fori_loop(0, blocks, block, 0)

    @pl.when(rest > BLK // 4)
    def _():
        run(pl.multiple_of(start + blocks * BLK, 16), BLK // 2, blocks > 0)

    @pl.when((rest > 0) & (rest <= BLK // 4))
    def _():
        run(pl.multiple_of(start + blocks * BLK, 16), BLK // 4, blocks > 0)


def routed_blocks(meta, slots_ref, x_ref, up_ref, down_ref, x_out, y_ref):
    def run(base, size, unused):
        rows = product(slot_pick(slots_ref, base, size), x_ref[...]).astype(jnp.bfloat16)
        x_out[pl.ds(base, size), :] = rows
        total = None
        for cut in range(0, FF, CUT):
            pre_act = product(rows, up_columns(up_ref[0], cut))
            part = product(gelu_only(pre_act).astype(jnp.bfloat16), down_ref[0, cut : cut + CUT])
            total = part if total is None else total + part
        y_ref[pl.ds(base, size), :] = total

    over_blocks(meta, run)


def forward_kernel(
    meta, slot_at, slots_ref, x_ref, up_ref, down_ref, routed_ref, x_out, y_ref
):
    routed_blocks(meta, slots_ref, x_ref, up_ref, down_ref, x_out, y_ref)

    @pl.when(pl.program_id(0) == EXPERTS - 1)
    def _():
        def group(number, unused):
            for step in range(8):
                token = number * 8 + step
                for k in range(2):
                    routed_ref[k, pl.ds(token, 1), :] = y_ref[pl.ds(slot_at[k, token], 1), :]
            return unused

        lax.fori_loop(0, x_ref.shape[0] // 8, group, 0)


def head_kernel(
    token_scale,
    meta,
    slot_at,
    slots_ref,
    x_ref,
    up_ref,
    down_ref,
    logits_ref,
    routes_ref,
    shared_ref,
    middle_ref,
    noise_ref,
    mods_ref,
    fin_ref,
    head_ref,
    pair_out,
    both_out,
    state_out,
    logits_out,
    thin_out,
    gate_out,
    fin_out,
    loss_out,
    x_out,
    routed_ref,
    y_ref,
):
    routed_blocks(meta, slots_ref, x_ref, up_ref, down_ref, x_out, y_ref)
    low = jnp.bfloat16

    @pl.when(pl.program_id(0) == EXPERTS - 1)
    def _():
        gate_out[...] = jnp.zeros_like(gate_out)
        fin_out[...] = jnp.zeros_like(fin_out)
        thin_out[...] = jnp.zeros_like(thin_out)
        loss_out[...] = jnp.zeros_like(loss_out)
        lane = lax.broadcasted_iota(jnp.int32, (PATCHES, 128), 1)

        def latent(lat, unused):
            base = pl.multiple_of(lat * PATCHES, PATCHES)
            span = pl.ds(base, PATCHES)

            def group(number, unused):
                for step in range(32):
                    token = number * 32 + step
                    for k in range(2):
                        routed_ref[k, pl.ds(token, 1), :] = y_ref[
                            pl.ds(slot_at[k, base + token], 1), :
                        ]
                return unused

            lax.fori_loop(0, PATCHES // 32, group, 0)
            hot = [
                (lane == routes_ref[span, k : k + 1]).astype(jnp.float32) for k in range(2)
            ]
            picked = [jnp.sum(hot[k] * logits_ref[span, :], 1, keepdims=True) for k in range(2)]
            most = jnp.maximum(picked[0], picked[1])
            powers = [jnp.exp(picked[k] - most) for k in range(2)]
            gates = [powers[k] / (powers[0] + powers[1]) for k in range(2)]
            moe_out = gates[0] * routed_ref[0] + gates[1] * routed_ref[1] + shared_ref[span, :]
            gate_moe = mods_ref[pl.ds(lat, 1), 5 * D :]
            normed, inv_std = layer_norm(middle_ref[span, :] + gate_moe * moe_out)
            scale = 1.0 + fin_ref[pl.ds(lat, 1), D:]
            head_in = (normed * scale + fin_ref[pl.ds(lat, 1), :D]).astype(low)
            errors = product(head_in, head_ref[...]) - noise_ref[span, :]
            loss_out[...] += jnp.sum(jnp.sum(errors * errors, 1, keepdims=True), 0, keepdims=True)
            errors = (errors * token_scale).astype(low)
            grads = contract(errors, head_ref[...], 1, 1)
            fin_out[pl.ds(lat, 1), :D] = jnp.sum(grads, 0, keepdims=True)
            fin_out[pl.ds(lat, 1), D:] = jnp.sum(grads * normed, 0, keepdims=True)
            state = norm_back(grads * scale, normed, inv_std)
            state_out[span, :] = state
            gate_out[pl.ds(lat, 1), :] = jnp.sum(moe_out * state, 0, keepdims=True)
            grads = gate_moe * state
            both_out[span, :] = grads.astype(low)
            slopes = []
            for k in range(2):
                slopes.append(jnp.sum(routed_ref[k] * grads, 1, keepdims=True))
                pair_out[k, span, :] = (gates[k] * grads).astype(low)
            usual = gates[0] * slopes[0] + gates[1] * slopes[1]
            grad_logits = (
                hot[0] * (gates[0] * (slopes[0] - usual)) + hot[1] * (gates[1] * (slopes[1] - usual))
            )
            logits_out[span, :] = grad_logits
            thin_out[...] += contract(x_ref[span, :], grad_logits.astype(low), 0, 0) + pltpu.roll(
                contract(head_in, errors, 0, 0), EXPERTS, 1
            )
            return unused

        lax.fori_loop(0, x_ref.shape[0] // PATCHES, latent, 0)


def experts_and_head(slot_of, meta, moe_in, up_full, down_full, token_scale, members):
    tokens = moe_in.shape[0]
    full, low = jnp.float32, jnp.bfloat16
    shapes = (
        ((2, tokens, D), low),
        ((tokens, D), low),
        ((tokens, D), full),
        ((tokens, 128), full),
        ((D, 128), full),
        ((8, D), full),
        ((8, 2 * D), full),
        ((1, 1), full),
        ((slot_room(tokens), D), low),
    )
    return pl.pallas_call(
        functools.partial(head_kernel, token_scale),
        grid_spec=pltpu.PrefetchScalarGridSpec(
            num_scalar_prefetch=2,
            grid=(EXPERTS,),
            in_specs=[
                whole_block((2, tokens)),
                whole_block((tokens, D)),
                pl.BlockSpec((1, NARROW_PIECES, D, D), lambda e, *unused: (e, 0, 0, 0)),
                pl.BlockSpec((1, FF, D), lambda e, *unused: (e, 0, 0)),
            ]
            + [whole_block(member.shape) for member in members],
            out_specs=[whole_block(shape) for shape, kind in shapes],
            scratch_shapes=[
                pltpu.VMEM((2, PATCHES, D), full),
                pltpu.VMEM((slot_room(tokens), D), full),
            ],
        ),
        out_shape=[jax.ShapeDtypeStruct(shape, kind) for shape, kind in shapes],
        compiler_params=pltpu.CompilerParams(vmem_limit_bytes=VMEM_ROOM),
        name="experts_and_head",
    )(meta, slot_of, slot_of, moe_in, up_full, down_full, *members)


def slot_room(tokens):
    return tokens * 2 + EXPERTS * 16 + BLK


def whole_block(shape):
    return pl.BlockSpec(shape, lambda e, *unused: (0,) * len(shape))


def experts_forward(slot_of, meta, moe_in, up_full, down_full):
    tokens = moe_in.shape[0]
    return pl.pallas_call(
        forward_kernel,
        grid_spec=pltpu.PrefetchScalarGridSpec(
            num_scalar_prefetch=2,
            grid=(EXPERTS,),
            in_specs=[
                whole_block((2, tokens)),
                whole_block((tokens, D)),
                pl.BlockSpec((1, NARROW_PIECES, D, D), lambda e, *unused: (e, 0, 0, 0)),
                pl.BlockSpec((1, FF, D), lambda e, *unused: (e, 0, 0)),
            ],
            out_specs=[whole_block((2, tokens, D)), whole_block((slot_room(tokens), D))],
            scratch_shapes=[pltpu.VMEM((slot_room(tokens), D), jnp.float32)],
        ),
        out_shape=[
            jax.ShapeDtypeStruct((2, tokens, D), jnp.float32),
            jax.ShapeDtypeStruct((slot_room(tokens), D), jnp.bfloat16),
        ],
        compiler_params=pltpu.CompilerParams(vmem_limit_bytes=VMEM_ROOM),
        cost_estimate=pl.CostEstimate(
            flops=20_000_000_000, bytes_accessed=50_000_000, transcendentals=0
        ),
        name="experts_forward",
    )(meta, slot_of, slot_of, moe_in, up_full, down_full)


def backward_kernel(
    meta,
    slot_at,
    slots_ref,
    x_ref,
    pair_ref,
    up_ref,
    down_ref,
    up_out,
    down_out,
    dx_slots,
    up_sum,
    down_sum,
):
    stack_id = pl.program_id(0)
    tokens = pair_ref.shape[1]

    @pl.when(meta[1, stack_id] == 0)
    def _():
        up_sum[...] = jnp.zeros_like(up_sum)
        down_sum[...] = jnp.zeros_like(down_sum)

    def expert(rows, grads, later):
        total = None
        for cut in range(0, FF, CUT):
            up_part = up_columns(up_ref[0], cut)
            activated, slope = gelu_slope(product(rows, up_part))
            grad_act = contract(grads, down_ref[0, cut : cut + CUT], 1, 1)
            grad_pre = (grad_act * slope).astype(jnp.bfloat16)
            down_part = contract(activated.astype(jnp.bfloat16), grads, 0, 0)
            up_grad = contract(rows, grad_pre, 0, 0)
            down_sum[cut : cut + CUT, :] = down_part + jnp.where(
                later, down_sum[cut : cut + CUT, :], 0.0
            )
            up_sum[:, cut : cut + CUT] = up_grad + jnp.where(
                later, up_sum[:, cut : cut + CUT], 0.0
            )
            part = contract(grad_pre, up_part, 1, 1)
            total = part if total is None else total + part
        return total

    stop = meta[0, stack_id] + meta[1, stack_id]

    def run(base, size, later):
        place = base + lax.broadcasted_iota(jnp.int32, (size, tokens), 0)
        place = jnp.where(place < stop, place, -1)
        grads = None
        for k in range(2):
            part = product((slots_ref[k : k + 1, :] == place).astype(jnp.bfloat16), pair_ref[k])
            grads = part if grads is None else grads + part
        dx_slots[pl.ds(base, size), :] = expert(
            x_ref[pl.ds(base, size), :], grads.astype(jnp.bfloat16), later
        )

    over_blocks(meta, run)
    for n in range(NARROW_PIECES):
        up_out[0, :, n] = (
            up_sum[:, n * D : (n + 1) * D]
            .astype(jnp.bfloat16)
            .reshape(WIDE_PIECES, PIECE, D)
        )
    down_out[0] = down_sum[...].astype(jnp.bfloat16).reshape(WIDE_PIECES, NARROW_PIECES, PIECE, D)


def experts_backward(slot_of, meta, slot_rows, grad_pair, up_full, down_full):
    tokens = slot_of.shape[1]
    slabs = (EXPERTS, WIDE_PIECES, NARROW_PIECES, PIECE, D)
    slab_spec = pl.BlockSpec((1,) + slabs[1:], lambda e, *unused: (e, 0, 0, 0, 0))
    return pl.pallas_call(
        backward_kernel,
        grid_spec=pltpu.PrefetchScalarGridSpec(
            num_scalar_prefetch=2,
            grid=(EXPERTS,),
            in_specs=[
                whole_block((2, tokens)),
                whole_block(slot_rows.shape),
                whole_block((2, tokens, D)),
                pl.BlockSpec((1, NARROW_PIECES, D, D), lambda e, *unused: (e, 0, 0, 0)),
                pl.BlockSpec((1, FF, D), lambda e, *unused: (e, 0, 0)),
            ],
            out_specs=[slab_spec, slab_spec, whole_block(slot_rows.shape)],
            scratch_shapes=[
                pltpu.VMEM((D, FF), jnp.float32),
                pltpu.VMEM((FF, D), jnp.float32),
            ],
        ),
        out_shape=[
            jax.ShapeDtypeStruct(slabs, jnp.bfloat16),
            jax.ShapeDtypeStruct(slabs, jnp.bfloat16),
            jax.ShapeDtypeStruct(slot_rows.shape, jnp.float32),
        ],
        compiler_params=pltpu.CompilerParams(vmem_limit_bytes=VMEM_ROOM),
        cost_estimate=pl.CostEstimate(
            flops=45_000_000_000, bytes_accessed=90_000_000, transcendentals=0
        ),
        name="experts_backward",
    )(meta, slot_of, slot_of, slot_rows, grad_pair, up_full, down_full)


def reduce_kernel(
    slot_at,
    down_ref,
    up_ref,
    up_all,
    down_all,
    moe_in_far,
    grad_both_far,
    dx_routed_far,
    grad_logits_far,
    middle_far,
    qkv_far,
    attended_far,
    grad_state_far,
    patches_far,
    places_far,
    mods_far,
    mats_all_far,
    bias_rows_far,
    pre_time_far,
    cond_far,
    freq_low_far,
    grad_gate_far,
    grad_fin_far,
    thin_in_far,
    label_parts_far,
    out_ref,
    rows_ref,
    lat_ref,
    bias_ref,
    own,
    got_core,
    out_one,
    keep_one,
    got_one,
    out_two,
    keep_two,
    got_two,
    got_last,
    keep_z,
    out_z,
    got_z,
    got_pair,
    row_parts,
    late,
    up_here,
    down_here,
    up_sum,
    down_sum,
    dx_sum,
    grad_mid,
    grad_att,
    grad_qkv,
    qkv_sum,
    proj_sum,
    patch_sum,
    grad_mods,
    lat_full,
    lat_low,
    own_sem,
    core_send,
    core_recv,
    one_send,
    one_recv,
    two_send,
    two_recv,
    z_send,
    z_recv,
    row_send,
    row_recv,
    lat_own,
    lat_send,
    lat_recv,
    here_sem,
    core_free,
    one_free,
    load_sem,
    moe_in,
    grad_both,
    dx_routed,
    grad_logits,
    middle,
    qkv,
    attended,
    grad_state,
    patches,
    places,
    mods,
    mats_all,
    bias_rows,
    pre_time,
    cond,
    freq_low,
    grad_gate,
    grad_fin,
    thin_in,
    label_parts,
):
    full, low = jnp.float32, jnp.bfloat16
    loads = [
        pltpu.make_async_copy(far, near, load_sem.at[number])
        for number, (far, near) in enumerate(
            (
                (moe_in_far, moe_in),
                (grad_both_far, grad_both),
                (dx_routed_far, dx_routed),
                (grad_logits_far, grad_logits),
                (middle_far, middle),
                (qkv_far, qkv),
                (attended_far, attended),
                (grad_state_far, grad_state),
                (patches_far, patches),
                (places_far, places),
                (mods_far, mods),
                (mats_all_far, mats_all),
                (bias_rows_far, bias_rows),
                (pre_time_far, pre_time),
                (cond_far, cond),
                (freq_low_far, freq_low),
                (grad_gate_far, grad_gate),
                (grad_fin_far, grad_fin),
                (thin_in_far, thin_in),
                (label_parts_far, label_parts),
            )
        )
    ]
    for load in loads:
        load.start()
    n_down, n_up, n_late = down_ref.shape[0], up_ref.shape[0], late.shape[0]
    slabs = n_down + n_up + n_late
    ahead, ring = 2, got_core.shape[0]
    wide, narrow = lax.axis_index(WIDE), lax.axis_index(NARROW)
    z, x = wide // 2, wide % 2
    y, c = narrow // 2, narrow % 2
    x_one, y_one = x + (1 - c) * (1 - 2 * x), y + c * (1 - 2 * y)
    x_two, y_two = x + c * (1 - 2 * x), y + (1 - c) * (1 - 2 * y)
    to_one = (z * 2 + x_one, y_one * 2 + c)
    to_two = (z * 2 + x_two, y_two * 2 + c)
    first_mine = x * (1 - c) + y * c
    second_mine = y * (1 - c) + x * c
    first_step, second_step = 2 - c, 1 + c
    mates = [
        (wide, (y + (k // 2) * (1 - 2 * y)) * 2 + c + (k % 2) * (1 - 2 * c)) for k in range(1, 4)
    ]
    levels = [(((z + k) % 4) * 2 + x, narrow) for k in range(1, 4)]
    to_x, to_core = (z * 2 + 1 - x, narrow), mates[0]
    barrier = pltpu.get_barrier_semaphore()
    for target in mates + levels + [to_x]:
        pl.semaphore_signal(barrier, inc=1, device_id=target, device_id_type=MESH_ID)
    pl.semaphore_wait(barrier, 7)

    def remote(source, target, send, recv, device):
        return pltpu.make_async_remote_copy(
            src_ref=source,
            dst_ref=target,
            send_sem=send,
            recv_sem=recv,
            device_id=device,
            device_id_type=MESH_ID,
        )

    def core_copy(source, s):
        return remote(
            source.at[:, 1 - c],
            got_core.at[s % ring],
            core_send.at[s % 4],
            core_recv.at[s % ring],
            to_core,
        )

    def own_copy(source, s):
        return pltpu.make_async_copy(source.at[:, c], own.at[s % 3], own_sem.at[s % 3])

    def one_copy(s):
        return remote(
            out_one.at[s % 2], got_one.at[s % ring], one_send.at[s % 2], one_recv.at[s % ring], to_one
        )

    def two_copy(s, turned=False):
        if turned:
            start, end = out_two.at[s % 2, 0], got_last.at[s // 2]
        else:
            start, end = out_two.at[s % 2], got_two.at[s // 2]
        return remote(start, end, two_send.at[s % 2], two_recv.at[s], to_two)

    def z_copy(s, k, turned=False):
        start, end = out_z.at[s % 2, (z + k) % 4], got_pair.at[s // 2, k - 1]
        if not turned:
            start, end = start.at[0], got_z.at[s // 2, k - 1]
        return remote(start, end, z_send.at[s % 2, k - 1], z_recv.at[s, k - 1], levels[k - 1])

    def by_order(s, run):
        turned = s % 2 == 1

        @pl.when(turned)
        def _():
            run(True)

        @pl.when(jnp.logical_not(turned))
        def _():
            run(False)

    def row_copy(r, k):
        mate = mates[k - 1]
        return remote(
            row_parts.at[r % 2, mate[1]],
            rows_ref.at[r, narrow],
            row_send.at[r % 2, k - 1],
            row_recv.at[r, k - 1],
            mate,
        )

    def lat_level(k):
        return remote(
            lat_low, lat_ref.at[z, x, y, c], lat_send.at[k - 1], lat_recv.at[k - 1], levels[k - 1]
        )

    def lat_x():
        spot = lat_ref.at[:, x, y, c]
        return remote(spot, spot, lat_send.at[3], lat_recv.at[3], to_x)

    def lat_y():
        spot = lat_ref.at[:, :, y, c]
        return remote(spot, spot, lat_send.at[4], lat_recv.at[4], mates[1])

    def lat_core():
        spot = lat_ref.at[:, :, :, c]
        return remote(spot, spot, lat_send.at[5], lat_recv.at[5], to_core)

    def lat_own_copy():
        return pltpu.make_async_copy(lat_low, lat_ref.at[z, x, y, c], lat_own.at[0])

    def begin(source, s):
        @pl.when(s >= 4)
        def _():
            core_copy(source, s).wait_send()

        @pl.when(s >= ring)
        def _():
            pl.semaphore_wait(core_free, 1)

        core_copy(source, s).start()
        own_copy(source, s).start()

    def stage_core(s):
        own_copy(down_ref.at[0], s).wait()
        core_copy(down_ref.at[0], s).wait_recv()

        @pl.when(s >= 2)
        def _():
            one_copy(s).wait_send()

        @pl.when(s >= ring)
        def _():
            pl.semaphore_wait(one_free, 1)

        for level in range(4):
            for other in range(2):
                place = level * 2 + other
                base = level * 4 + other * second_step
                send_at = base + (1 - first_mine) * first_step
                out_one[s % 2, place] = (
                    own[s % 3, send_at].astype(full) + got_core[s % ring, send_at].astype(full)
                ).astype(low)
        one_copy(s).start()
        for level in range(4):
            for other in range(2):
                place = level * 2 + other
                base = level * 4 + other * second_step
                keep_at = base + first_mine * first_step
                keep_one[s % 3, place] = own[s % 3, keep_at].astype(full) + got_core[
                    s % ring, keep_at
                ].astype(full)

        @pl.when(s < slabs - ring)
        def _():
            pl.semaphore_signal(core_free, inc=1, device_id=to_core, device_id_type=MESH_ID)

    def stage_one(s):
        one_copy(s).wait_recv()

        def run(turned):
            @pl.when(s >= 2)
            def _():
                sent(s, turned)

            if turned:
                for level in range(4):
                    for other in range(2):
                        out_z[s % 2, level, other] = (
                            keep_one[s % 3, level * 2 + other]
                            + got_one[s % ring, level * 2 + other].astype(full)
                        ).astype(low)
                for k in range(1, 4):
                    z_copy(s, k, True).start()
                for other in range(2):
                    keep_two[s % 3, other] = keep_one[s % 3, z * 2 + other] + got_one[
                        s % ring, z * 2 + other
                    ].astype(full)
            else:
                for level in range(4):
                    send_at = level * 2 + 1 - second_mine
                    out_two[s % 2, level] = (
                        keep_one[s % 3, send_at] + got_one[s % ring, send_at].astype(full)
                    ).astype(low)
                two_copy(s).start()
                for level in range(4):
                    keep_at = level * 2 + second_mine
                    keep_two[s % 3, level] = keep_one[s % 3, keep_at] + got_one[
                        s % ring, keep_at
                    ].astype(full)

        by_order(s, run)

        @pl.when(s < slabs - ring)
        def _():
            pl.semaphore_signal(one_free, inc=1, device_id=to_one, device_id_type=MESH_ID)

    def sent(s, turned):
        if turned:
            for k in range(1, 4):
                z_copy(s, k, True).wait_send()
        else:
            two_copy(s).wait_send()

    def sent_last(s, turned):
        if turned:
            two_copy(s, True).wait_send()
        else:
            for k in range(1, 4):
                z_copy(s, k).wait_send()

    def stage_two(s):
        def run(turned):
            if turned:
                for k in range(1, 4):
                    z_copy(s, k, True).wait_recv()
            else:
                two_copy(s).wait_recv()

            @pl.when(s >= 2)
            def _():
                sent_last(s, turned)

            if turned:

                def gathered(other):
                    total = keep_two[s % 3, other]
                    for k in range(3):
                        total = total + got_pair[s // 2, k, other].astype(full)
                    return total

                out_two[s % 2, 0] = gathered(1 - second_mine).astype(low)
                two_copy(s, True).start()
                keep_z[s % 3] = gathered(second_mine)
            else:
                for level in range(4):
                    out_z[s % 2, level, 0] = (
                        keep_two[s % 3, level] + got_two[s // 2, level].astype(full)
                    ).astype(low)
                for k in range(1, 4):
                    z_copy(s, k).start()
                keep_z[s % 3] = keep_two[s % 3, z] + got_two[s // 2, z].astype(full)

        by_order(s, run)

    def direct_place(s):
        late_at = s - n_down - n_up
        return (s < n_down) | ((late_at >= 0) & (late_at < SHARED))

    def row_place(s):
        return jnp.where(s < n_down + n_up, s - n_down, s - n_down - SHARED)

    def finish(s):
        def run(turned):
            if turned:
                two_copy(s, True).wait_recv()
                keep_z[s % 3] += got_last[s // 2].astype(full)
            else:
                for k in range(1, 4):
                    z_copy(s, k).wait_recv()
                total = keep_z[s % 3]
                for k in range(3):
                    total = total + got_z[s // 2, k].astype(full)
                keep_z[s % 3] = total

        by_order(s, run)
        total = keep_z[s % 3]

        @pl.when(direct_place(s))
        def _():
            out_ref[jnp.clip(jnp.where(s < n_down, s, s - n_up), 0, n_down + SHARED - 1)] = total

        @pl.when(jnp.logical_not(direct_place(s)))
        def _():
            r = row_place(s)

            @pl.when(r >= 2)
            def _():
                for k in range(1, 4):
                    row_copy(r, k).wait_send()

            for n in range(NARROW_PIECES):
                row_parts[r % 2, n] = jnp.concatenate(
                    [total[n * ROWS : (n + 1) * ROWS], jnp.zeros((16 - ROWS, D), full)], 0
                ).astype(low)
            rows_ref[r, narrow] = row_parts[r % 2, narrow]
            for k in range(1, 4):
                row_copy(r, k).start()

    def rows_in(s):
        @pl.when(jnp.logical_not(direct_place(s)))
        def _():
            for k in range(1, 4):
                row_copy(row_place(s), k).wait_recv()

    tokens = moe_in.shape[0]
    lats = tokens // PATCHES

    def matrix(number, start, stop):
        chunk = mats_all[number // 2, number % 2]
        return chunk.reshape(D, chunk.shape[-1])[:, start:stop]

    def mod_row(start, number):
        return mods[pl.ds(start // PATCHES, 1), number * D : (number + 1) * D]

    def keep_mod(start, number, values):
        grad_mods[pl.ds(start // PATCHES, 1), number * D : (number + 1) * D] = jnp.sum(
            values, 0, keepdims=True
        )

    def add_bias(number, values):
        for k in range(values.shape[1] // D):
            bias_ref[number + k : number + k + 1, :] += jnp.sum(
                values[:, k * D : (k + 1) * D], 0, keepdims=True
            )

    def prepare():
        bias_ref[...] = jnp.zeros_like(bias_ref)
        qkv_sum[...] = jnp.zeros_like(qkv_sum)
        proj_sum[...] = jnp.zeros_like(proj_sum)
        patch_sum[...] = jnp.zeros_like(patch_sum)
        grad_mods[...] = jnp.zeros_like(grad_mods)

    def fetch(shared_id):
        e = EXPERTS + shared_id
        first = pltpu.make_async_copy(down_all.at[e], down_here, here_sem.at[0])
        second = pltpu.make_async_copy(up_all.at[e], up_here, here_sem.at[1])
        first.start()
        second.start()
        first.wait()
        second.wait()
        up_sum[...] = jnp.zeros_like(up_sum)
        down_sum[...] = jnp.zeros_like(down_sum)

    def shared_block(shared_id, start):
        span = pl.ds(start, PATCHES)
        rows, grads = moe_in[span, :], grad_both[span, :]
        total = jnp.zeros((PATCHES, D), full) if shared_id == 0 else dx_sum[span, :]
        for cut in range(0, FF, CUT):
            up_part = up_columns(up_here, cut)
            activated, slope = gelu_slope(product(rows, up_part))
            grad_act = contract(grads, down_here[cut : cut + CUT], 1, 1)
            grad_pre = (grad_act * slope).astype(low)
            down_sum[cut : cut + CUT, :] += contract(activated.astype(low), grads, 0, 0)
            up_sum[:, cut : cut + CUT] += contract(rows, grad_pre, 0, 0)
            total = total + contract(grad_pre, up_part, 1, 1)
        dx_sum[span, :] = total

    def shared_slabs(shared_id):
        for w in range(WIDE_PIECES):
            for n in range(NARROW_PIECES):
                at = (w * NARROW_PIECES + n) * PIECE
                late[shared_id, w * 2 + n // 2, n % 2] = down_sum[at : at + PIECE, :].astype(low)
                late[SHARED + shared_id, w * 2 + n // 2, n % 2] = up_sum[
                    w * PIECE : (w + 1) * PIECE, n * D : (n + 1) * D
                ].astype(low)

    def back_rows(start):
        def group(number, unused):
            for step in range(8):
                token = start + number * 8 + step
                dx_sum[pl.ds(token, 1), :] += (
                    dx_routed[pl.ds(slot_at[0, token], 1), :]
                    + dx_routed[pl.ds(slot_at[1, token], 1), :]
                )
            return unused

        lax.fori_loop(0, PATCHES // 8, group, 0)

    def back_out(start):
        span = pl.ds(start, PATCHES)
        grads = dx_sum[span, :] + contract(
            grad_logits[span, :].astype(low), matrix(0, 4 * D, 4 * D + 128), 1, 1
        )
        normed, inv_std = layer_norm(middle[span, :])
        keep_mod(start, 3, grads)
        keep_mod(start, 4, grads * normed)
        grads = grad_state[span, :] + norm_back(
            grads * (1.0 + mod_row(start, 4)), normed, inv_std
        )
        grad_mid[...] = grads
        proj = matrix(0, 3 * D, 4 * D)
        rows = attended[span, :]
        keep_mod(start, 2, (product(rows, proj) + bias_rows[3:4, :]) * grads)
        grads = grads * mod_row(start, 2)
        add_bias(3, grads)
        grads = grads.astype(low)
        proj_sum[...] += contract(rows, grads, 0, 0)
        grad_att[...] = contract(grads, proj, 1, 1).astype(low)

    def back_pair(pair, start):
        span = pl.ds(start, PATCHES)
        lane = lax.broadcasted_iota(jnp.int32, (PATCHES, 2 * HD), 1)
        at = pair * 2 * HD
        queries = qkv[span, at : at + 2 * HD]
        keys = qkv[span, D + at : D + at + 2 * HD]
        values = qkv[span, 2 * D + at : 2 * D + at + 2 * HD]
        grads = grad_att[:, at : at + 2 * HD]
        sums = None
        for half in range(2):
            mine = (lane < HD) if half == 0 else (lane >= HD)
            scores = contract(jnp.where(mine, queries, 0), keys, 1, 1) * HD ** (-0.5)
            powers = jnp.exp(scores - jnp.max(scores, 1, keepdims=True))
            probs = powers / jnp.sum(powers, 1, keepdims=True)
            grad_mine = jnp.where(mine, grads, 0)
            grad_probs = contract(grad_mine, values, 1, 1)
            grad_scores = (
                probs
                * (grad_probs - jnp.sum(probs * grad_probs, 1, keepdims=True))
                * HD ** (-0.5)
            ).astype(low)
            parts = (
                product(grad_scores, jnp.where(mine, keys, 0)),
                contract(grad_scores, jnp.where(mine, queries, 0), 0, 0),
                contract(probs.astype(low), grad_mine, 0, 0),
            )
            sums = parts if sums is None else [a + b for a, b in zip(sums, parts)]
        for k in range(3):
            where = k * D + at
            grad_qkv[:, where : where + 2 * HD] = sums[k].astype(low)
            bias_ref[k : k + 1, at : at + 2 * HD] += jnp.sum(sums[k], 0, keepdims=True)

    def back_in(start):
        span = pl.ds(start, PATCHES)
        emb = contract(patches[span, :], matrix(2, 4 * D, 4 * D + 128), 1, 1)
        emb = emb + bias_rows[10:11, :] + places[...]
        normed, inv_std = layer_norm(emb)
        rows = (normed * (1.0 + mod_row(start, 1)) + mod_row(start, 0)).astype(low)
        qkv_sum[...] += contract(rows, grad_qkv[...], 0, 0)
        grads = contract(grad_qkv[...], matrix(0, 0, 3 * D), 1, 1)
        keep_mod(start, 0, grads)
        keep_mod(start, 1, grads * normed)
        grads = grad_mid[...] + norm_back(grads * (1.0 + mod_row(start, 1)), normed, inv_std)
        add_bias(10, grads)
        patch_sum[...] += contract(grads.astype(low), patches[span, :], 0, 0)

    def silu_slope(values):
        gate = jax.nn.sigmoid(values)
        return gate + values * gate * (1.0 - gate)

    def back_conditions():
        grad_mods[:, 5 * D :] = grad_gate[...]
        grads = grad_mods[...]
        mod_low, fin_low = grads.astype(low), grad_fin[...].astype(low)
        grad_act = (
            contract(mod_low[:, : 4 * D], matrix(1, 0, 4 * D), 1, 1)
            + contract(mod_low[:, 4 * D :], matrix(2, 0, 2 * D), 1, 1)
            + contract(fin_low, matrix(2, 2 * D, 4 * D), 1, 1)
        )
        grad_cond = silu_slope(cond[...]) * grad_act
        high = grad_cond.astype(low)
        grad_time = silu_slope(pre_time[...]) * contract(high, matrix(3, 1024, 1408), 1, 1)
        add_bias(4, grads)
        add_bias(11, grad_time)
        add_bias(12, grad_cond)
        add_bias(13, grad_fin[...])
        high = high.astype(full)
        rest = grad_cond - high
        middle_part = rest.astype(low).astype(full)
        act = jax.nn.silu(cond[...]).astype(low).astype(full)
        hid = jax.nn.silu(pre_time[...]).astype(low).astype(full)
        mod_low, fin_low = mod_low.astype(full), fin_low.astype(full)
        quarters = (
            jnp.concatenate([act, hid, mod_low[:, : 2 * D]], 1),
            mod_low[:, 2 * D :],
            jnp.concatenate([fin_low, high, grad_time.astype(low).astype(full)], 1),
            jnp.concatenate(
                [
                    freq_low[...].astype(full),
                    middle_part,
                    rest - middle_part,
                    label_parts[...].astype(full),
                    jnp.zeros((8, D), full),
                ],
                1,
            ),
        )
        for lat in range(lats):
            for k in range(4):
                lat_full[lat * 4 + k : lat * 4 + k + 1, :] = quarters[k][lat : lat + 1, :]
        lat_low[...] = lat_full[...].astype(low)

    def last_slabs():
        for w in range(WIDE_PIECES):
            span = slice(w * PIECE, (w + 1) * PIECE)
            for n in range(3):
                late[2 * SHARED, w * 2 + n // 2, n % 2] = qkv_sum[
                    span, n * D : (n + 1) * D
                ].astype(low)
            late[2 * SHARED, w * 2 + 1, 1] = proj_sum[span, :].astype(low)
            thin = thin_in[span, :] + pltpu.roll(patch_sum[span, :], EXPERTS + PD, 1)
            for n in range(NARROW_PIECES):
                late[2 * SHARED + 1, w * 2 + n // 2, n % 2] = jnp.zeros((PIECE, D), low)
            late[2 * SHARED + 1, w * 2, 0, :, :128] = thin.astype(low)

    first_lat = SHARED * lats
    units = (
        back_rows,
        back_out,
        lambda start: back_pair(0, start),
        lambda start: back_pair(1, start),
        lambda start: back_pair(2, start),
        back_in,
    )
    after = first_lat + len(units) * lats

    def tick(t, unused):
        first = 0
        for source, count in ((down_ref, n_down), (up_ref, n_up), (late, n_late)):

            @pl.when((t >= first) & (t < first + count))
            def _():
                begin(source.at[jnp.clip(t - first, 0, count - 1)], t)

            first += count

        for lag, stage in enumerate((stage_core, stage_one, stage_two, finish, rows_in)):
            s = t - ahead - 2 * lag

            @pl.when((s >= 0) & (s < slabs))
            def _():
                stage(s)

        @pl.when(t == 0)
        def _():
            prepare()
            for load in loads[:3]:
                load.wait()

        @pl.when(t == first_lat)
        def _():
            for load in loads[3:]:
                load.wait()

        for shared_id in range(SHARED):
            start_at = shared_id * lats

            @pl.when(t == start_at)
            def _():
                fetch(shared_id)

            @pl.when((t >= start_at) & (t < start_at + lats))
            def _():
                shared_block(
                    shared_id,
                    pl.multiple_of(jnp.clip(t - start_at, 0, lats - 1) * PATCHES, PATCHES),
                )

            @pl.when(t == start_at + lats - 1)
            def _():
                shared_slabs(shared_id)

        for number, unit in enumerate(units):

            @pl.when((t >= first_lat) & (t < after) & ((t - first_lat) % len(units) == number))
            def _():
                lat = jnp.clip((t - first_lat) // len(units), 0, lats - 1)
                unit(pl.multiple_of(lat * PATCHES, PATCHES))

        @pl.when(t == after)
        def _():
            back_conditions()
            lat_own_copy().start()
            for k in range(1, 4):
                lat_level(k).start()
            lat_own_copy().wait()

        @pl.when(t == after + 1)
        def _():
            last_slabs()

        @pl.when(t == after + 3)
        def _():
            for k in range(1, 4):
                lat_level(k).wait_recv()
            lat_x().start()

        @pl.when(t == after + 5)
        def _():
            lat_x().wait_recv()
            lat_y().start()

        @pl.when(t == after + 7)
        def _():
            lat_y().wait_recv()
            lat_core().start()

        return unused

    lax.fori_loop(0, slabs + ahead + 8, tick, 0)
    for back in range(4):
        core_copy(down_ref.at[0], slabs - 1 - back).wait_send()
    turned = rows_ref.shape[0]
    for back in range(2):
        s = slabs - 1 - back
        one_copy(s).wait_send()
        sent(s, s % 2 == 1)
        sent_last(s, s % 2 == 1)
        for k in range(1, 4):
            row_copy(turned - 1 - back, k).wait_send()
    for k in range(1, 4):
        lat_level(k).wait_send()
    lat_x().wait_send()
    lat_y().wait_send()
    lat_core().wait()


def reduce_slabs(slot_of, down_slabs, up_slabs, up_all, down_all, members):
    n_late = 2 * SHARED + 2
    routed = down_slabs.shape[0]
    slabs = 2 * routed + n_late
    direct, turned = routed + SHARED, routed + SHARED + 2
    ring = 4
    low, full = jnp.bfloat16, jnp.float32
    sources = [
        member.reshape(routed, WIDE_PIECES * NARROW_PIECES // 2, 2, PIECE, D)
        for member in (down_slabs, up_slabs)
    ]
    tokens = members[0].shape[0]
    dma, regular = pltpu.SemaphoreType.DMA, pltpu.SemaphoreType.REGULAR
    vmem, anywhere = pl.BlockSpec(memory_space=pltpu.VMEM), pl.BlockSpec(memory_space=pl.ANY)
    sums, rows, lats, bias_sum = pl.pallas_call(
        reduce_kernel,
        out_shape=[
            jax.ShapeDtypeStruct((direct, PIECE, D), full),
            jax.ShapeDtypeStruct((turned, NARROW_PIECES, 16, D), low),
            jax.ShapeDtypeStruct((4, 2, 2, 2, LAT_ROWS, LAT_COLS), low),
            jax.ShapeDtypeStruct((16, D), full),
        ],
        in_specs=[pl.BlockSpec(memory_space=pltpu.SMEM)] + [anywhere] * (4 + len(members)),
        out_specs=[vmem, vmem, anywhere, vmem],
        scratch_shapes=[
            pltpu.VMEM((3, 16, PIECE, D), low),
            pltpu.VMEM((ring, 16, PIECE, D), low),
            pltpu.VMEM((2, 8, PIECE, D), low),
            pltpu.VMEM((3, 8, PIECE, D), full),
            pltpu.VMEM((ring, 8, PIECE, D), low),
            pltpu.VMEM((2, 4, PIECE, D), low),
            pltpu.VMEM((3, 4, PIECE, D), full),
            pltpu.VMEM(((slabs + 1) // 2, 4, PIECE, D), low),
            pltpu.VMEM(((slabs + 1) // 2, PIECE, D), low),
            pltpu.VMEM((3, PIECE, D), full),
            pltpu.VMEM((2, 4, 2, PIECE, D), low),
            pltpu.VMEM(((slabs + 1) // 2, 3, PIECE, D), low),
            pltpu.VMEM((slabs // 2, 3, 2, PIECE, D), low),
            pltpu.VMEM((2, NARROW_PIECES, 16, D), low),
            pltpu.VMEM((n_late, 16, 2, PIECE, D), low),
            pltpu.VMEM((NARROW_PIECES, D, D), low),
            pltpu.VMEM((FF, D), low),
            pltpu.VMEM((D, FF), full),
            pltpu.VMEM((FF, D), full),
            pltpu.VMEM((tokens, D), full),
            pltpu.VMEM((PATCHES, D), full),
            pltpu.VMEM((PATCHES, D), low),
            pltpu.VMEM((PATCHES, 3 * D), low),
            pltpu.VMEM((D, 3 * D), full),
            pltpu.VMEM((D, D), full),
            pltpu.VMEM((D, 128), full),
            pltpu.VMEM((8, 6 * D), full),
            pltpu.VMEM((LAT_ROWS, LAT_COLS), full),
            pltpu.VMEM((LAT_ROWS, LAT_COLS), low),
            dma((3,)),
            dma((4,)),
            dma((ring,)),
            dma((2,)),
            dma((ring,)),
            dma((2,)),
            dma((slabs,)),
            dma((2, 3)),
            dma((slabs, 3)),
            dma((2, 3)),
            dma((turned, 3)),
            dma((1,)),
            dma((6,)),
            dma((6,)),
            dma((2,)),
            regular,
            regular,
            dma((len(members),)),
        ]
        + [pltpu.VMEM(member.shape, member.dtype) for member in members],
        compiler_params=pltpu.CompilerParams(
            collective_id=0, has_side_effects=True, vmem_limit_bytes=REDUCE_ROOM
        ),
        name="reduce_slabs",
    )(slot_of, *sources, up_all, down_all, *members)
    return sums, rows, lats.reshape(-1, LAT_COLS), bias_sum


def plain_grads(
    down_slabs, up_slabs, mats_slabs, thin, grad_bias, lows, grad_cond, labels, row_count
):
    def scattered(member):
        return lax.psum_scatter(member, AXES, scatter_dimension=1, tiled=True)

    proj_grad = scattered(mats_slabs)
    row_start = lax.axis_index(AXES) * row_count
    thin_grad = lax.psum_scatter(thin, AXES, scatter_dimension=0, tiled=True)
    bias_grad = lax.psum_scatter(grad_bias, AXES, scatter_dimension=0, tiled=True)
    grad_mod, grad_time2, grad_fin, grad_time1, grad_table = latent_grads(
        lows, grad_cond, labels, row_start, row_count
    )
    mats_grad = jnp.concatenate(
        [proj_grad[0], grad_mod, grad_time2, grad_fin, thin_grad, grad_time1, grad_table], 1
    )
    return (mats_grad, scattered(up_slabs), scattered(down_slabs), bias_grad)


def spread(value, place):
    lane = lax.broadcasted_iota(jnp.int32, (1, 128), 1)
    return jnp.where(lane == place, value, 0.0)


def pick(row, place):
    lane = lax.broadcasted_iota(jnp.int32, (1, 128), 1)
    return jnp.sum(jnp.where(lane == place, row, 0.0), 1, keepdims=True)


def total(values):
    return jnp.sum(jnp.sum(values, 1, keepdims=True), 0, keepdims=True)


def turn_line(values):
    count = max(values.shape)
    same = lax.broadcasted_iota(jnp.int32, (count, count), 0) == lax.broadcasted_iota(
        jnp.int32, (count, count), 1
    )
    across = 1 if values.shape[0] == 1 else 0
    return jnp.sum(jnp.where(same, values, 0.0), across, keepdims=True)


def joined(chunks):
    chunks = chunks.astype(jnp.float32)
    return jnp.concatenate([chunks[j][:ROWS] for j in range(NARROW_PIECES)], 1)


def by_piece(values, start_last, width_last):
    bounds = [sum(column_widths()[:k]) for k in range(len(column_widths()) + 1)]
    last_lane = lax.broadcasted_iota(jnp.int32, (ROWS, width_last), 1) + start_last
    chosen_value = values[0]
    for k in range(6, len(column_widths())):
        chosen_value = jnp.where(last_lane >= bounds[k], values[k - 5], chosen_value)
    return chosen_value


def factored(grad, row, col, mean):
    return grad * lax.rsqrt(row * col / mean)


def update_kernel(
    sums_ref,
    rows_ref,
    lat_ref,
    bias_sum,
    loss_ref,
    mats_row,
    mats_col,
    up_row,
    up_col,
    down_row,
    down_col,
    bias_state,
    mats_grad,
    mats_row_new,
    mats_col_new,
    up_row_new,
    up_col_new,
    down_row_new,
    down_col_new,
    bias_grad,
    bias_state_new,
    line_out,
    squares_out,
    part,
    got_plane,
    got_level,
    result,
    squares_plane,
    squares_level,
    sems,
):
    full, low = jnp.float32, jnp.bfloat16
    wide, narrow = lax.axis_index(WIDE), lax.axis_index(NARROW)
    z, spot = wide // 2, (wide % 2) * 4 + narrow

    def plane_device(k):
        there = (spot + k) % 8
        return (z * 2 + there // 4, there % 4)

    def level_device(k):
        return (((z + k) % 4) * 2 + wide % 2, narrow)

    barrier = pltpu.get_barrier_semaphore()
    for k in range(1, 8):
        pl.semaphore_signal(barrier, inc=1, device_id=plane_device(k), device_id_type=MESH_ID)
    for k in range(1, 4):
        pl.semaphore_signal(barrier, inc=1, device_id=level_device(k), device_id_type=MESH_ID)
    pl.semaphore_wait(barrier, 10)

    def remote(source, target, phase, k, device):
        return pltpu.make_async_remote_copy(
            src_ref=source,
            dst_ref=target,
            send_sem=sems.at[0, phase, k],
            recv_sem=sems.at[1, phase, k],
            device_id=device,
            device_id_type=MESH_ID,
        )

    def exchange(copies):
        for copy in copies:
            copy.start()
        for copy in copies:
            copy.wait()

    count = lat_ref.shape[0] // 4
    order = lax.broadcasted_iota(jnp.int32, (count, count * 4), 0) * 4
    place = lax.broadcasted_iota(jnp.int32, (count, count * 4), 1)
    quarters = [
        product((place == order + k).astype(low), lat_ref[...]).astype(low) for k in range(4)
    ]
    owner_row = (wide * NARROW_PIECES + narrow) * ROWS
    chosen = (
        lax.broadcasted_iota(jnp.int32, (16, D), 1)
        == lax.broadcasted_iota(jnp.int32, (16, D), 0) + owner_row
    ).astype(low)

    def rows_of(member):
        return contract(chosen, member, 1, 1).astype(low)

    act_rows = rows_of(quarters[0][:, :D])
    hid_rows = rows_of(quarters[0][:, D : 2 * D])
    high = quarters[2][:, 2 * D : 3 * D]
    for j in range(NARROW_PIECES):
        mats_grad[:, j * D : (j + 1) * D] = rows_ref[EXPERTS + SHARED, j].astype(full)[:ROWS]
    mats_grad[:, 4 * D : 6 * D] = product(act_rows, quarters[0][:, 2 * D :])[:ROWS]
    mats_grad[:, 6 * D : 10 * D] = product(act_rows, quarters[1])[:ROWS]
    mats_grad[:, 10 * D : 11 * D] = product(hid_rows, high)[:ROWS]
    mats_grad[:, 11 * D : 13 * D] = product(act_rows, quarters[2][:, : 2 * D])[:ROWS]
    time_rows = rows_of(quarters[2][:, 3 * D :])
    time_one = product(time_rows, quarters[3][:, :FREQ])
    label_at = FREQ + 2 * D
    labels = quarters[3][:, label_at : label_at + 128].astype(full)
    label = labels[:, 0:1] * 32.0 + labels[:, 1:2]
    label_hot = (
        lax.broadcasted_iota(jnp.int32, (count, 1024), 1).astype(full) == label
    ).astype(low)
    table = (
        product(rows_of(high), label_hot)
        + product(rows_of(quarters[3][:, FREQ : FREQ + D]), label_hot)
        + product(rows_of(quarters[3][:, FREQ + D : FREQ + 2 * D]), label_hot)
    )
    start_last = 13 * D
    width_last = mats_grad.shape[1] - start_last
    room = 11 * 128
    thin = rows_ref[EXPERTS + SHARED + 1, 0].astype(full)[:, :128]
    thin = jnp.where(
        lax.broadcasted_iota(jnp.int32, (16, 128), 1) < EXPERTS + 2 * PD, thin, 0.0
    )

    def padded(member):
        return jnp.concatenate(
            [member, jnp.zeros((16, room - member.shape[1]), full)], 1
        )

    last = (
        padded(thin)
        + pltpu.roll(padded(time_one), EXPERTS + 2 * PD, 1)
        + pltpu.roll(padded(table), EXPERTS + 2 * PD + FREQ, 1)
    )
    mats_grad[:, start_last:] = last[:ROWS, :width_last]

    part[...] = jnp.zeros_like(part)
    widths = column_widths()
    mats_at, line_at, bias_at = 360, 416, 432
    total_cols = mats_grad.shape[1]
    cuts = [(at, min(at + 128, total_cols)) for at in range(0, total_cols, 128)]
    for number, (begin, end) in enumerate(cuts):
        values = mats_grad[:, begin:end]
        part[mats_at + number : mats_at + number + 1, : end - begin] = jnp.sum(
            values * values + eps_fact, 0, keepdims=True
        )
    bounds = [sum(widths[:k]) for k in range(len(widths) + 1)]
    last_lane = lax.broadcasted_iota(jnp.int32, (ROWS, width_last), 1) + start_last
    last_sq = mats_grad[:, start_last:] * mats_grad[:, start_last:] + eps_fact
    line = spread(loss_ref[...], 46)
    for k in range(len(widths)):
        if k < 5:
            values = mats_grad[:, bounds[k] : bounds[k + 1]]
            sq = values * values + eps_fact
        else:
            sq = jnp.where((last_lane >= bounds[k]) & (last_lane < bounds[k + 1]), last_sq, 0.0)
        new = decay * turn_line(mats_row[k : k + 1, :]) + (1.0 - decay) * (
            jnp.sum(sq, 1, keepdims=True) / widths[k]
        )
        mats_row_new[k : k + 1, :] = turn_line(new)
        line = line + spread(jnp.sum(new, 0, keepdims=True), k)

    def begin_up(e, line):
        values = joined(rows_ref[e])
        sq = values * values + eps_fact
        new = decay * turn_line(up_row[pl.ds(e, 1), :]) + (1.0 - decay) * (jnp.sum(sq, 1, keepdims=True) / FF)
        up_row_new[pl.ds(e, 1), :] = turn_line(new)
        cols = jnp.sum(sq, 0, keepdims=True)
        for k in range(FF // 128):
            part[pl.ds(24 * k + e, 1), :] = cols[:, 128 * k : 128 * (k + 1)]
        return line + spread(jnp.sum(new, 0, keepdims=True), 10 + e)

    def begin_down(e, line):
        values = sums_ref[e]
        sq = values * values + eps_fact
        new = decay * turn_line(down_row[pl.ds(e, 1), :]) + (1.0 - decay) * (jnp.sum(sq, 1, keepdims=True) / D)
        down_row_new[pl.ds(e, 1), :] = turn_line(new)
        cols = jnp.sum(sq, 0, keepdims=True)
        for k in range(D // 128):
            part[pl.ds(24 * (12 + k) + e, 1), :] = cols[:, 128 * k : 128 * (k + 1)]
        return line + spread(jnp.sum(new, 0, keepdims=True), 28 + e)

    line = lax.fori_loop(0, EXPERTS + SHARED, begin_up, line, unroll=True)
    line = lax.fori_loop(0, EXPERTS + SHARED, begin_down, line, unroll=True)
    part[line_at : line_at + 1, :] = line
    for k in range(D // 128):
        part[bias_at + 16 * k : bias_at + 16 * (k + 1), :] = bias_sum[:, 128 * k : 128 * (k + 1)]

    exchange(
        [
            remote(
                part.at[pl.ds(((spot + k) % 8) * 64, 64)], got_plane.at[k], 0, k, plane_device(k)
            )
            for k in range(1, 8)
        ]
    )
    here = part[pl.ds(pl.multiple_of(spot * 64, 64), 64), :]
    for k in range(1, 8):
        here = here + got_plane[k]
    got_level[z] = here.reshape(4, 16, 128)
    exchange(
        [remote(got_level.at[z], got_level.at[z], 1, k, level_device(k)) for k in range(1, 4)]
    )
    result[spot] = got_level[0] + got_level[1] + got_level[2] + got_level[3]
    exchange(
        [remote(result.at[spot], result.at[spot], 3, k, plane_device(k)) for k in range(1, 8)]
    )

    def sums_row(row, width=128):
        if isinstance(row, int):
            return result[row // 64, (row // 16) % 4, row % 16 : row % 16 + 1, :width]
        return result[row // 64, (row // 16) % 4, pl.ds(row % 16, 1), :width]

    line = sums_row(line_at)
    line_out[...] = line
    room = bias_grad.shape[1]
    begin = (wide * NARROW_PIECES + narrow) * room
    parts = []
    for k in range(3):
        block = jnp.minimum(begin // 128 + k, 47)
        parts.append(sums_row(bias_at + (block % 3) * 16 + block // 3))
    parts = jnp.broadcast_to(jnp.concatenate(parts, 1), (8, D))
    bias_grad[...] = pltpu.roll(parts, (D - begin % 128) % D, 1)[0:1, :room]
    for number, (begin, end) in enumerate(cuts):
        mats_col_new[:, begin:end] = decay * mats_col[:, begin:end] + (1.0 - decay) * (
            sums_row(mats_at + number, end - begin) / D
        )

    squares = jnp.zeros((1, 128), full)
    for k in range(5):
        begin, end = bounds[k], bounds[k + 1]
        step = factored(
            mats_grad[:, begin:end],
            turn_line(mats_row_new[k : k + 1, :]),
            mats_col_new[:, begin:end],
            pick(line, k) / D,
        )
        squares = squares + spread(total(step * step), k)
    last = range(5, len(widths))
    step_last = factored(
        mats_grad[:, start_last:],
        by_piece([turn_line(mats_row_new[k : k + 1, :]) for k in last], start_last, width_last),
        mats_col_new[:, start_last:],
        by_piece([pick(line, k) / D for k in last], start_last, width_last),
    )
    for k in last:
        inside = (last_lane >= bounds[k]) & (last_lane < bounds[k + 1])
        squares = squares + spread(total(jnp.where(inside, step_last * step_last, 0.0)), k)

    def step_up(e, squares):
        cols = jnp.concatenate([sums_row(24 * k + e) for k in range(FF // 128)], 1)
        new = decay * up_col[pl.ds(e, 1), :] + (1.0 - decay) * (cols / D)
        up_col_new[pl.ds(e, 1), :] = new
        row = turn_line(up_row_new[pl.ds(e, 1), :])
        step = factored(joined(rows_ref[e]), row, new, pick(line, 10 + e) / D)
        return squares + spread(total(step * step), 10 + e)

    def step_down(e, squares):
        cols = jnp.concatenate([sums_row(24 * (12 + k) + e) for k in range(D // 128)], 1)
        new = decay * down_col[pl.ds(e, 1), :] + (1.0 - decay) * (cols / FF)
        down_col_new[pl.ds(e, 1), :] = new
        row = turn_line(down_row_new[pl.ds(e, 1), :])
        step = factored(sums_ref[e], row, new, pick(line, 28 + e) / FF)
        return squares + spread(total(step * step), 28 + e)

    squares = lax.fori_loop(0, EXPERTS + SHARED, step_up, squares, unroll=True)
    squares = lax.fori_loop(0, EXPERTS + SHARED, step_down, squares, unroll=True)
    state = decay * bias_state[...] + (1.0 - decay) * (
        bias_grad[...] * bias_grad[...] + eps_fact
    )
    bias_state_new[...] = state
    bias_step = bias_grad[...] * lax.rsqrt(state)
    squares = squares + spread(total(bias_step * bias_step), 46)
    squares_plane[spot] = jnp.broadcast_to(squares, (8, 128))
    exchange(
        [
            remote(squares_plane.at[spot], squares_plane.at[spot], 4, k, plane_device(k))
            for k in range(1, 8)
        ]
    )
    squares_level[z] = jnp.sum(squares_plane[...], 0)
    exchange(
        [
            remote(squares_level.at[z], squares_level.at[z], 5, k, level_device(k))
            for k in range(1, 4)
        ]
    )
    squares_out[...] = jnp.sum(squares_level[...], 0)[0:1]


def settle_kernel(
    total_tokens,
    sums_ref,
    rows_ref,
    up_ref,
    down_ref,
    mats_ref,
    bias_ref,
    mats_grad,
    mats_row,
    mats_col,
    up_row,
    up_col,
    down_row,
    down_col,
    bias_grad,
    bias_state,
    line_ref,
    squares_ref,
    loss_out,
    mats_grad_out,
    mats_new,
    mats_copy,
    mats_row_out,
    mats_col_out,
    up_grad,
    up_new,
    up_copy,
    up_row_out,
    up_col_out,
    down_grad,
    down_new,
    down_copy,
    down_row_out,
    down_col_out,
    bias_grad_out,
    bias_new,
    bias_copy,
    bias_state_out,
):
    line, squares = line_ref[...], squares_ref[...]
    low = jnp.bfloat16
    group = up_ref.shape[0]

    def clipped(place, entries):
        rms = jnp.sqrt(pick(squares, place) / entries)
        return jnp.maximum(1.0, rms / clip_level)

    def settle(new_ref, copy_ref, index, master, step, limit):
        value = master - learn_rate * (step / limit)
        new_ref[index] = value
        copy_ref[index] = value.astype(low)

    for i in range(group):
        e = pl.program_id(0) * group + i
        grad = joined(rows_ref[i])
        up_grad[i] = grad
        step = factored(
            grad,
            turn_line(up_row[pl.ds(e, 1), :]),
            up_col[pl.ds(e, 1), :],
            pick(line, 10 + e) / D,
        )
        settle(up_new, up_copy, i, up_ref[i], step, clipped(10 + e, D * FF))
        grad = sums_ref[i]
        down_grad[i] = grad
        step = factored(
            grad,
            turn_line(down_row[pl.ds(e, 1), :]),
            down_col[pl.ds(e, 1), :],
            pick(line, 28 + e) / FF,
        )
        settle(down_new, down_copy, i, down_ref[i], step, clipped(28 + e, D * FF))

    @pl.when(pl.program_id(0) == 0)
    def _():
        widths = column_widths()
        bounds = [sum(widths[:k]) for k in range(len(widths) + 1)]
        start_last = bounds[5]
        width_last = bounds[-1] - start_last
        loss_out[...] = pick(line, 46) / total_tokens
        for given, out in (
            (mats_grad, mats_grad_out),
            (mats_row, mats_row_out),
            (mats_col, mats_col_out),
            (up_row, up_row_out),
            (up_col, up_col_out),
            (down_row, down_row_out),
            (down_col, down_col_out),
            (bias_grad, bias_grad_out),
            (bias_state, bias_state_out),
        ):
            out[...] = given[...]
        for k in range(6):
            if k < 5:
                index = (slice(None), slice(bounds[k], bounds[k + 1]))
                row, mean = turn_line(mats_row[k : k + 1, :]), pick(line, k) / D
                limit = clipped(k, D * widths[k])
            else:
                last = range(5, len(widths))
                index = (slice(None), slice(start_last, None))
                row, mean, limit = [
                    by_piece(values, start_last, width_last)
                    for values in (
                        [turn_line(mats_row[j : j + 1, :]) for j in last],
                        [pick(line, j) / D for j in last],
                        [clipped(j, D * widths[j]) for j in last],
                    )
                ]
            step = factored(mats_grad[index], row, mats_col[index], mean)
            settle(mats_new, mats_copy, index, mats_ref[index], step, limit)
        index = (slice(None), slice(None))
        step = bias_grad[...] * lax.rsqrt(bias_state[...])
        settle(bias_new, bias_copy, index, bias_ref[...], step, clipped(46, 15 * D))


def update_kernel_call(sums, rows, lat, bias_sum, masters, factors, loss_part, total_tokens):
    mats, up_weights, down_weights, biases = masters
    mats_row, mats_col, up_row, up_col, down_row, down_col, bias_state = factors
    full, low = jnp.float32, jnp.bfloat16
    mats_col, bias_state, biases = [
        member.reshape(1, -1) for member in (mats_col, bias_state, biases)
    ]

    def like(member, kind=full):
        return jax.ShapeDtypeStruct(member.shape, kind)

    row = jax.ShapeDtypeStruct((1, 128), full)
    rows_like = [mats_row, mats_col, up_row, up_col, down_row, down_col, bias_state, bias_state]
    vmem = pl.BlockSpec(memory_space=pltpu.VMEM)
    dma = pltpu.SemaphoreType.DMA
    found = pl.pallas_call(
        update_kernel,
        out_shape=[like(member) for member in [mats] + rows_like] + [row, row],
        in_specs=[vmem] * 12,
        out_specs=[vmem] * 11,
        scratch_shapes=[
            pltpu.VMEM((512, 128), full),
            pltpu.VMEM((8, 64, 128), full),
            pltpu.VMEM((4, 4, 16, 128), full),
            pltpu.VMEM((8, 4, 16, 128), full),
            pltpu.VMEM((8, 8, 128), full),
            pltpu.VMEM((4, 8, 128), full),
            dma((2, 6, 8)),
        ],
        compiler_params=pltpu.CompilerParams(
            collective_id=1, has_side_effects=True, vmem_limit_bytes=VMEM_ROOM
        ),
        name="update",
    )(
        sums,
        rows,
        lat,
        bias_sum,
        loss_part.reshape(1, 1),
        mats_row,
        mats_col,
        up_row,
        up_col,
        down_row,
        down_col,
        bias_state,
    )
    group = 3
    wholes = [biases] + list(found)

    def whole(member):
        return pl.BlockSpec(member.shape, lambda g: (0,) * len(member.shape))

    def parts(member):
        rest = member.shape[1:]
        return pl.BlockSpec((group,) + rest, lambda g: (g,) + (0,) * len(rest))

    one = jax.ShapeDtypeStruct((1, 1), full)
    outs = (
        [(one, whole(one))]
        + [(like(mats, kind), whole(mats)) for kind in (full, full, low)]
        + [(like(member), whole(member)) for member in (mats_row, mats_col)]
        + [(like(up_weights, kind), parts(up_weights)) for kind in (full, full, low)]
        + [(like(member), whole(member)) for member in (up_row, up_col)]
        + [(like(down_weights, kind), parts(down_weights)) for kind in (full, full, low)]
        + [(like(member), whole(member)) for member in (down_row, down_col)]
        + [(like(biases, kind), whole(biases)) for kind in (full, full, low, full)]
    )
    outs = list(
        pl.pallas_call(
            functools.partial(settle_kernel, total_tokens),
            grid=(up_weights.shape[0] // group,),
            in_specs=[parts(member) for member in (sums, rows, up_weights, down_weights)]
            + [whole(member) for member in [mats] + wholes],
            out_shape=[shape for shape, spec in outs],
            out_specs=[spec for shape, spec in outs],
            compiler_params=pltpu.CompilerParams(vmem_limit_bytes=VMEM_ROOM),
            name="finish",
        )(sums, rows, up_weights, down_weights, mats, *wholes)
    )
    outs[0] = outs[0][0, 0]
    for at in (5, 16, 17, 18, 19):
        outs[at] = outs[at].reshape(-1)
    return tuple(outs)


def gather_kernel(
    mats_in,
    bias_in,
    down_in,
    up_in,
    patches,
    places,
    freq_low,
    label_hot,
    mats_far,
    bias_out,
    down_out,
    up_out,
    mods_out,
    fin_out,
    time_out,
    cond_out,
    head_out,
    qkv_out_far,
    att_out_far,
    middle_out_far,
    moe_out_far,
    logits_out_far,
    shared_out_far,
    mats_got,
    mats_own,
    up_got,
    up_wide,
    up_own,
    embedded,
    down_here,
    up_here,
    near_send,
    near_recv,
    own_sem,
    level_send,
    level_recv,
    one_send,
    one_recv,
    two_send,
    two_recv,
    core_send,
    core_recv,
    bias_send,
    bias_recv,
    here_sem,
    mats_sem,
    mats_out,
    qkv_out,
    att_out,
    middle_out,
    moe_out,
    logits_out,
    shared_out,
):
    leaves = [
        pltpu.make_async_copy(near, far, mats_sem.at[number])
        for number, (near, far) in enumerate(
            (
                (mats_out, mats_far),
                (qkv_out, qkv_out_far),
                (att_out, att_out_far),
                (middle_out, middle_out_far),
                (moe_out, moe_out_far),
                (logits_out, logits_out_far),
                (shared_out, shared_out_far),
            )
        )
    ]
    n_down, n_up = down_in.shape[0], up_own.shape[0]
    lead, n_mats = 3, mats_out.shape[4]
    after_mats = lead + n_mats
    first_up = n_down + n_mats
    slabs = first_up + n_up
    wide, narrow = lax.axis_index(WIDE), lax.axis_index(NARROW)
    z, x = wide // 2, wide % 2
    y, c = narrow // 2, narrow % 2
    mates = [
        (wide, (y + (k // 2) * (1 - 2 * y)) * 2 + c + (k % 2) * (1 - 2 * c)) for k in range(1, 4)
    ]
    levels = [(((z + k) % 4) * 2 + x, narrow) for k in range(1, 4)]
    to_x = (z * 2 + 1 - x, narrow)
    to_core, to_y = mates[0], mates[1]
    to_one = (z * 2 + x + (1 - c) * (1 - 2 * x), (y + c * (1 - 2 * y)) * 2 + c)
    to_two = (z * 2 + x + c * (1 - 2 * x), (y + (1 - c) * (1 - 2 * y)) * 2 + c)
    barrier = pltpu.get_barrier_semaphore()
    for target in mates + levels + [to_x]:
        pl.semaphore_signal(barrier, inc=1, device_id=target, device_id_type=MESH_ID)
    pl.semaphore_wait(barrier, 7)

    def remote(source, target, send, recv, device):
        return pltpu.make_async_remote_copy(
            src_ref=source,
            dst_ref=target,
            send_sem=send,
            recv_sem=recv,
            device_id=device,
            device_id_type=MESH_ID,
        )

    def near_mats(k):
        return remote(
            mats_in.at[mates[k - 1][1]],
            mats_got.at[narrow],
            near_send.at[0, k],
            near_recv.at[0, k],
            mates[k - 1],
        )

    def near_up(k):
        return remote(
            up_in.at[mates[k - 1][1]],
            up_got.at[narrow],
            near_send.at[1, k],
            near_recv.at[1, k],
            mates[k - 1],
        )

    own_mats = pltpu.make_async_copy(mats_in.at[narrow], mats_got.at[narrow], own_sem.at[0])
    own_up = pltpu.make_async_copy(up_in.at[narrow], up_got.at[narrow], own_sem.at[1])
    own_bias = pltpu.make_async_copy(bias_in, bias_out.at[z, x, y, c], own_sem.at[2])
    own_mats.start()
    own_up.start()
    own_bias.start()
    for k in range(1, 4):
        near_mats(k).start()

    def bias_level(k):
        return remote(
            bias_in, bias_out.at[z, x, y, c], bias_send.at[k - 1], bias_recv.at[k - 1], levels[k - 1]
        )

    def bias_x():
        part = bias_out.at[:, x, y, c]
        return remote(part, part, bias_send.at[3], bias_recv.at[3], to_x)

    def bias_y():
        part = bias_out.at[:, :, y, c]
        return remote(part, part, bias_send.at[4], bias_recv.at[4], to_y)

    def bias_core():
        part = bias_out.at[:, :, :, c]
        return remote(part, part, bias_send.at[5], bias_recv.at[5], to_core)

    for k in range(1, 4):
        bias_level(k).start()
    for k in range(1, 4):
        near_up(k).start()

    def mats_ready():
        own_mats.wait()
        for k in range(1, 4):
            near_mats(k).wait_recv()
        for n in range(NARROW_PIECES):
            mats_own[n * ROWS : (n + 1) * ROWS] = mats_got[n].astype(jnp.float32)[:ROWS]
        for n in range(n_mats):
            mats_got[n, :, :] = mats_own[16 * n : 16 * (n + 1)].astype(jnp.bfloat16)

    own_bias.wait()

    def turn(number):
        return (number + EXPERTS) % n_up

    def down_at(s):
        return turn(jnp.where(s < lead, s, s - n_mats))

    def source(kind, s):
        if kind == 0:
            return mats_got.at[s - lead]
        if kind == 1:
            return down_in.at[down_at(s)]
        return up_own.at[turn(s - first_up)]

    def piece(kind, s, at):
        z_at, x_at, y_at, c_at = at
        if kind == 0:
            return mats_out.at[y_at, c_at, z_at, x_at, s - lead]
        if kind == 1:
            return down_out.at[down_at(s), z_at, x_at, y_at, c_at]
        return up_out.at[turn(s - first_up), y_at, c_at, z_at, x_at]

    every = slice(None)

    def own_copy(kind, s):
        return pltpu.make_async_copy(
            source(kind, s), piece(kind, s, (z, x, y, c)), own_sem.at[3 + s % 4]
        )

    def level_copy(kind, s, k, turned=False, first=0):
        if turned:
            part = piece(kind, s, (z, x, every, c) if first == 0 else (z, every, y, c))
            start = part
        else:
            part = piece(kind, s, (z, x, y, c))
            start = source(kind, s)
        return remote(
            start, part, level_send.at[s % 12, k - 1], level_recv.at[s, k - 1], levels[k - 1]
        )

    def both_parts(kind, s, first):
        return piece(kind, s, (every, x, every, c) if first else (every, every, y, c))

    def one_copy(kind, s, turned=False, first=0):
        part = both_parts(kind, s, 1 - first) if turned else piece(kind, s, (every, x, y, c))
        return remote(part, part, one_send.at[s % 12], one_recv.at[s], to_one)

    def two_copy(kind, s, turned=False, first=0):
        if turned:
            part, start = piece(kind, s, (z, x, y, c)), source(kind, s)
        else:
            part = both_parts(kind, s, first)
            start = part
        return remote(start, part, two_send.at[s % 12], two_recv.at[s], to_two)

    def core_copy(kind, s):
        part = piece(kind, s, (every, every, every, c))
        return remote(part, part, core_send.at[s % 12], core_recv.at[s], to_core)

    def by_order(kind, s, run):
        if kind == 0:
            run(False)
            return
        turned = (s % 5 == 1) | (s % 5 == 3)

        @pl.when(turned)
        def _():
            run(True)

        @pl.when(jnp.logical_not(turned))
        def _():
            run(False)

    def by_core(run):
        for first in range(2):

            @pl.when(c == first)
            def _():
                run(first)

    def stage_level(kind, s):
        own_copy(kind, s).start()

        def run(turned):
            if turned:
                two_copy(kind, s, True).start()
            else:
                for k in range(1, 4):
                    level_copy(kind, s, k).start()

        by_order(kind, s, run)

    def stage_one(kind, s):
        own_copy(kind, s).wait()

        def run(turned):
            if turned:
                two_copy(kind, s, True).wait_recv()

                def send(first):
                    for k in range(1, 4):
                        level_copy(kind, s, k, True, first).start()

                by_core(send)
            else:
                for k in range(1, 4):
                    level_copy(kind, s, k).wait_recv()
                one_copy(kind, s).start()

        by_order(kind, s, run)

    def stage_two(kind, s):
        def run(turned):
            if turned:
                for k in range(1, 4):
                    level_copy(kind, s, k, True).wait_recv()
                by_core(lambda first: one_copy(kind, s, True, first).start())
            else:
                one_copy(kind, s).wait_recv()
                by_core(lambda first: two_copy(kind, s, False, first).start())

        by_order(kind, s, run)

    def stage_core(kind, s):
        def run(turned):
            if turned:
                one_copy(kind, s, True).wait_recv()
            else:
                two_copy(kind, s).wait_recv()

        by_order(kind, s, run)
        core_copy(kind, s).start()

    def stage_last(kind, s):
        core_copy(kind, s).wait_recv()

    def stage_sent(kind, s):
        def run(turned):
            for k in range(1, 4):
                level_copy(kind, s, k, turned).wait_send()
            one_copy(kind, s, turned).wait_send()
            two_copy(kind, s, turned).wait_send()

        by_order(kind, s, run)
        core_copy(kind, s).wait_send()

    stages = (
        (stage_sent, 12),
        (stage_level, 0),
        (stage_one, 3),
        (stage_two, 6),
        (stage_core, 9),
        (stage_last, 12),
    )

    lats = patches.shape[0] // PATCHES
    ready, shared_at = after_mats + 12, first_up + SHARED + 12
    low, full = jnp.bfloat16, jnp.float32

    def matrix(number, begin, end):
        chunk = mats_out[number // 2, number % 2]
        return chunk.reshape(D, chunk.shape[-1])[:, begin:end]

    def bias_rows():
        return jnp.sum(bias_out[...].astype(full).reshape(-1, 16, D), 0)

    def wide_row(rows, begin, end):
        return jnp.concatenate([rows[k : k + 1] for k in range(begin, end)], 1)

    def conditions():
        rows = bias_rows()
        pre_time = contract(freq_low[...], matrix(3, 1408, 1664), 1, 1) + rows[11:12]
        hid_time = jax.nn.silu(pre_time).astype(low)
        cond = (
            product(hid_time, matrix(3, 1024, 1408))
            + rows[12:13]
            + contract(label_hot[...], matrix(3, 0, 1024), 1, 1)
        )
        act = jax.nn.silu(cond).astype(low)
        time_out[...] = pre_time
        cond_out[...] = cond
        head_out[...] = matrix(1, 4 * D, 4 * D + 128)
        mods_out[:, : 4 * D] = product(act, matrix(1, 0, 4 * D)) + wide_row(rows, 4, 8)
        mods_out[:, 4 * D :] = product(act, matrix(2, 0, 2 * D)) + wide_row(rows, 8, 10)
        fin_out[...] = product(act, matrix(2, 2 * D, 4 * D)) + wide_row(rows, 13, 15)

    def mod_row(start, number):
        return mods_out[pl.ds(start // PATCHES, 1), number * D : (number + 1) * D]

    def attention_in(start):
        rows = bias_rows()
        span = pl.ds(start, PATCHES)
        emb = contract(patches[span, :], matrix(2, 4 * D, 4 * D + 128), 1, 1)
        emb = emb + rows[10:11] + places[...]
        embedded[...] = emb
        normed, unused_std = layer_norm(emb)
        attn_in = (normed * (1.0 + mod_row(start, 1)) + mod_row(start, 0)).astype(low)
        qkv_out[span, :] = (
            product(attn_in, matrix(0, 0, 3 * D)) + wide_row(rows, 0, 3)
        ).astype(low)

    def attention_heads(start):
        span = pl.ds(start, PATCHES)
        lane = lax.broadcasted_iota(jnp.int32, (PATCHES, 2 * HD), 1)
        for pair in range(HEADS // 2):
            at = pair * 2 * HD
            queries = qkv_out[span, at : at + 2 * HD]
            keys = qkv_out[span, D + at : D + at + 2 * HD]
            values = qkv_out[span, 2 * D + at : 2 * D + at + 2 * HD]
            halves = []
            for half in range(2):
                mine = (lane < HD) if half == 0 else (lane >= HD)
                scores = contract(jnp.where(mine, queries, 0), keys, 1, 1) * HD ** (-0.5)
                powers = jnp.exp(scores - jnp.max(scores, 1, keepdims=True))
                probs = (powers / jnp.sum(powers, 1, keepdims=True)).astype(low)
                halves.append(product(probs, values))
            att_out[span, at : at + 2 * HD] = jnp.where(lane < HD, halves[0], halves[1]).astype(low)

    def attention_out(start):
        rows = bias_rows()
        span = pl.ds(start, PATCHES)
        attn = product(att_out[span, :], matrix(0, 3 * D, 4 * D)) + rows[3:4]
        middle = embedded[...] + mod_row(start, 2) * attn
        middle_out[span, :] = middle
        normed, unused_std = layer_norm(middle)
        moe_in = (normed * (1.0 + mod_row(start, 4)) + mod_row(start, 3)).astype(low)
        moe_out[span, :] = moe_in
        logits_out[span, :] = product(moe_in, matrix(0, 4 * D, 4 * D + 128))

    def fetch(shared_id):
        e = EXPERTS + shared_id
        first = pltpu.make_async_copy(down_out.at[e], down_here, here_sem.at[0])
        second = pltpu.make_async_copy(up_out.at[e], up_here, here_sem.at[1])
        first.start()
        second.start()
        first.wait()
        second.wait()

    def shared_block(shared_id, start):
        span = pl.ds(start, PATCHES)
        rows = moe_out[span, :]
        chunks = [up_here[n // 2, n % 2].reshape(D, D) for n in range(NARROW_PIECES)]
        down = down_here[...].reshape(FF, D)
        total = None
        for cut in range(0, FF, CUT):
            pre_act = product(rows, up_columns(chunks, cut))
            part = product(gelu_only(pre_act).astype(low), down[cut : cut + CUT])
            total = part if total is None else total + part
        if shared_id == 0:
            shared_out[span, :] = total
        else:
            shared_out[span, :] += total

    def tick(t, unused):
        @pl.when(t == 1)
        def _():
            for k in range(1, 4):
                bias_level(k).wait_recv()
            bias_x().start()

        @pl.when(t == 2)
        def _():
            bias_x().wait_recv()
            bias_y().start()

        @pl.when(t == 3)
        def _():
            bias_y().wait_recv()
            bias_core().start()

        @pl.when(t == 6)
        def _():
            own_up.wait()
            for k in range(1, 4):
                near_up(k).wait_recv()
            for n in range(NARROW_PIECES):
                up_wide[n] = up_got[n].astype(jnp.float32)

            for e in range(n_up):
                up_own[e] = jnp.concatenate(
                    [up_wide[n, e * ROWS : (e + 1) * ROWS] for n in range(NARROW_PIECES)], 0
                ).astype(jnp.bfloat16)

        @pl.when(t == 2)
        def _():
            mats_ready()

        for stage, lag in stages:
            s = t - lag

            @pl.when((s >= lead) & (s < after_mats))
            def _():
                stage(0, jnp.clip(s, lead, after_mats - 1))

            @pl.when(((s >= 0) & (s < lead)) | ((s >= after_mats) & (s < first_up)))
            def _():
                stage(1, jnp.clip(s, 0, first_up - 1))

            @pl.when((s >= first_up) & (s < slabs))
            def _():
                stage(2, jnp.clip(s, first_up, slabs - 1))

        @pl.when(t == ready)
        def _():
            bias_core().wait_recv()
            conditions()

        for number, unit in enumerate((attention_in, attention_heads, attention_out)):

            @pl.when((t > ready) & (t <= ready + 3 * lats) & ((t - ready - 1) % 3 == number))
            def _():
                unit(pl.multiple_of(jnp.clip((t - ready - 1) // 3, 0, lats - 1) * PATCHES, PATCHES))

        @pl.when(t == ready + 3 * lats + 1)
        def _():
            for leave in leaves[:-1]:
                leave.start()

        for shared_id in range(SHARED):
            begin = shared_at + shared_id * lats

            @pl.when(t == begin)
            def _():
                fetch(shared_id)

            @pl.when((t >= begin) & (t < begin + lats))
            def _():
                shared_block(
                    shared_id, pl.multiple_of(jnp.clip(t - begin, 0, lats - 1) * PATCHES, PATCHES)
                )

        @pl.when(t == shared_at + SHARED * lats)
        def _():
            leaves[-1].start()

        return unused

    lax.fori_loop(0, slabs + 12, tick, 0)
    for leave in leaves:
        leave.wait()
    for k in range(1, 4):
        near_mats(k).wait_send()
        near_up(k).wait_send()
        bias_level(k).wait_send()
    bias_x().wait_send()
    bias_y().wait_send()
    bias_core().wait_send()


def gather_weights(
    mats, up_weights, down_weights, biases, patches, places, freq_low, label_hot
):
    low = jnp.bfloat16
    owner = lax.axis_index(AXES)
    m = mats.astype(low)
    rows = m.shape[0]

    thin = 13 * D

    def thin_part(at):
        return jnp.pad(m[:, at : at + 16], ((0, 0), (0, 112)))

    mats_in = jnp.stack(
        [
            jnp.concatenate([m[:, : 4 * D], thin_part(thin)], 1),
            jnp.concatenate([m[:, 4 * D : 8 * D], thin_part(thin + 16)], 1),
            jnp.concatenate(
                [m[:, 8 * D : 10 * D], m[:, 11 * D : 13 * D], thin_part(thin + 32)], 1
            ),
            jnp.concatenate(
                [
                    m[:, thin + 48 + FREQ :],
                    jnp.zeros((rows, 24), low),
                    m[:, 10 * D : 11 * D],
                    m[:, thin + 48 : thin + 48 + FREQ],
                ],
                1,
            ),
        ],
        0,
    )
    mats_in = jnp.pad(mats_in, ((0, 0), (0, 16 - rows), (0, 0)))
    line = lax.dynamic_update_slice(
        jnp.zeros((16 * D,), low), biases.astype(low), (owner * biases.shape[0],)
    )
    n_up = up_weights.shape[0]
    up_in = (
        up_weights.astype(low)
        .reshape(n_up, rows, NARROW_PIECES, D)
        .transpose(2, 0, 1, 3)
        .reshape(NARROW_PIECES, n_up * rows, D)
    )
    room = (n_up * rows + 15) // 16 * 16
    up_in = jnp.pad(up_in, ((0, 0), (0, room - n_up * rows), (0, 0)))
    slabs = 3 + 2 * n_up
    spread = mats_in.shape[2]
    dma = pltpu.SemaphoreType.DMA
    anywhere = pl.BlockSpec(memory_space=pl.ANY)
    tokens = patches.shape[0]
    full, vmem = jnp.float32, pl.BlockSpec(memory_space=pltpu.VMEM)
    outs = pl.pallas_call(
        gather_kernel,
        out_shape=[
            jax.ShapeDtypeStruct((2, 2, 4, 2, 3, 16, spread), low),
            jax.ShapeDtypeStruct((4, 2, 2, 2, 16, D), low),
            jax.ShapeDtypeStruct((n_up, 4, 2, 2, 2, PIECE, D), low),
            jax.ShapeDtypeStruct((n_up, 2, 2, 4, 2, PIECE, D), low),
            jax.ShapeDtypeStruct((8, 6 * D), full),
            jax.ShapeDtypeStruct((8, 2 * D), full),
            jax.ShapeDtypeStruct((8, D), full),
            jax.ShapeDtypeStruct((8, D), full),
            jax.ShapeDtypeStruct((D, 128), low),
            jax.ShapeDtypeStruct((tokens, 3 * D), low),
            jax.ShapeDtypeStruct((tokens, D), low),
            jax.ShapeDtypeStruct((tokens, D), full),
            jax.ShapeDtypeStruct((tokens, D), low),
            jax.ShapeDtypeStruct((tokens, 128), full),
            jax.ShapeDtypeStruct((tokens, D), full),
        ],
        in_specs=[anywhere] * 4 + [vmem] * 4,
        out_specs=[anywhere, vmem] + [anywhere] * 2 + [vmem] * 5 + [anywhere] * 6,
        scratch_shapes=[
            pltpu.VMEM((NARROW_PIECES, 16, spread), low),
            pltpu.VMEM((PIECE, spread), jnp.float32),
            pltpu.VMEM((NARROW_PIECES, room, D), low),
            pltpu.VMEM((NARROW_PIECES, room, D), jnp.float32),
            pltpu.VMEM((n_up, PIECE, D), low),
            pltpu.VMEM((PATCHES, D), full),
            pltpu.VMEM((4, 2, 2, 2, PIECE, D), low),
            pltpu.VMEM((2, 2, 4, 2, PIECE, D), low),
            dma((2, 4)),
            dma((2, 4)),
            dma((7,)),
            dma((12, 3)),
            dma((slabs, 3)),
            dma((12,)),
            dma((slabs,)),
            dma((12,)),
            dma((slabs,)),
            dma((12,)),
            dma((slabs,)),
            dma((6,)),
            dma((6,)),
            dma((2,)),
            dma((7,)),
            pltpu.VMEM((2, 2, 4, 2, 3, 16, spread), low),
            pltpu.VMEM((tokens, 3 * D), low),
            pltpu.VMEM((tokens, D), low),
            pltpu.VMEM((tokens, D), full),
            pltpu.VMEM((tokens, D), low),
            pltpu.VMEM((tokens, 128), full),
            pltpu.VMEM((tokens, D), full),
        ],
        compiler_params=pltpu.CompilerParams(
            collective_id=2, has_side_effects=True, vmem_limit_bytes=VMEM_ROOM
        ),
        name="gather_weights",
    )(
        mats_in,
        line.reshape(16, D),
        down_weights.astype(low),
        up_in,
        patches,
        places,
        freq_low,
        label_hot,
    )
    return outs


def split_weights(weights):
    mats_full, up_full, down_full, bias_full = weights
    matrices = cut_pieces(mats_full, column_widths(), 1)
    vectors = [member.astype(jnp.float32) for member in cut_pieces(bias_full, bias_widths(), 0)]
    up_full = up_full.reshape(-1, D, NARROW_PIECES, D).transpose(0, 2, 1, 3)
    return (matrices, vectors, up_full, down_full)


def forward(weights, latents, noise, timesteps, labels, routes):
    matrices, vectors, up_full, down_full = weights
    w_qkv, w_proj, w_mod, w_time2, w_final, w_router, w_head, w_patch, w_time1, w_table = matrices
    b_qkv, b_proj, b_mod, b_patch, b_time1, b_time2, b_final = vectors
    num_latents = latents.shape[0]
    rows_here = num_latents * PATCHES
    steps_f = timesteps.astype(jnp.float32)
    signal, spread = noise_level(steps_f)
    noisy = signal[:, None] * latents + spread[:, None] * noise
    patches = noisy.reshape(rows_here, PD).astype(jnp.bfloat16)
    embedded = (
        contract(patches, w_patch, 1, 1).reshape(num_latents, PATCHES, D)
        + b_patch
        + positions()[None]
    )
    freq_low = time_features(steps_f).astype(jnp.bfloat16)
    pre_time = contract(freq_low, w_time1, 1, 1) + b_time1
    hid_time = jax.nn.silu(pre_time).astype(jnp.bfloat16)
    label_hot = (labels[:, None] == jnp.arange(CLASSES, dtype=jnp.int32)[None, :]).astype(
        jnp.float32
    )
    label_emb = lax.dot_general(
        label_hot,
        w_table.astype(jnp.float32),
        (((1,), (1,)), ((), ())),
        precision=lax.Precision.HIGHEST,
        preferred_element_type=jnp.float32,
    )
    cond = product(hid_time, w_time2) + b_time2 + label_emb
    cond_act = jax.nn.silu(cond).astype(jnp.bfloat16)
    modulation = product(cond_act, w_mod) + b_mod
    final_mod = product(cond_act, w_final) + b_final
    shift_attn, scale_attn, gate_attn, shift_moe, scale_moe, gate_moe = [
        member[:, None, :] for member in jnp.split(modulation, 6, 1)
    ]
    shift_fin, scale_fin = [member[:, None, :] for member in jnp.split(final_mod, 2, 1)]
    normed_one, inv_one = layer_norm(embedded)
    attn_in = (
        (normed_one * (1.0 + scale_attn) + shift_attn).astype(jnp.bfloat16).reshape(rows_here, D)
    )
    qkv_out = (
        (product(attn_in, w_qkv) + b_qkv)
        .astype(jnp.bfloat16)
        .reshape(num_latents, PATCHES, 3, HEADS, HD)
    )
    scores = jnp.einsum(
        LQK, qkv_out[:, :, 0], qkv_out[:, :, 1], preferred_element_type=jnp.float32
    ) * HD ** (-0.5)
    log_totals = jax.nn.logsumexp(scores, -1)
    probs_low = jax.nn.softmax(scores, -1).astype(jnp.bfloat16)
    attended = (
        jnp.einsum(
            "lhqk,lkhd->lqhd", probs_low, qkv_out[:, :, 2], preferred_element_type=jnp.float32
        )
        .astype(jnp.bfloat16)
        .reshape(rows_here, D)
    )
    attn_out = (product(attended, w_proj) + b_proj).reshape(num_latents, PATCHES, D)
    middle = embedded + gate_attn * attn_out
    normed_two, inv_two = layer_norm(middle)
    moe_in = (normed_two * (1.0 + scale_moe) + shift_moe).astype(jnp.bfloat16).reshape(rows_here, D)
    logits = product(moe_in, w_router)
    route_hot = (routes[:, :, None] == jnp.arange(EXPERTS, dtype=jnp.int32)[None, None, :]).astype(
        jnp.float32
    )
    gate_vals = jax.nn.softmax(jnp.sum(route_hot * logits[:, None, :], 2), -1)
    slot_of, slot_meta = pack_slots(routes)
    routed, slot_rows = experts_forward(slot_of, slot_meta, moe_in, up_full, down_full)
    moe_out = gate_vals[:, 0:1] * routed[0] + gate_vals[:, 1:2] * routed[1]
    for shared_id in range(EXPERTS, EXPERTS + SHARED):
        for cut in range(0, FF, CUT):
            pre_act = product(moe_in, up_columns(up_full[shared_id], cut))
            activated = gelu_only(pre_act).astype(jnp.bfloat16)
            moe_out = moe_out + product(activated, down_full[shared_id, cut : cut + CUT])
    moe_out = moe_out.reshape(num_latents, PATCHES, D)
    final_state = middle + gate_moe * moe_out
    normed_fin, inv_fin = layer_norm(final_state)
    head_in = (
        (normed_fin * (1.0 + scale_fin) + shift_fin).astype(jnp.bfloat16).reshape(rows_here, D)
    )
    errors = product(head_in, w_head) - noise.reshape(rows_here, PD)
    return SimpleNamespace(
        patches=patches,
        freq_low=freq_low,
        pre_time=pre_time,
        hid_time=hid_time,
        label_hot=label_hot,
        cond=cond,
        cond_act=cond_act,
        scale_attn=scale_attn,
        gate_attn=gate_attn,
        scale_moe=scale_moe,
        gate_moe=gate_moe,
        scale_fin=scale_fin,
        normed_one=normed_one,
        inv_one=inv_one,
        attn_in=attn_in,
        qkv_out=qkv_out,
        log_totals=log_totals,
        attended=attended,
        attn_out=attn_out,
        normed_two=normed_two,
        inv_two=inv_two,
        moe_in=moe_in,
        route_hot=route_hot,
        gate_vals=gate_vals,
        slot_of=slot_of,
        slot_meta=slot_meta,
        slot_rows=slot_rows,
        routed=routed,
        moe_out=moe_out,
        normed_fin=normed_fin,
        inv_fin=inv_fin,
        head_in=head_in,
        errors=errors,
    )


def forward_fused(mats, up_weights, down_weights, biases, latents, noise, timesteps, labels):
    num_latents = latents.shape[0]
    rows_here = num_latents * PATCHES
    steps_f = timesteps.astype(jnp.float32)
    signal, spread = noise_level(steps_f)
    noisy = signal[:, None] * latents + spread[:, None] * noise
    patches = noisy.reshape(rows_here, PD).astype(jnp.bfloat16)
    freq_low = time_features(steps_f).astype(jnp.bfloat16)
    label_low = (labels[:, None] == jnp.arange(1024, dtype=jnp.int32)[None, :]).astype(jnp.bfloat16)
    less = ((0, 8 - num_latents), (0, 0))
    outs = gather_weights(
        mats,
        up_weights,
        down_weights,
        biases,
        jnp.pad(patches, ((0, 0), (0, 128 - PD))),
        positions(),
        jnp.pad(freq_low, less),
        jnp.pad(label_low, less),
    )
    n_up = outs[3].shape[0]
    return SimpleNamespace(
        patches=jnp.pad(patches, ((0, 0), (0, 128 - PD))),
        freq_low=jnp.pad(freq_low, less),
        mats_full=outs[0],
        bias_full=outs[1],
        down_full=outs[2].reshape(n_up, FF, D),
        up_full=outs[3].reshape(n_up, NARROW_PIECES, D, D),
        mods=outs[4],
        fin=outs[5],
        pre_time=outs[6],
        cond=outs[7],
        head=outs[8],
        qkv=outs[9],
        attended=outs[10],
        middle=outs[11],
        moe_in=outs[12],
        logits=outs[13],
        shared_out=outs[14],
    )


def backward_fused(fused, latents, noise, labels, routes, total_tokens):
    num_latents = latents.shape[0]
    rows_here = num_latents * PATCHES
    line = jnp.sum(fused.bias_full.reshape(-1, 16, D).astype(jnp.float32), 0)
    slot_of, slot_meta = pack_slots(routes)
    members = (
        fused.logits,
        routes,
        fused.shared_out,
        fused.middle,
        jnp.pad(noise.reshape(rows_here, PD), ((0, 0), (0, 128 - PD))),
        fused.mods,
        fused.fin,
        fused.head,
    )
    (
        grad_pair,
        grad_both,
        grad_state,
        grad_logits,
        thin,
        grad_gate,
        grad_fin,
        loss_part,
        slot_rows,
    ) = (
        experts_and_head(
            slot_of,
            slot_meta,
            fused.moe_in,
            fused.up_full,
            fused.down_full,
            2.0 / total_tokens,
            members,
        )
    )
    up_slabs, down_slabs, dx_routed = experts_backward(
        slot_of, slot_meta, slot_rows, grad_pair, fused.up_full, fused.down_full
    )
    label_parts = jnp.stack([labels // 32, labels % 32], 1).astype(jnp.bfloat16)
    members = (
        fused.moe_in,
        grad_both,
        dx_routed,
        grad_logits,
        fused.middle,
        fused.qkv,
        fused.attended,
        grad_state,
        fused.patches,
        positions(),
        fused.mods,
        fused.mats_full,
        line,
        fused.pre_time,
        fused.cond,
        fused.freq_low,
        grad_gate,
        grad_fin,
        thin,
        jnp.pad(label_parts, ((0, 8 - num_latents), (0, 126))),
    )
    return loss_part, reduce_slabs(
        slot_of, down_slabs, up_slabs, fused.up_full, fused.down_full, members
    )


def backward(weights, kept, total_tokens):
    matrices, vectors, up_full, down_full = weights
    w_qkv, w_proj, w_mod, w_time2, w_final, w_router, w_head, w_patch, w_time1, w_table = matrices
    num_latents = kept.normed_one.shape[0]
    rows_here = num_latents * PATCHES
    grad_head, grad_head_in, unused = linear_back(
        kept.errors * (2.0 / total_tokens), kept.head_in, w_head
    )
    grad_head_in = grad_head_in.reshape(num_latents, PATCHES, D)
    grad_final_mod = jnp.concatenate(
        [jnp.sum(grad_head_in, 1), jnp.sum(grad_head_in * kept.normed_fin, 1)], 1
    )
    grad_state = norm_back(
        grad_head_in * (1.0 + kept.scale_fin), kept.normed_fin, kept.inv_fin
    )
    grad_gate_moe = jnp.sum(kept.moe_out * grad_state, 1)
    grad_moe = (kept.gate_moe * grad_state).reshape(rows_here, D)
    grad_moe_low = grad_moe.astype(jnp.bfloat16)
    moe_in = kept.moe_in
    gate_vals = kept.gate_vals
    routed = kept.routed
    grad_gates = jnp.stack([jnp.sum(routed[k] * grad_moe, 1) for k in range(2)], 1)
    grad_pair = jnp.stack(
        [(gate_vals[:, k : k + 1] * grad_moe).astype(jnp.bfloat16) for k in range(2)], 0
    )
    up_slabs, down_slabs, dx_slots = experts_backward(
        kept.slot_of, kept.slot_meta, kept.slot_rows, grad_pair, up_full, down_full
    )
    place = jnp.arange(dx_slots.shape[0], dtype=jnp.int32)[None, :]
    used = place < jnp.max(kept.slot_meta[0] + kept.slot_meta[1])
    dx_slots = jnp.where(used.T, dx_slots, 0.0)
    slot_hot = [(kept.slot_of[k][:, None] == place).astype(jnp.float32) for k in range(2)]
    grad_moe_in = jnp.dot(slot_hot[0] + slot_hot[1], dx_slots, precision=lax.Precision.HIGHEST)
    up_all = [up_slabs.transpose(0, 1, 3, 2, 4).reshape(-1, D, FF)]
    down_all = [down_slabs.reshape(-1, FF, D)]
    for shared_id in range(EXPERTS, EXPERTS + SHARED):
        up_part = jnp.concatenate([up_full[shared_id, k] for k in range(NARROW_PIECES)], 1)
        activated, slope = gelu_slope(product(moe_in, up_part))
        grad_act = contract(grad_moe_low, down_full[shared_id], 1, 1)
        grad_pre = (grad_act * slope).astype(jnp.bfloat16)
        down_all.append(contract(activated.astype(jnp.bfloat16), grad_moe_low, 0, 0)[None])
        up_all.append(contract(moe_in, grad_pre, 0, 0)[None])
        grad_moe_in = grad_moe_in + contract(grad_pre, up_part, 1, 1)
    up_slabs = jnp.concatenate([member.astype(jnp.float32) for member in up_all], 0)
    down_slabs = jnp.concatenate([member.astype(jnp.float32) for member in down_all], 0)
    grad_picked = gate_vals * (grad_gates - jnp.sum(gate_vals * grad_gates, 1, keepdims=True))
    grad_logits = jnp.sum(kept.route_hot * grad_picked[:, :, None], 1)
    grad_router, grad_from_router, unused = linear_back(grad_logits, moe_in, w_router)
    grad_moe_in = (grad_moe_in + grad_from_router).reshape(num_latents, PATCHES, D)
    grad_middle = grad_state + norm_back(
        grad_moe_in * (1.0 + kept.scale_moe), kept.normed_two, kept.inv_two
    )
    grad_gate_attn = jnp.sum(kept.attn_out * grad_middle, 1)
    grad_proj, grad_attended, grad_b_proj = linear_back(
        (kept.gate_attn * grad_middle).reshape(rows_here, D), kept.attended, w_proj
    )
    grad_att_low = grad_attended.astype(jnp.bfloat16).reshape(num_latents, PATCHES, HEADS, HD)
    qkv_out = kept.qkv_out
    queries = qkv_out[:, :, 0]
    key_rows = qkv_out[:, :, 1]
    values = qkv_out[:, :, 2]
    scores = jnp.einsum(
        LQK, queries, key_rows, preferred_element_type=jnp.float32
    ) * HD ** (-0.5)
    probs = jnp.exp(scores - kept.log_totals[..., None])
    probs_low = probs.astype(jnp.bfloat16)
    grad_values = jnp.einsum(
        "lhqk,lqhd->lkhd", probs_low, grad_att_low, preferred_element_type=jnp.float32
    )
    grad_probs = jnp.einsum(
        LQK, grad_att_low, values, preferred_element_type=jnp.float32
    )
    grad_scores = (
        probs * (grad_probs - jnp.sum(probs * grad_probs, -1, keepdims=True)) * HD ** (-0.5)
    ).astype(jnp.bfloat16)
    grad_queries = jnp.einsum(
        "lhqk,lkhd->lqhd", grad_scores, key_rows, preferred_element_type=jnp.float32
    )
    grad_keys = jnp.einsum(
        "lhqk,lqhd->lkhd", grad_scores, queries, preferred_element_type=jnp.float32
    )
    grad_qkv = jnp.stack([grad_queries, grad_keys, grad_values], 2).reshape(rows_here, 3 * D)
    grad_w_qkv, grad_attn_in, grad_b_qkv = linear_back(grad_qkv, kept.attn_in, w_qkv)
    grad_attn_in = grad_attn_in.reshape(num_latents, PATCHES, D)
    grad_embedded = grad_middle + norm_back(
        grad_attn_in * (1.0 + kept.scale_attn), kept.normed_one, kept.inv_one
    )
    grad_emb_flat = grad_embedded.reshape(rows_here, D)
    grad_patch = contract(grad_emb_flat.astype(jnp.bfloat16), kept.patches, 0, 0)
    grad_b_patch = jnp.sum(grad_emb_flat, 0)
    grad_modulation = jnp.concatenate(
        [
            jnp.sum(grad_attn_in, 1),
            jnp.sum(grad_attn_in * kept.normed_one, 1),
            grad_gate_attn,
            jnp.sum(grad_moe_in, 1),
            jnp.sum(grad_moe_in * kept.normed_two, 1),
            grad_gate_moe,
        ],
        1,
    )
    grad_mod_low = grad_modulation.astype(jnp.bfloat16)
    grad_fin_low = grad_final_mod.astype(jnp.bfloat16)
    grad_act = contract(grad_mod_low, w_mod, 1, 1) + contract(grad_fin_low, w_final, 1, 1)
    grad_cond = slope_back(jax.nn.silu, kept.cond, grad_act)
    grad_cond_low = grad_cond.astype(jnp.bfloat16)
    grad_hid_time = contract(grad_cond_low, w_time2, 1, 1)
    grad_pre_time = slope_back(jax.nn.silu, kept.pre_time, grad_hid_time)
    grad_time_low = grad_pre_time.astype(jnp.bfloat16)
    mats_slabs = jnp.concatenate([grad_w_qkv, grad_proj], 1)[None]
    thin = jnp.concatenate([grad_router, grad_head, grad_patch], 1)
    grad_bias = jnp.concatenate(
        [
            grad_b_qkv,
            grad_b_proj,
            jnp.sum(grad_modulation, 0),
            grad_b_patch,
            jnp.sum(grad_pre_time, 0),
            jnp.sum(grad_cond, 0),
            jnp.sum(grad_final_mod, 0),
        ]
    )
    lows = jnp.concatenate(
        [
            kept.cond_act,
            kept.hid_time,
            grad_mod_low,
            grad_fin_low,
            grad_cond_low,
            grad_time_low,
            kept.freq_low,
        ],
        1,
    )
    return (up_slabs, down_slabs, mats_slabs, thin, grad_bias, lows, grad_cond)


def latent_grads(lows, grad_cond, labels, row_start, row_count):
    lows = lax.all_gather(lows, AXES, axis=0, tiled=True)
    grad_cond = lax.all_gather(grad_cond, AXES, axis=0, tiled=True)
    labels = lax.all_gather(labels, AXES, axis=0, tiled=True)
    cond_act, hid_time, grad_mod, grad_fin, grad_low, grad_time, freq_low = cut_pieces(
        lows, [D, D, 6 * D, 2 * D, D, D, FREQ], 1
    )

    def rows_of(member):
        return lax.dynamic_slice_in_dim(member, row_start, row_count, 1)

    label_hot = (labels[:, None] == jnp.arange(CLASSES, dtype=jnp.int32)[None, :]).astype(
        jnp.float32
    )
    grad_table = lax.dot_general(
        rows_of(grad_cond),
        label_hot,
        (((0,), (0,)), ((), ())),
        precision=lax.Precision.HIGHEST,
        preferred_element_type=jnp.float32,
    )
    return (
        contract(rows_of(cond_act), grad_mod, 0, 0),
        contract(rows_of(hid_time), grad_low, 0, 0),
        contract(rows_of(cond_act), grad_fin, 0, 0),
        contract(rows_of(grad_time), freq_low, 0, 0),
        grad_table,
    )


def factor_start(grad, row_old):
    squares = grad * grad + eps_fact
    row_new = decay * row_old + (1.0 - decay) * jnp.mean(squares, 2)
    return (row_new, jnp.sum(squares, 1), jnp.sum(row_new, 1))


def factor_update(grad, row_new, col_total, row_total, col_old, row_count):
    col_new = decay * col_old + (1.0 - decay) * (col_total / row_count)
    row_mean = row_total / row_count
    update = grad * lax.rsqrt(row_new[:, :, None] * col_new[:, None, :] / row_mean[:, None, None])
    return (col_new, update, jnp.sum(update * update, (1, 2)))


def clip_apply(master, update, square_total, entry_count):
    update_rms = jnp.sqrt(square_total / entry_count)
    return master - learn_rate * (update / jnp.maximum(1.0, update_rms / clip_level)[:, None, None])


def update_plain(grads, masters, factors, loss_part):
    mats_grad, up_grad, down_grad, bias_grad = grads
    mats, up_weights, down_weights, biases = masters
    mats_row, mats_col, up_row, up_col, down_row, down_col, bias_state = factors
    widths = column_widths()
    grad_pieces = cut_pieces(mats_grad, widths, 1)
    starts = [
        factor_start(grad_pieces[k][None], mats_row[k][None]) for k in range(len(widths))
    ]
    up_row_new, up_col_part, up_row_part = factor_start(up_grad, up_row)
    down_row_new, down_col_part, down_row_part = factor_start(down_grad, down_row)
    col_totals, row_totals, up_cols, up_rows, down_cols, down_rows, loss_total = lax.psum(
        (
            jnp.concatenate([member[1] for member in starts], 1)[0],
            jnp.concatenate([member[2] for member in starts], 0),
            up_col_part,
            up_row_part,
            down_col_part,
            down_row_part,
            loss_part,
        ),
        AXES,
    )
    col_total_pieces = cut_pieces(col_totals, widths, 0)
    col_old_pieces = cut_pieces(mats_col, widths, 0)
    steps = [
        factor_update(
            grad_pieces[k][None],
            starts[k][0],
            col_total_pieces[k][None],
            row_totals[k][None],
            col_old_pieces[k][None],
            D,
        )
        for k in range(len(widths))
    ]
    up_col_new, up_update, up_square = factor_update(
        up_grad, up_row_new, up_cols, up_rows, up_col, D
    )
    down_col_new, down_update, down_square = factor_update(
        down_grad, down_row_new, down_cols, down_rows, down_col, FF
    )
    bias_state_new = decay * bias_state + (1.0 - decay) * (bias_grad * bias_grad + eps_fact)
    bias_update = bias_grad * lax.rsqrt(bias_state_new)
    square_mats, square_up, square_down, square_bias = lax.psum(
        (
            jnp.concatenate([member[2] for member in steps], 0),
            up_square,
            down_square,
            jnp.sum(bias_update * bias_update),
        ),
        AXES,
    )
    master_pieces = cut_pieces(mats, widths, 1)
    mats_new = jnp.concatenate(
        [
            clip_apply(
                master_pieces[k][None], steps[k][1], square_mats[k][None], D * widths[k]
            )[0]
            for k in range(len(widths))
        ],
        1,
    )
    up_new = clip_apply(up_weights, up_update, square_up, D * FF)
    down_new = clip_apply(down_weights, down_update, square_down, D * FF)
    bias_rms = jnp.sqrt(square_bias / (15 * D))
    bias_new = biases - learn_rate * (bias_update / jnp.maximum(1.0, bias_rms / clip_level))
    return (
        loss_total,
        mats_grad,
        mats_new,
        mats_new.astype(jnp.bfloat16),
        jnp.concatenate([member[0] for member in starts], 0),
        jnp.concatenate([member[0][0] for member in steps], 0),
        up_grad,
        up_new,
        up_new.astype(jnp.bfloat16),
        up_row_new,
        up_col_new,
        down_grad,
        down_new,
        down_new.astype(jnp.bfloat16),
        down_row_new,
        down_col_new,
        bias_grad,
        bias_new,
        bias_new.astype(jnp.bfloat16),
        bias_state_new,
    )


def body(
    latents,
    noise,
    timesteps,
    labels,
    routes,
    mats,
    up_weights,
    down_weights,
    biases,
    *factors,
):
    rows_here = mats.shape[0]
    total_tokens = latents.shape[0] * PATCHES * lax.axis_size(AXES)
    masters = (mats, up_weights, down_weights, biases)
    if lax.axis_size(WIDE) == WIDE_PIECES and lax.axis_size(NARROW) == NARROW_PIECES:
        fused = forward_fused(
            mats, up_weights, down_weights, biases, latents, noise, timesteps, labels
        )
        loss_part, (sums, turned, lat, bias_sum) = backward_fused(
            fused, latents, noise, labels, routes, total_tokens
        )
        return update_kernel_call(
            sums, turned, lat, bias_sum, masters, factors, loss_part, total_tokens
        )
    else:
        flat = jnp.concatenate([mats.reshape(-1), biases], 0).astype(jnp.bfloat16)
        flat = lax.all_gather(flat, AXES, axis=0, tiled=False)
        gathered = split_weights(
            (
                flat[:, : rows_here * mats.shape[1]].reshape(-1, mats.shape[1]),
                lax.all_gather(up_weights.astype(jnp.bfloat16), AXES, axis=1, tiled=True),
                lax.all_gather(down_weights.astype(jnp.bfloat16), AXES, axis=1, tiled=True),
                flat[:, rows_here * mats.shape[1] :].reshape(-1),
            )
        )
        kept = forward(gathered, latents, noise, timesteps, labels, routes)
        members = backward(gathered, kept, total_tokens)
        up_slabs, down_slabs, mats_slabs, thin, grad_bias, lows, grad_cond = members
        loss_part = jnp.sum(kept.errors * kept.errors)
        grads = plain_grads(
            down_slabs, up_slabs, mats_slabs, thin, grad_bias, lows, grad_cond, labels, rows_here
        )
        outs = update_plain(grads, masters, factors, loss_part)
    return (outs[0] / total_tokens,) + tuple(outs[1:])


def solution(mesh):
    rows = P(AXES, None)
    middle_rows = P(None, AXES, None)
    row_factor = P(None, AXES)
    line = P(AXES)
    in_specs = (
        (rows, rows, line, line, rows)
        + (rows, middle_rows, middle_rows, line)
        + (row_factor, P(), row_factor, P(), row_factor, P(), line)
    )
    out_specs = (
        (P(), rows, rows, rows, row_factor, P())
        + (middle_rows, middle_rows, middle_rows, row_factor, P()) * 2
        + (line, line, line, line)
    )
    return jax.shard_map(body, mesh=mesh, in_specs=in_specs, out_specs=out_specs, check_vma=False)
```
